32 devices in a mesh: dp: 8 (over y, x, core), tensor: 4 (over z).
Axes of the slice: x: 2, y: 2, z: 4, core: 2. Of those that a mesh axis runs over, the one named last changes fastest.
Arguments:
- block_input: bfloat16 [8192, 2048], P(('dp', 'tensor')), may hold values from -6 to 6
- cotangent: bfloat16 [8192, 2048], P(('dp', 'tensor')), may hold values from -6 to 6
- noise_embed: bfloat16 [32, 2048], P('dp'), may hold values from -6 to 6
- image_sizes: int32 [8, 4], P('dp'), may hold values from 0 to 1024, as said below
- attend_weight: bfloat16 [2048, 6144], P('dp', 'tensor'), may hold values from -0.125 to 0.125
- merge_weight: bfloat16 [2048, 2048], P('tensor', 'dp'), may hold values from -1 to 1
- up_weight: bfloat16 [2048, 8192], P('dp', 'tensor'), may hold values from -0.125 to 0.125
- down_weight: bfloat16 [8192, 2048], P('tensor', 'dp'), may hold values from -0.125 to 0.125
- modulate_weight: bfloat16 [2048, 12288], P('dp', 'tensor'), may hold values from -0.1875 to 0.1875
Outputs:
- block_output: bfloat16 [8192, 2048], P(('dp', 'tensor'))
- input_grad: bfloat16 [8192, 2048], P(('dp', 'tensor'))
- noise_grad: float32 [32, 2048], P('dp')
- attend_grad: float32 [2048, 6144], P('dp', 'tensor')
- merge_grad: float32 [2048, 2048], P('tensor', 'dp')
- up_grad: float32 [2048, 8192], P('dp', 'tensor')
- down_grad: float32 [8192, 2048], P('tensor', 'dp')
- modulate_grad: float32 [2048, 12288], P('dp', 'tensor')
The draws below stay inside these ranges and needn't reach their ends.
Inputs may be any that keep to these rules, and one draw needn't show every extreme that they name: `image_sizes`: each row lists the token counts of one bucket's images in order, each a multiple of 256, the first one nonzero; a row sums to at most 1024, and some row holds one image of 1024 tokens and empty slots.
All inputs are finite; a program needn't handle non-finite values.
Results may differ from the reference program's by a relative error of at most 0.02.
The reference program's roundings to bfloat16 on the way count: a program that leaves them out, or rounds other values in their place, can miss the bound.
Values may be sent and summed in bfloat16 or wider, within the bound.
A program may use at most 320 MiB of HBM per device.

```python
import jax
import jax.numpy as jnp
from jax import lax

D = 2048
HEADS = 16
HEAD_DIM = 128
FF = 8192
TOK_DEV = 1024
IMG_DEV = 4
TOKENS = 8192
IMAGES = 32
N_DP = 8


def draw_image_sizes(key, part):
    groups = IMAGES // IMG_DEV
    unit_size = TOK_DEV // 4
    first_key, second_key, third_key = jax.random.split(key, 3)
    leading = jax.random.randint(first_key, (groups, 1), 1, 5)
    trailing = jax.random.randint(third_key, (groups, IMG_DEV - 1), 0, 5)
    units = jnp.concatenate([leading, trailing], axis=1).astype(jnp.int32)
    before = jnp.cumsum(units, axis=1) - units
    capped = jnp.clip(jnp.minimum(units, 4 - before), 0, 4)
    counts = unit_size * capped
    full_row = jax.random.randint(second_key, (), 0, groups)
    row_ids = jnp.arange(groups)[:, None]
    slot_ids = jnp.arange(IMG_DEV)[None, :]
    single_image = jnp.where(slot_ids == 0, TOK_DEV, 0)
    return jnp.where(row_ids == full_row, single_image, counts).astype(jnp.int32)


def with_spikes(array, key, source, target, blocks, factor):
    owner, partner = [(jnp.arange(array.shape[axis_at]) // (array.shape[axis_at] // blocks)).reshape([-1 if axis == axis_at else 1 for axis in range(array.ndim)]) for axis_at in (source, target)]
    chosen = jax.random.permutation(key, blocks)[partner]
    strong = (owner == chosen) | (owner == (partner + blocks // 2) % blocks)
    return jnp.where(strong, factor * array, array)


def steps_of(own_key, extent, shards, low, top_value):
    def one(axis_at, shards_of):
        draws = jax.random.uniform(jax.random.fold_in(jax.random.fold_in(own_key, 6), axis_at), (shards_of,), jnp.float32, low / len(shards), top_value / len(shards))
        return jnp.repeat(jnp.exp(draws), extent[axis_at] // shards_of).reshape((-1,) + (1,) * (len(extent) - axis_at - 1))

    loudness = one(*shards[0])
    for cut in shards[1:]:
        loudness = loudness * one(*cut)
    return loudness


def bell_draw(rng, extent, width, most, cuts=(), held_as=jnp.bfloat16):
    drawn = width * jax.random.normal(rng, extent, jnp.float32)
    if cuts:
        drawn = drawn * steps_of(rng, extent, cuts, -0.22, 0.18)
    return jnp.clip(drawn, -most, most).astype(held_as)


def noise_with(rng, dims, spread, reach, cuts, heavy, kind=jnp.bfloat16):
    values = spread * jax.random.normal(rng, dims, jnp.float32)
    if cuts:
        values = values * steps_of(rng, dims, cuts, -0.22, 0.18)
    return jnp.clip(with_spikes(values, jax.random.fold_in(rng, 3), *heavy), -reach, reach).astype(kind)


def setup_inputs(seed: int = 0) -> dict:
    key_list = jax.random.split(jax.random.key(seed), 10)
    return {
        "block_input": noise_with(key_list[0], (TOKENS, D), 1.0, 6.0, ((0, 32),), (0, 1, 32, 2.75)),
        "cotangent": noise_with(key_list[1], (TOKENS, D), 1.0, 6.0, ((0, 32),), (0, 1, 32, 2.75)),
        "noise_embed": bell_draw(key_list[2], (IMAGES, D), 1.0, 6.0, ((0, 8),)),
        "image_sizes": draw_image_sizes(jax.random.fold_in(key_list[9], 71), 0),
        "attend_weight": bell_draw(key_list[4], (D, 3 * HEADS * HEAD_DIM), D ** -0.5, 0.125, ((0, 8), (1, 4))),
        "merge_weight": bell_draw(key_list[5], (HEADS * HEAD_DIM, D), (D // 64) ** -0.5, 1.0, ((0, 4), (1, 8))),
        "up_weight": bell_draw(key_list[6], (D, FF), D ** -0.5, 0.125, ((0, 8), (1, 4))),
        "down_weight": bell_draw(key_list[7], (FF, D), (FF // 4) ** -0.5, 0.125, ((0, 4), (1, 8))),
        "modulate_weight": bell_draw(key_list[8], (D, 6 * D), (D // 2) ** -0.5, 0.1875, ((0, 8), (1, 4))),
    }


@jax.custom_vjp
def low(v):
    return lax.optimization_barrier(v.astype(jnp.bfloat16)).astype(jnp.float32)

@jax.custom_vjp
def low_back(v):
    return v

def low_keep(v):
    return (low(v), None)

def low_pass(kept, grad):
    return (grad,)

def back_keep(v):
    return (v, None)

def back_low(kept, grad):
    return (low(grad),)
low.defvjp(low_keep, low_pass)
low_back.defvjp(back_keep, back_low)
exact_mode = lax.Precision.HIGHEST

def normalize(values):
    return values * lax.rsqrt(lax.optimization_barrier(jnp.mean(values * values, axis=-1, keepdims=True)) + 1e-06)

def layer(inputs, noise, sizes_row, attend, merge, upward, downward, modulate):
    tokens = inputs.shape[0]
    ends = jnp.cumsum(sizes_row).astype(jnp.int32)
    places = jnp.arange(tokens, dtype=jnp.int32)
    image_of = lax.optimization_barrier(jnp.sum((places[:, None] >= ends[None, :]).astype(jnp.int32), axis=1))
    select = (image_of[:, None] == jnp.arange(IMG_DEV, dtype=jnp.int32)[None, :]).astype(jnp.float32)
    noise_low = low(jax.nn.silu(noise))
    modulation = low_back(jnp.dot(noise_low, modulate, precision=exact_mode))
    parts = [jnp.dot(select, modulation[:, number * D:(number + 1) * D], precision=exact_mode) for number in range(6)]
    shift_first, scale_first, gate_first, shift_second, scale_second, gate_second = parts
    hidden_first = low(normalize(inputs) * (1.0 + scale_first) + shift_first)
    packed = jnp.dot(hidden_first, attend, precision=exact_mode).reshape(tokens, HEADS, 3, HEAD_DIM)
    queries = low_back(low(packed[:, :, 0]))
    keys = low_back(low(packed[:, :, 1]))
    values = low_back(low(packed[:, :, 2]))
    scores = jnp.einsum('qhd,khd->hqk', queries, keys, precision=exact_mode) * HEAD_DIM ** (-0.5)
    scores = low_back(scores)
    same_image = image_of[:, None] == image_of[None, :]
    scores = jnp.where(same_image[None], scores, -1e+30)
    highest = lax.optimization_barrier(jnp.max(scores, axis=-1, keepdims=True))
    powers = jnp.exp(scores - highest)
    probs = low(powers / lax.optimization_barrier(jnp.sum(powers, axis=-1, keepdims=True)))
    attended = jnp.einsum('hqk,khd->qhd', probs, values, precision=exact_mode)
    attended = low_back(low(attended)).reshape(tokens, HEADS * HEAD_DIM)
    attn_out = low_back(jnp.dot(attended, merge, precision=exact_mode))
    middle = inputs + gate_first * attn_out
    hidden_second = low(normalize(middle) * (1.0 + scale_second) + shift_second)
    pre_act = low_back(jnp.dot(hidden_second, upward, precision=exact_mode))
    activated = low(jax.nn.gelu(pre_act, approximate=False))
    mlp_out = low_back(jnp.dot(activated, downward, precision=exact_mode))
    return middle + gate_second * mlp_out

def reference(block_input, cotangent, noise_embed, image_sizes, attend_weight, merge_weight, up_weight, down_weight, modulate_weight):
    weights = (attend_weight.astype(jnp.float32), merge_weight.astype(jnp.float32), up_weight.astype(jnp.float32), down_weight.astype(jnp.float32), modulate_weight.astype(jnp.float32))
    inputs = block_input.astype(jnp.float32).reshape(N_DP, TOK_DEV, D)
    cotan_all = cotangent.astype(jnp.float32).reshape(N_DP, TOK_DEV, D)
    noise_all = noise_embed.astype(jnp.float32).reshape(N_DP, IMG_DEV, D)

    def bucket_step(running, pieces):
        rows_now, cotan_now, noise_now, sizes_now = pieces

        def forward(inputs_now, noise_in, attend, merge, upward, downward, modulate):
            return layer(inputs_now, noise_in, sizes_now, attend, merge, upward, downward, modulate)
        result, pull_back = jax.vjp(forward, rows_now, noise_now, *weights)
        grads = pull_back(cotan_now)
        running = tuple((total + grad for total, grad in zip(running, grads[2:])))
        return (running, (result, grads[0], grads[1]))
    zeros = tuple((jnp.zeros_like(weight) for weight in weights))
    sums, stacked = lax.scan(bucket_step, zeros, (inputs, cotan_all, noise_all, image_sizes))
    results, input_grads, noise_grads = stacked
    return (results.reshape(TOKENS, D).astype(jnp.bfloat16), input_grads.reshape(TOKENS, D).astype(jnp.bfloat16), noise_grads.reshape(IMAGES, D), sums[0], sums[1], sums[2], sums[3], sums[4])
```

```python
import jax
import jax.numpy as jnp
from jax import lax
from jax.sharding import PartitionSpec as P

HEAD_DIM = 128
MASKED = -1e30


def normalize(values):
    return values * lax.rsqrt(jnp.mean(values * values, axis=-1, keepdims=True) + 1e-06)


def modulate_rows(values, scale_part, shift_part):
    return normalize(values) * (1.0 + scale_part) + shift_part


def gelu_exact(values):
    return jax.nn.gelu(values, approximate=False)


def dot(a, b, dims=(((1,), (0,)), ((), ()))):
    return lax.dot_general(a, b, dims, preferred_element_type=jnp.float32)


ROWS_ROWS = (((0,), (0,)), ((), ()))
COLS_COLS = (((1,), (1,)), ((), ()))


def gather_line(own, n, i):
    to_right, to_left = own, own
    lefts, rights = [own], [own]
    for step in range(1, n):
        to_right = lax.ppermute(to_right, "tensor", [(j, j + 1) for j in range(step - 1, n - 1)])
        to_left = lax.ppermute(to_left, "tensor", [(j, j - 1) for j in range(1, n - step + 1)])
        lefts.append(to_right)
        rights.append(to_left)
    return [own] + [jnp.where(i >= s, lefts[s], rights[n - s]) for s in range(1, n)]


def scatter_line(parts, n):
    from_left = from_right = None
    for m in range(n - 1, 0, -1):
        right_part, left_part = parts[n - m], parts[m]
        if from_left is not None:
            right_part = right_part + from_left
            left_part = left_part + from_right
        from_left = lax.ppermute(
            right_part.astype(jnp.bfloat16), "tensor", [(j, j + 1) for j in range(n - m)]
        ).astype(jnp.float32)
        from_right = lax.ppermute(
            left_part.astype(jnp.bfloat16), "tensor", [(j, j - 1) for j in range(m, n)]
        ).astype(jnp.float32)
    return parts[0] + from_left + from_right if from_left is not None else parts[0]


def head_scores(query_part, keys, image_rows, image_of, score_scale):
    scores = (
        jnp.einsum("qhd,khd->hqk", query_part, keys, preferred_element_type=jnp.float32)
        * score_scale
    )
    same_image = image_rows[:, None] == image_of[None, :]
    return jnp.where(same_image[None], scores, MASKED)


def attention_forward(queries, keys, values, image_of, block_rows, score_scale):
    outputs = []
    log_parts = []
    for number in range(queries.shape[0] // block_rows):
        rows = slice(number * block_rows, (number + 1) * block_rows)
        scores = head_scores(queries[rows], keys, image_of[rows], image_of, score_scale)
        highest = jnp.max(scores, axis=-1, keepdims=True)
        powers = jnp.exp(scores - highest)
        totals = jnp.sum(powers, axis=-1, keepdims=True)
        probs = powers / totals
        log_parts.append(highest + jnp.log(totals))
        outputs.append(
            jnp.einsum(
                "hqk,khd->qhd",
                probs.astype(jnp.bfloat16),
                values,
                preferred_element_type=jnp.float32,
            ).astype(jnp.bfloat16)
        )
    return (jnp.concatenate(outputs, axis=0), log_parts)


def attention_backward(
    queries, keys, values, grad_out, image_of, log_parts, block_rows, score_scale
):
    key_grad = jnp.zeros(keys.shape, jnp.float32)
    value_grad = jnp.zeros(values.shape, jnp.float32)
    query_grads = []
    for number in range(queries.shape[0] // block_rows):
        rows = slice(number * block_rows, (number + 1) * block_rows)
        query_part = queries[rows]
        grad_part = grad_out[rows]
        scores = head_scores(query_part, keys, image_of[rows], image_of, score_scale)
        probs = jnp.exp(scores - log_parts[number])
        grad_probs = jnp.einsum(
            "qhd,khd->hqk", grad_part, values, preferred_element_type=jnp.float32
        )
        inner = jnp.sum(probs * grad_probs, axis=-1, keepdims=True)
        grad_scores = (probs * (grad_probs - inner)).astype(jnp.bfloat16)
        query_grads.append(
            (
                jnp.einsum("hqk,khd->qhd", grad_scores, keys, preferred_element_type=jnp.float32)
                * score_scale
            ).astype(jnp.bfloat16)
        )
        key_grad = (
            key_grad
            + jnp.einsum(
                "hqk,qhd->khd", grad_scores, query_part, preferred_element_type=jnp.float32
            )
            * score_scale
        )
        value_grad = value_grad + jnp.einsum(
            "hqk,qhd->khd",
            probs.astype(jnp.bfloat16),
            grad_part,
            preferred_element_type=jnp.float32,
        )
    query_all = jnp.concatenate(query_grads, axis=0)
    stacked = jnp.stack(
        [query_all, key_grad.astype(jnp.bfloat16), value_grad.astype(jnp.bfloat16)], axis=2
    )
    return stacked.reshape(queries.shape[0], -1)


def on_device(
    block_input,
    cotangent,
    noise_embed,
    image_sizes,
    attend_weight,
    merge_weight,
    up_weight,
    down_weight,
    modulate_weight,
):
    n = lax.axis_size("tensor")
    n_dp = lax.axis_size("dp")
    place = lax.axis_index("tensor")
    dp_place = lax.axis_index("dp")
    rows, width = block_input.shape
    tokens = n * rows
    images = image_sizes.shape[1]
    k_rows = modulate_weight.shape[0]

    noise_all = lax.all_gather(noise_embed, "dp", axis=0, tiled=True)
    noise_low_all = jax.nn.silu(noise_all.astype(jnp.float32)).astype(jnp.bfloat16)
    noise_low_cols = lax.dynamic_slice_in_dim(noise_low_all, dp_place * k_rows, k_rows, 1)
    modulation_terms = dot(noise_low_cols, modulate_weight)
    modulation_cols = lax.psum_scatter(modulation_terms, "dp", scatter_dimension=0, tiled=True)
    modulation = lax.all_gather(modulation_cols, "tensor", axis=1, tiled=True)

    attend_full = lax.all_gather(attend_weight, "dp", axis=0, tiled=True)
    merge_full = lax.all_gather(merge_weight, "dp", axis=1, tiled=True)
    up_full = lax.all_gather(up_weight, "dp", axis=0, tiled=True)
    down_full = lax.all_gather(down_weight, "dp", axis=1, tiled=True)

    sizes_row = image_sizes[0]
    ends = [sum(sizes_row[j] for j in range(last + 1)) for last in range(images)]

    def image_at(places):
        return sum((places >= end).astype(jnp.int32) for end in ends)

    blocks = [lax.rem(place - s + n, n) for s in range(n)]
    own_images = image_at(place * rows + jnp.arange(rows, dtype=jnp.int32))
    image_of = jnp.concatenate(
        [image_at(block * rows + jnp.arange(rows, dtype=jnp.int32)) for block in blocks]
    )
    select = [(own_images == j).astype(jnp.float32)[:, None] for j in range(images)]

    def per_slot(number):
        table = modulation[:, number * width : (number + 1) * width]
        return sum(select[j] * table[j : j + 1] for j in range(images))

    shift_first, scale_first, gate_first, shift_second, scale_second, gate_second = [
        per_slot(number) for number in range(6)
    ]
    inputs = block_input.astype(jnp.float32)
    grad_rows = cotangent.astype(jnp.float32)
    hidden_first_f, back_first = jax.vjp(modulate_rows, inputs, scale_first, shift_first)
    hidden_first = gather_line(hidden_first_f.astype(jnp.bfloat16), n, place)
    d_mlp = gather_line((gate_second * grad_rows).astype(jnp.bfloat16), n, place)

    heads_local = attend_full.shape[1] // (3 * HEAD_DIM)
    packed = jnp.concatenate([dot(part, attend_full).astype(jnp.bfloat16) for part in hidden_first])
    packed = packed.reshape(tokens, heads_local, 3, HEAD_DIM)
    queries, keys, values = packed[:, :, 0], packed[:, :, 1], packed[:, :, 2]
    block_rows = min(512, tokens)
    score_scale = HEAD_DIM ** (-0.5)
    attended3, log_parts = attention_forward(
        queries, keys, values, image_of, block_rows, score_scale
    )
    attended = attended3.reshape(tokens, heads_local * HEAD_DIM)

    def slots(array):
        return [array[s * rows : (s + 1) * rows] for s in range(n)]

    attn_out = scatter_line([dot(part, merge_full) for part in slots(attended)], n)
    middle = inputs + gate_first * attn_out
    hidden_second_f, back_second = jax.vjp(modulate_rows, middle, scale_second, shift_second)
    hidden_second = gather_line(hidden_second_f.astype(jnp.bfloat16), n, place)
    activated, mlp_terms, d_pre, d_hidden_terms = [], [], [], []
    for s in range(n):
        pre_act = dot(hidden_second[s], up_full)
        activated_f, gelu_back = jax.vjp(gelu_exact, pre_act)
        activated.append(activated_f.astype(jnp.bfloat16))
        mlp_terms.append(dot(activated[s], down_full))
        d_act = dot(d_mlp[s], down_full, COLS_COLS)
        d_pre.append(gelu_back(d_act)[0].astype(jnp.bfloat16))
        d_hidden_terms.append(dot(d_pre[s], up_full, COLS_COLS))
    d_hidden_second = scatter_line(d_hidden_terms, n)
    mlp_out = scatter_line(mlp_terms, n)
    block_output = (middle + gate_second * mlp_out).astype(jnp.bfloat16)
    d_gate_second = grad_rows * mlp_out
    d_mid_norm, d_scale_second, d_shift_second = back_second(d_hidden_second)
    d_middle = grad_rows + d_mid_norm
    d_gate_first = d_middle * attn_out
    d_attn_parts = gather_line((gate_first * d_middle).astype(jnp.bfloat16), n, place)
    d_attn = jnp.concatenate(d_attn_parts)

    down_local = dot(jnp.concatenate(activated), jnp.concatenate(d_mlp), ROWS_ROWS)
    up_local = dot(jnp.concatenate(hidden_second), jnp.concatenate(d_pre), ROWS_ROWS)
    down_part = lax.psum_scatter(
        down_local.astype(jnp.bfloat16), "dp", scatter_dimension=1, tiled=True
    ).astype(jnp.float32)
    up_part = lax.psum_scatter(
        up_local.astype(jnp.bfloat16), "dp", scatter_dimension=0, tiled=True
    ).astype(jnp.float32)

    merge_local = dot(attended, d_attn, ROWS_ROWS)
    merge_part = lax.psum_scatter(
        merge_local.astype(jnp.bfloat16), "dp", scatter_dimension=1, tiled=True
    ).astype(jnp.float32)
    d_attended = dot(d_attn, merge_full, COLS_COLS).astype(jnp.bfloat16)
    d_qkv = attention_backward(
        queries,
        keys,
        values,
        d_attended.reshape(tokens, heads_local, HEAD_DIM),
        image_of,
        log_parts,
        block_rows,
        score_scale,
    )
    attend_local = dot(jnp.concatenate(hidden_first), d_qkv, ROWS_ROWS)
    attend_part = lax.psum_scatter(
        attend_local.astype(jnp.bfloat16), "dp", scatter_dimension=0, tiled=True
    ).astype(jnp.float32)
    d_hidden_first = scatter_line([dot(part, attend_full, COLS_COLS) for part in slots(d_qkv)], n)
    d_in_norm, d_scale_first, d_shift_first = back_first(d_hidden_first)
    input_grad = (d_middle + d_in_norm).astype(jnp.bfloat16)

    token_grads = [
        d_shift_first,
        d_scale_first,
        d_gate_first,
        d_shift_second,
        d_scale_second,
        d_gate_second,
    ]
    image_rows = [
        jnp.concatenate(
            [jnp.sum(part * select[j], axis=0, keepdims=True) for part in token_grads], axis=1
        )
        for j in range(images)
    ]
    d_mod_terms = jnp.concatenate(image_rows, axis=0)
    d_mod_cols = lax.psum_scatter(
        d_mod_terms, "tensor", scatter_dimension=1, tiled=True
    ).astype(jnp.bfloat16)
    d_mod_all = lax.all_gather(d_mod_cols, "dp", axis=0, tiled=True)
    modulate_part = dot(noise_low_cols, d_mod_all, ROWS_ROWS)
    noise_terms = dot(d_mod_all, modulate_weight, COLS_COLS)
    noise_cols = lax.psum(noise_terms, "tensor")
    noise_sum = lax.all_to_all(noise_cols, "dp", split_axis=0, concat_axis=1, tiled=True)
    silu_back = jax.vjp(jax.nn.silu, noise_embed.astype(jnp.float32))[1]
    noise_grad = silu_back(noise_sum)[0]
    return (
        block_output,
        input_grad,
        noise_grad,
        attend_part,
        merge_part,
        up_part,
        down_part,
        modulate_part,
    )


def solution(mesh):
    whole_rows = P(("dp", "tensor"), None)
    by_dp = P("dp", None)
    tall = P("dp", "tensor")
    wide = P("tensor", "dp")
    return jax.shard_map(
        on_device,
        mesh=mesh,
        in_specs=(whole_rows, whole_rows, by_dp, by_dp, tall, wide, tall, wide, tall),
        out_specs=(whole_rows, whole_rows, by_dp, tall, wide, tall, wide, tall),
        check_vma=False,
    )
```

```python
import functools
import math

import jax
import jax.numpy as jnp
from jax import lax
from jax.experimental import pallas as pl
from jax.experimental.pallas import tpu as pltpu
from jax.sharding import PartitionSpec as P

HEAD_DIM = 128
MASKED = -1e30


def normalize(values):
    return values * lax.rsqrt(jnp.mean(values * values, axis=-1, keepdims=True) + 1e-06)


def modulate_rows(values, scale_part, shift_part):
    return normalize(values) * (1.0 + scale_part) + shift_part


def gelu_exact(values):
    return jax.nn.gelu(values, approximate=False)


def dot(a, b, dims=(((1,), (0,)), ((), ()))):
    return lax.dot_general(a, b, dims, preferred_element_type=jnp.float32)


ROWS_ROWS = (((0,), (0,)), ((), ()))
COLS_COLS = (((1,), (1,)), ((), ()))


MESH = pl.DeviceIdType.MESH
HBM = pl.BlockSpec(memory_space=pl.ANY)
VMEM = pl.BlockSpec(memory_space=pltpu.VMEM)
DMA = pltpu.SemaphoreType.DMA


def rows_of(j, rows):
    return pl.ds(pl.multiple_of(j * rows, rows), rows)


def beside(step):
    return (lax.axis_index("dp"), lax.axis_index("tensor") + step)


def greet_line(n, i):
    barrier = pltpu.get_barrier_semaphore()

    @pl.when(i > 0)
    def _():
        pl.semaphore_signal(barrier, inc=1, device_id=beside(-1), device_id_type=MESH)

    @pl.when(i < n - 1)
    def _():
        pl.semaphore_signal(barrier, inc=1, device_id=beside(1), device_id_type=MESH)

    pl.semaphore_wait(barrier, jnp.where(i > 0, 1, 0) + jnp.where(i < n - 1, 1, 0))


class LineGather:
    def __init__(self, n, i, rows, own, full, to_left, to_right, arrived):
        self.n, self.i, self.rows, self.own, self.full = n, i, rows, own, full
        self.to_left, self.to_right, self.arrived = to_left, to_right, arrived

    def copy(self, j, step, source=None):
        place = self.full.at[rows_of(j, self.rows)]
        return pltpu.make_async_remote_copy(
            src_ref=place if source is None else source,
            dst_ref=place,
            send_sem=(self.to_right if step > 0 else self.to_left).at[j],
            recv_sem=self.arrived.at[j],
            device_id=beside(step),
            device_id_type=MESH,
        )

    def start(self):
        @pl.when(self.i > 0)
        def _():
            self.copy(self.i, -1, self.own).start()

        @pl.when(self.i < self.n - 1)
        def _():
            self.copy(self.i, 1, self.own).start()

    def step(self, s):
        for side in (-1, 1):
            j = self.i + side * s
            there = (j >= 0) & (j < self.n)
            more = (self.i > 0) if side > 0 else (self.i < self.n - 1)

            @pl.when(there)
            def _():
                self.copy(j, side).wait_recv()

            @pl.when(there & more)
            def _():
                self.copy(j, -side).start()

    def finish(self):
        @pl.when(self.i > 0)
        def _():
            self.copy(self.i, -1, self.own).wait_send()

        @pl.when(self.i < self.n - 1)
        def _():
            self.copy(self.i, 1, self.own).wait_send()

        for j in range(self.n):

            @pl.when((j < self.i) & (self.i < self.n - 1))
            def _():
                self.copy(j, 1).wait_send()

            @pl.when((j > self.i) & (self.i > 0))
            def _():
                self.copy(j, -1).wait_send()


class LineScatter:
    def __init__(self, n, i, rows, width, part, got, sent, arrived):
        self.n, self.i, self.rows, self.width = n, i, rows, width
        self.part, self.got, self.sent, self.arrived = part, got, sent, arrived
        self.pieces = part.shape[1] // width

    def columns(self, c):
        return pl.ds(pl.multiple_of(c * self.width, self.width), self.width)

    def copy(self, j, slot, c, step):
        return pltpu.make_async_remote_copy(
            src_ref=self.part.at[rows_of(j, self.rows), self.columns(c)],
            dst_ref=self.got.at[rows_of(slot, self.rows), self.columns(c)],
            send_sem=self.sent.at[j, c],
            recv_sem=self.arrived.at[slot, c],
            device_id=beside(step),
            device_id_type=MESH,
        )

    def slot_there(self, j, step):
        if step > 0:
            return j
        return jnp.where(j == self.i - 1, self.n, j)

    def at_end(self, j, c):
        @pl.when((self.i == 0) & (j > 0))
        def _():
            self.copy(j, j, c, 1).start()

        @pl.when((self.i == self.n - 1) & (j < self.i))
        def _():
            self.copy(j, self.slot_there(j, -1), c, -1).start()

    def pass_on(self, t, c, near):
        n, i = self.n, self.i
        rightward = (2 * i < n - 1) if near else (2 * i >= n - 1)
        j = jnp.where(rightward, t, n - 1 - t)
        step = jnp.where(rightward, 1, -1)
        right = rightward & (i > 0) & (j > i)
        left = jnp.logical_not(rightward) & (i < n - 1) & (j < i)

        @pl.when(right | left)
        def _():
            self.add(j, j, c)
            slot = jnp.where(left & (j == i - 1), n, j)
            self.copy(j, slot, c, step).start()

    def add(self, j, slot, c):
        self.copy(j, slot, c, 1).wait_recv()
        here = (rows_of(j, self.rows), self.columns(c))
        there = (rows_of(slot, self.rows), self.columns(c))
        total = self.part[here].astype(jnp.float32) + self.got[there].astype(jnp.float32)
        self.part[here] = total.astype(self.part.dtype)

    def own(self, c, out):
        i, n = self.i, self.n
        columns = self.columns(c)
        out[:, columns] = self.part[rows_of(i, self.rows), columns].astype(out.dtype)

        @pl.when(i > 0)
        def _():
            self.copy(i, i, c, 1).wait_recv()
            out[:, columns] += self.got[rows_of(i, self.rows), columns].astype(out.dtype)

        @pl.when(i < n - 1)
        def _():
            self.copy(i, n, c, -1).wait_recv()
            out[:, columns] += self.got[rows_of(n, self.rows), columns].astype(out.dtype)

    def all_sent(self):
        def one(j, carry):
            @pl.when(j != self.i)
            def _():
                for c in range(self.pieces):
                    self.copy(j, 0, c, 1).wait_send()

            return carry

        lax.fori_loop(0, self.n, one, 0)


def mm(a, b):
    return lax.dot_general(a, b, (((1,), (0,)), ((), ())), preferred_element_type=jnp.float32)


def mm_nt(a, b):
    return lax.dot_general(a, b, (((1,), (1,)), ((), ())), preferred_element_type=jnp.float32)


def mm_tn(a, b):
    return lax.dot_general(a, b, (((0,), (0,)), ((), ())), preferred_element_type=jnp.float32)


def call(kernel, collective_id, name, in_specs, outs, out_specs, scratch, flops=0, limit=60):
    return pl.pallas_call(
        kernel,
        out_shape=outs,
        in_specs=in_specs,
        out_specs=out_specs,
        scratch_shapes=scratch,
        compiler_params=pltpu.CompilerParams(
            collective_id=collective_id,
            has_side_effects=True,
            vmem_limit_bytes=limit * 1024 * 1024,
        ),
        cost_estimate=pl.CostEstimate(flops=flops, bytes_accessed=1 << 20, transcendentals=0),
        name=name,
    )


def gather_kernel(n, rows, count, *refs):
    own, full = refs[:count], refs[count : 2 * count]
    to_left, to_right, arrived, local = refs[2 * count :]
    i = lax.axis_index("tensor")
    copies = [
        pltpu.make_async_copy(own[a], full[a].at[rows_of(i, rows)], local.at[a])
        for a in range(count)
    ]
    for copy in copies:
        copy.start()
    greet_line(n, i)
    lines = [
        LineGather(n, i, rows, own[a], full[a], to_left.at[a], to_right.at[a], arrived.at[a])
        for a in range(count)
    ]
    for line in lines:
        line.start()
        for s in range(1, n):
            line.step(s)
    for line in lines:
        line.finish()
    for copy in copies:
        copy.wait()


def gather_rows(n, arrays, collective_id):
    count = len(arrays)
    rows, width = arrays[0].shape
    sems = [DMA((count, n))] * 3 + [DMA((count,))]
    return call(
        functools.partial(gather_kernel, n, rows, count),
        collective_id,
        "gather_rows",
        [HBM] * count,
        [jax.ShapeDtypeStruct((n * rows, width), a.dtype) for a in arrays],
        [HBM] * count,
        sems,
    )(*arrays)


def scatter_kernel(n, rows, width, parts_in, out, part, got, sent, arrived, local):
    i = lax.axis_index("tensor")
    copy = pltpu.make_async_copy(parts_in, part, local)
    copy.start()
    greet_line(n, i)
    copy.wait()
    line = LineScatter(n, i, rows, width, part, got, sent, arrived)
    for t in range(n - 1, 0, -1):
        for j in (t, n - 1 - t):
            for c in range(line.pieces):
                if j == t:
                    pl.when(i == 0)(functools.partial(line.at_end, j, c))
                else:
                    pl.when(i == n - 1)(functools.partial(line.at_end, j, c))
    for t in range(n - 1, 1, -1):
        for near in (True, False):
            for c in range(line.pieces):
                line.pass_on(t, c, near)
    for c in range(line.pieces):
        line.own(c, out)
    line.all_sent()


def scatter_rows(n, parts, collective_id, pieces=4):
    total, columns = parts.shape
    rows = total // n
    width = columns // pieces
    return call(
        functools.partial(scatter_kernel, n, rows, width),
        collective_id,
        "scatter_rows",
        [HBM],
        jax.ShapeDtypeStruct((rows, columns), jnp.float32),
        VMEM,
        [
            pltpu.VMEM((total, columns), jnp.bfloat16),
            pltpu.VMEM((total + rows, columns), jnp.bfloat16),
            DMA((n, pieces)),
            DMA((n + 1, pieces)),
            DMA,
        ],
    )(parts)


def ffn_kernel(
    n,
    tile,
    grad_tile,
    own_hidden,
    table,
    d_mlp_hbm,
    up_hbm,
    down_hbm,
    d_hidden,
    mlp_part,
    up_grad,
    down_grad,
    up,
    down,
    d_mlp,
    hidden,
    activated,
    d_pre,
    part,
    got,
    stage,
    to_left,
    to_right,
    arrived,
    sent,
    came,
    local,
    stage_sem,
):
    i = lax.axis_index("tensor")
    rows, width = own_hidden.shape
    units = up.shape[1]
    loads = [
        pltpu.make_async_copy(source, target, local.at[k])
        for k, (source, target) in enumerate(((up_hbm, up), (d_mlp_hbm, d_mlp), (down_hbm, down)))
    ]
    for load in loads:
        load.start()
    greet_line(n, i)
    line = LineGather(n, i, rows, own_hidden, hidden, to_left, to_right, arrived)
    line.start()
    sums = LineScatter(n, i, rows, tile, part, got, sent, came)
    hidden[rows_of(i, rows), :] = own_hidden[...]
    for load in loads:
        load.wait()

    def one_block(j):
        here = rows_of(j, rows)

        def gated(c, carry):
            at = pl.ds(pl.multiple_of(c * tile, tile), tile)
            d_mlp[here, at] = (d_mlp[here, at].astype(jnp.float32) * table[j, 5:6, at]).astype(
                jnp.bfloat16
            )
            return carry

        lax.fori_loop(0, width // tile, gated, 0)

        def first(c, carry):
            at = pl.ds(pl.multiple_of(c * tile, tile), tile)
            pre = mm(hidden[here, :], up[:, at])
            d_act = mm_nt(d_mlp[here, :], down[at, :])
            cdf = 0.5 * (1.0 + lax.erf(pre * (0.5**0.5)))
            density = jnp.exp(-0.5 * pre * pre) * ((0.5 / math.pi) ** 0.5)
            activated[here, at] = (pre * cdf).astype(jnp.bfloat16)
            d_pre[here, at] = (d_act * (cdf + pre * density)).astype(jnp.bfloat16)
            return carry

        lax.fori_loop(0, units // tile, first, 0)

        def second(c, carry):
            at = pl.ds(pl.multiple_of(c * tile, tile), tile)
            part[here, at] = mm_nt(d_pre[here, :], up[at, :]).astype(jnp.bfloat16)
            sums.at_end(j, c)
            return carry

        lax.fori_loop(0, width // tile, second, 0)

        def third(c, carry):
            at = pl.ds(pl.multiple_of(c * tile, tile), tile)
            mlp_part[here, at] = mm(activated[here, :], down[:, at]).astype(jnp.bfloat16)
            return carry

        lax.fori_loop(0, width // tile, third, 0)

    def visit(q, carry):
        s = (q + 1) // 2
        side = 1 - 2 * (q % 2)
        j = i + s * side

        @pl.when(q % 2 == 1)
        def _():
            line.step(s)

        @pl.when((j >= 0) & (j < n))
        def _():
            one_block(j)

        return carry

    lax.fori_loop(0, 2 * n - 1, visit, 0)

    count = (width // grad_tile) * (units // grad_tile)
    turns = 2 * max(n - 2, 1) * sums.pieces
    per_turn = -(-2 * count // turns)

    def square(ref, row, column):
        return ref.at[
            pl.ds(pl.multiple_of(row * grad_tile, grad_tile), grad_tile),
            pl.ds(pl.multiple_of(column * grad_tile, grad_tile), grad_tile),
        ]

    def put(slot, target):
        return pltpu.make_async_copy(stage.at[slot], target, stage_sem.at[slot])

    def one_grad(k, left, right, target):
        wide = right.shape[1] // grad_tile
        row, column = k // wide, k % wide
        slot = k % 2

        @pl.when(k >= 2)
        def _():
            put(slot, square(target, 0, 0)).wait()

        a = left[:, pl.ds(pl.multiple_of(row * grad_tile, grad_tile), grad_tile)]
        b = right[:, pl.ds(pl.multiple_of(column * grad_tile, grad_tile), grad_tile)]
        stage[slot] = mm_tn(a, b).astype(jnp.bfloat16)
        put(slot, square(target, row, column)).start()

    def tail(k, carry):
        t, c = 2 + k // (2 * sums.pieces), k % sums.pieces
        for near in (True, False):

            @pl.when((k // sums.pieces) % 2 == (0 if near else 1))
            def _():
                sums.pass_on(t, c, near)

        for extra in range(per_turn):
            item = k * per_turn + extra

            @pl.when(item < count)
            def _():
                one_grad(item, hidden, d_pre, up_grad)

            @pl.when(item == count)
            def _():
                for slot in range(2):
                    put(slot, square(up_grad, 0, 0)).wait()

            @pl.when((item >= count) & (item < 2 * count))
            def _():
                one_grad(item - count, activated, d_mlp, down_grad)

        return carry

    lax.fori_loop(0, turns, tail, 0)
    for slot in range(2):
        put(slot, square(down_grad, 0, 0)).wait()
    for c in range(sums.pieces):
        sums.own(c, d_hidden)
    line.finish()
    sums.all_sent()


def ffn(n, own_hidden, table, cotangents, up, down, collective_id, tile=512, grad_tile=512):
    rows, width = own_hidden.shape
    units = up.shape[1]
    pieces = width // tile
    low = jnp.bfloat16
    return call(
        functools.partial(ffn_kernel, n, tile, grad_tile),
        collective_id,
        "ffn",
        [VMEM, VMEM, HBM, HBM, HBM],
        [
            jax.ShapeDtypeStruct((rows, width), jnp.float32),
            jax.ShapeDtypeStruct((n * rows, width), low),
            jax.ShapeDtypeStruct((width, units), low),
            jax.ShapeDtypeStruct((units, width), low),
        ],
        [VMEM, VMEM, HBM, HBM],
        [
            pltpu.VMEM((width, units), low),
            pltpu.VMEM((units, width), low),
            pltpu.VMEM((n * rows, width), low),
            pltpu.VMEM((n * rows, width), low),
            pltpu.VMEM((n * rows, units), low),
            pltpu.VMEM((n * rows, units), low),
            pltpu.VMEM((n * rows, width), low),
            pltpu.VMEM(((n + 1) * rows, width), low),
            pltpu.VMEM((2, grad_tile, grad_tile), low),
            DMA((n,)),
            DMA((n,)),
            DMA((n,)),
            DMA((n, pieces)),
            DMA((n + 1, pieces)),
            DMA((3,)),
            DMA((2,)),
        ],
        flops=12 * n * rows * width * units,
    )(own_hidden, table, cotangents, up, down)


class PlaneGather:
    def __init__(self, n_dp, d, own, view, height, sent, came):
        self.n_dp, self.d, self.own, self.view, self.height = n_dp, d, own, view, height
        self.sent, self.came = sent, came
        self.square = n_dp == 8
        self.peers = [2 * k for k in range(1, n_dp // 2)]

    def copy(self, k, source, target, peer):
        return pltpu.make_async_remote_copy(
            src_ref=source,
            dst_ref=target,
            send_sem=self.sent.at[k],
            recv_sem=self.came.at[k],
            device_id=(self.d ^ peer, lax.axis_index("tensor")),
            device_id_type=MESH,
        )

    def slab(self, flip, half=None):
        if half is None:
            return self.view(self.d ^ flip, 0, self.height)
        return self.view(self.d ^ flip, half * (self.height // 2), self.height // 2)

    def owns(self):
        peers = [2, 4] if self.square else self.peers
        return [
            self.copy(k, self.own, self.slab(0), peer) for k, peer in enumerate([1] + peers)
        ]

    def relay_of(self, k):
        flip, half, peer = ((2, 0, 4), (4, 1, 2))[k - 1]
        return self.copy(2 + k, self.slab(flip, half), self.slab(flip, half), peer)

    def across(self):
        return [
            self.copy(3, self.slab(6, 0), self.slab(6, 0), 4),
            self.copy(4, self.slab(6, 1), self.slab(6, 1), 2),
        ]

    def hand(self, flip):
        base = 5 if self.square else len(self.peers) + 1
        k = base + flip // 2 - 1
        return self.copy(k, self.slab(flip), self.slab(flip), 1)

    def handed(self, flip):
        base = 5 if self.square else len(self.peers) + 1
        k = base + flip // 2 - 1
        return self.copy(k, self.slab(flip ^ 1), self.slab(flip ^ 1), 1)

    def start(self):
        for copy in self.owns():
            copy.start()

    def relay(self):
        if not self.square:
            return
        for k, flip in ((1, 2), (2, 4)):
            self.copy(k, self.own, self.slab(flip), flip).wait_recv()
            self.relay_of(k).start()
            self.hand(flip).start()

    def close(self):
        if self.square:
            for copy in self.across():
                copy.wait_recv()
            self.hand(6).start()
        else:
            for k, flip in enumerate(self.peers):
                self.copy(k + 1, self.own, self.slab(flip), flip).wait_recv()
                self.hand(flip).start()
        self.copy(0, self.own, self.slab(1), 1).wait_recv()
        for flip in self.peers:
            self.handed(flip).wait_recv()

    def finish(self):
        for copy in self.owns():
            copy.wait_send()
        if self.square:
            for k in (1, 2):
                self.relay_of(k).wait_send()
        for flip in self.peers:
            self.hand(flip).wait_send()


def plane_sems(n_dp):
    return 8 if n_dp == 8 else n_dp - 1


def greet_all(n, n_dp, d, i):
    barrier = pltpu.get_barrier_semaphore()
    for flip in range(1, n_dp):
        pl.semaphore_signal(barrier, inc=1, device_id=(d ^ flip, i), device_id_type=MESH)
    for turn in range(1, n):
        pl.semaphore_signal(
            barrier, inc=1, device_id=(d, lax.rem(i + turn, n)), device_id_type=MESH
        )
    pl.semaphore_wait(barrier, n_dp + n - 2)


def front_kernel(
    n,
    n_dp,
    heads,
    tile,
    x_own,
    cot_own,
    noise,
    mod_w,
    chosen,
    bias,
    attend_w,
    merge_w,
    up_w,
    down_w,
    cot_full,
    hidden,
    qkv,
    lse,
    attended,
    att_rows,
    attn_out,
    middle,
    hidden_second,
    table,
    attend_full,
    merge_full,
    up_full,
    down_full,
    x_full,
    attend,
    merge,
    noise_all,
    terms,
    terms_all,
    columns,
    noise_sem,
    terms_sem,
    column_sem,
    x_sem,
    cot_sem,
    merge_sem,
    weight_sent,
    weight_came,
    out_sem,
    att_sem,
    local,
):
    d, i = lax.axis_index("dp"), lax.axis_index("tensor")
    rows, width = x_own.shape
    k_rows, own_cols = mod_w.shape
    head_cols = heads * HEAD_DIM
    low, f32 = jnp.bfloat16, jnp.float32
    merge_rows, merge_cols = merge_w.shape
    down_cols = down_w.shape[1]
    merge_slab = merge.at[:, pl.ds(pl.multiple_of(d * merge_cols, merge_cols), merge_cols)]

    def row_view(full, height):
        return lambda at, start, count: full.at[
            pl.ds(pl.multiple_of(at * height + start, 16), count), :
        ]

    def column_view(full, wide):
        return lambda at, start, count: full.at[
            pl.ds(start, count), pl.ds(pl.multiple_of(at * wide, wide), wide)
        ]

    weights = [
        PlaneGather(n_dp, d, own, view, height, weight_sent.at[k], weight_came.at[k])
        for k, (own, view, height) in enumerate(
            (
                (attend_w, row_view(attend, k_rows), k_rows),
                (merge_slab, column_view(merge, merge_cols), n * merge_rows),
                (up_w, row_view(up_full, k_rows), k_rows),
                (down_w, column_view(down_full, down_cols), down_w.shape[0]),
            )
        )
    ]
    attend_g, merge_g, up_g, down_g = weights
    copies = [
        pltpu.make_async_copy(source, target, local.at[k])
        for k, (source, target) in enumerate(
            (
                (cot_own, cot_full.at[rows_of(i, rows)]),
                (attend_w, attend_g.slab(0)),
                (merge_w, merge_slab.at[rows_of(i, merge_rows)]),
                (up_w, up_g.slab(0)),
                (down_w, down_g.slab(0)),
            )
        )
    ]
    for copy in copies:
        copy.start()
    greet_all(n, n_dp, d, i)

    def to_plane(source, target, sems, flip):
        return pltpu.make_async_remote_copy(
            src_ref=source.at[d ^ flip],
            dst_ref=target.at[d],
            send_sem=sems.at[0, flip],
            recv_sem=sems.at[1, flip],
            device_id=(d ^ flip, i),
            device_id_type=MESH,
        )

    def from_plane(target, sems, flip):
        return pltpu.make_async_remote_copy(
            src_ref=target.at[d ^ flip],
            dst_ref=target.at[d ^ flip],
            send_sem=sems.at[0, flip],
            recv_sem=sems.at[1, flip],
            device_id=(d ^ flip, i),
            device_id_type=MESH,
        )

    for flip in range(1, n_dp):
        to_plane(noise, noise_all, noise_sem, flip).start()
    merge_line = LineGather(
        n, i, merge_rows, merge_w, merge_slab, merge_sem.at[0], merge_sem.at[1], merge_sem.at[2]
    )
    x_line = LineGather(n, i, rows, x_own, x_full, x_sem.at[0], x_sem.at[1], x_sem.at[2])
    cot_line = LineGather(
        n, i, rows, cot_own, cot_full, cot_sem.at[0], cot_sem.at[1], cot_sem.at[2]
    )
    x_line.start()
    attend_g.start()
    merge_line.start()
    noise_all[d] = noise[d]
    x_full[rows_of(i, rows), :] = x_own[...]
    for flip in range(1, n_dp):
        from_plane(noise_all, noise_sem, flip).wait_recv()
    images = noise_all[...].reshape(n_dp * 8, k_rows).astype(low)
    for c in range(own_cols // tile):
        terms[:, :, c * tile : (c + 1) * tile] = mm(
            images, mod_w[:, c * tile : (c + 1) * tile]
        ).reshape(n_dp, 8, tile)
    for flip in range(1, n_dp):
        to_plane(terms, terms_all, terms_sem, flip).start()
    terms_all[d] = terms[d]
    for flip in range(1, n_dp):
        from_plane(terms_all, terms_sem, flip).wait_recv()
    columns[pl.ds(pl.multiple_of(i * 8, 8), 8), :] = jnp.sum(terms_all[...], axis=0)
    own_columns = columns.at[pl.ds(pl.multiple_of(i * 8, 8), 8)]
    column_line = LineGather(
        n, i, 8, own_columns, columns, column_sem.at[0], column_sem.at[1], column_sem.at[2]
    )
    column_line.start()
    for s in range(1, n):
        column_line.step(s)
    unit = math.gcd(width, own_cols)

    def fill(j, carry):
        for number in range(6):
            for start in range(0, width, unit):
                at = number * width + start
                part = columns[at // own_cols * 8 : at // own_cols * 8 + 8, pl.ds(at % own_cols, unit)]
                table[j, number : number + 1, start : start + unit] = jnp.sum(
                    part * chosen[j][:, :1], axis=0, keepdims=True
                )
        return carry

    lax.fori_loop(0, n, fill, 0)
    x_line.step(1)
    attend_g.relay()
    merge_line.step(1)
    for copy in copies:
        copy.wait()
    attend_g.close()
    up_g.start()
    keep_attend = pltpu.make_async_copy(attend, attend_full, out_sem.at[0])
    keep_merge = pltpu.make_async_copy(merge, merge_full, out_sem.at[1])
    keep_attend.start()

    def tiles(count):
        return [slice(c * tile, (c + 1) * tile) for c in range(count // tile)]

    def one_block(j):
        here = rows_of(j, rows)
        squares = jnp.zeros((rows, 1), f32)
        for at in tiles(width):
            v = x_full[here, at].astype(f32)
            squares += jnp.sum(v * v, axis=1, keepdims=True)
        root = lax.rsqrt(squares * (1.0 / width) + 1e-06)
        for at in tiles(width):
            v = x_full[here, at].astype(f32) * root
            hidden[here, at] = (v * (1.0 + table[j, 1:2, at]) + table[j, 0:1, at]).astype(low)
        wide = qkv.shape[1]
        step = math.gcd(wide, 512)
        for c in range(wide // step):
            at = slice(c * step, (c + 1) * step)
            qkv[here, at] = mm(hidden[here, :], attend[:, at]).astype(low)

    def visit(q, carry):
        s = (q + 1) // 2
        side = 1 - 2 * (q % 2)
        j = i + s * side

        @pl.when((q % 2 == 1) & (s + 1 < n))
        def _():
            x_line.step(s + 1)
            merge_line.step(s + 1)

        @pl.when(q == 2 * n - 5)
        def _():
            up_g.relay()
            merge_g.start()
            cot_line.start()

        @pl.when((j >= 0) & (j < n))
        def _():
            one_block(j)

        return carry

    lax.fori_loop(0, 2 * n - 1, visit, 0)

    area = min(256, n * rows)
    areas = n * rows // area
    owners = area // rows

    def to_owner(j):
        return pltpu.make_async_remote_copy(
            src_ref=attended.at[rows_of(j, rows), :],
            dst_ref=att_rows.at[:, pl.ds(pl.multiple_of(i * head_cols, head_cols), head_cols)],
            send_sem=att_sem.at[0, j],
            recv_sem=att_sem.at[1, i],
            device_id=(d, j),
            device_id_type=MESH,
        )

    def from_source(t):
        return pltpu.make_async_remote_copy(
            src_ref=attended.at[rows_of(t, rows), :],
            dst_ref=att_rows.at[:, pl.ds(pl.multiple_of(t * head_cols, head_cols), head_cols)],
            send_sem=att_sem.at[0, t],
            recv_sem=att_sem.at[1, t],
            device_id=(d, t),
            device_id_type=MESH,
        )

    def attend_area(turn, carry):
        here_at = lax.rem(i // owners + 1 + turn, areas)
        here = rows_of(here_at, area)
        for h in range(heads):
            first = h * 3 * HEAD_DIM
            q = qkv[here, first : first + HEAD_DIM]
            parts = []
            for b in range(areas):
                key = qkv[b * area : (b + 1) * area, first + HEAD_DIM : first + 2 * HEAD_DIM]
                parts.append(mm_nt(key, q) * HEAD_DIM ** (-0.5) + bias[here_at, b])
            highest = parts[0].max(axis=0, keepdims=True)
            for part in parts[1:]:
                highest = jnp.maximum(highest, part.max(axis=0, keepdims=True))
            parts = [jnp.exp(part - highest) for part in parts]
            totals = sum(jnp.sum(part, axis=0, keepdims=True) for part in parts)
            inverse = 1.0 / totals
            out = jnp.zeros((HEAD_DIM, area), f32)
            for b in range(areas):
                value = qkv[b * area : (b + 1) * area, first + 2 * HEAD_DIM : first + 3 * HEAD_DIM]
                out += mm_tn(value, (parts[b] * inverse).astype(low))
            attended[here, h * HEAD_DIM : (h + 1) * HEAD_DIM] = out.T.astype(low)
            lse[pl.ds(here_at * heads + h, 1), :] = highest + jnp.log(totals)
        for k in range(owners):
            j = here_at * owners + k

            @pl.when(j != i)
            def _():
                to_owner(j).start()

        @pl.when(turn == (areas - 1) // 2)
        def _():
            up_g.close()
            cot_line.step(1)

        @pl.when(turn == areas - 1)
        def _():
            merge_g.relay()
            down_g.start()

        return carry

    lax.fori_loop(0, areas, attend_area, 0)
    att_rows[:, pl.ds(pl.multiple_of(i * head_cols, head_cols), head_cols)] = attended[
        rows_of(i, rows), :
    ]
    if n > 2:
        cot_line.step(2)
    merge_g.close()
    keep_merge.start()
    for turn in range(1, n):
        from_source(lax.rem(i + turn, n)).wait_recv()
    squares = jnp.zeros((rows, 1), f32)
    for at in tiles(width):
        out = mm(att_rows[...], merge[:, at])
        attn_out[:, at] = out
        v = x_own[:, at].astype(f32) + table[i, 2:3, at] * out
        middle[:, at] = v
        squares += jnp.sum(v * v, axis=1, keepdims=True)
    root = lax.rsqrt(squares * (1.0 / width) + 1e-06)
    for at in tiles(width):
        v = middle[:, at] * root
        hidden_second[:, at] = (v * (1.0 + table[i, 4:5, at]) + table[i, 3:4, at]).astype(low)
    down_g.relay()
    for s in range(3, n):
        cot_line.step(s)
    down_g.close()
    keep_attend.wait()
    keep_merge.wait()
    for flip in range(1, n_dp):
        to_plane(noise, noise_all, noise_sem, flip).wait_send()
        to_plane(terms, terms_all, terms_sem, flip).wait_send()
    for line in (merge_line, x_line, column_line, cot_line):
        line.finish()
    for turn in range(1, n):
        to_owner(lax.rem(i + turn, n)).wait_send()
    for weight in weights:
        weight.finish()


def front(n, n_dp, x, cot, noise, mod_w, chosen, bias, attend_w, merge_w, up_w, down_w, number):
    rows, width = x.shape
    k_rows, own_cols = mod_w.shape
    wide = attend_w.shape[1]
    heads = wide // (3 * HEAD_DIM)
    total = n * rows
    areas = bias.shape[0]
    low, f32 = jnp.bfloat16, jnp.float32
    sds = jax.ShapeDtypeStruct
    count = plane_sems(n_dp)
    return call(
        functools.partial(front_kernel, n, n_dp, heads, 512),
        number,
        "front",
        [VMEM] * 5 + [pl.BlockSpec(memory_space=pltpu.SMEM)] + [VMEM] * 4,
        [
            sds((total, width), low),
            sds((total, width), low),
            sds((total, wide), low),
            sds((areas * heads, total // areas), f32),
            sds((total, heads * HEAD_DIM), low),
            sds((rows, width), low),
            sds((rows, width), f32),
            sds((rows, width), f32),
            sds((rows, width), low),
            sds((n, 8, width), f32),
            sds((n_dp * k_rows, wide), low),
            sds((n * merge_w.shape[0], n_dp * merge_w.shape[1]), low),
            sds((n_dp * k_rows, up_w.shape[1]), low),
            sds((down_w.shape[0], n_dp * down_w.shape[1]), low),
        ],
        [HBM] + [VMEM] * 9 + [HBM] * 4,
        [
            pltpu.VMEM((total, width), low),
            pltpu.VMEM((n_dp * k_rows, wide), low),
            pltpu.VMEM((n * merge_w.shape[0], n_dp * merge_w.shape[1]), low),
            pltpu.VMEM((n_dp, 8, k_rows), f32),
            pltpu.VMEM((n_dp, 8, own_cols), f32),
            pltpu.VMEM((n_dp, 8, own_cols), f32),
            pltpu.VMEM((n * 8, own_cols), f32),
            DMA((2, n_dp)),
            DMA((2, n_dp)),
            DMA((3, n)),
            DMA((3, n)),
            DMA((3, n)),
            DMA((3, n)),
            DMA((4, count)),
            DMA((4, count)),
            DMA((2,)),
            DMA((2, n)),
            DMA((5,)),
        ],
        flops=2 * total * width * wide,
    )(x, cot, noise, mod_w, chosen, bias, attend_w, merge_w, up_w, down_w)


def attention_backward(packed, grad_out, attended, lse, image_of, heads, score_scale):
    tokens = packed.shape[0]
    areas = lse.shape[0] // heads
    split = packed.reshape(tokens, heads, 3, HEAD_DIM)
    queries, keys, values = split[:, :, 0], split[:, :, 1], split[:, :, 2]
    grads = grad_out.reshape(tokens, heads, HEAD_DIM)
    logs = lse.reshape(areas, heads, -1).transpose(1, 0, 2).reshape(heads, tokens)
    scores = (
        jnp.einsum("qhd,khd->hqk", queries, keys, preferred_element_type=jnp.float32)
        * score_scale
    )
    same_image = image_of[:, None] == image_of[None, :]
    scores = jnp.where(same_image[None], scores, MASKED)
    probs = jnp.exp(scores - logs[:, :, None])
    grad_probs = jnp.einsum("qhd,khd->hqk", grads, values, preferred_element_type=jnp.float32)
    inner = jnp.sum(probs * grad_probs, axis=-1, keepdims=True)
    grad_scores = (probs * (grad_probs - inner)).astype(jnp.bfloat16)

    def product(form, a, b):
        return jnp.einsum(form, a, b, preferred_element_type=jnp.float32)

    d_queries = product("hqk,khd->qhd", grad_scores, keys) * score_scale
    d_keys = product("hqk,qhd->khd", grad_scores, queries) * score_scale
    d_values = product("hqk,qhd->khd", probs.astype(jnp.bfloat16), grads)
    return jnp.stack([d_queries, d_keys, d_values], axis=2).astype(jnp.bfloat16).reshape(tokens, -1)


def on_device(
    block_input,
    cotangent,
    noise_embed,
    image_sizes,
    attend_weight,
    merge_weight,
    up_weight,
    down_weight,
    modulate_weight,
):
    n = lax.axis_size("tensor")
    n_dp = lax.axis_size("dp")
    place = lax.axis_index("tensor")
    dp_place = lax.axis_index("dp")
    rows, width = block_input.shape
    tokens = n * rows
    images = image_sizes.shape[1]
    k_rows = modulate_weight.shape[0]

    sizes_row = image_sizes[0]
    ends = [sum(sizes_row[j] for j in range(last + 1)) for last in range(images)]

    def image_at(places):
        return sum((places >= end).astype(jnp.int32) for end in ends)

    image_of = image_at(jnp.arange(tokens, dtype=jnp.int32))
    block_images = image_at(jnp.arange(n, dtype=jnp.int32) * rows)
    chosen = (block_images[:, None] == jnp.arange(8, dtype=jnp.int32)[None, :]) & (
        jnp.arange(8) < images
    )[None]
    chosen = jnp.broadcast_to(chosen.astype(jnp.float32)[:, :, None], (n, 8, 128))
    area = min(256, tokens)
    area_images = image_at(jnp.arange(tokens // area, dtype=jnp.int32) * area)
    bias = jnp.where(area_images[:, None] == area_images[None, :], 0.0, MASKED)
    noise_low = jax.nn.silu(noise_embed.astype(jnp.float32)).astype(jnp.bfloat16)
    noise_slabs = noise_low.astype(jnp.float32).reshape(images, n_dp, k_rows).transpose(1, 0, 2)
    noise_slabs = jnp.pad(noise_slabs, ((0, 0), (0, 8 - images), (0, 0)))
    noise_low_cols = lax.dynamic_slice_in_dim(
        lax.all_gather(noise_low, "dp", axis=0, tiled=True), dp_place * k_rows, k_rows, 1
    )
    (
        cot_full,
        hidden_first,
        packed,
        lse,
        attended,
        att_rows,
        attn_out,
        middle,
        hidden_second,
        table,
        attend_full,
        merge_full,
        up_full,
        down_full,
    ) = front(
        n,
        n_dp,
        block_input,
        cotangent,
        noise_slabs,
        modulate_weight,
        chosen,
        bias,
        attend_weight,
        merge_weight,
        up_weight,
        down_weight,
        0,
    )
    heads_local = packed.shape[1] // (3 * HEAD_DIM)
    score_scale = HEAD_DIM ** (-0.5)
    own_table = lax.dynamic_index_in_dim(table, place, 0, keepdims=False)
    shift_first, scale_first, gate_first, shift_second, scale_second, gate_second = [
        own_table[number : number + 1] for number in range(6)
    ]
    inputs = block_input.astype(jnp.float32)
    grad_rows = cotangent.astype(jnp.float32)
    own_image = lax.dynamic_index_in_dim(block_images, place, 0, keepdims=False)

    def rows_back(values, scale_part):
        return jax.vjp(modulate_rows, values, jnp.broadcast_to(scale_part, values.shape), jnp.zeros_like(values))[1]

    back_first = rows_back(inputs, scale_first)
    back_second = rows_back(middle, scale_second)
    d_hidden_second, mlp_part, up_local, down_local = ffn(
        n, hidden_second, table, cot_full, up_full, down_full, 2
    )
    mlp_out = scatter_rows(n, mlp_part, 3)
    block_output = (middle + gate_second * mlp_out).astype(jnp.bfloat16)
    d_gate_second = grad_rows * mlp_out
    d_mid_norm, d_scale_second, d_shift_second = back_second(d_hidden_second)
    d_middle = grad_rows + d_mid_norm
    d_gate_first = d_middle * attn_out
    d_attn = gather_rows(n, [(gate_first * d_middle).astype(jnp.bfloat16)], 4)[0]

    down_part = lax.psum_scatter(
        down_local, "dp", scatter_dimension=1, tiled=True
    ).astype(jnp.float32)
    up_part = lax.psum_scatter(
        up_local, "dp", scatter_dimension=0, tiled=True
    ).astype(jnp.float32)

    own_heads = heads_local * HEAD_DIM
    merge_own = lax.dynamic_slice_in_dim(merge_full, place * own_heads, own_heads, 0)
    merge_local = dot(attended, d_attn, ROWS_ROWS)
    merge_part = lax.psum_scatter(
        merge_local.astype(jnp.bfloat16), "dp", scatter_dimension=1, tiled=True
    ).astype(jnp.float32)
    d_attended = dot(d_attn, merge_own, COLS_COLS).astype(jnp.bfloat16)
    d_qkv = attention_backward(
        packed, d_attended, attended, lse, image_of, heads_local, score_scale
    )
    attend_local = dot(hidden_first, d_qkv, ROWS_ROWS)
    attend_part = lax.psum_scatter(
        attend_local.astype(jnp.bfloat16), "dp", scatter_dimension=0, tiled=True
    ).astype(jnp.float32)
    d_hidden_first = scatter_rows(
        n, dot(d_qkv, attend_full, COLS_COLS).astype(jnp.bfloat16), 5
    )
    d_in_norm, d_scale_first, d_shift_first = back_first(d_hidden_first)
    input_grad = (d_middle + d_in_norm).astype(jnp.bfloat16)

    token_grads = [
        d_shift_first,
        d_scale_first,
        d_gate_first,
        d_shift_second,
        d_scale_second,
        d_gate_second,
    ]
    image_rows = [
        jnp.concatenate(
            [jnp.where(own_image == j, jnp.sum(part, axis=0, keepdims=True), 0.0) for part in token_grads], axis=1
        )
        for j in range(images)
    ]
    d_mod_terms = jnp.concatenate(image_rows, axis=0)
    d_mod_cols = lax.psum_scatter(
        d_mod_terms, "tensor", scatter_dimension=1, tiled=True
    ).astype(jnp.bfloat16)
    d_mod_all = lax.all_gather(d_mod_cols, "dp", axis=0, tiled=True)
    modulate_part = dot(noise_low_cols, d_mod_all, ROWS_ROWS)
    noise_terms = dot(d_mod_all, modulate_weight, COLS_COLS)
    noise_cols = lax.psum(noise_terms, "tensor")
    noise_sum = lax.all_to_all(noise_cols, "dp", split_axis=0, concat_axis=1, tiled=True)
    silu_back = jax.vjp(jax.nn.silu, noise_embed.astype(jnp.float32))[1]
    noise_grad = silu_back(noise_sum)[0]
    return (
        block_output,
        input_grad,
        noise_grad,
        attend_part,
        merge_part,
        up_part,
        down_part,
        modulate_part,
    )


def solution(mesh):
    whole_rows = P(("dp", "tensor"), None)
    by_dp = P("dp", None)
    tall = P("dp", "tensor")
    wide = P("tensor", "dp")
    return jax.shard_map(
        on_device,
        mesh=mesh,
        in_specs=(whole_rows, whole_rows, by_dp, by_dp, tall, wide, tall, wide, tall),
        out_specs=(whole_rows, whole_rows, by_dp, tall, wide, tall, wide, tall),
        check_vma=False,
    )
```

```python
import functools
import math

import jax
import jax.numpy as jnp
from jax import lax
from jax.experimental import pallas as pl
from jax.experimental.pallas import tpu as pltpu
from jax.sharding import PartitionSpec as P

HEAD_DIM = 128
MASKED = -1e30


def dot(a, b, dims=(((1,), (0,)), ((), ()))):
    return lax.dot_general(a, b, dims, preferred_element_type=jnp.float32)


ROWS_ROWS = (((0,), (0,)), ((), ()))


MESH = pl.DeviceIdType.MESH
HBM = pl.BlockSpec(memory_space=pl.ANY)
VMEM = pl.BlockSpec(memory_space=pltpu.VMEM)
DMA = pltpu.SemaphoreType.DMA


def rows_of(j, rows):
    return pl.ds(pl.multiple_of(j * rows, rows), rows)


def beside(step):
    return (lax.axis_index("dp"), lax.axis_index("tensor") + step)


def greet_line(n, i):
    barrier = pltpu.get_barrier_semaphore()

    @pl.when(i > 0)
    def _():
        pl.semaphore_signal(barrier, inc=1, device_id=beside(-1), device_id_type=MESH)

    @pl.when(i < n - 1)
    def _():
        pl.semaphore_signal(barrier, inc=1, device_id=beside(1), device_id_type=MESH)

    pl.semaphore_wait(barrier, jnp.where(i > 0, 1, 0) + jnp.where(i < n - 1, 1, 0))


class LineGather:
    def __init__(self, n, i, rows, own, full, to_left, to_right, arrived):
        self.n, self.i, self.rows, self.own, self.full = n, i, rows, own, full
        self.to_left, self.to_right, self.arrived = to_left, to_right, arrived

    def copy(self, j, step, source=None):
        place = self.full.at[rows_of(j, self.rows)]
        return pltpu.make_async_remote_copy(
            src_ref=place if source is None else source,
            dst_ref=place,
            send_sem=(self.to_right if step > 0 else self.to_left).at[j],
            recv_sem=self.arrived.at[j],
            device_id=beside(step),
            device_id_type=MESH,
        )

    def start(self):
        @pl.when(self.i > 0)
        def _():
            self.copy(self.i, -1, self.own).start()

        @pl.when(self.i < self.n - 1)
        def _():
            self.copy(self.i, 1, self.own).start()

    def step(self, s):
        for side in (-1, 1):
            j = self.i + side * s
            there = (j >= 0) & (j < self.n)
            more = (self.i > 0) if side > 0 else (self.i < self.n - 1)

            @pl.when(there)
            def _():
                self.copy(j, side).wait_recv()

            @pl.when(there & more)
            def _():
                self.copy(j, -side).start()

    def finish(self):
        @pl.when(self.i > 0)
        def _():
            self.copy(self.i, -1, self.own).wait_send()

        @pl.when(self.i < self.n - 1)
        def _():
            self.copy(self.i, 1, self.own).wait_send()

        for j in range(self.n):

            @pl.when((j < self.i) & (self.i < self.n - 1))
            def _():
                self.copy(j, 1).wait_send()

            @pl.when((j > self.i) & (self.i > 0))
            def _():
                self.copy(j, -1).wait_send()


class LineScatter:
    def __init__(self, n, i, rows, width, part, got, sent, arrived):
        self.n, self.i, self.rows, self.width = n, i, rows, width
        self.part, self.got, self.sent, self.arrived = part, got, sent, arrived
        self.pieces = part.shape[1] // width

    def columns(self, c):
        if isinstance(c, int):
            return pl.ds(c * self.width, self.width)
        return pl.ds(pl.multiple_of(c * self.width, self.width), self.width)

    def copy(self, j, slot, c, step):
        return pltpu.make_async_remote_copy(
            src_ref=self.part.at[rows_of(j, self.rows), self.columns(c)],
            dst_ref=self.got.at[rows_of(slot, self.rows), self.columns(c)],
            send_sem=self.sent.at[j, c],
            recv_sem=self.arrived.at[slot, c],
            device_id=beside(step),
            device_id_type=MESH,
        )

    def slot_there(self, j, step):
        if step > 0:
            return j
        return jnp.where(j == self.i - 1, self.n, j)

    def at_end(self, j, c):
        @pl.when((self.i == 0) & (j > 0))
        def _():
            self.copy(j, j, c, 1).start()

        @pl.when((self.i == self.n - 1) & (j < self.i))
        def _():
            self.copy(j, self.slot_there(j, -1), c, -1).start()

    def pass_on(self, t, c, near):
        n, i = self.n, self.i
        rightward = (2 * i < n - 1) if near else (2 * i >= n - 1)
        j = jnp.where(rightward, t, n - 1 - t)
        step = jnp.where(rightward, 1, -1)
        right = rightward & (i > 0) & (j > i)
        left = jnp.logical_not(rightward) & (i < n - 1) & (j < i)

        @pl.when(right | left)
        def _():
            self.add(j, j, c)
            slot = jnp.where(left & (j == i - 1), n, j)
            self.copy(j, slot, c, step).start()

    def add(self, j, slot, c):
        self.copy(j, slot, c, 1).wait_recv()
        here = (rows_of(j, self.rows), self.columns(c))
        there = (rows_of(slot, self.rows), self.columns(c))
        total = self.part[here].astype(jnp.float32) + self.got[there].astype(jnp.float32)
        self.part[here] = total.astype(self.part.dtype)

    def own(self, c, out):
        i, n = self.i, self.n
        columns = self.columns(c)
        out[:, columns] = self.part[rows_of(i, self.rows), columns].astype(out.dtype)

        @pl.when(i > 0)
        def _():
            self.copy(i, i, c, 1).wait_recv()
            out[:, columns] += self.got[rows_of(i, self.rows), columns].astype(out.dtype)

        @pl.when(i < n - 1)
        def _():
            self.copy(i, n, c, -1).wait_recv()
            out[:, columns] += self.got[rows_of(n, self.rows), columns].astype(out.dtype)

    def own_value(self, c):
        i, n = self.i, self.n

        @pl.when(i > 0)
        def _():
            self.copy(i, i, c, 1).wait_recv()

        @pl.when(i < n - 1)
        def _():
            self.copy(i, n, c, -1).wait_recv()

        return self.own_total(c)

    def own_total(self, c):
        i, n, columns = self.i, self.n, self.columns(c)
        total = self.part[rows_of(i, self.rows), columns].astype(jnp.float32)
        left = self.got[rows_of(i, self.rows), columns].astype(jnp.float32)
        right = self.got[rows_of(n, self.rows), columns].astype(jnp.float32)
        return total + jnp.where(i > 0, left, 0.0) + jnp.where(i < n - 1, right, 0.0)

    def all_sent(self):
        def one(j, carry):
            @pl.when(j != self.i)
            def _():
                for c in range(self.pieces):
                    self.copy(j, 0, c, 1).wait_send()

            return carry

        lax.fori_loop(0, self.n, one, 0)


def mm(a, b):
    return lax.dot_general(a, b, (((1,), (0,)), ((), ())), preferred_element_type=jnp.float32)


def mm_nt(a, b):
    return lax.dot_general(a, b, (((1,), (1,)), ((), ())), preferred_element_type=jnp.float32)


def mm_tn(a, b):
    return lax.dot_general(a, b, (((0,), (0,)), ((), ())), preferred_element_type=jnp.float32)


def call(kernel, collective_id, name, in_specs, outs, out_specs, scratch, flops=0, limit=60):
    return pl.pallas_call(
        kernel,
        out_shape=outs,
        in_specs=in_specs,
        out_specs=out_specs,
        scratch_shapes=scratch,
        compiler_params=pltpu.CompilerParams(
            collective_id=collective_id,
            has_side_effects=True,
            vmem_limit_bytes=limit * 1024 * 1024,
        ),
        cost_estimate=pl.CostEstimate(flops=flops, bytes_accessed=1 << 20, transcendentals=0),
        name=name,
    )


def ffn_kernel(
    n,
    tile,
    grad_tile,
    own_hidden,
    table,
    d_mlp_hbm,
    up_hbm,
    down_hbm,
    d_hidden,
    mlp_part,
    up_grad,
    down_grad,
    up,
    down,
    d_mlp,
    hidden,
    activated,
    d_pre,
    part,
    got,
    stage,
    to_left,
    to_right,
    arrived,
    sent,
    came,
    local,
    stage_sem,
):
    i = lax.axis_index("tensor")
    rows, width = own_hidden.shape
    units = up.shape[1]
    loads = [
        pltpu.make_async_copy(source, target, local.at[k])
        for k, (source, target) in enumerate(((up_hbm, up), (d_mlp_hbm, d_mlp), (down_hbm, down)))
    ]
    for load in loads:
        load.start()
    greet_line(n, i)
    line = LineGather(n, i, rows, own_hidden, hidden, to_left, to_right, arrived)
    line.start()
    sums = LineScatter(n, i, rows, tile, part, got, sent, came)
    hidden[rows_of(i, rows), :] = own_hidden[...]
    for load in loads:
        load.wait()

    def one_block(j):
        here = rows_of(j, rows)

        def gated(c, carry):
            at = pl.ds(pl.multiple_of(c * tile, tile), tile)
            d_mlp[here, at] = (d_mlp[here, at].astype(jnp.float32) * table[j, 5:6, at]).astype(
                jnp.bfloat16
            )
            return carry

        lax.fori_loop(0, width // tile, gated, 0)

        def first(c, carry):
            at = pl.ds(pl.multiple_of(c * tile, tile), tile)
            pre = mm(hidden[here, :], up[:, at])
            d_act = mm_nt(d_mlp[here, :], down[at, :])
            cdf = 0.5 * (1.0 + lax.erf(pre * (0.5**0.5)))
            density = jnp.exp(-0.5 * pre * pre) * ((0.5 / math.pi) ** 0.5)
            activated[here, at] = (pre * cdf).astype(jnp.bfloat16)
            d_pre[here, at] = (d_act * (cdf + pre * density)).astype(jnp.bfloat16)
            return carry

        lax.fori_loop(0, units // tile, first, 0)

        def second(c, carry):
            at = pl.ds(pl.multiple_of(c * tile, tile), tile)
            part[here, at] = mm_nt(d_pre[here, :], up[at, :]).astype(jnp.bfloat16)
            sums.at_end(j, c)
            return carry

        lax.fori_loop(0, width // tile, second, 0)

        def third(c, carry):
            at = pl.ds(pl.multiple_of(c * tile, tile), tile)
            mlp_part[here, at] = mm(activated[here, :], down[:, at]).astype(jnp.bfloat16)
            return carry

        lax.fori_loop(0, width // tile, third, 0)

    def visit(q, carry):
        s = (q + 1) // 2
        side = 1 - 2 * (q % 2)
        j = i + s * side

        @pl.when(q % 2 == 1)
        def _():
            line.step(s)

        @pl.when((j >= 0) & (j < n))
        def _():
            one_block(j)

        return carry

    lax.fori_loop(0, 2 * n - 1, visit, 0)

    count = (width // grad_tile) * (units // grad_tile)
    turns = 2 * max(n - 2, 1) * sums.pieces
    per_turn = -(-2 * count // turns)

    def square(ref, row, column):
        return ref.at[
            pl.ds(pl.multiple_of(row * grad_tile, grad_tile), grad_tile),
            pl.ds(pl.multiple_of(column * grad_tile, grad_tile), grad_tile),
        ]

    def put(slot, target):
        return pltpu.make_async_copy(stage.at[slot], target, stage_sem.at[slot])

    def one_grad(k, left, right, target):
        wide = right.shape[1] // grad_tile
        row, column = k // wide, k % wide
        slot = k % 2

        @pl.when(k >= 2)
        def _():
            put(slot, square(target, 0, 0)).wait()

        a = left[:, pl.ds(pl.multiple_of(row * grad_tile, grad_tile), grad_tile)]
        b = right[:, pl.ds(pl.multiple_of(column * grad_tile, grad_tile), grad_tile)]
        stage[slot] = mm_tn(a, b).astype(jnp.bfloat16)
        put(slot, square(target, row, column)).start()

    def tail(k, carry):
        t, c = 2 + k // (2 * sums.pieces), k % sums.pieces
        for near in (True, False):

            @pl.when((k // sums.pieces) % 2 == (0 if near else 1))
            def _():
                sums.pass_on(t, c, near)

        for extra in range(per_turn):
            item = k * per_turn + extra

            @pl.when(item < count)
            def _():
                one_grad(item, hidden, d_pre, up_grad)

            @pl.when(item == count)
            def _():
                for slot in range(2):
                    put(slot, square(up_grad, 0, 0)).wait()

            @pl.when((item >= count) & (item < 2 * count))
            def _():
                one_grad(item - count, activated, d_mlp, down_grad)

        return carry

    lax.fori_loop(0, turns, tail, 0)
    for slot in range(2):
        put(slot, square(down_grad, 0, 0)).wait()
    for c in range(sums.pieces):
        sums.own(c, d_hidden)
    line.finish()
    sums.all_sent()


def ffn(n, own_hidden, table, cotangents, up, down, collective_id, tile=512, grad_tile=512):
    rows, width = own_hidden.shape
    units = up.shape[1]
    pieces = width // tile
    low = jnp.bfloat16
    return call(
        functools.partial(ffn_kernel, n, tile, grad_tile),
        collective_id,
        "ffn",
        [VMEM, VMEM, HBM, HBM, HBM],
        [
            jax.ShapeDtypeStruct((rows, width), jnp.float32),
            jax.ShapeDtypeStruct((n * rows, width), low),
            jax.ShapeDtypeStruct((width, units), low),
            jax.ShapeDtypeStruct((units, width), low),
        ],
        [VMEM, VMEM, HBM, HBM],
        [
            pltpu.VMEM((width, units), low),
            pltpu.VMEM((units, width), low),
            pltpu.VMEM((n * rows, width), low),
            pltpu.VMEM((n * rows, width), low),
            pltpu.VMEM((n * rows, units), low),
            pltpu.VMEM((n * rows, units), low),
            pltpu.VMEM((n * rows, width), low),
            pltpu.VMEM(((n + 1) * rows, width), low),
            pltpu.VMEM((2, grad_tile, grad_tile), low),
            DMA((n,)),
            DMA((n,)),
            DMA((n,)),
            DMA((n, pieces)),
            DMA((n + 1, pieces)),
            DMA((3,)),
            DMA((2,)),
        ],
        flops=12 * n * rows * width * units,
    )(own_hidden, table, cotangents, up, down)


class PlaneGather:
    def __init__(self, n_dp, d, own, view, height, sent, came):
        self.n_dp, self.d, self.own, self.view, self.height = n_dp, d, own, view, height
        self.sent, self.came = sent, came
        self.square = n_dp == 8
        self.peers = [2 * k for k in range(1, n_dp // 2)]

    def copy(self, k, source, target, peer):
        return pltpu.make_async_remote_copy(
            src_ref=source,
            dst_ref=target,
            send_sem=self.sent.at[k],
            recv_sem=self.came.at[k],
            device_id=(self.d ^ peer, lax.axis_index("tensor")),
            device_id_type=MESH,
        )

    def slab(self, flip, half=None):
        if half is None:
            return self.view(self.d ^ flip, 0, self.height)
        return self.view(self.d ^ flip, half * (self.height // 2), self.height // 2)

    def owns(self):
        peers = [2, 4] if self.square else self.peers
        return [
            self.copy(k, self.own, self.slab(0), peer) for k, peer in enumerate([1] + peers)
        ]

    def relay_of(self, k):
        flip, half, peer = ((2, 0, 4), (4, 1, 2))[k - 1]
        return self.copy(2 + k, self.slab(flip, half), self.slab(flip, half), peer)

    def across(self):
        return [
            self.copy(3, self.slab(6, 0), self.slab(6, 0), 4),
            self.copy(4, self.slab(6, 1), self.slab(6, 1), 2),
        ]

    def hand(self, flip):
        base = 5 if self.square else len(self.peers) + 1
        k = base + flip // 2 - 1
        return self.copy(k, self.slab(flip), self.slab(flip), 1)

    def handed(self, flip):
        base = 5 if self.square else len(self.peers) + 1
        k = base + flip // 2 - 1
        return self.copy(k, self.slab(flip ^ 1), self.slab(flip ^ 1), 1)

    def start(self):
        for copy in self.owns():
            copy.start()

    def relay(self):
        if not self.square:
            return
        for k, flip in ((1, 2), (2, 4)):
            self.copy(k, self.own, self.slab(flip), flip).wait_recv()
            self.relay_of(k).start()
            self.hand(flip).start()

    def close(self):
        if self.square:
            for copy in self.across():
                copy.wait_recv()
            self.hand(6).start()
        else:
            for k, flip in enumerate(self.peers):
                self.copy(k + 1, self.own, self.slab(flip), flip).wait_recv()
                self.hand(flip).start()
        self.copy(0, self.own, self.slab(1), 1).wait_recv()
        for flip in self.peers:
            self.handed(flip).wait_recv()

    def finish(self):
        for copy in self.owns():
            copy.wait_send()
        if self.square:
            for k in (1, 2):
                self.relay_of(k).wait_send()
        for flip in self.peers:
            self.hand(flip).wait_send()


def plane_sems(n_dp):
    return 8 if n_dp == 8 else n_dp - 1


def greet_all(n, n_dp, d, i):
    barrier = pltpu.get_barrier_semaphore()
    for flip in range(1, n_dp):
        pl.semaphore_signal(barrier, inc=1, device_id=(d ^ flip, i), device_id_type=MESH)
    for turn in range(1, n):
        pl.semaphore_signal(
            barrier, inc=1, device_id=(d, lax.rem(i + turn, n)), device_id_type=MESH
        )
    pl.semaphore_wait(barrier, n_dp + n - 2)


def front_kernel(
    n,
    n_dp,
    heads,
    tile,
    x_own,
    cot_own,
    noise,
    mod_w,
    chosen,
    bias,
    attend_w,
    merge_w,
    up_w,
    down_w,
    cot_full,
    hidden,
    qkv,
    lse,
    attended,
    att_rows,
    attn_out,
    middle,
    hidden_second,
    table,
    attend_full,
    merge_full,
    up_full,
    down_full,
    noise_all,
    x_full,
    attend,
    merge,
    terms,
    terms_all,
    columns,
    noise_sem,
    terms_sem,
    column_sem,
    x_sem,
    cot_sem,
    merge_sem,
    weight_sent,
    weight_came,
    out_sem,
    att_sem,
    local,
):
    d, i = lax.axis_index("dp"), lax.axis_index("tensor")
    rows, width = x_own.shape
    k_rows, own_cols = mod_w.shape
    head_cols = heads * HEAD_DIM
    low, f32 = jnp.bfloat16, jnp.float32
    merge_rows, merge_cols = merge_w.shape
    down_cols = down_w.shape[1]
    merge_slab = merge.at[:, pl.ds(pl.multiple_of(d * merge_cols, merge_cols), merge_cols)]

    def row_view(full, height):
        return lambda at, start, count: full.at[
            pl.ds(pl.multiple_of(at * height + start, 16), count), :
        ]

    def column_view(full, wide):
        return lambda at, start, count: full.at[
            pl.ds(start, count), pl.ds(pl.multiple_of(at * wide, wide), wide)
        ]

    weights = [
        PlaneGather(n_dp, d, own, view, height, weight_sent.at[k], weight_came.at[k])
        for k, (own, view, height) in enumerate(
            (
                (attend_w, row_view(attend, k_rows), k_rows),
                (merge_slab, column_view(merge, merge_cols), n * merge_rows),
                (up_w, row_view(up_full, k_rows), k_rows),
                (down_w, column_view(down_full, down_cols), down_w.shape[0]),
            )
        )
    ]
    attend_g, merge_g, up_g, down_g = weights
    copies = [
        pltpu.make_async_copy(source, target, local.at[k])
        for k, (source, target) in enumerate(
            (
                (cot_own, cot_full.at[rows_of(i, rows)]),
                (attend_w, attend_g.slab(0)),
                (merge_w, merge_slab.at[rows_of(i, merge_rows)]),
                (up_w, up_g.slab(0)),
                (down_w, down_g.slab(0)),
            )
        )
    ]
    for copy in copies:
        copy.start()
    greet_all(n, n_dp, d, i)

    def to_plane(source, target, sems, flip):
        return pltpu.make_async_remote_copy(
            src_ref=source.at[d ^ flip],
            dst_ref=target.at[d],
            send_sem=sems.at[0, flip],
            recv_sem=sems.at[1, flip],
            device_id=(d ^ flip, i),
            device_id_type=MESH,
        )

    def from_plane(target, sems, flip):
        return pltpu.make_async_remote_copy(
            src_ref=target.at[d ^ flip],
            dst_ref=target.at[d ^ flip],
            send_sem=sems.at[0, flip],
            recv_sem=sems.at[1, flip],
            device_id=(d ^ flip, i),
            device_id_type=MESH,
        )

    for flip in range(1, n_dp):
        to_plane(noise, noise_all, noise_sem, flip).start()
    merge_line = LineGather(
        n, i, merge_rows, merge_w, merge_slab, merge_sem.at[0], merge_sem.at[1], merge_sem.at[2]
    )
    x_line = LineGather(n, i, rows, x_own, x_full, x_sem.at[0], x_sem.at[1], x_sem.at[2])
    cot_line = LineGather(
        n, i, rows, cot_own, cot_full, cot_sem.at[0], cot_sem.at[1], cot_sem.at[2]
    )
    x_line.start()
    attend_g.start()
    merge_line.start()
    noise_all[d] = noise[d]
    x_full[rows_of(i, rows), :] = x_own[...]
    for flip in range(1, n_dp):
        from_plane(noise_all, noise_sem, flip).wait_recv()
    images = noise_all[...].reshape(n_dp * 8, k_rows).astype(low)
    for c in range(own_cols // tile):
        terms[:, :, c * tile : (c + 1) * tile] = mm(
            images, mod_w[:, c * tile : (c + 1) * tile]
        ).reshape(n_dp, 8, tile)
    for flip in range(1, n_dp):
        to_plane(terms, terms_all, terms_sem, flip).start()
    terms_all[d] = terms[d]
    for flip in range(1, n_dp):
        from_plane(terms_all, terms_sem, flip).wait_recv()
    columns[pl.ds(pl.multiple_of(i * 8, 8), 8), :] = jnp.sum(terms_all[...], axis=0)
    own_columns = columns.at[pl.ds(pl.multiple_of(i * 8, 8), 8)]
    column_line = LineGather(
        n, i, 8, own_columns, columns, column_sem.at[0], column_sem.at[1], column_sem.at[2]
    )
    column_line.start()
    for s in range(1, n):
        column_line.step(s)
    unit = math.gcd(width, own_cols)

    def fill(j, carry):
        for number in range(6):
            for start in range(0, width, unit):
                at = number * width + start
                part = columns[at // own_cols * 8 : at // own_cols * 8 + 8, pl.ds(at % own_cols, unit)]
                table[j, number : number + 1, start : start + unit] = jnp.sum(
                    part * chosen[j][:, :1], axis=0, keepdims=True
                )
        return carry

    lax.fori_loop(0, n, fill, 0)
    x_line.step(1)
    attend_g.relay()
    merge_line.step(1)
    for copy in copies:
        copy.wait()
    attend_g.close()
    up_g.start()
    keep_attend = pltpu.make_async_copy(attend, attend_full, out_sem.at[0])
    keep_merge = pltpu.make_async_copy(merge, merge_full, out_sem.at[1])
    keep_attend.start()

    def tiles(count):
        return [slice(c * tile, (c + 1) * tile) for c in range(count // tile)]

    def one_block(j):
        here = rows_of(j, rows)
        squares = jnp.zeros((rows, 1), f32)
        for at in tiles(width):
            v = x_full[here, at].astype(f32)
            squares += jnp.sum(v * v, axis=1, keepdims=True)
        root = lax.rsqrt(squares * (1.0 / width) + 1e-06)
        for at in tiles(width):
            v = x_full[here, at].astype(f32) * root
            hidden[here, at] = (v * (1.0 + table[j, 1:2, at]) + table[j, 0:1, at]).astype(low)
        wide = qkv.shape[1]
        step = math.gcd(wide, 512)
        for c in range(wide // step):
            at = slice(c * step, (c + 1) * step)
            qkv[here, at] = mm(hidden[here, :], attend[:, at]).astype(low)

    def visit(q, carry):
        s = (q + 1) // 2
        side = 1 - 2 * (q % 2)
        j = i + s * side

        @pl.when((q % 2 == 1) & (s + 1 < n))
        def _():
            x_line.step(s + 1)
            merge_line.step(s + 1)

        @pl.when(q == 2 * n - 5)
        def _():
            up_g.relay()
            merge_g.start()
            cot_line.start()

        @pl.when((j >= 0) & (j < n))
        def _():
            one_block(j)

        return carry

    lax.fori_loop(0, 2 * n - 1, visit, 0)

    area = min(256, n * rows)
    areas = n * rows // area
    owners = area // rows

    def to_owner(j):
        return pltpu.make_async_remote_copy(
            src_ref=attended.at[rows_of(j, rows), :],
            dst_ref=att_rows.at[:, pl.ds(pl.multiple_of(i * head_cols, head_cols), head_cols)],
            send_sem=att_sem.at[0, j],
            recv_sem=att_sem.at[1, i],
            device_id=(d, j),
            device_id_type=MESH,
        )

    def from_source(t):
        return pltpu.make_async_remote_copy(
            src_ref=attended.at[rows_of(t, rows), :],
            dst_ref=att_rows.at[:, pl.ds(pl.multiple_of(t * head_cols, head_cols), head_cols)],
            send_sem=att_sem.at[0, t],
            recv_sem=att_sem.at[1, t],
            device_id=(d, t),
            device_id_type=MESH,
        )

    def attend_area(turn, carry):
        here_at = lax.rem(i // owners + 1 + turn, areas)
        here = rows_of(here_at, area)
        for h in range(heads):
            first = h * 3 * HEAD_DIM
            q = qkv[here, first : first + HEAD_DIM]
            parts = []
            for b in range(areas):
                key = qkv[b * area : (b + 1) * area, first + HEAD_DIM : first + 2 * HEAD_DIM]
                parts.append(mm_nt(key, q) * HEAD_DIM ** (-0.5) + bias[here_at, b])
            highest = parts[0].max(axis=0, keepdims=True)
            for part in parts[1:]:
                highest = jnp.maximum(highest, part.max(axis=0, keepdims=True))
            parts = [jnp.exp(part - highest) for part in parts]
            totals = sum(jnp.sum(part, axis=0, keepdims=True) for part in parts)
            inverse = 1.0 / totals
            out = jnp.zeros((HEAD_DIM, area), f32)
            for b in range(areas):
                value = qkv[b * area : (b + 1) * area, first + 2 * HEAD_DIM : first + 3 * HEAD_DIM]
                out += mm_tn(value, (parts[b] * inverse).astype(low))
            attended[here, h * HEAD_DIM : (h + 1) * HEAD_DIM] = out.T.astype(low)
            lse[pl.ds(here_at * heads + h, 1), :] = highest + jnp.log(totals)
        for k in range(owners):
            j = here_at * owners + k

            @pl.when(j != i)
            def _():
                to_owner(j).start()

        @pl.when(turn == (areas - 1) // 2)
        def _():
            up_g.close()
            cot_line.step(1)

        @pl.when(turn == areas - 1)
        def _():
            merge_g.relay()
            down_g.start()

        return carry

    lax.fori_loop(0, areas, attend_area, 0)
    att_rows[:, pl.ds(pl.multiple_of(i * head_cols, head_cols), head_cols)] = attended[
        rows_of(i, rows), :
    ]
    if n > 2:
        cot_line.step(2)
    merge_g.close()
    keep_merge.start()
    for turn in range(1, n):
        from_source(lax.rem(i + turn, n)).wait_recv()
    squares = jnp.zeros((rows, 1), f32)
    for at in tiles(width):
        out = mm(att_rows[...], merge[:, at])
        attn_out[:, at] = out
        v = x_own[:, at].astype(f32) + table[i, 2:3, at] * out
        middle[:, at] = v
        squares += jnp.sum(v * v, axis=1, keepdims=True)
    root = lax.rsqrt(squares * (1.0 / width) + 1e-06)
    for at in tiles(width):
        v = middle[:, at] * root
        hidden_second[:, at] = (v * (1.0 + table[i, 4:5, at]) + table[i, 3:4, at]).astype(low)
    down_g.relay()
    for s in range(3, n):
        cot_line.step(s)
    down_g.close()
    keep_attend.wait()
    keep_merge.wait()
    for flip in range(1, n_dp):
        to_plane(noise, noise_all, noise_sem, flip).wait_send()
        to_plane(terms, terms_all, terms_sem, flip).wait_send()
    for line in (merge_line, x_line, column_line, cot_line):
        line.finish()
    for turn in range(1, n):
        to_owner(lax.rem(i + turn, n)).wait_send()
    for weight in weights:
        weight.finish()


def front(n, n_dp, x, cot, noise, mod_w, chosen, bias, attend_w, merge_w, up_w, down_w, number):
    rows, width = x.shape
    k_rows, own_cols = mod_w.shape
    wide = attend_w.shape[1]
    heads = wide // (3 * HEAD_DIM)
    total = n * rows
    areas = bias.shape[0]
    low, f32 = jnp.bfloat16, jnp.float32
    sds = jax.ShapeDtypeStruct
    count = plane_sems(n_dp)
    return call(
        functools.partial(front_kernel, n, n_dp, heads, 512),
        number,
        "front",
        [VMEM] * 5 + [pl.BlockSpec(memory_space=pltpu.SMEM)] + [VMEM] * 4,
        [
            sds((total, width), low),
            sds((total, width), low),
            sds((total, wide), low),
            sds((areas * heads, total // areas), f32),
            sds((total, heads * HEAD_DIM), low),
            sds((rows, width), low),
            sds((rows, width), f32),
            sds((rows, width), f32),
            sds((rows, width), low),
            sds((n, 8, width), f32),
            sds((n_dp * k_rows, wide), low),
            sds((n * merge_w.shape[0], n_dp * merge_w.shape[1]), low),
            sds((n_dp * k_rows, up_w.shape[1]), low),
            sds((down_w.shape[0], n_dp * down_w.shape[1]), low),
            sds((n_dp, 8, k_rows), f32),
        ],
        [HBM] + [VMEM] * 9 + [HBM] * 4 + [VMEM],
        [
            pltpu.VMEM((total, width), low),
            pltpu.VMEM((n_dp * k_rows, wide), low),
            pltpu.VMEM((n * merge_w.shape[0], n_dp * merge_w.shape[1]), low),
            pltpu.VMEM((n_dp, 8, own_cols), f32),
            pltpu.VMEM((n_dp, 8, own_cols), f32),
            pltpu.VMEM((n * 8, own_cols), f32),
            DMA((2, n_dp)),
            DMA((2, n_dp)),
            DMA((3, n)),
            DMA((3, n)),
            DMA((3, n)),
            DMA((3, n)),
            DMA((4, count)),
            DMA((4, count)),
            DMA((2,)),
            DMA((2, n)),
            DMA((5,)),
        ],
        flops=2 * total * width * wide,
    )(x, cot, noise, mod_w, chosen, bias, attend_w, merge_w, up_w, down_w)


class PlaneScatter:
    def __init__(self, n_dp, d, theirs, own, swapped, landed, sems):
        self.chips, self.d = n_dp // 2, d
        self.chip, self.side = d // 2, lax.rem(d, 2)
        self.theirs, self.own, self.swapped, self.landed, self.sems = theirs, own, swapped, landed, sems

    def remote(self, source, target, sent, came, device):
        return pltpu.make_async_remote_copy(
            src_ref=source,
            dst_ref=target,
            send_sem=sent,
            recv_sem=came,
            device_id=(device, lax.axis_index("tensor")),
            device_id_type=MESH,
        )

    def swap(self, m):
        return self.remote(
            self.theirs(m), self.swapped.at[m], self.sems.at[0, m], self.sems.at[1, m], self.d ^ 1
        )

    def send(self, m):
        return self.remote(
            self.own.at[m],
            self.landed.at[self.chip],
            self.sems.at[2, m],
            self.sems.at[3, self.chip],
            2 * m + self.side,
        )

    def come(self, m):
        return self.remote(
            self.own.at[m],
            self.landed.at[m],
            self.sems.at[2, m],
            self.sems.at[3, m],
            2 * m + self.side,
        )

    def keep(self):
        return pltpu.make_async_copy(
            self.own.at[self.chip], self.landed.at[self.chip], self.sems.at[2, self.chip]
        )

    def swap_all(self):
        def one(m, carry):
            self.swap(m).start()
            return carry

        lax.fori_loop(0, self.chips, one, 0)

    def add_and_send(self):
        _, height, wide = self.own.shape
        chunk = math.gcd(height, 64 if wide > 512 else 256)

        def one(k, carry):
            m = self.chip ^ (self.chips - 1 - k)
            self.swap(m).wait_recv()

            def add(c, inner):
                at = pl.ds(pl.multiple_of(c * chunk, chunk), chunk)
                total = self.own[m, at, :].astype(jnp.float32) + self.swapped[m, at, :].astype(
                    jnp.float32
                )
                self.own[m, at, :] = total.astype(self.own.dtype)
                return inner

            lax.fori_loop(0, height // chunk, add, 0)

            @pl.when(m != self.chip)
            def _():
                self.send(m).start()

            return carry

        lax.fori_loop(0, self.chips, one, 0)
        self.keep().start()

    def landed_all(self):
        for k in range(1, self.chips):
            self.come(self.chip ^ k).wait_recv()
        self.keep().wait()

    def finish(self):
        for m in range(self.chips):
            self.swap(m).wait_send()
        for k in range(1, self.chips):
            self.send(self.chip ^ k).wait_send()


def flows(n, pieces, sums, turn):
    far, rest = turn // ((n - 2) * pieces), lax.rem(turn, (n - 2) * pieces)
    t, c = n - 1 - rest // pieces, lax.rem(rest, pieces)
    for near in (True, False):

        @pl.when(far == (0 if near else 1))
        def _():
            sums.pass_on(t, c, near)


def back_kernel(
    n,
    n_dp,
    heads,
    tile,
    d_hidden,
    cot,
    middle,
    attn_out,
    table,
    att_rows,
    qkv,
    lse,
    bias,
    mlp_hbm,
    merge_hbm,
    up_hbm,
    down_hbm,
    block_out,
    d_middle,
    d_qkv,
    sums_out,
    merge_grad,
    up_landed,
    down_landed,
    part,
    got,
    merge,
    d_att,
    d_send,
    d_attn,
    d_keys,
    d_values,
    up_own,
    up_swapped,
    down_own,
    down_swapped,
    stage,
    mlp_sent,
    mlp_came,
    up_sems,
    down_sems,
    att_sem,
    merge_sem,
    load_sem,
    stage_sem,
    own_sem,
):
    d, i = lax.axis_index("dp"), lax.axis_index("tensor")
    rows, width = middle.shape
    low, f32 = jnp.bfloat16, jnp.float32
    head_cols = heads * HEAD_DIM
    chips = n_dp // 2
    k_rows, down_cols = up_own.shape[1], down_own.shape[2]
    side = lax.rem(d, 2)

    def up_slab(at):
        return up_hbm.at[pl.ds(pl.multiple_of(at * k_rows, k_rows), k_rows), :]

    def down_slab(at):
        return down_hbm.at[:, pl.ds(pl.multiple_of(at * down_cols, down_cols), down_cols)]

    load_mlp = pltpu.make_async_copy(mlp_hbm, part, load_sem.at[0])
    load_mlp.start()

    def load_merge(t, slot):
        return pltpu.make_async_copy(
            merge_hbm.at[pl.ds(pl.multiple_of(t * head_cols, head_cols), head_cols), :],
            merge.at[slot],
            merge_sem.at[slot],
        )

    load_merge(0, 0).start()
    for m in range(chips):
        pltpu.make_async_copy(up_slab(2 * m + side), up_own.at[m], own_sem.at[0, m]).start()
        pltpu.make_async_copy(down_slab(2 * m + side), down_own.at[m], own_sem.at[1, m]).start()
    greet_all(n, n_dp, d, i)
    up = PlaneScatter(
        n_dp, d, lambda m: up_slab(2 * m + 1 - side), up_own, up_swapped, up_landed, up_sems
    )
    down = PlaneScatter(
        n_dp, d, lambda m: down_slab(2 * m + 1 - side), down_own, down_swapped, down_landed, down_sems
    )
    up.swap_all()
    down.swap_all()
    load_mlp.wait()
    sums = LineScatter(n, i, rows, tile, part, got, mlp_sent, mlp_came)
    pieces = sums.pieces

    def ends(k, carry):
        t, c = n - 1 - k // pieces, lax.rem(k, pieces)
        pl.when(i == 0)(functools.partial(sums.at_end, t, c))
        pl.when(i == n - 1)(functools.partial(sums.at_end, n - 1 - t, c))
        return carry

    lax.fori_loop(0, (n - 1) * pieces, ends, 0)

    tiles = [slice(c * tile, (c + 1) * tile) for c in range(width // tile)]
    squares = jnp.zeros((rows, 1), f32)
    for at in tiles:
        squares += jnp.sum(middle[:, at] * middle[:, at], axis=1, keepdims=True)
    root = lax.rsqrt(squares * (1.0 / width) + 1e-06)
    mean = jnp.zeros((rows, 1), f32)
    for at in tiles:
        v = middle[:, at] * root
        dh = d_hidden[:, at]
        mean += jnp.sum(dh * (1.0 + table[i, 4:5, at]) * v, axis=1, keepdims=True)
        sums_out[3:4, at] = jnp.sum(dh, axis=0, keepdims=True)
        sums_out[4:5, at] = jnp.sum(dh * v, axis=0, keepdims=True)
    mean = mean * (1.0 / width)
    for at in tiles:
        v = middle[:, at] * root
        u = d_hidden[:, at] * (1.0 + table[i, 4:5, at])
        dm = cot[:, at].astype(f32) + root * (u - v * mean)
        d_middle[:, at] = dm
        d_attn[:, at] = (table[i, 2:3, at] * dm).astype(low)
        sums_out[2:3, at] = jnp.sum(dm * attn_out[:, at], axis=0, keepdims=True)

    def to_heads(t):
        return pltpu.make_async_remote_copy(
            src_ref=d_send.at[t],
            dst_ref=d_att.at[rows_of(i, rows), :],
            send_sem=att_sem.at[0, t],
            recv_sem=att_sem.at[1, i],
            device_id=(d, t),
            device_id_type=MESH,
        )

    def from_rows(t):
        return pltpu.make_async_remote_copy(
            src_ref=d_send.at[t],
            dst_ref=d_att.at[rows_of(t, rows), :],
            send_sem=att_sem.at[0, t],
            recv_sem=att_sem.at[1, t],
            device_id=(d, t),
            device_id_type=MESH,
        )

    def head_part(t, carry):
        slot = lax.rem(t, 2)

        @pl.when(t + 1 < n)
        def _():
            load_merge(t + 1, 1 - slot).start()

        load_merge(t, slot).wait()
        d_send[t] = mm_nt(d_attn[...], merge[slot]).astype(low)

        @pl.when(t != i)
        def _():
            to_heads(t).start()

        return carry

    lax.fori_loop(0, n, head_part, 0)
    d_att[rows_of(i, rows), :] = d_send[i]
    for m in range(chips):
        pltpu.make_async_copy(up_slab(2 * m + side), up_own.at[m], own_sem.at[0, m]).wait()
        pltpu.make_async_copy(down_slab(2 * m + side), down_own.at[m], own_sem.at[1, m]).wait()
    up.add_and_send()

    wide = width // tile

    def square(row, column):
        return merge_grad.at[
            pl.ds(pl.multiple_of(row * tile, tile), tile),
            pl.ds(pl.multiple_of(column * tile, tile), tile),
        ]

    def merge_one(k, carry):
        row, column = k // wide, lax.rem(k, wide)
        slot = lax.rem(k, 2)

        @pl.when(k >= 2)
        def _():
            pltpu.make_async_copy(stage.at[slot], square(0, 0), stage_sem.at[slot]).wait()

        a = att_rows[:, pl.ds(pl.multiple_of(row * tile, tile), tile)]
        b = d_attn[:, pl.ds(pl.multiple_of(column * tile, tile), tile)]
        stage[slot] = mm_tn(a, b).astype(low)
        pltpu.make_async_copy(stage.at[slot], square(row, column), stage_sem.at[slot]).start()
        return carry

    lax.fori_loop(0, wide * wide, merge_one, 0)
    for slot in range(2):
        pltpu.make_async_copy(stage.at[slot], square(0, 0), stage_sem.at[slot]).wait()
    for turn in range(1, n):
        from_rows(lax.rem(i + turn, n)).wait_recv()

    area = lse.shape[1]
    areas = n * rows // area
    d_keys[...] = jnp.zeros_like(d_keys)
    d_values[...] = jnp.zeros_like(d_values)
    turns = 2 * max(n - 2, 0) * pieces
    per_area = -(-turns // areas)
    scale = HEAD_DIM ** (-0.5)

    def back_area(here_at, carry):
        here = rows_of(here_at, area)
        for h in range(heads):
            first = h * 3 * HEAD_DIM
            head = slice(h * HEAD_DIM, (h + 1) * HEAD_DIM)
            q = qkv[here, first : first + HEAD_DIM]
            g = d_att[here, head]
            log_row = lse[pl.ds(here_at * heads + h, 1), :]
            probs, d_probs = [], []
            inner = jnp.zeros((1, area), f32)
            for b in range(areas):
                key = qkv[b * area : (b + 1) * area, first + HEAD_DIM : first + 2 * HEAD_DIM]
                value = qkv[b * area : (b + 1) * area, first + 2 * HEAD_DIM : first + 3 * HEAD_DIM]
                scores = mm_nt(key, q) * scale + bias[here_at, b]
                probs.append(jnp.exp(scores - log_row))
                d_probs.append(mm_nt(value, g))
                inner += jnp.sum(probs[b] * d_probs[b], axis=0, keepdims=True)
            d_query = jnp.zeros((HEAD_DIM, area), f32)
            for b in range(areas):
                at = slice(b * area, (b + 1) * area)
                key = qkv[at, first + HEAD_DIM : first + 2 * HEAD_DIM]
                d_scores = (probs[b] * (d_probs[b] - inner)).astype(low)
                d_values[at, head] += mm(probs[b].astype(low), g)
                d_keys[at, head] += mm(d_scores, q)
                d_query += mm_tn(key, d_scores)
            d_qkv[here, first : first + HEAD_DIM] = (d_query * scale).T.astype(low)

        @pl.when(here_at == 0)
        def _():
            down.add_and_send()

        for extra in range(per_area):
            turn = here_at * per_area + extra

            @pl.when(turn < turns)
            def _():
                flows(n, pieces, sums, turn)

        return carry

    lax.fori_loop(0, areas, back_area, 0)
    for h in range(heads):
        first = h * 3 * HEAD_DIM
        head = slice(h * HEAD_DIM, (h + 1) * HEAD_DIM)
        d_qkv[:, first + HEAD_DIM : first + 2 * HEAD_DIM] = (d_keys[:, head] * scale).astype(low)
        d_qkv[:, first + 2 * HEAD_DIM : first + 3 * HEAD_DIM] = d_values[:, head].astype(low)
    for c, at in enumerate(tiles):
        total = sums.own_value(c)
        block_out[:, at] = (middle[:, at] + table[i, 5:6, at] * total).astype(low)
        sums_out[5:6, at] = jnp.sum(cot[:, at].astype(f32) * total, axis=0, keepdims=True)
    sums_out[0:2, :] = jnp.zeros((2, width), f32)
    sums_out[6:8, :] = jnp.zeros((2, width), f32)
    for scatter in (up, down):
        scatter.landed_all()
        scatter.finish()
    for turn in range(1, n):
        to_heads(lax.rem(i + turn, n)).wait_send()
    sums.all_sent()


def back(n, n_dp, operands, shapes, number, tile=512):
    (rows, width), wide, units, k_rows, down_cols, areas = shapes
    heads = wide // (3 * HEAD_DIM)
    total, chips, pieces = n * rows, n_dp // 2, width // tile
    low, f32 = jnp.bfloat16, jnp.float32
    sds = jax.ShapeDtypeStruct
    return call(
        functools.partial(back_kernel, n, n_dp, heads, tile),
        number,
        "back",
        [VMEM] * 8 + [pl.BlockSpec(memory_space=pltpu.SMEM)] + [HBM] * 4,
        [
            sds((rows, width), low),
            sds((rows, width), f32),
            sds((total, wide), low),
            sds((8, width), f32),
            sds((width, width), low),
            sds((chips, k_rows, units), low),
            sds((chips, units, down_cols), low),
        ],
        [VMEM] * 4 + [HBM] * 3,
        [
            pltpu.VMEM((total, width), low),
            pltpu.VMEM((total + rows, width), low),
            pltpu.VMEM((2, heads * HEAD_DIM, width), low),
            pltpu.VMEM((total, heads * HEAD_DIM), low),
            pltpu.VMEM((n, rows, heads * HEAD_DIM), low),
            pltpu.VMEM((rows, width), low),
            pltpu.VMEM((total, heads * HEAD_DIM), f32),
            pltpu.VMEM((total, heads * HEAD_DIM), f32),
            pltpu.VMEM((chips, k_rows, units), low),
            pltpu.VMEM((chips, k_rows, units), low),
            pltpu.VMEM((chips, units, down_cols), low),
            pltpu.VMEM((chips, units, down_cols), low),
            pltpu.VMEM((2, tile, tile), low),
            DMA((n, pieces)),
            DMA((n + 1, pieces)),
            DMA((4, chips)),
            DMA((4, chips)),
            DMA((2, n)),
            DMA((2,)),
            DMA((1,)),
            DMA((2,)),
            DMA((2, chips)),
        ],
        flops=20 * total * total * wide // 3,
    )(*operands)


def last_kernel(
    n,
    n_dp,
    tile,
    d_qkv,
    hidden,
    x_own,
    d_middle,
    sums_in,
    table,
    chosen,
    mod_w,
    merge_hbm,
    attend_hbm,
    input_grad,
    d_mod_all,
    noise_sum,
    attend_landed,
    merge_out,
    attend,
    part,
    got,
    grad_own,
    grad_theirs,
    grad_swapped,
    merge_own,
    merge_swapped,
    merge_landed,
    merge_part,
    merge_got,
    sums_all,
    shares,
    shares_all,
    terms,
    terms_all,
    noise_parts,
    sent,
    came,
    merge_sent,
    merge_came,
    grad_sems,
    merge_sems,
    share_sem,
    mod_sem,
    term_sem,
    noise_sem,
    load_sem,
    own_sem,
):
    d, i = lax.axis_index("dp"), lax.axis_index("tensor")
    rows, width = x_own.shape
    low, f32 = jnp.bfloat16, jnp.float32
    chips = n_dp // 2
    side = lax.rem(d, 2)
    k_rows, own_cols = mod_w.shape
    merge_cols = merge_own.shape[2]
    merge_rows = merge_out.shape[0]

    def merge_slab(at):
        return merge_hbm.at[:, pl.ds(pl.multiple_of(at * merge_cols, merge_cols), merge_cols)]

    load = pltpu.make_async_copy(attend_hbm, attend, load_sem)
    load.start()
    for m in range(chips):
        pltpu.make_async_copy(merge_slab(2 * m + side), merge_own.at[m], own_sem.at[m]).start()
    greet_all(n, n_dp, d, i)
    merge = PlaneScatter(
        n_dp,
        d,
        lambda m: merge_slab(2 * m + 1 - side),
        merge_own,
        merge_swapped,
        merge_landed,
        merge_sems,
    )
    grad = PlaneScatter(
        n_dp, d, lambda m: grad_theirs.at[m], grad_own, grad_swapped, attend_landed, grad_sems
    )
    merge.swap_all()
    sums = LineScatter(n, i, rows, tile, part, got, sent, came)
    pieces = sums.pieces
    load.wait()

    def partial_block(q, carry):
        j = jnp.where(2 * i < n - 1, n - 1 - q, q)
        here = rows_of(j, rows)

        def one(c, inner):
            at = pl.ds(pl.multiple_of(c * tile, tile), tile)
            part[here, at] = mm_nt(d_qkv[here, :], attend[at, :]).astype(low)
            sums.at_end(j, c)
            return inner

        lax.fori_loop(0, pieces, one, 0)
        return carry

    lax.fori_loop(0, n, partial_block, 0)
    for m in range(chips):
        pltpu.make_async_copy(merge_slab(2 * m + side), merge_own.at[m], own_sem.at[m]).wait()
    merge.add_and_send()

    def slab_grad(at):
        columns = pl.ds(pl.multiple_of(at * k_rows, k_rows), k_rows)
        return mm_tn(hidden[:, columns], d_qkv[...]).astype(low)

    def for_them(m, carry):
        grad_theirs[m] = slab_grad(2 * m + 1 - side)
        grad.swap(m).start()
        return carry

    def for_us(m, carry):
        grad_own[m] = slab_grad(2 * m + side)
        return carry

    lax.fori_loop(0, chips, for_them, 0)
    lax.fori_loop(0, chips, for_us, 0)
    grad.add_and_send()
    turns = 2 * max(n - 2, 0) * pieces

    def pass_by(turn, carry):
        flows(n, pieces, sums, turn)
        return carry

    lax.fori_loop(0, turns, pass_by, 0)

    merge.landed_all()
    merge_sums = LineScatter(
        n, i, merge_rows, merge_cols, merge_part, merge_got, merge_sent, merge_came
    )

    def merge_block(q, carry):
        j = jnp.where(2 * i < n - 1, n - 1 - q, q)
        here = rows_of(j, merge_rows)
        total = merge_landed[0, here, :].astype(f32)
        for m in range(1, chips):
            total += merge_landed[m, here, :].astype(f32)
        merge_part[here, :] = total.astype(low)
        merge_sums.at_end(j, 0)
        return carry

    lax.fori_loop(0, n, merge_block, 0)

    tiles = [slice(c * tile, (c + 1) * tile) for c in range(width // tile)]
    squares = jnp.zeros((rows, 1), f32)
    for at in tiles:
        v = x_own[:, at].astype(f32)
        squares += jnp.sum(v * v, axis=1, keepdims=True)
    root = lax.rsqrt(squares * (1.0 / width) + 1e-06)
    mean = jnp.zeros((rows, 1), f32)
    sums_all[...] = sums_in[...]
    for c, at in enumerate(tiles):
        v = x_own[:, at].astype(f32) * root
        dh = sums.own_value(c)
        mean += jnp.sum(dh * (1.0 + table[i, 1:2, at]) * v, axis=1, keepdims=True)
        sums_all[0:1, at] = jnp.sum(dh, axis=0, keepdims=True)
        sums_all[1:2, at] = jnp.sum(dh * v, axis=0, keepdims=True)

    unit = math.gcd(width, own_cols)
    for number in range(6):
        for start in range(0, width, unit):
            at = number * width + start
            shares[at // own_cols, :, at % own_cols : at % own_cols + unit] = (
                chosen[i][:, :1] * sums_all[number : number + 1, start : start + unit]
            )

    def to_line(source, target, sems, turn, whole=False):
        t = lax.rem(i + turn, n)
        return pltpu.make_async_remote_copy(
            src_ref=source if whole else source.at[t],
            dst_ref=target.at[i],
            send_sem=sems.at[0, t],
            recv_sem=sems.at[1, i],
            device_id=(d, t),
            device_id_type=MESH,
        )

    def from_line(source, target, sems, turn, whole=False):
        t = lax.rem(i + turn, n)
        return pltpu.make_async_remote_copy(
            src_ref=source if whole else source.at[t],
            dst_ref=target.at[t],
            send_sem=sems.at[0, t],
            recv_sem=sems.at[1, t],
            device_id=(d, t),
            device_id_type=MESH,
        )

    def to_plane(source, target, sems, flip):
        return pltpu.make_async_remote_copy(
            src_ref=source,
            dst_ref=target.at[d],
            send_sem=sems.at[0, flip],
            recv_sem=sems.at[1, flip],
            device_id=(d ^ flip, i),
            device_id_type=MESH,
        )

    def from_plane(source, target, sems, flip):
        return pltpu.make_async_remote_copy(
            src_ref=source,
            dst_ref=target.at[d ^ flip],
            send_sem=sems.at[0, flip],
            recv_sem=sems.at[1, flip],
            device_id=(d ^ flip, i),
            device_id_type=MESH,
        )

    for turn in range(1, n):
        to_line(shares, shares_all, share_sem, turn).start()
    mean = mean * (1.0 / width)
    for c, at in enumerate(tiles):
        v = x_own[:, at].astype(f32) * root
        u = sums.own_total(c) * (1.0 + table[i, 1:2, at])
        input_grad[:, at] = (d_middle[:, at] + root * (u - v * mean)).astype(low)
    shares_all[i] = shares[i]
    for turn in range(1, n):
        from_line(shares, shares_all, share_sem, turn).wait_recv()
    d_mod_all[d] = jnp.sum(shares_all[...], axis=0).astype(low).astype(f32)
    own_mod = d_mod_all.at[d]
    for flip in range(1, n_dp):
        to_plane(own_mod, d_mod_all, mod_sem, flip).start()
    for t in range(n - 1, 1, -1):
        for near in (True, False):
            merge_sums.pass_on(t, 0, near)
    for flip in range(1, n_dp):
        from_plane(own_mod, d_mod_all, mod_sem, flip).wait_recv()
    flat = d_mod_all[...].reshape(n_dp * 8, own_cols).astype(low)
    terms[...] = mm_nt(flat, mod_w[...]).reshape(n_dp, 8, k_rows)
    for turn in range(1, n):
        to_line(terms, terms_all, term_sem, turn, True).start()
    terms_all[i] = terms[...]
    for turn in range(1, n):
        from_line(terms, terms_all, term_sem, turn, True).wait_recv()
    noise_parts[...] = jnp.sum(terms_all[...], axis=0)
    for flip in range(1, n_dp):
        to_plane(noise_parts.at[d ^ flip], noise_sum, noise_sem, flip).start()
    noise_sum[d] = noise_parts[d]
    merge_out[...] = merge_sums.own_value(0)
    for flip in range(1, n_dp):
        from_plane(noise_parts.at[d ^ flip], noise_sum, noise_sem, flip).wait_recv()
    grad.landed_all()
    grad.finish()
    merge.finish()
    for turn in range(1, n):
        to_line(shares, shares_all, share_sem, turn).wait_send()
        to_line(terms, terms_all, term_sem, turn, True).wait_send()
    for flip in range(1, n_dp):
        to_plane(own_mod, d_mod_all, mod_sem, flip).wait_send()
        to_plane(noise_parts.at[d ^ flip], noise_sum, noise_sem, flip).wait_send()
    sums.all_sent()
    merge_sums.all_sent()


def last(n, n_dp, operands, shapes, number, tile=512):
    (rows, width), wide, k_rows, own_cols, (merge_rows, merge_cols) = shapes
    total, chips, pieces = n * rows, n_dp // 2, width // tile
    low, f32 = jnp.bfloat16, jnp.float32
    sds = jax.ShapeDtypeStruct
    return call(
        functools.partial(last_kernel, n, n_dp, tile),
        number,
        "last",
        [VMEM] * 8 + [HBM] * 2,
        [
            sds((rows, width), low),
            sds((n_dp, 8, own_cols), f32),
            sds((n_dp, 8, k_rows), f32),
            sds((chips, k_rows, wide), low),
            sds((merge_rows, merge_cols), f32),
        ],
        [VMEM] * 3 + [HBM] + [VMEM],
        [
            pltpu.VMEM((width, wide), low),
            pltpu.VMEM((total, width), low),
            pltpu.VMEM((total + rows, width), low),
            pltpu.VMEM((chips, k_rows, wide), low),
            pltpu.VMEM((chips, k_rows, wide), low),
            pltpu.VMEM((chips, k_rows, wide), low),
            pltpu.VMEM((chips, n * merge_rows, merge_cols), low),
            pltpu.VMEM((chips, n * merge_rows, merge_cols), low),
            pltpu.VMEM((chips, n * merge_rows, merge_cols), low),
            pltpu.VMEM((n * merge_rows, merge_cols), low),
            pltpu.VMEM(((n + 1) * merge_rows, merge_cols), low),
            pltpu.VMEM((8, width), f32),
            pltpu.VMEM((n, 8, own_cols), f32),
            pltpu.VMEM((n, 8, own_cols), f32),
            pltpu.VMEM((n_dp, 8, k_rows), f32),
            pltpu.VMEM((n, n_dp, 8, k_rows), f32),
            pltpu.VMEM((n_dp, 8, k_rows), f32),
            DMA((n, pieces)),
            DMA((n + 1, pieces)),
            DMA((n, 1)),
            DMA((n + 1, 1)),
            DMA((4, chips)),
            DMA((4, chips)),
            DMA((2, n)),
            DMA((2, n_dp)),
            DMA((2, n)),
            DMA((2, n_dp)),
            DMA,
            DMA((chips,)),
        ],
        flops=4 * total * width * wide,
    )(*operands)


def on_device(
    block_input,
    cotangent,
    noise_embed,
    image_sizes,
    attend_weight,
    merge_weight,
    up_weight,
    down_weight,
    modulate_weight,
):
    n = lax.axis_size("tensor")
    n_dp = lax.axis_size("dp")
    rows, width = block_input.shape
    tokens = n * rows
    images = image_sizes.shape[1]
    k_rows = modulate_weight.shape[0]

    sizes_row = image_sizes[0]
    ends = [sum(sizes_row[j] for j in range(last + 1)) for last in range(images)]

    def image_at(places):
        return sum((places >= end).astype(jnp.int32) for end in ends)

    block_images = image_at(jnp.arange(n, dtype=jnp.int32) * rows)
    chosen = (block_images[:, None] == jnp.arange(8, dtype=jnp.int32)[None, :]) & (
        jnp.arange(8) < images
    )[None]
    chosen = jnp.broadcast_to(chosen.astype(jnp.float32)[:, :, None], (n, 8, 128))
    area = min(256, tokens)
    area_images = image_at(jnp.arange(tokens // area, dtype=jnp.int32) * area)
    bias = jnp.where(area_images[:, None] == area_images[None, :], 0.0, MASKED)
    noise_low = jax.nn.silu(noise_embed.astype(jnp.float32)).astype(jnp.bfloat16)
    noise_slabs = noise_low.astype(jnp.float32).reshape(images, n_dp, k_rows).transpose(1, 0, 2)
    noise_slabs = jnp.pad(noise_slabs, ((0, 0), (0, 8 - images), (0, 0)))
    (
        cot_full,
        hidden_first,
        packed,
        lse,
        _,
        att_rows,
        attn_out,
        middle,
        hidden_second,
        table,
        attend_full,
        merge_full,
        up_full,
        down_full,
        noise_all,
    ) = front(
        n,
        n_dp,
        block_input,
        cotangent,
        noise_slabs,
        modulate_weight,
        chosen,
        bias,
        attend_weight,
        merge_weight,
        up_weight,
        down_weight,
        0,
    )
    d_hidden_second, mlp_part, up_local, down_local = ffn(
        n, hidden_second, table, cot_full, up_full, down_full, 1
    )
    units = up_full.shape[1]
    wide = packed.shape[1]
    (
        block_output,
        d_middle,
        d_qkv,
        row_sums,
        merge_local,
        up_landed,
        down_landed,
    ) = back(
        n,
        n_dp,
        (
            d_hidden_second,
            cotangent,
            middle,
            attn_out,
            table,
            att_rows,
            packed,
            lse,
            bias,
            mlp_part,
            merge_full,
            up_local,
            down_local,
        ),
        (block_input.shape, wide, units, k_rows, down_weight.shape[1], bias.shape[0]),
        2,
    )
    input_grad, d_mod_all, noise_sums, attend_landed, merge_part = last(
        n,
        n_dp,
        (
            d_qkv,
            hidden_first,
            block_input,
            d_middle,
            row_sums,
            table,
            chosen,
            modulate_weight,
            merge_local,
            attend_full,
        ),
        (block_input.shape, wide, k_rows, modulate_weight.shape[1], merge_weight.shape),
        3,
    )

    def chip_sum(landed):
        return jnp.sum(landed.astype(jnp.float32), axis=0)

    up_part, down_part, attend_part = map(chip_sum, (up_landed, down_landed, attend_landed))
    modulate_part = dot(
        noise_all.reshape(n_dp * 8, k_rows).astype(jnp.bfloat16),
        d_mod_all.reshape(n_dp * 8, -1).astype(jnp.bfloat16),
        ROWS_ROWS,
    )
    noise_sum = noise_sums[:, :images].transpose(1, 0, 2).reshape(images, width)
    silu_back = jax.vjp(jax.nn.silu, noise_embed.astype(jnp.float32))[1]
    noise_grad = silu_back(noise_sum)[0]
    return (
        block_output,
        input_grad,
        noise_grad,
        attend_part,
        merge_part,
        up_part,
        down_part,
        modulate_part,
    )


def solution(mesh):
    whole_rows = P(("dp", "tensor"), None)
    by_dp = P("dp", None)
    tall = P("dp", "tensor")
    wide = P("tensor", "dp")
    return jax.shard_map(
        on_device,
        mesh=mesh,
        in_specs=(whole_rows, whole_rows, by_dp, by_dp, tall, wide, tall, wide, tall),
        out_specs=(whole_rows, whole_rows, by_dp, tall, wide, tall, wide, tall),
        check_vma=False,
    )
```

```python
import functools
import math

import jax
import jax.numpy as jnp
from jax import lax
from jax.experimental import pallas as pl
from jax.experimental.pallas import tpu as pltpu
from jax.sharding import PartitionSpec as P

HEAD_DIM = 128
MASKED = -1e30


def dot(a, b, dims=(((1,), (0,)), ((), ()))):
    return lax.dot_general(a, b, dims, preferred_element_type=jnp.float32)


ROWS_ROWS = (((0,), (0,)), ((), ()))


MESH = pl.DeviceIdType.MESH
HBM = pl.BlockSpec(memory_space=pl.ANY)
VMEM = pl.BlockSpec(memory_space=pltpu.VMEM)
DMA = pltpu.SemaphoreType.DMA


def rows_of(j, rows):
    return pl.ds(pl.multiple_of(j * rows, rows), rows)


def beside(step):
    return (lax.axis_index("dp"), lax.axis_index("tensor") + step)


def greet_line(n, i):
    barrier = pltpu.get_barrier_semaphore()

    @pl.when(i > 0)
    def _():
        pl.semaphore_signal(barrier, inc=1, device_id=beside(-1), device_id_type=MESH)

    @pl.when(i < n - 1)
    def _():
        pl.semaphore_signal(barrier, inc=1, device_id=beside(1), device_id_type=MESH)

    pl.semaphore_wait(barrier, jnp.where(i > 0, 1, 0) + jnp.where(i < n - 1, 1, 0))


class LineGather:
    def __init__(self, n, i, rows, own, full, to_left, to_right, arrived):
        self.n, self.i, self.rows, self.own, self.full = n, i, rows, own, full
        self.to_left, self.to_right, self.arrived = to_left, to_right, arrived

    def copy(self, j, step, source=None):
        place = self.full.at[rows_of(j, self.rows)]
        return pltpu.make_async_remote_copy(
            src_ref=place if source is None else source,
            dst_ref=place,
            send_sem=(self.to_right if step > 0 else self.to_left).at[j],
            recv_sem=self.arrived.at[j],
            device_id=beside(step),
            device_id_type=MESH,
        )

    def start(self):
        @pl.when(self.i > 0)
        def _():
            self.copy(self.i, -1, self.own).start()

        @pl.when(self.i < self.n - 1)
        def _():
            self.copy(self.i, 1, self.own).start()

    def step(self, s):
        for side in (-1, 1):
            j = self.i + side * s
            there = (j >= 0) & (j < self.n)
            more = (self.i > 0) if side > 0 else (self.i < self.n - 1)

            @pl.when(there)
            def _():
                self.copy(j, side).wait_recv()

            @pl.when(there & more)
            def _():
                self.copy(j, -side).start()

    def finish(self):
        @pl.when(self.i > 0)
        def _():
            self.copy(self.i, -1, self.own).wait_send()

        @pl.when(self.i < self.n - 1)
        def _():
            self.copy(self.i, 1, self.own).wait_send()

        for j in range(self.n):

            @pl.when((j < self.i) & (self.i < self.n - 1))
            def _():
                self.copy(j, 1).wait_send()

            @pl.when((j > self.i) & (self.i > 0))
            def _():
                self.copy(j, -1).wait_send()


class LineScatter:
    def __init__(self, n, i, rows, width, part, got, sent, arrived):
        self.n, self.i, self.rows, self.width = n, i, rows, width
        self.part, self.got, self.sent, self.arrived = part, got, sent, arrived
        self.pieces = part.shape[1] // width

    def columns(self, c):
        if isinstance(c, int):
            return pl.ds(c * self.width, self.width)
        return pl.ds(pl.multiple_of(c * self.width, self.width), self.width)

    def copy(self, j, slot, c, step):
        return pltpu.make_async_remote_copy(
            src_ref=self.part.at[rows_of(j, self.rows), self.columns(c)],
            dst_ref=self.got.at[rows_of(slot, self.rows), self.columns(c)],
            send_sem=self.sent.at[j, c],
            recv_sem=self.arrived.at[slot, c],
            device_id=beside(step),
            device_id_type=MESH,
        )

    def slot_there(self, j, step):
        if step > 0:
            return j
        return jnp.where(j == self.i - 1, self.n, j)

    def at_end(self, j, c):
        @pl.when((self.i == 0) & (j > 0))
        def _():
            self.copy(j, j, c, 1).start()

        @pl.when((self.i == self.n - 1) & (j < self.i))
        def _():
            self.copy(j, self.slot_there(j, -1), c, -1).start()

    def pass_on(self, t, c, near):
        n, i = self.n, self.i
        rightward = (2 * i < n - 1) if near else (2 * i >= n - 1)
        j = jnp.where(rightward, t, n - 1 - t)
        step = jnp.where(rightward, 1, -1)
        right = rightward & (i > 0) & (j > i)
        left = jnp.logical_not(rightward) & (i < n - 1) & (j < i)

        @pl.when(right | left)
        def _():
            self.add(j, j, c)
            slot = jnp.where(left & (j == i - 1), n, j)
            self.copy(j, slot, c, step).start()

    def add(self, j, slot, c):
        self.copy(j, slot, c, 1).wait_recv()
        here = (rows_of(j, self.rows), self.columns(c))
        there = (rows_of(slot, self.rows), self.columns(c))
        total = self.part[here].astype(jnp.float32) + self.got[there].astype(jnp.float32)
        self.part[here] = total.astype(self.part.dtype)

    def own(self, c, out):
        i, n = self.i, self.n
        columns = self.columns(c)
        out[:, columns] = self.part[rows_of(i, self.rows), columns].astype(out.dtype)

        @pl.when(i > 0)
        def _():
            self.copy(i, i, c, 1).wait_recv()
            out[:, columns] += self.got[rows_of(i, self.rows), columns].astype(out.dtype)

        @pl.when(i < n - 1)
        def _():
            self.copy(i, n, c, -1).wait_recv()
            out[:, columns] += self.got[rows_of(n, self.rows), columns].astype(out.dtype)

    def own_value(self, c):
        i, n = self.i, self.n

        @pl.when(i > 0)
        def _():
            self.copy(i, i, c, 1).wait_recv()

        @pl.when(i < n - 1)
        def _():
            self.copy(i, n, c, -1).wait_recv()

        return self.own_total(c)

    def own_total(self, c):
        i, n, columns = self.i, self.n, self.columns(c)
        total = self.part[rows_of(i, self.rows), columns].astype(jnp.float32)
        left = self.got[rows_of(i, self.rows), columns].astype(jnp.float32)
        right = self.got[rows_of(n, self.rows), columns].astype(jnp.float32)
        return total + jnp.where(i > 0, left, 0.0) + jnp.where(i < n - 1, right, 0.0)

    def all_sent(self):
        def one(j, carry):
            @pl.when(j != self.i)
            def _():
                for c in range(self.pieces):
                    self.copy(j, 0, c, 1).wait_send()

            return carry

        lax.fori_loop(0, self.n, one, 0)


def mm(a, b):
    return lax.dot_general(a, b, (((1,), (0,)), ((), ())), preferred_element_type=jnp.float32)


def mm_nt(a, b):
    return lax.dot_general(a, b, (((1,), (1,)), ((), ())), preferred_element_type=jnp.float32)


def mm_tn(a, b):
    return lax.dot_general(a, b, (((0,), (0,)), ((), ())), preferred_element_type=jnp.float32)


def call(kernel, collective_id, name, in_specs, outs, out_specs, scratch, flops=0, limit=60):
    return pl.pallas_call(
        kernel,
        out_shape=outs,
        in_specs=in_specs,
        out_specs=out_specs,
        scratch_shapes=scratch,
        compiler_params=pltpu.CompilerParams(
            collective_id=collective_id,
            has_side_effects=True,
            vmem_limit_bytes=limit * 1024 * 1024,
        ),
        cost_estimate=pl.CostEstimate(flops=flops, bytes_accessed=1 << 20, transcendentals=0),
        name=name,
    )


def ffn_kernel(
    n,
    tile,
    grad_tile,
    own_hidden,
    table,
    d_mlp_hbm,
    up_hbm,
    down_hbm,
    d_hidden,
    mlp_part,
    up_grad,
    down_grad,
    up,
    down,
    d_mlp,
    hidden,
    activated,
    d_pre,
    part,
    got,
    stage,
    to_left,
    to_right,
    arrived,
    sent,
    came,
    local,
    stage_sem,
):
    i = lax.axis_index("tensor")
    rows, width = own_hidden.shape
    units = up.shape[1]
    loads = [
        pltpu.make_async_copy(source, target, local.at[k])
        for k, (source, target) in enumerate(((up_hbm, up), (d_mlp_hbm, d_mlp), (down_hbm, down)))
    ]
    for load in loads:
        load.start()
    greet_line(n, i)
    line = LineGather(n, i, rows, own_hidden, hidden, to_left, to_right, arrived)
    line.start()
    sums = LineScatter(n, i, rows, tile, part, got, sent, came)
    hidden[rows_of(i, rows), :] = own_hidden[...]
    for load in loads:
        load.wait()

    def one_block(j):
        here = rows_of(j, rows)

        def gated(c, carry):
            at = pl.ds(pl.multiple_of(c * tile, tile), tile)
            d_mlp[here, at] = (d_mlp[here, at].astype(jnp.float32) * table[j, 5:6, at]).astype(
                jnp.bfloat16
            )
            return carry

        lax.fori_loop(0, width // tile, gated, 0)

        def first(c, carry):
            at = pl.ds(pl.multiple_of(c * tile, tile), tile)
            pre = mm(hidden[here, :], up[:, at])
            d_act = mm_nt(d_mlp[here, :], down[at, :])
            cdf = 0.5 * (1.0 + lax.erf(pre * (0.5**0.5)))
            density = jnp.exp(-0.5 * pre * pre) * ((0.5 / math.pi) ** 0.5)
            activated[here, at] = (pre * cdf).astype(jnp.bfloat16)
            d_pre[here, at] = (d_act * (cdf + pre * density)).astype(jnp.bfloat16)
            return carry

        lax.fori_loop(0, units // tile, first, 0)

        def second(c, carry):
            at = pl.ds(pl.multiple_of(c * tile, tile), tile)
            part[here, at] = mm_nt(d_pre[here, :], up[at, :]).astype(jnp.bfloat16)
            sums.at_end(j, c)
            return carry

        lax.fori_loop(0, width // tile, second, 0)

        def third(c, carry):
            at = pl.ds(pl.multiple_of(c * tile, tile), tile)
            mlp_part[here, at] = mm(activated[here, :], down[:, at]).astype(jnp.bfloat16)
            return carry

        lax.fori_loop(0, width // tile, third, 0)

    def visit(q, carry):
        s = (q + 1) // 2
        side = 1 - 2 * (q % 2)
        j = i + s * side

        @pl.when(q % 2 == 1)
        def _():
            line.step(s)

        @pl.when((j >= 0) & (j < n))
        def _():
            one_block(j)

        return carry

    lax.fori_loop(0, 2 * n - 1, visit, 0)

    count = (width // grad_tile) * (units // grad_tile)
    turns = 2 * max(n - 2, 1) * sums.pieces
    per_turn = -(-2 * count // turns)

    def square(ref, row, column):
        return ref.at[
            pl.ds(pl.multiple_of(row * grad_tile, grad_tile), grad_tile),
            pl.ds(pl.multiple_of(column * grad_tile, grad_tile), grad_tile),
        ]

    def put(slot, target):
        return pltpu.make_async_copy(stage.at[slot], target, stage_sem.at[slot])

    def one_grad(k, left, right, target):
        wide = right.shape[1] // grad_tile
        row, column = k // wide, k % wide
        slot = k % 2

        @pl.when(k >= 2)
        def _():
            put(slot, square(target, 0, 0)).wait()

        a = left[:, pl.ds(pl.multiple_of(row * grad_tile, grad_tile), grad_tile)]
        b = right[:, pl.ds(pl.multiple_of(column * grad_tile, grad_tile), grad_tile)]
        stage[slot] = mm_tn(a, b).astype(jnp.bfloat16)
        put(slot, square(target, row, column)).start()

    def tail(k, carry):
        t, c = 2 + k // (2 * sums.pieces), k % sums.pieces
        for near in (True, False):

            @pl.when((k // sums.pieces) % 2 == (0 if near else 1))
            def _():
                sums.pass_on(t, c, near)

        for extra in range(per_turn):
            item = k * per_turn + extra

            @pl.when(item < count)
            def _():
                one_grad(item, hidden, d_pre, up_grad)

            @pl.when(item == count)
            def _():
                for slot in range(2):
                    put(slot, square(up_grad, 0, 0)).wait()

            @pl.when((item >= count) & (item < 2 * count))
            def _():
                one_grad(item - count, activated, d_mlp, down_grad)

        return carry

    lax.fori_loop(0, turns, tail, 0)
    for slot in range(2):
        put(slot, square(down_grad, 0, 0)).wait()
    for c in range(sums.pieces):
        sums.own(c, d_hidden)
    line.finish()
    sums.all_sent()


def ffn(n, own_hidden, table, cotangents, up, down, collective_id, tile=512, grad_tile=512):
    rows, width = own_hidden.shape
    units = up.shape[1]
    pieces = width // tile
    low = jnp.bfloat16
    return call(
        functools.partial(ffn_kernel, n, tile, grad_tile),
        collective_id,
        "ffn",
        [VMEM, VMEM, HBM, HBM, HBM],
        [
            jax.ShapeDtypeStruct((rows, width), jnp.float32),
            jax.ShapeDtypeStruct((n * rows, width), low),
            jax.ShapeDtypeStruct((width, units), low),
            jax.ShapeDtypeStruct((units, width), low),
        ],
        [VMEM, VMEM, HBM, HBM],
        [
            pltpu.VMEM((width, units), low),
            pltpu.VMEM((units, width), low),
            pltpu.VMEM((n * rows, width), low),
            pltpu.VMEM((n * rows, width), low),
            pltpu.VMEM((n * rows, units), low),
            pltpu.VMEM((n * rows, units), low),
            pltpu.VMEM((n * rows, width), low),
            pltpu.VMEM(((n + 1) * rows, width), low),
            pltpu.VMEM((2, grad_tile, grad_tile), low),
            DMA((n,)),
            DMA((n,)),
            DMA((n,)),
            DMA((n, pieces)),
            DMA((n + 1, pieces)),
            DMA((3,)),
            DMA((2,)),
        ],
        flops=12 * n * rows * width * units,
    )(own_hidden, table, cotangents, up, down)


class PlaneGather:
    def __init__(self, n_dp, d, own, view, height, sent, came):
        self.n_dp, self.d, self.own, self.view, self.height = n_dp, d, own, view, height
        self.sent, self.came = sent, came
        self.square = n_dp == 8
        self.peers = [2 * k for k in range(1, n_dp // 2)]

    def copy(self, k, source, target, peer):
        return pltpu.make_async_remote_copy(
            src_ref=source,
            dst_ref=target,
            send_sem=self.sent.at[k],
            recv_sem=self.came.at[k],
            device_id=(self.d ^ peer, lax.axis_index("tensor")),
            device_id_type=MESH,
        )

    def slab(self, flip, half=None):
        if half is None:
            return self.view(self.d ^ flip, 0, self.height)
        return self.view(self.d ^ flip, half * (self.height // 2), self.height // 2)

    def owns(self):
        peers = [2, 4] if self.square else self.peers
        return [
            self.copy(k, self.own, self.slab(0), peer) for k, peer in enumerate([1] + peers)
        ]

    def relay_of(self, k):
        flip, half, peer = ((2, 0, 4), (4, 1, 2))[k - 1]
        return self.copy(2 + k, self.slab(flip, half), self.slab(flip, half), peer)

    def across(self):
        return [
            self.copy(3, self.slab(6, 0), self.slab(6, 0), 4),
            self.copy(4, self.slab(6, 1), self.slab(6, 1), 2),
        ]

    def hand(self, flip):
        base = 5 if self.square else len(self.peers) + 1
        k = base + flip // 2 - 1
        return self.copy(k, self.slab(flip), self.slab(flip), 1)

    def handed(self, flip):
        base = 5 if self.square else len(self.peers) + 1
        k = base + flip // 2 - 1
        return self.copy(k, self.slab(flip ^ 1), self.slab(flip ^ 1), 1)

    def start(self):
        for copy in self.owns():
            copy.start()

    def relay(self):
        if not self.square:
            return
        for k, flip in ((1, 2), (2, 4)):
            self.copy(k, self.own, self.slab(flip), flip).wait_recv()
            self.relay_of(k).start()
            self.hand(flip).start()

    def close(self):
        if self.square:
            for copy in self.across():
                copy.wait_recv()
            self.hand(6).start()
        else:
            for k, flip in enumerate(self.peers):
                self.copy(k + 1, self.own, self.slab(flip), flip).wait_recv()
                self.hand(flip).start()
        self.copy(0, self.own, self.slab(1), 1).wait_recv()
        for flip in self.peers:
            self.handed(flip).wait_recv()

    def finish(self):
        for copy in self.owns():
            copy.wait_send()
        if self.square:
            for k in (1, 2):
                self.relay_of(k).wait_send()
        for flip in self.peers:
            self.hand(flip).wait_send()


def plane_sems(n_dp):
    return 8 if n_dp == 8 else n_dp - 1


def greet_all(n, n_dp, d, i):
    barrier = pltpu.get_barrier_semaphore()
    for flip in range(1, n_dp):
        pl.semaphore_signal(barrier, inc=1, device_id=(d ^ flip, i), device_id_type=MESH)
    for turn in range(1, n):
        pl.semaphore_signal(
            barrier, inc=1, device_id=(d, lax.rem(i + turn, n)), device_id_type=MESH
        )
    pl.semaphore_wait(barrier, n_dp + n - 2)


def front_kernel(
    n,
    n_dp,
    heads,
    tile,
    x_own,
    cot_own,
    noise,
    mod_w,
    chosen,
    bias,
    attend_w,
    merge_w,
    up_w,
    down_w,
    cot_full,
    hidden,
    qkv,
    lse,
    attended,
    att_rows,
    attn_out,
    middle,
    hidden_second,
    table,
    attend_full,
    merge_full,
    up_full,
    down_full,
    noise_all,
    x_full,
    attend,
    merge,
    terms,
    terms_all,
    columns,
    noise_sem,
    terms_sem,
    column_sem,
    x_sem,
    cot_sem,
    merge_sem,
    weight_sent,
    weight_came,
    out_sem,
    att_sem,
    local,
):
    d, i = lax.axis_index("dp"), lax.axis_index("tensor")
    rows, width = x_own.shape
    k_rows, own_cols = mod_w.shape
    head_cols = heads * HEAD_DIM
    low, f32 = jnp.bfloat16, jnp.float32
    merge_rows, merge_cols = merge_w.shape
    down_cols = down_w.shape[1]
    merge_slab = merge.at[:, pl.ds(pl.multiple_of(d * merge_cols, merge_cols), merge_cols)]

    def row_view(full, height):
        return lambda at, start, count: full.at[
            pl.ds(pl.multiple_of(at * height + start, 16), count), :
        ]

    def column_view(full, wide):
        return lambda at, start, count: full.at[
            pl.ds(start, count), pl.ds(pl.multiple_of(at * wide, wide), wide)
        ]

    weights = [
        PlaneGather(n_dp, d, own, view, height, weight_sent.at[k], weight_came.at[k])
        for k, (own, view, height) in enumerate(
            (
                (attend_w, row_view(attend, k_rows), k_rows),
                (merge_slab, column_view(merge, merge_cols), n * merge_rows),
                (up_w, row_view(up_full, k_rows), k_rows),
                (down_w, column_view(down_full, down_cols), down_w.shape[0]),
            )
        )
    ]
    attend_g, merge_g, up_g, down_g = weights
    copies = [
        pltpu.make_async_copy(source, target, local.at[k])
        for k, (source, target) in enumerate(
            (
                (cot_own, cot_full.at[rows_of(i, rows)]),
                (attend_w, attend_g.slab(0)),
                (merge_w, merge_slab.at[rows_of(i, merge_rows)]),
                (up_w, up_g.slab(0)),
                (down_w, down_g.slab(0)),
            )
        )
    ]
    for copy in copies:
        copy.start()
    greet_all(n, n_dp, d, i)

    def to_plane(source, target, sems, flip):
        return pltpu.make_async_remote_copy(
            src_ref=source.at[d ^ flip],
            dst_ref=target.at[d],
            send_sem=sems.at[0, flip],
            recv_sem=sems.at[1, flip],
            device_id=(d ^ flip, i),
            device_id_type=MESH,
        )

    def from_plane(target, sems, flip):
        return pltpu.make_async_remote_copy(
            src_ref=target.at[d ^ flip],
            dst_ref=target.at[d ^ flip],
            send_sem=sems.at[0, flip],
            recv_sem=sems.at[1, flip],
            device_id=(d ^ flip, i),
            device_id_type=MESH,
        )

    for flip in range(1, n_dp):
        to_plane(noise, noise_all, noise_sem, flip).start()
    merge_line = LineGather(
        n, i, merge_rows, merge_w, merge_slab, merge_sem.at[0], merge_sem.at[1], merge_sem.at[2]
    )
    x_line = LineGather(n, i, rows, x_own, x_full, x_sem.at[0], x_sem.at[1], x_sem.at[2])
    cot_line = LineGather(
        n, i, rows, cot_own, cot_full, cot_sem.at[0], cot_sem.at[1], cot_sem.at[2]
    )
    x_line.start()
    noise_all[d] = noise[d]
    x_full[rows_of(i, rows), :] = x_own[...]
    for flip in range(1, n_dp):
        from_plane(noise_all, noise_sem, flip).wait_recv()
    pictures = noise.shape[1]
    images = noise_all[...].reshape(n_dp * pictures, k_rows).astype(low)
    for c in range(own_cols // tile):
        terms[:, :, c * tile : (c + 1) * tile] = mm(
            images, mod_w[:, c * tile : (c + 1) * tile]
        ).reshape(n_dp, pictures, tile)
    for flip in range(1, n_dp):
        to_plane(terms, terms_all, terms_sem, flip).start()
    attend_g.start()
    terms_all[d] = terms[d]
    for flip in range(1, n_dp):
        from_plane(terms_all, terms_sem, flip).wait_recv()
    columns[i] = jnp.sum(terms_all[...], axis=0)

    def to_line(turn):
        t = lax.rem(i + turn, n)
        return pltpu.make_async_remote_copy(
            src_ref=columns.at[i],
            dst_ref=columns.at[i],
            send_sem=column_sem.at[0, t],
            recv_sem=column_sem.at[1, i],
            device_id=(d, t),
            device_id_type=MESH,
        )

    def from_line(turn):
        t = lax.rem(i + turn, n)
        return pltpu.make_async_remote_copy(
            src_ref=columns.at[t],
            dst_ref=columns.at[t],
            send_sem=column_sem.at[0, t],
            recv_sem=column_sem.at[1, t],
            device_id=(d, t),
            device_id_type=MESH,
        )

    for turn in range(1, n):
        to_line(turn).start()
    merge_line.start()
    x_line.step(1)
    for turn in range(1, n):
        from_line(turn).wait_recv()
    unit = math.gcd(width, own_cols)

    def fill(j, carry):
        for number in range(6):
            for start in range(0, width, unit):
                at = number * width + start
                part = columns[at // own_cols, :, at % own_cols : at % own_cols + unit]
                table[j, number : number + 1, start : start + unit] = jnp.sum(
                    part * chosen[j][:, :1], axis=0, keepdims=True
                )
        return carry

    lax.fori_loop(0, n, fill, 0)
    attend_g.relay()
    merge_line.step(1)
    for copy in copies:
        copy.wait()
    attend_g.close()
    up_g.start()
    keep_attend = pltpu.make_async_copy(attend, attend_full, out_sem.at[0])
    keep_merge = pltpu.make_async_copy(merge, merge_full, out_sem.at[1])
    keep_attend.start()

    def tiles(count):
        return [slice(c * tile, (c + 1) * tile) for c in range(count // tile)]

    def one_block(j):
        here = rows_of(j, rows)
        squares = jnp.zeros((rows, 1), f32)
        for at in tiles(width):
            v = x_full[here, at].astype(f32)
            squares += jnp.sum(v * v, axis=1, keepdims=True)
        root = lax.rsqrt(squares * (1.0 / width) + 1e-06)
        for at in tiles(width):
            v = x_full[here, at].astype(f32) * root
            hidden[here, at] = (v * (1.0 + table[j, 1:2, at]) + table[j, 0:1, at]).astype(low)
        wide = qkv.shape[1]
        step = math.gcd(wide, 512)
        for c in range(wide // step):
            at = slice(c * step, (c + 1) * step)
            qkv[here, at] = mm(hidden[here, :], attend[:, at]).astype(low)

    def visit(q, carry):
        s = (q + 1) // 2
        side = 1 - 2 * (q % 2)
        j = i + s * side

        @pl.when((q % 2 == 1) & (s + 1 < n))
        def _():
            x_line.step(s + 1)
            merge_line.step(s + 1)

        @pl.when(q == 2 * n - 5)
        def _():
            up_g.relay()
            merge_g.start()
            cot_line.start()

        @pl.when((j >= 0) & (j < n))
        def _():
            one_block(j)

        return carry

    lax.fori_loop(0, 2 * n - 1, visit, 0)

    area = min(256, n * rows)
    areas = n * rows // area
    owners = area // rows

    def to_owner(j):
        return pltpu.make_async_remote_copy(
            src_ref=attended.at[rows_of(j, rows), :],
            dst_ref=att_rows.at[:, pl.ds(pl.multiple_of(i * head_cols, head_cols), head_cols)],
            send_sem=att_sem.at[0, j],
            recv_sem=att_sem.at[1, i],
            device_id=(d, j),
            device_id_type=MESH,
        )

    def from_source(t):
        return pltpu.make_async_remote_copy(
            src_ref=attended.at[rows_of(t, rows), :],
            dst_ref=att_rows.at[:, pl.ds(pl.multiple_of(t * head_cols, head_cols), head_cols)],
            send_sem=att_sem.at[0, t],
            recv_sem=att_sem.at[1, t],
            device_id=(d, t),
            device_id_type=MESH,
        )

    def attend_area(turn, carry):
        here_at = lax.rem(i // owners + 1 + turn, areas)
        here = rows_of(here_at, area)
        for h in range(heads):
            first = h * 3 * HEAD_DIM
            q = qkv[here, first : first + HEAD_DIM]
            parts = []
            for b in range(areas):
                key = qkv[b * area : (b + 1) * area, first + HEAD_DIM : first + 2 * HEAD_DIM]
                parts.append(mm_nt(key, q) * HEAD_DIM ** (-0.5) + bias[here_at, b])
            highest = parts[0].max(axis=0, keepdims=True)
            for part in parts[1:]:
                highest = jnp.maximum(highest, part.max(axis=0, keepdims=True))
            parts = [jnp.exp(part - highest) for part in parts]
            totals = sum(jnp.sum(part, axis=0, keepdims=True) for part in parts)
            inverse = 1.0 / totals
            out = jnp.zeros((HEAD_DIM, area), f32)
            for b in range(areas):
                value = qkv[b * area : (b + 1) * area, first + 2 * HEAD_DIM : first + 3 * HEAD_DIM]
                out += mm_tn(value, (parts[b] * inverse).astype(low))
            attended[here, h * HEAD_DIM : (h + 1) * HEAD_DIM] = out.T.astype(low)
            lse[pl.ds(here_at * heads + h, 1), :] = highest + jnp.log(totals)
        for k in range(owners):
            j = here_at * owners + k

            @pl.when(j != i)
            def _():
                to_owner(j).start()

        @pl.when(turn == (areas - 1) // 2)
        def _():
            up_g.close()
            cot_line.step(1)

        @pl.when(turn == areas - 1)
        def _():
            merge_g.relay()
            down_g.start()

        return carry

    lax.fori_loop(0, areas, attend_area, 0)
    att_rows[:, pl.ds(pl.multiple_of(i * head_cols, head_cols), head_cols)] = attended[
        rows_of(i, rows), :
    ]
    if n > 2:
        cot_line.step(2)
    merge_g.close()
    keep_merge.start()
    for turn in range(1, n):
        from_source(lax.rem(i + turn, n)).wait_recv()
    squares = jnp.zeros((rows, 1), f32)
    for at in tiles(width):
        out = mm(att_rows[...], merge[:, at])
        attn_out[:, at] = out
        v = x_own[:, at].astype(f32) + table[i, 2:3, at] * out
        middle[:, at] = v
        squares += jnp.sum(v * v, axis=1, keepdims=True)
    root = lax.rsqrt(squares * (1.0 / width) + 1e-06)
    for at in tiles(width):
        v = middle[:, at] * root
        hidden_second[:, at] = (v * (1.0 + table[i, 4:5, at]) + table[i, 3:4, at]).astype(low)
    down_g.relay()
    for s in range(3, n):
        cot_line.step(s)
    down_g.close()
    keep_attend.wait()
    keep_merge.wait()
    for flip in range(1, n_dp):
        to_plane(noise, noise_all, noise_sem, flip).wait_send()
        to_plane(terms, terms_all, terms_sem, flip).wait_send()
    for line in (merge_line, x_line, cot_line):
        line.finish()
    for turn in range(1, n):
        to_line(turn).wait_send()
    for turn in range(1, n):
        to_owner(lax.rem(i + turn, n)).wait_send()
    for weight in weights:
        weight.finish()


def front(n, n_dp, x, cot, noise, mod_w, chosen, bias, attend_w, merge_w, up_w, down_w, number):
    rows, width = x.shape
    k_rows, own_cols = mod_w.shape
    wide = attend_w.shape[1]
    heads = wide // (3 * HEAD_DIM)
    total = n * rows
    areas = bias.shape[0]
    low, f32 = jnp.bfloat16, jnp.float32
    sds = jax.ShapeDtypeStruct
    count = plane_sems(n_dp)
    return call(
        functools.partial(front_kernel, n, n_dp, heads, 512),
        number,
        "front",
        [VMEM] * 5 + [pl.BlockSpec(memory_space=pltpu.SMEM)] + [VMEM] * 4,
        [
            sds((total, width), low),
            sds((total, width), low),
            sds((total, wide), low),
            sds((areas * heads, total // areas), f32),
            sds((total, heads * HEAD_DIM), low),
            sds((rows, width), low),
            sds((rows, width), f32),
            sds((rows, width), f32),
            sds((rows, width), low),
            sds((n, 8, width), f32),
            sds((n_dp * k_rows, wide), low),
            sds((n * merge_w.shape[0], n_dp * merge_w.shape[1]), low),
            sds((n_dp * k_rows, up_w.shape[1]), low),
            sds((down_w.shape[0], n_dp * down_w.shape[1]), low),
            sds(noise.shape, f32),
        ],
        [HBM] + [VMEM] * 9 + [HBM] * 4 + [VMEM],
        [
            pltpu.VMEM((total, width), low),
            pltpu.VMEM((n_dp * k_rows, wide), low),
            pltpu.VMEM((n * merge_w.shape[0], n_dp * merge_w.shape[1]), low),
            pltpu.VMEM((n_dp, noise.shape[1], own_cols), f32),
            pltpu.VMEM((n_dp, noise.shape[1], own_cols), f32),
            pltpu.VMEM((n, noise.shape[1], own_cols), f32),
            DMA((2, n_dp)),
            DMA((2, n_dp)),
            DMA((3, n)),
            DMA((3, n)),
            DMA((3, n)),
            DMA((3, n)),
            DMA((4, count)),
            DMA((4, count)),
            DMA((2,)),
            DMA((2, n)),
            DMA((5,)),
        ],
        flops=2 * total * width * wide,
    )(x, cot, noise, mod_w, chosen, bias, attend_w, merge_w, up_w, down_w)


class PlaneScatter:
    def __init__(self, n_dp, d, theirs, own, swapped, via, landed, sems):
        self.chips, self.d, self.square = n_dp // 2, d, n_dp == 8
        self.chip, self.side = d // 2, lax.rem(d, 2)
        self.theirs, self.own, self.swapped, self.via = theirs, own, swapped, via
        self.landed, self.sems = landed, sems

    def remote(self, source, target, sent, came, device):
        return pltpu.make_async_remote_copy(
            src_ref=source,
            dst_ref=target,
            send_sem=sent,
            recv_sem=came,
            device_id=(device, lax.axis_index("tensor")),
            device_id_type=MESH,
        )

    def swap(self, m):
        return self.remote(
            self.theirs(m), self.swapped.at[m], self.sems.at[0, m], self.sems.at[1, m], self.d ^ 1
        )

    def half(self, ref, which):
        height = self.own.shape[1] // 2
        return ref.at[pl.ds(which * height, height), :]

    def step(self, k):
        slab, which, peer = ((1, 0, 1), (3, 0, 1), (2, 1, 2), (3, 1, 2), (2, 0, 2), (1, 1, 1))[k]
        target = self.via if slab == 3 else self.landed.at[1 if k < 4 else 2]
        return self.remote(
            self.half(self.own.at[self.chip ^ slab], which),
            self.half(target, which),
            self.sems.at[2, k],
            self.sems.at[3, k],
            2 * (self.chip ^ peer) + self.side,
        )

    def send(self, m, slot, sem):
        return self.remote(
            self.own.at[m],
            self.landed.at[slot],
            self.sems.at[2, m],
            self.sems.at[3, sem],
            2 * m + self.side,
        )

    def keep(self):
        slot = 0 if self.square else self.chip
        return pltpu.make_async_copy(
            self.own.at[self.chip], self.landed.at[slot], self.sems.at[2, 6 if self.square else self.chip]
        )

    def swap_all(self):
        def one(m, carry):
            self.swap(m).start()
            return carry

        lax.fori_loop(0, self.chips, one, 0)

    def add(self, target, source):
        height, wide = target.shape
        chunk = math.gcd(height, 64 if wide > 512 else 256)

        def one(c, carry):
            at = pl.ds(pl.multiple_of(c * chunk, chunk), chunk)
            total = target[at, :].astype(jnp.float32) + source[at, :].astype(jnp.float32)
            target[at, :] = total.astype(target.dtype)
            return carry

        lax.fori_loop(0, height // chunk, one, 0)

    def add_and_send(self):
        def one(k, carry):
            m = self.chip ^ (self.chips - 1 - k)
            self.swap(m).wait_recv()
            self.add(self.own.at[m], self.swapped.at[m])
            if not self.square:

                @pl.when(m != self.chip)
                def _():
                    self.send(m, self.chip, self.chip).start()

            return carry

        lax.fori_loop(0, self.chips, one, 0)
        if self.square:
            for k in (1, 3, 0, 2):
                self.step(k).start()
        self.keep().start()

    def relay(self):
        if self.square:
            for k, slab, which in ((1, 2, 0), (3, 1, 1)):
                self.step(k).wait_recv()
                self.step(k).wait_send()
                self.add(self.half(self.own.at[self.chip ^ slab], which), self.half(self.via, which))
                self.step(4 if k == 1 else 5).start()

    def landed_all(self):
        if self.square:
            for k in (0, 2, 4, 5):
                self.step(k).wait_recv()
        else:
            for k in range(1, self.chips):
                self.send(self.chip ^ k, self.chip ^ k, self.chip ^ k).wait_recv()
        self.keep().wait()

    def finish(self):
        for m in range(self.chips):
            self.swap(m).wait_send()
        if self.square:
            for k in (0, 2, 4, 5):
                self.step(k).wait_send()
        else:
            for k in range(1, self.chips):
                self.send(self.chip ^ k, self.chip, self.chip).wait_send()


def plane_slots(n_dp):
    return 3 if n_dp == 8 else n_dp // 2


def scatter_sems(n_dp):
    return DMA((4, max(7, n_dp // 2)))


def flows(n, pieces, sums, turn):
    far, rest = turn // ((n - 2) * pieces), lax.rem(turn, (n - 2) * pieces)
    t, c = n - 1 - rest // pieces, lax.rem(rest, pieces)
    for near in (True, False):

        @pl.when(far == (0 if near else 1))
        def _():
            sums.pass_on(t, c, near)


def back_kernel(
    n,
    n_dp,
    heads,
    tile,
    d_hidden,
    cot,
    middle,
    attn_out,
    table,
    att_rows,
    qkv,
    lse,
    bias,
    mlp_hbm,
    merge_hbm,
    up_hbm,
    down_hbm,
    block_out,
    d_middle,
    d_qkv,
    sums_out,
    merge_grad,
    up_landed,
    down_landed,
    part,
    got,
    merge,
    d_att,
    d_send,
    d_attn,
    d_keys,
    d_values,
    up_own,
    up_swapped,
    up_via,
    down_own,
    down_swapped,
    down_via,
    stage,
    mlp_sent,
    mlp_came,
    up_sems,
    down_sems,
    att_sem,
    merge_sem,
    load_sem,
    stage_sem,
    own_sem,
):
    d, i = lax.axis_index("dp"), lax.axis_index("tensor")
    rows, width = middle.shape
    low, f32 = jnp.bfloat16, jnp.float32
    head_cols = heads * HEAD_DIM
    chips = n_dp // 2
    k_rows, down_cols = up_own.shape[1], down_own.shape[2]
    side = lax.rem(d, 2)

    def up_slab(at):
        return up_hbm.at[pl.ds(pl.multiple_of(at * k_rows, k_rows), k_rows), :]

    def down_slab(at):
        return down_hbm.at[:, pl.ds(pl.multiple_of(at * down_cols, down_cols), down_cols)]

    load_mlp = pltpu.make_async_copy(mlp_hbm, part, load_sem.at[0])
    load_mlp.start()

    some = merge.shape[1]
    shares = head_cols // some

    def load_merge(k, slot):
        return pltpu.make_async_copy(
            merge_hbm.at[pl.ds(pl.multiple_of(k * some, some), some), :],
            merge.at[slot],
            merge_sem.at[slot],
        )

    load_merge(0, 0).start()
    for m in range(chips):
        pltpu.make_async_copy(up_slab(2 * m + side), up_own.at[m], own_sem.at[0, m]).start()
        pltpu.make_async_copy(down_slab(2 * m + side), down_own.at[m], own_sem.at[1, m]).start()
    greet_all(n, n_dp, d, i)
    up = PlaneScatter(
        n_dp, d, lambda m: up_slab(2 * m + 1 - side), up_own, up_swapped, up_via, up_landed, up_sems
    )
    down = PlaneScatter(
        n_dp,
        d,
        lambda m: down_slab(2 * m + 1 - side),
        down_own,
        down_swapped,
        down_via,
        down_landed,
        down_sems,
    )
    up.swap_all()
    down.swap_all()
    load_mlp.wait()
    sums = LineScatter(n, i, rows, tile, part, got, mlp_sent, mlp_came)
    pieces = sums.pieces

    def ends(k, carry):
        t, c = n - 1 - k // pieces, lax.rem(k, pieces)
        pl.when(i == 0)(functools.partial(sums.at_end, t, c))
        pl.when(i == n - 1)(functools.partial(sums.at_end, n - 1 - t, c))
        return carry

    lax.fori_loop(0, min(n - 1, 1) * pieces, ends, 0)

    tiles = [slice(c * tile, (c + 1) * tile) for c in range(width // tile)]
    squares = jnp.zeros((rows, 1), f32)
    for at in tiles:
        squares += jnp.sum(middle[:, at] * middle[:, at], axis=1, keepdims=True)
    root = lax.rsqrt(squares * (1.0 / width) + 1e-06)
    mean = jnp.zeros((rows, 1), f32)
    for at in tiles:
        v = middle[:, at] * root
        dh = d_hidden[:, at]
        mean += jnp.sum(dh * (1.0 + table[i, 4:5, at]) * v, axis=1, keepdims=True)
        sums_out[3:4, at] = jnp.sum(dh, axis=0, keepdims=True)
        sums_out[4:5, at] = jnp.sum(dh * v, axis=0, keepdims=True)
    mean = mean * (1.0 / width)
    for at in tiles:
        v = middle[:, at] * root
        u = d_hidden[:, at] * (1.0 + table[i, 4:5, at])
        dm = cot[:, at].astype(f32) + root * (u - v * mean)
        d_middle[:, at] = dm
        d_attn[:, at] = (table[i, 2:3, at] * dm).astype(low)
        sums_out[2:3, at] = jnp.sum(dm * attn_out[:, at], axis=0, keepdims=True)

    def to_heads(t):
        return pltpu.make_async_remote_copy(
            src_ref=d_send.at[t],
            dst_ref=d_att.at[rows_of(i, rows), :],
            send_sem=att_sem.at[0, t],
            recv_sem=att_sem.at[1, i],
            device_id=(d, t),
            device_id_type=MESH,
        )

    def from_rows(t):
        return pltpu.make_async_remote_copy(
            src_ref=d_send.at[t],
            dst_ref=d_att.at[rows_of(t, rows), :],
            send_sem=att_sem.at[0, t],
            recv_sem=att_sem.at[1, t],
            device_id=(d, t),
            device_id_type=MESH,
        )

    def head_part(t, carry):
        for share in range(shares):
            k = t * shares + share
            slot = lax.rem(k, 2)

            @pl.when(k + 1 < n * shares)
            def _():
                load_merge(k + 1, 1 - slot).start()

            load_merge(k, slot).wait()
            d_send[t, :, share * some : (share + 1) * some] = mm_nt(
                d_attn[...], merge[slot]
            ).astype(low)

        @pl.when(t != i)
        def _():
            to_heads(t).start()

        return carry

    lax.fori_loop(0, n, head_part, 0)
    lax.fori_loop(min(n - 1, 1) * pieces, (n - 1) * pieces, ends, 0)
    d_att[rows_of(i, rows), :] = d_send[i]
    for m in range(chips):
        pltpu.make_async_copy(up_slab(2 * m + side), up_own.at[m], own_sem.at[0, m]).wait()
        pltpu.make_async_copy(down_slab(2 * m + side), down_own.at[m], own_sem.at[1, m]).wait()
    up.add_and_send()

    wide = width // tile
    short = stage.shape[1]

    def square(row, column):
        return merge_grad.at[
            pl.ds(pl.multiple_of(row * short, short), short),
            pl.ds(pl.multiple_of(column * tile, tile), tile),
        ]

    def merge_one(k, carry):
        row, column = k // wide, lax.rem(k, wide)
        slot = lax.rem(k, 2)

        @pl.when(k >= 2)
        def _():
            pltpu.make_async_copy(stage.at[slot], square(0, 0), stage_sem.at[slot]).wait()

        a = att_rows[:, pl.ds(pl.multiple_of(row * short, short), short)]
        b = d_attn[:, pl.ds(pl.multiple_of(column * tile, tile), tile)]
        stage[slot] = mm_tn(a, b).astype(low)
        pltpu.make_async_copy(stage.at[slot], square(row, column), stage_sem.at[slot]).start()
        return carry

    lax.fori_loop(0, width // short * wide, merge_one, 0)
    for slot in range(2):
        pltpu.make_async_copy(stage.at[slot], square(0, 0), stage_sem.at[slot]).wait()
    down.add_and_send()
    for turn in range(1, n):
        from_rows(lax.rem(i + turn, n)).wait_recv()

    area = lse.shape[1]
    areas = n * rows // area
    d_keys[...] = jnp.zeros_like(d_keys)
    d_values[...] = jnp.zeros_like(d_values)
    turns = 2 * max(n - 2, 0) * pieces
    per_area = -(-turns // areas)
    scale = HEAD_DIM ** (-0.5)

    def back_area(here_at, carry):
        here = rows_of(here_at, area)
        for h in range(heads):
            first = h * 3 * HEAD_DIM
            head = slice(h * HEAD_DIM, (h + 1) * HEAD_DIM)
            q = qkv[here, first : first + HEAD_DIM]
            g = d_att[here, head]
            log_row = lse[pl.ds(here_at * heads + h, 1), :]
            probs, d_probs = [], []
            inner = jnp.zeros((1, area), f32)
            for b in range(areas):
                key = qkv[b * area : (b + 1) * area, first + HEAD_DIM : first + 2 * HEAD_DIM]
                value = qkv[b * area : (b + 1) * area, first + 2 * HEAD_DIM : first + 3 * HEAD_DIM]
                scores = mm_nt(key, q) * scale + bias[here_at, b]
                probs.append(jnp.exp(scores - log_row))
                d_probs.append(mm_nt(value, g))
                inner += jnp.sum(probs[b] * d_probs[b], axis=0, keepdims=True)
            d_query = jnp.zeros((HEAD_DIM, area), f32)
            for b in range(areas):
                at = slice(b * area, (b + 1) * area)
                key = qkv[at, first + HEAD_DIM : first + 2 * HEAD_DIM]
                d_scores = (probs[b] * (d_probs[b] - inner)).astype(low)
                d_values[at, head] += mm(probs[b].astype(low), g)
                d_keys[at, head] += mm(d_scores, q)
                d_query += mm_tn(key, d_scores)
            d_qkv[here, first : first + HEAD_DIM] = (d_query * scale).T.astype(low)

        @pl.when(here_at == 0)
        def _():
            up.relay()

        for extra in range(per_area):
            turn = here_at * per_area + extra

            @pl.when(turn < turns)
            def _():
                flows(n, pieces, sums, turn)

        return carry

    lax.fori_loop(0, areas, back_area, 0)
    for h in range(heads):
        first = h * 3 * HEAD_DIM
        head = slice(h * HEAD_DIM, (h + 1) * HEAD_DIM)
        d_qkv[:, first + HEAD_DIM : first + 2 * HEAD_DIM] = (d_keys[:, head] * scale).astype(low)
        d_qkv[:, first + 2 * HEAD_DIM : first + 3 * HEAD_DIM] = d_values[:, head].astype(low)
    for c, at in enumerate(tiles):
        total = sums.own_value(c)
        block_out[:, at] = (middle[:, at] + table[i, 5:6, at] * total).astype(low)
        sums_out[5:6, at] = jnp.sum(cot[:, at].astype(f32) * total, axis=0, keepdims=True)
    sums_out[0:2, :] = jnp.zeros((2, width), f32)
    sums_out[6:8, :] = jnp.zeros((2, width), f32)
    down.relay()
    for scatter in (up, down):
        scatter.landed_all()
        scatter.finish()
    for turn in range(1, n):
        to_heads(lax.rem(i + turn, n)).wait_send()
    sums.all_sent()


def back(n, n_dp, operands, shapes, number, tile=512):
    (rows, width), wide, units, k_rows, down_cols, areas = shapes
    heads = wide // (3 * HEAD_DIM)
    total, chips, pieces = n * rows, n_dp // 2, width // tile
    low, f32 = jnp.bfloat16, jnp.float32
    sds = jax.ShapeDtypeStruct
    return call(
        functools.partial(back_kernel, n, n_dp, heads, tile),
        number,
        "back",
        [VMEM] * 8 + [pl.BlockSpec(memory_space=pltpu.SMEM)] + [HBM] * 4,
        [
            sds((rows, width), low),
            sds((rows, width), f32),
            sds((total, wide), low),
            sds((8, width), f32),
            sds((width, width), low),
            sds((plane_slots(n_dp), k_rows, units), low),
            sds((plane_slots(n_dp), units, down_cols), low),
        ],
        [VMEM] * 4 + [HBM] * 3,
        [
            pltpu.VMEM((total, width), low),
            pltpu.VMEM((total + rows, width), low),
            pltpu.VMEM((2, math.gcd(256, heads * HEAD_DIM), width), low),
            pltpu.VMEM((total, heads * HEAD_DIM), low),
            pltpu.VMEM((n, rows, heads * HEAD_DIM), low),
            pltpu.VMEM((rows, width), low),
            pltpu.VMEM((total, heads * HEAD_DIM), f32),
            pltpu.VMEM((total, heads * HEAD_DIM), f32),
            pltpu.VMEM((chips, k_rows, units), low),
            pltpu.VMEM((chips, k_rows, units), low),
            pltpu.VMEM((k_rows, units), low),
            pltpu.VMEM((chips, units, down_cols), low),
            pltpu.VMEM((chips, units, down_cols), low),
            pltpu.VMEM((units, down_cols), low),
            pltpu.VMEM((2, tile // 2, tile), low),
            DMA((n, pieces)),
            DMA((n + 1, pieces)),
            scatter_sems(n_dp),
            scatter_sems(n_dp),
            DMA((2, n)),
            DMA((2,)),
            DMA((1,)),
            DMA((2,)),
            DMA((2, chips)),
        ],
        flops=20 * total * total * wide // 3,
    )(*operands)


def last_kernel(
    n,
    n_dp,
    tile,
    d_qkv,
    hidden,
    x_own,
    d_middle,
    sums_in,
    table,
    chosen,
    mod_w,
    merge_hbm,
    attend_hbm,
    input_grad,
    d_mod_all,
    noise_sum,
    attend_landed,
    merge_out,
    attend,
    part,
    got,
    grad_own,
    grad_theirs,
    grad_swapped,
    grad_via,
    merge_own,
    merge_swapped,
    merge_via,
    merge_landed,
    merge_part,
    merge_got,
    sums_all,
    shares,
    shares_all,
    terms,
    terms_all,
    noise_parts,
    sent,
    came,
    merge_sent,
    merge_came,
    grad_sems,
    merge_sems,
    share_sem,
    mod_sem,
    term_sem,
    noise_sem,
    load_sem,
    own_sem,
):
    d, i = lax.axis_index("dp"), lax.axis_index("tensor")
    rows, width = x_own.shape
    low, f32 = jnp.bfloat16, jnp.float32
    chips = n_dp // 2
    side = lax.rem(d, 2)
    k_rows, own_cols = mod_w.shape
    merge_cols = merge_own.shape[2]
    merge_rows = merge_out.shape[0]
    images = chosen.shape[1]

    def merge_slab(at):
        return merge_hbm.at[:, pl.ds(pl.multiple_of(at * merge_cols, merge_cols), merge_cols)]

    load = pltpu.make_async_copy(attend_hbm, attend, load_sem)
    load.start()
    for m in range(chips):
        pltpu.make_async_copy(merge_slab(2 * m + side), merge_own.at[m], own_sem.at[m]).start()
    greet_all(n, n_dp, d, i)
    merge = PlaneScatter(
        n_dp,
        d,
        lambda m: merge_slab(2 * m + 1 - side),
        merge_own,
        merge_swapped,
        merge_via,
        merge_landed,
        merge_sems,
    )
    grad = PlaneScatter(
        n_dp, d, lambda m: grad_theirs.at[m], grad_own, grad_swapped, grad_via, attend_landed, grad_sems
    )
    merge.swap_all()
    sums = LineScatter(n, i, rows, tile, part, got, sent, came)
    pieces = sums.pieces
    load.wait()

    def partial_block(q, carry):
        j = jnp.where(2 * i < n - 1, n - 1 - q, q)
        here = rows_of(j, rows)

        def one(c, inner):
            at = pl.ds(pl.multiple_of(c * tile, tile), tile)
            part[here, at] = mm_nt(d_qkv[here, :], attend[at, :]).astype(low)
            sums.at_end(j, c)
            return inner

        lax.fori_loop(0, pieces, one, 0)
        return carry

    partial_block(0, 0)
    for m in range(chips):
        pltpu.make_async_copy(merge_slab(2 * m + side), merge_own.at[m], own_sem.at[m]).wait()
    merge.add_and_send()
    lax.fori_loop(1, n, partial_block, 0)

    def slab_grad(at):
        columns = pl.ds(pl.multiple_of(at * k_rows, k_rows), k_rows)
        return mm_tn(hidden[:, columns], d_qkv[...]).astype(low)

    def for_them(m, carry):
        grad_theirs[m] = slab_grad(2 * m + 1 - side)
        grad.swap(m).start()
        return carry

    def for_us(m, carry):
        grad_own[m] = slab_grad(2 * m + side)
        return carry

    lax.fori_loop(0, chips, for_them, 0)
    lax.fori_loop(0, chips, for_us, 0)
    grad.add_and_send()
    merge.relay()
    turns = 2 * max(n - 2, 0) * pieces

    def pass_by(turn, carry):
        flows(n, pieces, sums, turn)
        return carry

    lax.fori_loop(0, turns, pass_by, 0)

    grad.relay()

    tiles = [slice(c * tile, (c + 1) * tile) for c in range(width // tile)]
    squares = jnp.zeros((rows, 1), f32)
    for at in tiles:
        v = x_own[:, at].astype(f32)
        squares += jnp.sum(v * v, axis=1, keepdims=True)
    root = lax.rsqrt(squares * (1.0 / width) + 1e-06)
    mean = jnp.zeros((rows, 1), f32)
    sums_all[...] = sums_in[...]
    for c, at in enumerate(tiles):
        v = x_own[:, at].astype(f32) * root
        dh = sums.own_value(c)
        mean += jnp.sum(dh * (1.0 + table[i, 1:2, at]) * v, axis=1, keepdims=True)
        sums_all[0:1, at] = jnp.sum(dh, axis=0, keepdims=True)
        sums_all[1:2, at] = jnp.sum(dh * v, axis=0, keepdims=True)

    unit = math.gcd(width, own_cols)
    for number in range(6):
        for start in range(0, width, unit):
            at = number * width + start
            shares[at // own_cols, :, at % own_cols : at % own_cols + unit] = (
                chosen[i][:, :1] * sums_all[number : number + 1, start : start + unit]
            )

    def to_line(source, target, sems, turn, whole=False):
        t = lax.rem(i + turn, n)
        return pltpu.make_async_remote_copy(
            src_ref=source if whole else source.at[t],
            dst_ref=target.at[i],
            send_sem=sems.at[0, t],
            recv_sem=sems.at[1, i],
            device_id=(d, t),
            device_id_type=MESH,
        )

    def from_line(source, target, sems, turn, whole=False):
        t = lax.rem(i + turn, n)
        return pltpu.make_async_remote_copy(
            src_ref=source if whole else source.at[t],
            dst_ref=target.at[t],
            send_sem=sems.at[0, t],
            recv_sem=sems.at[1, t],
            device_id=(d, t),
            device_id_type=MESH,
        )

    def to_plane(source, target, sems, flip):
        return pltpu.make_async_remote_copy(
            src_ref=source,
            dst_ref=target.at[d],
            send_sem=sems.at[0, flip],
            recv_sem=sems.at[1, flip],
            device_id=(d ^ flip, i),
            device_id_type=MESH,
        )

    def from_plane(source, target, sems, flip):
        return pltpu.make_async_remote_copy(
            src_ref=source,
            dst_ref=target.at[d ^ flip],
            send_sem=sems.at[0, flip],
            recv_sem=sems.at[1, flip],
            device_id=(d ^ flip, i),
            device_id_type=MESH,
        )

    for turn in range(1, n):
        to_line(shares, shares_all, share_sem, turn).start()

    merge.landed_all()
    merge_sums = LineScatter(
        n, i, merge_rows, merge_cols, merge_part, merge_got, merge_sent, merge_came
    )

    def merge_block(q, carry):
        j = jnp.where(2 * i < n - 1, n - 1 - q, q)
        here = rows_of(j, merge_rows)
        total = merge_landed[0, here, :].astype(f32)
        for m in range(1, merge_landed.shape[0]):
            total += merge_landed[m, here, :].astype(f32)
        merge_part[here, :] = total.astype(low)
        merge_sums.at_end(j, 0)
        return carry

    lax.fori_loop(0, n, merge_block, 0)

    mean = mean * (1.0 / width)
    for c, at in enumerate(tiles):
        v = x_own[:, at].astype(f32) * root
        u = sums.own_total(c) * (1.0 + table[i, 1:2, at])
        input_grad[:, at] = (d_middle[:, at] + root * (u - v * mean)).astype(low)
    shares_all[i] = shares[i]
    for turn in range(1, n):
        from_line(shares, shares_all, share_sem, turn).wait_recv()
    d_mod_all[d] = jnp.sum(shares_all[...], axis=0).astype(low).astype(f32)
    own_mod = d_mod_all.at[d]
    for flip in range(1, n_dp):
        to_plane(own_mod, d_mod_all, mod_sem, flip).start()
    for t in range(n - 1, 1, -1):
        for near in (True, False):
            merge_sums.pass_on(t, 0, near)
    for flip in range(1, n_dp):
        from_plane(own_mod, d_mod_all, mod_sem, flip).wait_recv()
    flat = d_mod_all[...].reshape(n_dp * images, own_cols).astype(low)
    terms[...] = mm_nt(flat, mod_w[...]).reshape(n_dp, images, k_rows)
    for turn in range(1, n):
        to_line(terms, terms_all, term_sem, turn, True).start()
    terms_all[i] = terms[...]
    for turn in range(1, n):
        from_line(terms, terms_all, term_sem, turn, True).wait_recv()
    noise_parts[...] = jnp.sum(terms_all[...], axis=0)
    for flip in range(1, n_dp):
        to_plane(noise_parts.at[d ^ flip], noise_sum, noise_sem, flip).start()
    noise_sum[d] = noise_parts[d]
    merge_out[...] = merge_sums.own_value(0)
    for flip in range(1, n_dp):
        from_plane(noise_parts.at[d ^ flip], noise_sum, noise_sem, flip).wait_recv()
    grad.landed_all()
    grad.finish()
    merge.finish()
    for turn in range(1, n):
        to_line(shares, shares_all, share_sem, turn).wait_send()
        to_line(terms, terms_all, term_sem, turn, True).wait_send()
    for flip in range(1, n_dp):
        to_plane(own_mod, d_mod_all, mod_sem, flip).wait_send()
        to_plane(noise_parts.at[d ^ flip], noise_sum, noise_sem, flip).wait_send()
    sums.all_sent()
    merge_sums.all_sent()


def last(n, n_dp, operands, shapes, number, tile=512):
    (rows, width), wide, k_rows, own_cols, (merge_rows, merge_cols), images = shapes
    total, chips, pieces = n * rows, n_dp // 2, width // tile
    low, f32 = jnp.bfloat16, jnp.float32
    sds = jax.ShapeDtypeStruct
    return call(
        functools.partial(last_kernel, n, n_dp, tile),
        number,
        "last",
        [VMEM] * 8 + [HBM] * 2,
        [
            sds((rows, width), low),
            sds((n_dp, images, own_cols), f32),
            sds((n_dp, images, k_rows), f32),
            sds((plane_slots(n_dp), k_rows, wide), low),
            sds((merge_rows, merge_cols), f32),
        ],
        [VMEM] * 3 + [HBM] + [VMEM],
        [
            pltpu.VMEM((width, wide), low),
            pltpu.VMEM((total, width), low),
            pltpu.VMEM((total + rows, width), low),
            pltpu.VMEM((chips, k_rows, wide), low),
            pltpu.VMEM((chips, k_rows, wide), low),
            pltpu.VMEM((chips, k_rows, wide), low),
            pltpu.VMEM((k_rows, wide), low),
            pltpu.VMEM((chips, n * merge_rows, merge_cols), low),
            pltpu.VMEM((chips, n * merge_rows, merge_cols), low),
            pltpu.VMEM((n * merge_rows, merge_cols), low),
            pltpu.VMEM((plane_slots(n_dp), n * merge_rows, merge_cols), low),
            pltpu.VMEM((n * merge_rows, merge_cols), low),
            pltpu.VMEM(((n + 1) * merge_rows, merge_cols), low),
            pltpu.VMEM((8, width), f32),
            pltpu.VMEM((n, images, own_cols), f32),
            pltpu.VMEM((n, images, own_cols), f32),
            pltpu.VMEM((n_dp, images, k_rows), f32),
            pltpu.VMEM((n, n_dp, images, k_rows), f32),
            pltpu.VMEM((n_dp, images, k_rows), f32),
            DMA((n, pieces)),
            DMA((n + 1, pieces)),
            DMA((n, 1)),
            DMA((n + 1, 1)),
            scatter_sems(n_dp),
            scatter_sems(n_dp),
            DMA((2, n)),
            DMA((2, n_dp)),
            DMA((2, n)),
            DMA((2, n_dp)),
            DMA,
            DMA((chips,)),
        ],
        flops=4 * total * width * wide,
    )(*operands)


def on_device(
    block_input,
    cotangent,
    noise_embed,
    image_sizes,
    attend_weight,
    merge_weight,
    up_weight,
    down_weight,
    modulate_weight,
):
    n = lax.axis_size("tensor")
    n_dp = lax.axis_size("dp")
    rows, width = block_input.shape
    tokens = n * rows
    images = image_sizes.shape[1]
    k_rows = modulate_weight.shape[0]

    sizes_row = image_sizes[0]
    ends = [sum(sizes_row[j] for j in range(last + 1)) for last in range(images)]

    def image_at(places):
        return sum((places >= end).astype(jnp.int32) for end in ends)

    block_images = image_at(jnp.arange(n, dtype=jnp.int32) * rows)
    chosen = block_images[:, None] == jnp.arange(images, dtype=jnp.int32)[None, :]
    chosen = jnp.broadcast_to(chosen.astype(jnp.float32)[:, :, None], (n, images, 128))
    area = min(256, tokens)
    area_images = image_at(jnp.arange(tokens // area, dtype=jnp.int32) * area)
    bias = jnp.where(area_images[:, None] == area_images[None, :], 0.0, MASKED)
    noise_low = jax.nn.silu(noise_embed.astype(jnp.float32)).astype(jnp.bfloat16)
    noise_slabs = noise_low.astype(jnp.float32).reshape(images, n_dp, k_rows).transpose(1, 0, 2)
    (
        cot_full,
        hidden_first,
        packed,
        lse,
        _,
        att_rows,
        attn_out,
        middle,
        hidden_second,
        table,
        attend_full,
        merge_full,
        up_full,
        down_full,
        noise_all,
    ) = front(
        n,
        n_dp,
        block_input,
        cotangent,
        noise_slabs,
        modulate_weight,
        chosen,
        bias,
        attend_weight,
        merge_weight,
        up_weight,
        down_weight,
        0,
    )
    d_hidden_second, mlp_part, up_local, down_local = ffn(
        n, hidden_second, table, cot_full, up_full, down_full, 1
    )
    units = up_full.shape[1]
    wide = packed.shape[1]
    (
        block_output,
        d_middle,
        d_qkv,
        row_sums,
        merge_local,
        up_landed,
        down_landed,
    ) = back(
        n,
        n_dp,
        (
            d_hidden_second,
            cotangent,
            middle,
            attn_out,
            table,
            att_rows,
            packed,
            lse,
            bias,
            mlp_part,
            merge_full,
            up_local,
            down_local,
        ),
        (block_input.shape, wide, units, k_rows, down_weight.shape[1], bias.shape[0]),
        2,
    )
    input_grad, d_mod_all, noise_sums, attend_landed, merge_part = last(
        n,
        n_dp,
        (
            d_qkv,
            hidden_first,
            block_input,
            d_middle,
            row_sums,
            table,
            chosen,
            modulate_weight,
            merge_local,
            attend_full,
        ),
        (
            block_input.shape,
            wide,
            k_rows,
            modulate_weight.shape[1],
            merge_weight.shape,
            images,
        ),
        3,
    )

    def chip_sum(landed):
        return jnp.sum(landed.astype(jnp.float32), axis=0)

    up_part, down_part, attend_part = map(chip_sum, (up_landed, down_landed, attend_landed))
    modulate_part = dot(
        noise_all.reshape(n_dp * images, k_rows).astype(jnp.bfloat16),
        d_mod_all.reshape(n_dp * images, -1).astype(jnp.bfloat16),
        ROWS_ROWS,
    )
    noise_sum = noise_sums.transpose(1, 0, 2).reshape(images, width)
    silu_back = jax.vjp(jax.nn.silu, noise_embed.astype(jnp.float32))[1]
    noise_grad = silu_back(noise_sum)[0]
    return (
        block_output,
        input_grad,
        noise_grad,
        attend_part,
        merge_part,
        up_part,
        down_part,
        modulate_part,
    )


def solution(mesh):
    whole_rows = P(("dp", "tensor"), None)
    by_dp = P("dp", None)
    tall = P("dp", "tensor")
    wide = P("tensor", "dp")
    return jax.shard_map(
        on_device,
        mesh=mesh,
        in_specs=(whole_rows, whole_rows, by_dp, by_dp, tall, wide, tall, wide, tall),
        out_specs=(whole_rows, whole_rows, by_dp, tall, wide, tall, wide, tall),
        check_vma=False,
    )
```

```python
import functools
import math

import jax
import jax.numpy as jnp
from jax import lax
from jax.experimental import pallas as pl
from jax.experimental.pallas import tpu as pltpu
from jax.sharding import PartitionSpec as P

HEAD_DIM = 128
MASKED = -1e30


def dot(a, b, dims=(((1,), (0,)), ((), ()))):
    return lax.dot_general(a, b, dims, preferred_element_type=jnp.float32)


ROWS_ROWS = (((0,), (0,)), ((), ()))


MESH = pl.DeviceIdType.MESH
HBM = pl.BlockSpec(memory_space=pl.ANY)
VMEM = pl.BlockSpec(memory_space=pltpu.VMEM)
DMA = pltpu.SemaphoreType.DMA


def rows_of(j, rows):
    return pl.ds(pl.multiple_of(j * rows, rows), rows)


def beside(step):
    return (lax.axis_index("dp"), lax.axis_index("tensor") + step)


def greet_line(n, i):
    barrier = pltpu.get_barrier_semaphore()

    @pl.when(i > 0)
    def _():
        pl.semaphore_signal(barrier, inc=1, device_id=beside(-1), device_id_type=MESH)

    @pl.when(i < n - 1)
    def _():
        pl.semaphore_signal(barrier, inc=1, device_id=beside(1), device_id_type=MESH)

    pl.semaphore_wait(barrier, jnp.where(i > 0, 1, 0) + jnp.where(i < n - 1, 1, 0))


class LineGather:
    def __init__(self, n, i, rows, own, full, to_left, to_right, arrived):
        self.n, self.i, self.rows, self.own, self.full = n, i, rows, own, full
        self.to_left, self.to_right, self.arrived = to_left, to_right, arrived

    def copy(self, j, step, source=None):
        place = self.full.at[rows_of(j, self.rows)]
        return pltpu.make_async_remote_copy(
            src_ref=place if source is None else source,
            dst_ref=place,
            send_sem=(self.to_right if step > 0 else self.to_left).at[j],
            recv_sem=self.arrived.at[j],
            device_id=beside(step),
            device_id_type=MESH,
        )

    def start(self):
        @pl.when(self.i > 0)
        def _():
            self.copy(self.i, -1, self.own).start()

        @pl.when(self.i < self.n - 1)
        def _():
            self.copy(self.i, 1, self.own).start()

    def step(self, s):
        for side in (-1, 1):
            j = self.i + side * s
            there = (j >= 0) & (j < self.n)
            more = (self.i > 0) if side > 0 else (self.i < self.n - 1)

            @pl.when(there)
            def _():
                self.copy(j, side).wait_recv()

            @pl.when(there & more)
            def _():
                self.copy(j, -side).start()

    def finish(self):
        @pl.when(self.i > 0)
        def _():
            self.copy(self.i, -1, self.own).wait_send()

        @pl.when(self.i < self.n - 1)
        def _():
            self.copy(self.i, 1, self.own).wait_send()

        for j in range(self.n):

            @pl.when((j < self.i) & (self.i < self.n - 1))
            def _():
                self.copy(j, 1).wait_send()

            @pl.when((j > self.i) & (self.i > 0))
            def _():
                self.copy(j, -1).wait_send()


class LineScatter:
    def __init__(self, n, i, rows, width, part, got, sent, arrived):
        self.n, self.i, self.rows, self.width = n, i, rows, width
        self.part, self.got, self.sent, self.arrived = part, got, sent, arrived
        self.pieces = part.shape[1] // width

    def columns(self, c):
        if isinstance(c, int):
            return pl.ds(c * self.width, self.width)
        return pl.ds(pl.multiple_of(c * self.width, self.width), self.width)

    def copy(self, j, slot, c, step):
        return pltpu.make_async_remote_copy(
            src_ref=self.part.at[rows_of(j, self.rows), self.columns(c)],
            dst_ref=self.got.at[rows_of(slot, self.rows), self.columns(c)],
            send_sem=self.sent.at[j, c],
            recv_sem=self.arrived.at[slot, c],
            device_id=beside(step),
            device_id_type=MESH,
        )

    def slot_there(self, j, step):
        if step > 0:
            return j
        return jnp.where(j == self.i - 1, self.n, j)

    def at_end(self, j, c):
        @pl.when((self.i == 0) & (j > 0))
        def _():
            self.copy(j, j, c, 1).start()

        @pl.when((self.i == self.n - 1) & (j < self.i))
        def _():
            self.copy(j, self.slot_there(j, -1), c, -1).start()

    def pass_on(self, t, c, near):
        n, i = self.n, self.i
        rightward = (2 * i < n - 1) if near else (2 * i >= n - 1)
        j = jnp.where(rightward, t, n - 1 - t)
        step = jnp.where(rightward, 1, -1)
        right = rightward & (i > 0) & (j > i)
        left = jnp.logical_not(rightward) & (i < n - 1) & (j < i)

        @pl.when(right | left)
        def _():
            self.add(j, j, c)
            slot = jnp.where(left & (j == i - 1), n, j)
            self.copy(j, slot, c, step).start()

    def add(self, j, slot, c):
        self.copy(j, slot, c, 1).wait_recv()
        here = (rows_of(j, self.rows), self.columns(c))
        there = (rows_of(slot, self.rows), self.columns(c))
        total = self.part[here].astype(jnp.float32) + self.got[there].astype(jnp.float32)
        self.part[here] = total.astype(self.part.dtype)

    def own(self, c, out):
        i, n = self.i, self.n
        columns = self.columns(c)
        out[:, columns] = self.part[rows_of(i, self.rows), columns].astype(out.dtype)

        @pl.when(i > 0)
        def _():
            self.copy(i, i, c, 1).wait_recv()
            out[:, columns] += self.got[rows_of(i, self.rows), columns].astype(out.dtype)

        @pl.when(i < n - 1)
        def _():
            self.copy(i, n, c, -1).wait_recv()
            out[:, columns] += self.got[rows_of(n, self.rows), columns].astype(out.dtype)

    def own_value(self, c):
        i, n = self.i, self.n

        @pl.when(i > 0)
        def _():
            self.copy(i, i, c, 1).wait_recv()

        @pl.when(i < n - 1)
        def _():
            self.copy(i, n, c, -1).wait_recv()

        return self.own_total(c)

    def own_total(self, c):
        i, n, columns = self.i, self.n, self.columns(c)
        total = self.part[rows_of(i, self.rows), columns].astype(jnp.float32)
        left = self.got[rows_of(i, self.rows), columns].astype(jnp.float32)
        right = self.got[rows_of(n, self.rows), columns].astype(jnp.float32)
        return total + jnp.where(i > 0, left, 0.0) + jnp.where(i < n - 1, right, 0.0)

    def all_sent(self):
        def one(j, carry):
            @pl.when(j != self.i)
            def _():
                for c in range(self.pieces):
                    self.copy(j, 0, c, 1).wait_send()

            return carry

        lax.fori_loop(0, self.n, one, 0)


def mm(a, b):
    return lax.dot_general(a, b, (((1,), (0,)), ((), ())), preferred_element_type=jnp.float32)


def mm_nt(a, b):
    return lax.dot_general(a, b, (((1,), (1,)), ((), ())), preferred_element_type=jnp.float32)


def mm_tn(a, b):
    return lax.dot_general(a, b, (((0,), (0,)), ((), ())), preferred_element_type=jnp.float32)


def call(kernel, collective_id, name, in_specs, outs, out_specs, scratch, flops=0, limit=60):
    return pl.pallas_call(
        kernel,
        out_shape=outs,
        in_specs=in_specs,
        out_specs=out_specs,
        scratch_shapes=scratch,
        compiler_params=pltpu.CompilerParams(
            collective_id=collective_id,
            has_side_effects=True,
            vmem_limit_bytes=limit * 1024 * 1024,
        ),
        cost_estimate=pl.CostEstimate(flops=flops, bytes_accessed=1 << 20, transcendentals=0),
        name=name,
    )


def ffn_kernel(
    n,
    tile,
    grad_tile,
    own_hidden,
    table,
    d_mlp_hbm,
    up_hbm,
    down_hbm,
    d_hidden,
    mlp_part,
    up_grad,
    down_grad,
    up,
    down,
    d_mlp,
    hidden,
    activated,
    d_pre,
    part,
    got,
    stage,
    mlp,
    to_left,
    to_right,
    arrived,
    sent,
    came,
    local,
    stage_sem,
):
    i = lax.axis_index("tensor")
    rows, width = own_hidden.shape
    units = up.shape[1]
    loads = [
        pltpu.make_async_copy(source, target, local.at[k])
        for k, (source, target) in enumerate(((up_hbm, up), (d_mlp_hbm, d_mlp), (down_hbm, down)))
    ]
    for load in loads:
        load.start()
    greet_line(n, i)
    line = LineGather(n, i, rows, own_hidden, hidden, to_left, to_right, arrived)
    first_core = lax.rem(lax.axis_index("dp"), 2) == 0
    pl.when(first_core)(line.start)
    piece = tile // 2
    sums = LineScatter(n, i, rows, piece, part, got, sent, came)
    hidden[rows_of(i, rows), :] = own_hidden[...]
    for load in loads:
        load.wait()

    def one_block(j):
        here = rows_of(j, rows)

        def gated(c, carry):
            at = pl.ds(pl.multiple_of(c * tile, tile), tile)
            d_mlp[here, at] = (d_mlp[here, at].astype(jnp.float32) * table[j, 5:6, at]).astype(
                jnp.bfloat16
            )
            return carry

        lax.fori_loop(0, width // tile, gated, 0)

        def first(c, carry):
            at = pl.ds(pl.multiple_of(c * tile, tile), tile)
            pre = mm(hidden[here, :], up[:, at])
            d_act = mm_nt(d_mlp[here, :], down[at, :])
            cdf = 0.5 * (1.0 + lax.erf(pre * (0.5**0.5)))
            density = jnp.exp(-0.5 * pre * pre) * ((0.5 / math.pi) ** 0.5)
            activated[here, at] = (pre * cdf).astype(jnp.bfloat16)
            d_pre[here, at] = (d_act * (cdf + pre * density)).astype(jnp.bfloat16)
            return carry

        lax.fori_loop(0, units // tile, first, 0)

        def second(c, carry):
            at = pl.ds(pl.multiple_of(c * tile, tile), tile)
            part[here, at] = mm_nt(d_pre[here, :], up[at, :]).astype(jnp.bfloat16)
            for k in range(tile // piece):
                sums.at_end(j, c * (tile // piece) + k)
            return carry

        lax.fori_loop(0, width // tile, second, 0)

        def third(c, carry):
            at = pl.ds(pl.multiple_of(c * tile, tile), tile)
            mlp[here, at] = mm(activated[here, :], down[:, at]).astype(jnp.bfloat16)
            return carry

        lax.fori_loop(0, width // tile, third, 0)

    def visit(q, carry):
        s = (q + 1) // 2
        side = 1 - 2 * (q % 2)
        j = i + s * side

        @pl.when(q % 2 == 1)
        def _():
            line.step(s)

        @pl.when((j >= 0) & (j < n))
        def _():
            one_block(j)

        @pl.when((q == 0) & jnp.logical_not(first_core))
        def _():
            line.start()

        return carry

    lax.fori_loop(0, 2 * n - 1, visit, 0)
    keep_mlp = pltpu.make_async_copy(mlp, mlp_part, local.at[3])
    keep_mlp.start()

    count = (width // grad_tile) * (units // grad_tile)
    turns = 2 * max(n - 2, 1) * sums.pieces
    per_turn = -(-2 * count // turns)

    def square(ref, row, column):
        return ref.at[
            pl.ds(pl.multiple_of(row * grad_tile, grad_tile), grad_tile),
            pl.ds(pl.multiple_of(column * grad_tile, grad_tile), grad_tile),
        ]

    def put(slot, target):
        return pltpu.make_async_copy(stage.at[slot], target, stage_sem.at[slot])

    def one_grad(k, left, right, target):
        wide = right.shape[1] // grad_tile
        row, column = k // wide, k % wide
        slot = k % 2

        @pl.when(k >= 2)
        def _():
            put(slot, square(target, 0, 0)).wait()

        a = left[:, pl.ds(pl.multiple_of(row * grad_tile, grad_tile), grad_tile)]
        b = right[:, pl.ds(pl.multiple_of(column * grad_tile, grad_tile), grad_tile)]
        stage[slot] = mm_tn(a, b).astype(jnp.bfloat16)
        put(slot, square(target, row, column)).start()

    def tail(k, carry):
        t, c = 2 + k // (2 * sums.pieces), k % sums.pieces
        for near in (True, False):

            @pl.when((k // sums.pieces) % 2 == (0 if near else 1))
            def _():
                sums.pass_on(t, c, near)

        for extra in range(per_turn):
            item = k * per_turn + extra

            @pl.when(item < count)
            def _():
                one_grad(item, hidden, d_pre, up_grad)

            @pl.when(item == count)
            def _():
                for slot in range(2):
                    put(slot, square(up_grad, 0, 0)).wait()

            @pl.when((item >= count) & (item < 2 * count))
            def _():
                one_grad(item - count, activated, d_mlp, down_grad)

        return carry

    lax.fori_loop(0, turns, tail, 0)
    for slot in range(2):
        put(slot, square(down_grad, 0, 0)).wait()
    for c in range(sums.pieces):
        sums.own(c, d_hidden)
    line.finish()
    sums.all_sent()
    keep_mlp.wait()


def ffn(n, own_hidden, table, cotangents, up, down, collective_id, tile=512, grad_tile=512):
    rows, width = own_hidden.shape
    units = up.shape[1]
    pieces = 2 * width // tile
    low = jnp.bfloat16
    return call(
        functools.partial(ffn_kernel, n, tile, grad_tile),
        collective_id,
        "ffn",
        [VMEM, VMEM, HBM, HBM, HBM],
        [
            jax.ShapeDtypeStruct((rows, width), jnp.float32),
            jax.ShapeDtypeStruct((n * rows, width), low),
            jax.ShapeDtypeStruct((width, units), low),
            jax.ShapeDtypeStruct((units, width), low),
        ],
        [VMEM, HBM, HBM, HBM],
        [
            pltpu.VMEM((width, units), low),
            pltpu.VMEM((units, width), low),
            pltpu.VMEM((n * rows, width), low),
            pltpu.VMEM((n * rows, width), low),
            pltpu.VMEM((n * rows, units), low),
            pltpu.VMEM((n * rows, units), low),
            pltpu.VMEM((n * rows, width), low),
            pltpu.VMEM(((n + 1) * rows, width), low),
            pltpu.VMEM((2, grad_tile, grad_tile), low),
            pltpu.VMEM((n * rows, width), low),
            DMA((n,)),
            DMA((n,)),
            DMA((n,)),
            DMA((n, pieces)),
            DMA((n + 1, pieces)),
            DMA((4,)),
            DMA((2,)),
        ],
        flops=12 * n * rows * width * units,
    )(own_hidden, table, cotangents, up, down)


def image_at(sizes, place):
    end, count = 0, 0
    for k in range(sizes.shape[1]):
        end = end + sizes[0, k]
        count = count + jnp.where(place >= end, 1, 0)
    return count


def image_at(sizes, place):
    end, count = 0, 0
    for k in range(sizes.shape[1]):
        end = end + sizes[0, k]
        count = count + jnp.where(place >= end, 1, 0)
    return count


class PlaneGather:
    def __init__(self, n_dp, d, own, view, height, sent, came):
        self.n_dp, self.d, self.own, self.view, self.height = n_dp, d, own, view, height
        self.sent, self.came = sent, came
        self.square = n_dp == 8
        self.peers = [2 * k for k in range(1, n_dp // 2)]

    def copy(self, k, source, target, peer):
        return pltpu.make_async_remote_copy(
            src_ref=source,
            dst_ref=target,
            send_sem=self.sent.at[k],
            recv_sem=self.came.at[k],
            device_id=(self.d ^ peer, lax.axis_index("tensor")),
            device_id_type=MESH,
        )

    def slab(self, flip, half=None):
        if half is None:
            return self.view(self.d ^ flip, 0, self.height)
        return self.view(self.d ^ flip, half * (self.height // 2), self.height // 2)

    def owns(self):
        peers = [2, 4] if self.square else self.peers
        return [
            self.copy(k, self.own, self.slab(0), peer) for k, peer in enumerate([1] + peers)
        ]

    def relay_of(self, k):
        flip, half, peer = ((2, 0, 4), (4, 1, 2))[k - 1]
        return self.copy(2 + k, self.slab(flip, half), self.slab(flip, half), peer)

    def across(self):
        return [
            self.copy(3, self.slab(6, 0), self.slab(6, 0), 4),
            self.copy(4, self.slab(6, 1), self.slab(6, 1), 2),
        ]

    def hand(self, flip):
        base = 5 if self.square else len(self.peers) + 1
        k = base + flip // 2 - 1
        return self.copy(k, self.slab(flip), self.slab(flip), 1)

    def handed(self, flip):
        base = 5 if self.square else len(self.peers) + 1
        k = base + flip // 2 - 1
        return self.copy(k, self.slab(flip ^ 1), self.slab(flip ^ 1), 1)

    def start(self):
        for copy in self.owns():
            copy.start()

    def relay(self):
        if not self.square:
            return
        for k, flip in ((1, 2), (2, 4)):
            self.copy(k, self.own, self.slab(flip), flip).wait_recv()
            self.relay_of(k).start()
            self.hand(flip).start()

    def close(self):
        if self.square:
            for copy in self.across():
                copy.wait_recv()
            self.hand(6).start()
        else:
            for k, flip in enumerate(self.peers):
                self.copy(k + 1, self.own, self.slab(flip), flip).wait_recv()
                self.hand(flip).start()
        self.copy(0, self.own, self.slab(1), 1).wait_recv()
        for flip in self.peers:
            self.handed(flip).wait_recv()

    def finish(self):
        for copy in self.owns():
            copy.wait_send()
        if self.square:
            for k in (1, 2):
                self.relay_of(k).wait_send()
        for flip in self.peers:
            self.hand(flip).wait_send()


def plane_sems(n_dp):
    return 8 if n_dp == 8 else n_dp - 1


def greet_all(n, n_dp, d, i):
    barrier = pltpu.get_barrier_semaphore()
    for flip in range(1, n_dp):
        pl.semaphore_signal(barrier, inc=1, device_id=(d ^ flip, i), device_id_type=MESH)
    for turn in range(1, n):
        pl.semaphore_signal(
            barrier, inc=1, device_id=(d, lax.rem(i + turn, n)), device_id_type=MESH
        )
    pl.semaphore_wait(barrier, n_dp + n - 2)


def front_kernel(
    n,
    n_dp,
    heads,
    tile,
    x_own,
    cot_own,
    noise_own,
    mod_w,
    sizes,
    attend_w,
    merge_w,
    up_w,
    down_w,
    cot_full,
    hidden_out,
    qkv_out,
    lse,
    att_rows,
    attn_out,
    middle,
    hidden_second,
    table,
    attend_full,
    merge_full,
    up_full,
    down_full,
    noise_all,
    x_full,
    attend,
    merge,
    noise,
    hidden,
    qkv,
    attended,
    terms,
    terms_all,
    columns,
    noise_sem,
    terms_sem,
    column_sem,
    x_sem,
    cot_sem,
    merge_sem,
    weight_sent,
    weight_came,
    out_sem,
    att_sem,
    local,
):
    d, i = lax.axis_index("dp"), lax.axis_index("tensor")
    rows, width = x_own.shape
    k_rows, own_cols = mod_w.shape
    head_cols = heads * HEAD_DIM
    low, f32 = jnp.bfloat16, jnp.float32
    merge_rows, merge_cols = merge_w.shape
    down_cols = down_w.shape[1]
    merge_slab = merge.at[:, pl.ds(pl.multiple_of(d * merge_cols, merge_cols), merge_cols)]

    def row_view(full, height):
        return lambda at, start, count: full.at[
            pl.ds(pl.multiple_of(at * height + start, 16), count), :
        ]

    def column_view(full, wide):
        return lambda at, start, count: full.at[
            pl.ds(start, count), pl.ds(pl.multiple_of(at * wide, wide), wide)
        ]

    weights = [
        PlaneGather(n_dp, d, own, view, height, weight_sent.at[k], weight_came.at[k])
        for k, (own, view, height) in enumerate(
            (
                (attend_w, row_view(attend, k_rows), k_rows),
                (merge_slab, column_view(merge, merge_cols), n * merge_rows),
                (up_w, row_view(up_full, k_rows), k_rows),
                (down_w, column_view(down_full, down_cols), down_w.shape[0]),
            )
        )
    ]
    attend_g, merge_g, up_g, down_g = weights
    copies = [
        pltpu.make_async_copy(source, target, local.at[k])
        for k, (source, target) in enumerate(
            (
                (attend_w, attend_g.slab(0)),
                (merge_w, merge_slab.at[rows_of(i, merge_rows)]),
                (cot_own, cot_full.at[rows_of(i, rows)]),
                (up_w, up_g.slab(0)),
                (down_w, down_g.slab(0)),
            )
        )
    ]
    for copy in copies:
        copy.start()
    greet_all(n, n_dp, d, i)

    def to_plane(source, target, sems, flip):
        return pltpu.make_async_remote_copy(
            src_ref=source.at[d ^ flip],
            dst_ref=target.at[d],
            send_sem=sems.at[0, flip],
            recv_sem=sems.at[1, flip],
            device_id=(d ^ flip, i),
            device_id_type=MESH,
        )

    def from_plane(target, sems, flip):
        return pltpu.make_async_remote_copy(
            src_ref=target.at[d ^ flip],
            dst_ref=target.at[d ^ flip],
            send_sem=sems.at[0, flip],
            recv_sem=sems.at[1, flip],
            device_id=(d ^ flip, i),
            device_id_type=MESH,
        )

    for k in range(n_dp):
        v = noise_own[:, k * k_rows : (k + 1) * k_rows].astype(f32)
        noise[k] = (v * (1.0 / (1.0 + jnp.exp(-v)))).astype(low).astype(f32)
    for flip in range(1, n_dp):
        to_plane(noise, noise_all, noise_sem, flip).start()
    merge_line = LineGather(
        n, i, merge_rows, merge_w, merge_slab, merge_sem.at[0], merge_sem.at[1], merge_sem.at[2]
    )
    x_line = LineGather(n, i, rows, x_own, x_full, x_sem.at[0], x_sem.at[1], x_sem.at[2])
    cot_line = LineGather(
        n, i, rows, cot_own, cot_full, cot_sem.at[0], cot_sem.at[1], cot_sem.at[2]
    )
    x_line.start()
    noise_all[d] = noise[d]
    x_full[rows_of(i, rows), :] = x_own[...]
    for flip in range(1, n_dp):
        from_plane(noise_all, noise_sem, flip).wait_recv()
    pictures = noise.shape[1]
    images = noise_all[...].reshape(n_dp * pictures, k_rows).astype(low)
    for c in range(own_cols // tile):
        terms[:, :, c * tile : (c + 1) * tile] = mm(
            images, mod_w[:, c * tile : (c + 1) * tile]
        ).reshape(n_dp, pictures, tile)
    for flip in range(1, n_dp):
        to_plane(terms, terms_all, terms_sem, flip).start()
    attend_g.start()
    terms_all[d] = terms[d]
    for flip in range(1, n_dp):
        from_plane(terms_all, terms_sem, flip).wait_recv()
    columns[i] = jnp.sum(terms_all[...], axis=0)

    def to_line(turn):
        t = lax.rem(i + turn, n)
        return pltpu.make_async_remote_copy(
            src_ref=columns.at[i],
            dst_ref=columns.at[i],
            send_sem=column_sem.at[0, t],
            recv_sem=column_sem.at[1, i],
            device_id=(d, t),
            device_id_type=MESH,
        )

    def from_line(turn):
        t = lax.rem(i + turn, n)
        return pltpu.make_async_remote_copy(
            src_ref=columns.at[t],
            dst_ref=columns.at[t],
            send_sem=column_sem.at[0, t],
            recv_sem=column_sem.at[1, t],
            device_id=(d, t),
            device_id_type=MESH,
        )

    for turn in range(1, n):
        to_line(turn).start()
    merge_line.start()
    x_line.step(1)
    for turn in range(1, n):
        from_line(turn).wait_recv()
    unit = math.gcd(width, own_cols)

    def fill(j, carry):
        image = image_at(sizes, j * rows)
        for number in range(6):
            for start in range(0, width, unit):
                at = number * width + start
                here = slice(at % own_cols, at % own_cols + unit)
                table[j, number : number + 1, start : start + unit] = sum(
                    columns[at // own_cols, k : k + 1, here] * jnp.where(image == k, 1.0, 0.0)
                    for k in range(pictures)
                )
        return carry

    lax.fori_loop(0, n, fill, 0)
    attend_g.relay()
    merge_line.step(1)
    for copy in copies[:2]:
        copy.wait()
    attend_g.close()
    up_g.start()
    keep_attend = pltpu.make_async_copy(attend, attend_full, out_sem.at[0])
    keep_merge = pltpu.make_async_copy(merge, merge_full, out_sem.at[1])
    keep_attend.start()
    keep_hidden = pltpu.make_async_copy(hidden, hidden_out, out_sem.at[2])
    keep_qkv = pltpu.make_async_copy(qkv, qkv_out, out_sem.at[3])

    def tiles(count):
        return [slice(c * tile, (c + 1) * tile) for c in range(count // tile)]

    def one_block(j):
        here = rows_of(j, rows)
        squares = jnp.zeros((rows, 1), f32)
        for at in tiles(width):
            v = x_full[here, at].astype(f32)
            squares += jnp.sum(v * v, axis=1, keepdims=True)
        root = lax.rsqrt(squares * (1.0 / width) + 1e-06)
        for at in tiles(width):
            v = x_full[here, at].astype(f32) * root
            hidden[here, at] = (v * (1.0 + table[j, 1:2, at]) + table[j, 0:1, at]).astype(low)
        wide = qkv.shape[1]
        step = math.gcd(wide, 512)
        for c in range(wide // step):
            at = slice(c * step, (c + 1) * step)
            qkv[here, at] = mm(hidden[here, :], attend[:, at]).astype(low)

    def visit(q, carry):
        s = (q + 1) // 2
        side = 1 - 2 * (q % 2)
        j = i + s * side

        @pl.when((q % 2 == 1) & (s + 1 < n))
        def _():
            x_line.step(s + 1)
            merge_line.step(s + 1)

        @pl.when(q == 2 * n - 5)
        def _():
            up_g.relay()
            merge_g.start()
            cot_line.start()

        @pl.when((j >= 0) & (j < n))
        def _():
            one_block(j)

        return carry

    lax.fori_loop(0, 2 * n - 1, visit, 0)

    keep_hidden.start()
    keep_qkv.start()

    area = min(256, n * rows)
    areas = n * rows // area
    owners = area // rows
    area_images = [image_at(sizes, b * area) for b in range(areas)]

    def to_owner(j):
        return pltpu.make_async_remote_copy(
            src_ref=attended.at[rows_of(j, rows), :],
            dst_ref=att_rows.at[:, pl.ds(pl.multiple_of(i * head_cols, head_cols), head_cols)],
            send_sem=att_sem.at[0, j],
            recv_sem=att_sem.at[1, i],
            device_id=(d, j),
            device_id_type=MESH,
        )

    def from_source(t):
        return pltpu.make_async_remote_copy(
            src_ref=attended.at[rows_of(t, rows), :],
            dst_ref=att_rows.at[:, pl.ds(pl.multiple_of(t * head_cols, head_cols), head_cols)],
            send_sem=att_sem.at[0, t],
            recv_sem=att_sem.at[1, t],
            device_id=(d, t),
            device_id_type=MESH,
        )

    def attend_area(turn, carry):
        here_at = lax.rem(i // owners + 1 + turn, areas)
        here = rows_of(here_at, area)
        image = image_at(sizes, here_at * area)
        for h in range(heads):
            first = h * 3 * HEAD_DIM
            q = qkv[here, first : first + HEAD_DIM]
            parts = []
            for b in range(areas):
                key = qkv[b * area : (b + 1) * area, first + HEAD_DIM : first + 2 * HEAD_DIM]
                parts.append(
                    mm_nt(key, q) * HEAD_DIM ** (-0.5)
                    + jnp.where(image == area_images[b], 0.0, MASKED)
                )
            highest = parts[0].max(axis=0, keepdims=True)
            for part in parts[1:]:
                highest = jnp.maximum(highest, part.max(axis=0, keepdims=True))
            parts = [jnp.exp(part - highest) for part in parts]
            totals = sum(jnp.sum(part, axis=0, keepdims=True) for part in parts)
            inverse = 1.0 / totals
            out = jnp.zeros((HEAD_DIM, area), f32)
            for b in range(areas):
                value = qkv[b * area : (b + 1) * area, first + 2 * HEAD_DIM : first + 3 * HEAD_DIM]
                out += mm_tn(value, (parts[b] * inverse).astype(low))
            attended[here, h * HEAD_DIM : (h + 1) * HEAD_DIM] = out.T.astype(low)
            lse[pl.ds(here_at * heads + h, 1), :] = highest + jnp.log(totals)
        for k in range(owners):
            j = here_at * owners + k

            @pl.when(j != i)
            def _():
                to_owner(j).start()

        @pl.when(turn == (areas - 1) // 2)
        def _():
            up_g.close()
            cot_line.step(1)

        @pl.when(turn == areas - 1)
        def _():
            merge_g.relay()
            down_g.start()

        return carry

    lax.fori_loop(0, areas, attend_area, 0)
    att_rows[:, pl.ds(pl.multiple_of(i * head_cols, head_cols), head_cols)] = attended[
        rows_of(i, rows), :
    ]
    if n > 2:
        cot_line.step(2)
    merge_g.close()
    keep_merge.start()
    for turn in range(1, n):
        from_source(lax.rem(i + turn, n)).wait_recv()
    squares = jnp.zeros((rows, 1), f32)
    for at in tiles(width):
        out = mm(att_rows[...], merge[:, at])
        attn_out[:, at] = out
        v = x_own[:, at].astype(f32) + table[i, 2:3, at] * out
        middle[:, at] = v
        squares += jnp.sum(v * v, axis=1, keepdims=True)
    root = lax.rsqrt(squares * (1.0 / width) + 1e-06)
    for at in tiles(width):
        v = middle[:, at] * root
        hidden_second[:, at] = (v * (1.0 + table[i, 4:5, at]) + table[i, 3:4, at]).astype(low)
    down_g.relay()
    for s in range(3, n):
        cot_line.step(s)
    down_g.close()
    for copy in copies[2:]:
        copy.wait()
    keep_attend.wait()
    keep_merge.wait()
    keep_hidden.wait()
    keep_qkv.wait()
    for flip in range(1, n_dp):
        to_plane(noise, noise_all, noise_sem, flip).wait_send()
        to_plane(terms, terms_all, terms_sem, flip).wait_send()
    for line in (merge_line, x_line, cot_line):
        line.finish()
    for turn in range(1, n):
        to_line(turn).wait_send()
    for turn in range(1, n):
        to_owner(lax.rem(i + turn, n)).wait_send()
    for weight in weights:
        weight.finish()


def front(n, n_dp, x, cot, noise, mod_w, sizes, attend_w, merge_w, up_w, down_w, number):
    rows, width = x.shape
    k_rows, own_cols = mod_w.shape
    wide = attend_w.shape[1]
    heads = wide // (3 * HEAD_DIM)
    total = n * rows
    areas = total // min(256, total)
    pictures = noise.shape[0]
    low, f32 = jnp.bfloat16, jnp.float32
    sds = jax.ShapeDtypeStruct
    count = plane_sems(n_dp)
    return call(
        functools.partial(front_kernel, n, n_dp, heads, 512),
        number,
        "front",
        [VMEM, HBM, VMEM, VMEM, pl.BlockSpec(memory_space=pltpu.SMEM), VMEM, VMEM, HBM, HBM],
        [
            sds((total, width), low),
            sds((total, width), low),
            sds((total, wide), low),
            sds((areas * heads, total // areas), f32),
            sds((rows, width), low),
            sds((rows, width), f32),
            sds((rows, width), f32),
            sds((rows, width), low),
            sds((n, 8, width), f32),
            sds((n_dp * k_rows, wide), low),
            sds((n * merge_w.shape[0], n_dp * merge_w.shape[1]), low),
            sds((n_dp * k_rows, up_w.shape[1]), low),
            sds((down_w.shape[0], n_dp * down_w.shape[1]), low),
            sds((n_dp, pictures, k_rows), f32),
        ],
        [HBM] * 3 + [VMEM] * 6 + [HBM] * 4 + [VMEM],
        [
            pltpu.VMEM((total, width), low),
            pltpu.VMEM((n_dp * k_rows, wide), low),
            pltpu.VMEM((n * merge_w.shape[0], n_dp * merge_w.shape[1]), low),
            pltpu.VMEM((n_dp, pictures, k_rows), f32),
            pltpu.VMEM((total, width), low),
            pltpu.VMEM((total, wide), low),
            pltpu.VMEM((total, heads * HEAD_DIM), low),
            pltpu.VMEM((n_dp, pictures, own_cols), f32),
            pltpu.VMEM((n_dp, pictures, own_cols), f32),
            pltpu.VMEM((n, pictures, own_cols), f32),
            DMA((2, n_dp)),
            DMA((2, n_dp)),
            DMA((3, n)),
            DMA((3, n)),
            DMA((3, n)),
            DMA((3, n)),
            DMA((4, count)),
            DMA((4, count)),
            DMA((4,)),
            DMA((2, n)),
            DMA((5,)),
        ],
        flops=2 * total * width * wide,
    )(x, cot, noise, mod_w, sizes, attend_w, merge_w, up_w, down_w)


class PlaneScatter:
    def __init__(self, n_dp, d, theirs, own, swapped, via, landed, sems):
        self.chips, self.d, self.square = n_dp // 2, d, n_dp == 8
        self.chip, self.side = d // 2, lax.rem(d, 2)
        self.theirs, self.own, self.swapped, self.via = theirs, own, swapped, via
        self.landed, self.sems = landed, sems

    def remote(self, source, target, sent, came, device):
        return pltpu.make_async_remote_copy(
            src_ref=source,
            dst_ref=target,
            send_sem=sent,
            recv_sem=came,
            device_id=(device, lax.axis_index("tensor")),
            device_id_type=MESH,
        )

    def swap(self, m):
        return self.remote(
            self.theirs(m), self.swapped.at[m], self.sems.at[0, m], self.sems.at[1, m], self.d ^ 1
        )

    def half(self, ref, which):
        height = self.own.shape[1] // 2
        return ref.at[pl.ds(which * height, height), :]

    def step(self, k):
        slab, which, peer = ((1, 0, 1), (3, 0, 1), (2, 1, 2), (3, 1, 2), (2, 0, 2), (1, 1, 1))[k]
        target = self.via if slab == 3 else self.landed.at[1 if k < 4 else 2]
        return self.remote(
            self.half(self.own.at[self.chip ^ slab], which),
            self.half(target, which),
            self.sems.at[2, k],
            self.sems.at[3, k],
            2 * (self.chip ^ peer) + self.side,
        )

    def send(self, m, slot, sem):
        return self.remote(
            self.own.at[m],
            self.landed.at[slot],
            self.sems.at[2, m],
            self.sems.at[3, sem],
            2 * m + self.side,
        )

    def keep(self):
        slot = 0 if self.square else self.chip
        return pltpu.make_async_copy(
            self.own.at[self.chip], self.landed.at[slot], self.sems.at[2, 6 if self.square else self.chip]
        )

    def swap_all(self):
        def one(m, carry):
            self.swap(m).start()
            return carry

        lax.fori_loop(0, self.chips, one, 0)

    def add(self, target, source):
        height, wide = target.shape
        chunk = math.gcd(height, 64 if wide > 512 else 256)

        def one(c, carry):
            at = pl.ds(pl.multiple_of(c * chunk, chunk), chunk)
            total = target[at, :].astype(jnp.float32) + source[at, :].astype(jnp.float32)
            target[at, :] = total.astype(target.dtype)
            return carry

        lax.fori_loop(0, height // chunk, one, 0)

    def add_and_send(self):
        def one(k, carry):
            m = self.chip ^ (self.chips - 1 - k)
            self.swap(m).wait_recv()
            self.add(self.own.at[m], self.swapped.at[m])
            if not self.square:

                @pl.when(m != self.chip)
                def _():
                    self.send(m, self.chip, self.chip).start()

            return carry

        lax.fori_loop(0, self.chips, one, 0)
        if self.square:
            for k in (1, 3, 0, 2):
                self.step(k).start()
        self.keep().start()

    def relay(self):
        if self.square:
            for k, slab, which in ((1, 2, 0), (3, 1, 1)):
                self.step(k).wait_recv()
                self.step(k).wait_send()
                self.add(self.half(self.own.at[self.chip ^ slab], which), self.half(self.via, which))
                self.step(4 if k == 1 else 5).start()

    def landed_all(self):
        if self.square:
            for k in (0, 2, 4, 5):
                self.step(k).wait_recv()
        else:
            for k in range(1, self.chips):
                self.send(self.chip ^ k, self.chip ^ k, self.chip ^ k).wait_recv()
        self.keep().wait()

    def finish(self):
        for m in range(self.chips):
            self.swap(m).wait_send()
        if self.square:
            for k in (0, 2, 4, 5):
                self.step(k).wait_send()
        else:
            for k in range(1, self.chips):
                self.send(self.chip ^ k, self.chip, self.chip).wait_send()


def plane_slots(n_dp):
    return 3 if n_dp == 8 else n_dp // 2


def scatter_sems(n_dp):
    return DMA((4, max(7, n_dp // 2)))


def flows(n, pieces, sums, turn):
    far, rest = turn // ((n - 2) * pieces), lax.rem(turn, (n - 2) * pieces)
    t, c = n - 1 - rest // pieces, lax.rem(rest, pieces)
    for near in (True, False):

        @pl.when(far == (0 if near else 1))
        def _():
            sums.pass_on(t, c, near)


def back_kernel(
    n,
    n_dp,
    heads,
    tile,
    d_hidden,
    middle,
    table,
    lse,
    sizes,
    cot_hbm,
    out_hbm,
    rows_hbm,
    qkv_hbm,
    mlp_hbm,
    merge_hbm,
    up_hbm,
    down_hbm,
    block_out,
    d_middle,
    d_qkv,
    sums_out,
    merge_grad,
    up_landed,
    down_landed,
    cot,
    attn_out,
    att_rows,
    qkv,
    part,
    got,
    merge,
    d_att,
    d_send,
    d_attn,
    d_keys,
    d_values,
    up_own,
    up_swapped,
    up_via,
    down_own,
    down_swapped,
    down_via,
    stage,
    mlp_sent,
    mlp_came,
    up_sems,
    down_sems,
    att_sem,
    merge_sem,
    load_sem,
    stage_sem,
    own_sem,
):
    d, i = lax.axis_index("dp"), lax.axis_index("tensor")
    rows, width = middle.shape
    low, f32 = jnp.bfloat16, jnp.float32
    head_cols = heads * HEAD_DIM
    chips = n_dp // 2
    k_rows, down_cols = up_own.shape[1], down_own.shape[2]
    side = lax.rem(d, 2)

    def up_slab(at):
        return up_hbm.at[pl.ds(pl.multiple_of(at * k_rows, k_rows), k_rows), :]

    def down_slab(at):
        return down_hbm.at[:, pl.ds(pl.multiple_of(at * down_cols, down_cols), down_cols)]

    load_mlp = pltpu.make_async_copy(mlp_hbm, part, load_sem.at[0])
    load_mlp.start()
    load_cot = pltpu.make_async_copy(cot_hbm, cot, load_sem.at[3])
    load_out = pltpu.make_async_copy(out_hbm, attn_out, load_sem.at[4])
    load_cot.start()
    load_out.start()
    load_rows = pltpu.make_async_copy(rows_hbm, att_rows, load_sem.at[1])
    load_qkv = pltpu.make_async_copy(qkv_hbm, qkv, load_sem.at[2])

    some = merge.shape[1]
    shares = head_cols // some

    def load_merge(k, slot):
        return pltpu.make_async_copy(
            merge_hbm.at[pl.ds(pl.multiple_of(k * some, some), some), :],
            merge.at[slot],
            merge_sem.at[slot],
        )

    load_merge(0, 0).start()
    for m in range(chips):
        pltpu.make_async_copy(up_slab(2 * m + side), up_own.at[m], own_sem.at[0, m]).start()
        pltpu.make_async_copy(down_slab(2 * m + side), down_own.at[m], own_sem.at[1, m]).start()
    load_rows.start()
    load_qkv.start()
    greet_all(n, n_dp, d, i)
    up = PlaneScatter(
        n_dp, d, lambda m: up_slab(2 * m + 1 - side), up_own, up_swapped, up_via, up_landed, up_sems
    )
    down = PlaneScatter(
        n_dp,
        d,
        lambda m: down_slab(2 * m + 1 - side),
        down_own,
        down_swapped,
        down_via,
        down_landed,
        down_sems,
    )
    up.swap_all()
    down.swap_all()
    load_mlp.wait()
    piece = tile // 2
    sums = LineScatter(n, i, rows, piece, part, got, mlp_sent, mlp_came)
    pieces = sums.pieces

    def ends(k, carry):
        t, c = n - 1 - k // pieces, lax.rem(k, pieces)
        pl.when(i == 0)(functools.partial(sums.at_end, t, c))
        pl.when(i == n - 1)(functools.partial(sums.at_end, n - 1 - t, c))
        return carry

    lax.fori_loop(0, min(n - 1, 1) * pieces, ends, 0)

    tiles = [slice(c * tile, (c + 1) * tile) for c in range(width // tile)]
    squares = jnp.zeros((rows, 1), f32)
    for at in tiles:
        squares += jnp.sum(middle[:, at] * middle[:, at], axis=1, keepdims=True)
    root = lax.rsqrt(squares * (1.0 / width) + 1e-06)
    mean = jnp.zeros((rows, 1), f32)
    for at in tiles:
        v = middle[:, at] * root
        dh = d_hidden[:, at]
        mean += jnp.sum(dh * (1.0 + table[i, 4:5, at]) * v, axis=1, keepdims=True)
        sums_out[3:4, at] = jnp.sum(dh, axis=0, keepdims=True)
        sums_out[4:5, at] = jnp.sum(dh * v, axis=0, keepdims=True)
    mean = mean * (1.0 / width)
    load_cot.wait()
    load_out.wait()
    for at in tiles:
        v = middle[:, at] * root
        u = d_hidden[:, at] * (1.0 + table[i, 4:5, at])
        dm = cot[:, at].astype(f32) + root * (u - v * mean)
        d_middle[:, at] = dm
        d_attn[:, at] = (table[i, 2:3, at] * dm).astype(low)
        sums_out[2:3, at] = jnp.sum(dm * attn_out[:, at], axis=0, keepdims=True)

    def to_heads(t):
        return pltpu.make_async_remote_copy(
            src_ref=d_send.at[t],
            dst_ref=d_att.at[rows_of(i, rows), :],
            send_sem=att_sem.at[0, t],
            recv_sem=att_sem.at[1, i],
            device_id=(d, t),
            device_id_type=MESH,
        )

    def from_rows(t):
        return pltpu.make_async_remote_copy(
            src_ref=d_send.at[t],
            dst_ref=d_att.at[rows_of(t, rows), :],
            send_sem=att_sem.at[0, t],
            recv_sem=att_sem.at[1, t],
            device_id=(d, t),
            device_id_type=MESH,
        )

    def head_part(t, carry):
        for share in range(shares):
            k = t * shares + share
            slot = lax.rem(k, 2)

            @pl.when(k + 1 < n * shares)
            def _():
                load_merge(k + 1, 1 - slot).start()

            load_merge(k, slot).wait()
            d_send[t, :, share * some : (share + 1) * some] = mm_nt(
                d_attn[...], merge[slot]
            ).astype(low)

        @pl.when(t != i)
        def _():
            to_heads(t).start()

        return carry

    lax.fori_loop(0, n, head_part, 0)
    lax.fori_loop(min(n - 1, 1) * pieces, (n - 1) * pieces, ends, 0)
    d_att[rows_of(i, rows), :] = d_send[i]
    for m in range(chips):
        pltpu.make_async_copy(up_slab(2 * m + side), up_own.at[m], own_sem.at[0, m]).wait()
        pltpu.make_async_copy(down_slab(2 * m + side), down_own.at[m], own_sem.at[1, m]).wait()
    up.add_and_send()

    load_rows.wait()
    load_qkv.wait()
    wide = width // tile
    short = stage.shape[1]

    def square(row, column):
        return merge_grad.at[
            pl.ds(pl.multiple_of(row * short, short), short),
            pl.ds(pl.multiple_of(column * tile, tile), tile),
        ]

    def merge_one(k, carry):
        row, column = k // wide, lax.rem(k, wide)
        slot = lax.rem(k, 2)

        @pl.when(k >= 2)
        def _():
            pltpu.make_async_copy(stage.at[slot], square(0, 0), stage_sem.at[slot]).wait()

        a = att_rows[:, pl.ds(pl.multiple_of(row * short, short), short)]
        b = d_attn[:, pl.ds(pl.multiple_of(column * tile, tile), tile)]
        stage[slot] = mm_tn(a, b).astype(low)
        pltpu.make_async_copy(stage.at[slot], square(row, column), stage_sem.at[slot]).start()
        return carry

    lax.fori_loop(0, width // short * wide, merge_one, 0)
    for slot in range(2):
        pltpu.make_async_copy(stage.at[slot], square(0, 0), stage_sem.at[slot]).wait()
    down.add_and_send()
    for turn in range(1, n):
        from_rows(lax.rem(i + turn, n)).wait_recv()

    area = lse.shape[1]
    areas = n * rows // area
    area_images = [image_at(sizes, b * area) for b in range(areas)]
    d_keys[...] = jnp.zeros_like(d_keys)
    d_values[...] = jnp.zeros_like(d_values)
    turns = 2 * max(n - 2, 0) * pieces
    scale = HEAD_DIM ** (-0.5)

    def back_area(here_at, carry):
        here = rows_of(here_at, area)
        image = image_at(sizes, here_at * area)
        for h in range(heads):
            first = h * 3 * HEAD_DIM
            head = slice(h * HEAD_DIM, (h + 1) * HEAD_DIM)
            q = qkv[here, first : first + HEAD_DIM]
            g = d_att[here, head]
            log_row = lse[pl.ds(here_at * heads + h, 1), :]
            probs, d_probs = [], []
            inner = jnp.zeros((1, area), f32)
            for b in range(areas):
                key = qkv[b * area : (b + 1) * area, first + HEAD_DIM : first + 2 * HEAD_DIM]
                value = qkv[b * area : (b + 1) * area, first + 2 * HEAD_DIM : first + 3 * HEAD_DIM]
                scores = mm_nt(key, q) * scale + jnp.where(image == area_images[b], 0.0, MASKED)
                probs.append(jnp.exp(scores - log_row))
                d_probs.append(mm_nt(value, g))
                inner += jnp.sum(probs[b] * d_probs[b], axis=0, keepdims=True)
            d_query = jnp.zeros((HEAD_DIM, area), f32)
            for b in range(areas):
                at = slice(b * area, (b + 1) * area)
                key = qkv[at, first + HEAD_DIM : first + 2 * HEAD_DIM]
                d_scores = (probs[b] * (d_probs[b] - inner)).astype(low)
                d_values[at, head] += mm(probs[b].astype(low), g)
                d_keys[at, head] += mm(d_scores, q)
                d_query += mm_tn(key, d_scores)
            d_qkv[here, first : first + HEAD_DIM] = (d_query * scale).T.astype(low)

        @pl.when(here_at == areas - 1)
        def _():
            up.relay()

        return carry

    def pass_by(turn, carry):
        flows(n, pieces, sums, turn)
        return carry

    early = min(turns, pieces)
    lax.fori_loop(0, early, pass_by, 0)
    lax.fori_loop(0, areas, back_area, 0)
    lax.fori_loop(early, turns, pass_by, 0)
    for h in range(heads):
        first = h * 3 * HEAD_DIM
        head = slice(h * HEAD_DIM, (h + 1) * HEAD_DIM)
        d_qkv[:, first + HEAD_DIM : first + 2 * HEAD_DIM] = (d_keys[:, head] * scale).astype(low)
        d_qkv[:, first + 2 * HEAD_DIM : first + 3 * HEAD_DIM] = d_values[:, head].astype(low)
    for c in range(pieces):
        at = slice(c * piece, (c + 1) * piece)
        total = sums.own_value(c)
        block_out[:, at] = (middle[:, at] + table[i, 5:6, at] * total).astype(low)
        sums_out[5:6, at] = jnp.sum(cot[:, at].astype(f32) * total, axis=0, keepdims=True)
    sums_out[0:2, :] = jnp.zeros((2, width), f32)
    sums_out[6:8, :] = jnp.zeros((2, width), f32)
    down.relay()
    for scatter in (up, down):
        scatter.landed_all()
        scatter.finish()
    for turn in range(1, n):
        to_heads(lax.rem(i + turn, n)).wait_send()
    sums.all_sent()


def back(n, n_dp, operands, shapes, number, tile=512):
    (rows, width), wide, units, k_rows, down_cols, areas = shapes
    heads = wide // (3 * HEAD_DIM)
    total, chips, pieces = n * rows, n_dp // 2, 2 * width // tile
    low, f32 = jnp.bfloat16, jnp.float32
    sds = jax.ShapeDtypeStruct
    return call(
        functools.partial(back_kernel, n, n_dp, heads, tile),
        number,
        "back",
        [VMEM] * 4 + [pl.BlockSpec(memory_space=pltpu.SMEM)] + [HBM] * 8,
        [
            sds((rows, width), low),
            sds((rows, width), f32),
            sds((total, wide), low),
            sds((8, width), f32),
            sds((width, width), low),
            sds((plane_slots(n_dp), k_rows, units), low),
            sds((plane_slots(n_dp), units, down_cols), low),
        ],
        [VMEM] * 4 + [HBM] * 3,
        [
            pltpu.VMEM((rows, width), low),
            pltpu.VMEM((rows, width), f32),
            pltpu.VMEM((rows, width), low),
            pltpu.VMEM((total, wide), low),
            pltpu.VMEM((total, width), low),
            pltpu.VMEM((total + rows, width), low),
            pltpu.VMEM((2, math.gcd(256, heads * HEAD_DIM), width), low),
            pltpu.VMEM((total, heads * HEAD_DIM), low),
            pltpu.VMEM((n, rows, heads * HEAD_DIM), low),
            pltpu.VMEM((rows, width), low),
            pltpu.VMEM((total, heads * HEAD_DIM), f32),
            pltpu.VMEM((total, heads * HEAD_DIM), f32),
            pltpu.VMEM((chips, k_rows, units), low),
            pltpu.VMEM((chips, k_rows, units), low),
            pltpu.VMEM((k_rows, units), low),
            pltpu.VMEM((chips, units, down_cols), low),
            pltpu.VMEM((chips, units, down_cols), low),
            pltpu.VMEM((units, down_cols), low),
            pltpu.VMEM((2, tile // 2, tile), low),
            DMA((n, pieces)),
            DMA((n + 1, pieces)),
            scatter_sems(n_dp),
            scatter_sems(n_dp),
            DMA((2, n)),
            DMA((2,)),
            DMA((5,)),
            DMA((2,)),
            DMA((2, chips)),
        ],
        flops=20 * total * total * wide // 3,
    )(*operands)


def last_kernel(
    n,
    n_dp,
    tile,
    d_qkv,
    sums_in,
    table,
    sizes,
    hidden_hbm,
    x_hbm,
    middle_hbm,
    mod_hbm,
    merge_hbm,
    attend_hbm,
    input_grad,
    d_mod_all,
    noise_sum,
    attend_landed,
    merge_out,
    hidden,
    x_own,
    d_middle,
    mod_w,
    attend,
    part,
    got,
    grad_own,
    grad_theirs,
    grad_swapped,
    grad_via,
    merge_own,
    merge_swapped,
    merge_via,
    merge_landed,
    merge_part,
    merge_got,
    sums_all,
    shares,
    shares_all,
    terms,
    terms_all,
    noise_parts,
    sent,
    came,
    merge_sent,
    merge_came,
    grad_sems,
    merge_sems,
    share_sem,
    mod_sem,
    term_sem,
    noise_sem,
    load_sem,
    own_sem,
    attend_sem,
):
    d, i = lax.axis_index("dp"), lax.axis_index("tensor")
    rows, width = input_grad.shape
    low, f32 = jnp.bfloat16, jnp.float32
    chips = n_dp // 2
    side = lax.rem(d, 2)
    k_rows, own_cols = mod_w.shape
    merge_cols = merge_own.shape[2]
    merge_rows = merge_out.shape[0]
    images = d_mod_all.shape[1]

    def merge_slab(at):
        return merge_hbm.at[:, pl.ds(pl.multiple_of(at * merge_cols, merge_cols), merge_cols)]

    load_hidden, load_x, load_middle, load_mod = (
        pltpu.make_async_copy(source, target, load_sem.at[k])
        for k, (source, target) in enumerate(
            (
                (hidden_hbm, hidden),
                (x_hbm, x_own),
                (middle_hbm, d_middle),
                (mod_hbm, mod_w),
            )
        )
    )

    def load_attend(c):
        at = pl.ds(pl.multiple_of(c * tile, tile), tile)
        return pltpu.make_async_copy(attend_hbm.at[at, :], attend.at[at, :], attend_sem.at[c])

    for c in range(width // tile):
        load_attend(c).start()
    for m in range(chips):
        pltpu.make_async_copy(merge_slab(2 * m + side), merge_own.at[m], own_sem.at[m]).start()
    greet_all(n, n_dp, d, i)
    merge = PlaneScatter(
        n_dp,
        d,
        lambda m: merge_slab(2 * m + 1 - side),
        merge_own,
        merge_swapped,
        merge_via,
        merge_landed,
        merge_sems,
    )
    grad = PlaneScatter(
        n_dp, d, lambda m: grad_theirs.at[m], grad_own, grad_swapped, grad_via, attend_landed, grad_sems
    )
    merge.swap_all()
    for late in (load_hidden, load_x, load_middle, load_mod):
        late.start()
    piece = tile // 2
    sums = LineScatter(n, i, rows, piece, part, got, sent, came)
    pieces = sums.pieces

    def partial_block(q, carry):
        j = jnp.where(2 * i < n - 1, n - 1 - q, q)
        here = rows_of(j, rows)

        def one(c, inner):
            at = pl.ds(pl.multiple_of(c * tile, tile), tile)

            @pl.when(q == 0)
            def _():
                load_attend(c).wait()

            part[here, at] = mm_nt(d_qkv[here, :], attend[at, :]).astype(low)
            for k in range(tile // piece):
                sums.at_end(j, c * (tile // piece) + k)
            return inner

        lax.fori_loop(0, width // tile, one, 0)
        return carry

    partial_block(0, 0)
    for m in range(chips):
        pltpu.make_async_copy(merge_slab(2 * m + side), merge_own.at[m], own_sem.at[m]).wait()
    merge.add_and_send()
    lax.fori_loop(1, n, partial_block, 0)

    def slab_grad(at):
        columns = pl.ds(pl.multiple_of(at * k_rows, k_rows), k_rows)
        return mm_tn(hidden[:, columns], d_qkv[...]).astype(low)

    def for_them(m, carry):
        grad_theirs[m] = slab_grad(2 * m + 1 - side)
        grad.swap(m).start()
        return carry

    def for_us(m, carry):
        grad_own[m] = slab_grad(2 * m + side)
        return carry

    load_hidden.wait()
    lax.fori_loop(0, chips, for_them, 0)
    lax.fori_loop(0, chips, for_us, 0)
    grad.add_and_send()
    merge.relay()
    turns = 2 * max(n - 2, 0) * pieces

    def pass_by(turn, carry):
        flows(n, pieces, sums, turn)
        return carry

    lax.fori_loop(0, turns, pass_by, 0)

    grad.relay()

    for late in (load_x, load_middle, load_mod):
        late.wait()
    tiles = [slice(c * piece, (c + 1) * piece) for c in range(pieces)]
    squares = jnp.zeros((rows, 1), f32)
    for at in tiles:
        v = x_own[:, at].astype(f32)
        squares += jnp.sum(v * v, axis=1, keepdims=True)
    root = lax.rsqrt(squares * (1.0 / width) + 1e-06)
    mean = jnp.zeros((rows, 1), f32)
    sums_all[...] = sums_in[...]
    for c, at in enumerate(tiles):
        v = x_own[:, at].astype(f32) * root
        dh = sums.own_value(c)
        mean += jnp.sum(dh * (1.0 + table[i, 1:2, at]) * v, axis=1, keepdims=True)
        sums_all[0:1, at] = jnp.sum(dh, axis=0, keepdims=True)
        sums_all[1:2, at] = jnp.sum(dh * v, axis=0, keepdims=True)

    unit = math.gcd(width, own_cols)
    image = image_at(sizes, i * rows)
    for number in range(6):
        for start in range(0, width, unit):
            at = number * width + start
            for k in range(images):
                shares[at // own_cols, k : k + 1, at % own_cols : at % own_cols + unit] = (
                    sums_all[number : number + 1, start : start + unit]
                    * jnp.where(image == k, 1.0, 0.0)
                )

    def to_line(source, target, sems, turn, whole=False):
        t = lax.rem(i + turn, n)
        return pltpu.make_async_remote_copy(
            src_ref=source if whole else source.at[t],
            dst_ref=target.at[i],
            send_sem=sems.at[0, t],
            recv_sem=sems.at[1, i],
            device_id=(d, t),
            device_id_type=MESH,
        )

    def from_line(source, target, sems, turn, whole=False):
        t = lax.rem(i + turn, n)
        return pltpu.make_async_remote_copy(
            src_ref=source if whole else source.at[t],
            dst_ref=target.at[t],
            send_sem=sems.at[0, t],
            recv_sem=sems.at[1, t],
            device_id=(d, t),
            device_id_type=MESH,
        )

    def to_plane(source, target, sems, flip):
        return pltpu.make_async_remote_copy(
            src_ref=source,
            dst_ref=target.at[d],
            send_sem=sems.at[0, flip],
            recv_sem=sems.at[1, flip],
            device_id=(d ^ flip, i),
            device_id_type=MESH,
        )

    def from_plane(source, target, sems, flip):
        return pltpu.make_async_remote_copy(
            src_ref=source,
            dst_ref=target.at[d ^ flip],
            send_sem=sems.at[0, flip],
            recv_sem=sems.at[1, flip],
            device_id=(d ^ flip, i),
            device_id_type=MESH,
        )

    for turn in range(1, n):
        to_line(shares, shares_all, share_sem, turn).start()

    merge.landed_all()
    merge_sums = LineScatter(
        n, i, merge_rows, merge_cols, merge_part, merge_got, merge_sent, merge_came
    )

    def merge_block(q, carry):
        j = jnp.where(2 * i < n - 1, n - 1 - q, q)
        here = rows_of(j, merge_rows)
        total = merge_landed[0, here, :].astype(f32)
        for m in range(1, merge_landed.shape[0]):
            total += merge_landed[m, here, :].astype(f32)
        merge_part[here, :] = total.astype(low)
        merge_sums.at_end(j, 0)
        return carry

    lax.fori_loop(0, n, merge_block, 0)

    mean = mean * (1.0 / width)
    for c, at in enumerate(tiles):
        v = x_own[:, at].astype(f32) * root
        u = sums.own_total(c) * (1.0 + table[i, 1:2, at])
        input_grad[:, at] = (d_middle[:, at] + root * (u - v * mean)).astype(low)
    shares_all[i] = shares[i]
    for turn in range(1, n):
        from_line(shares, shares_all, share_sem, turn).wait_recv()
    d_mod_all[d] = jnp.sum(shares_all[...], axis=0).astype(low).astype(f32)
    own_mod = d_mod_all.at[d]
    for flip in range(1, n_dp):
        to_plane(own_mod, d_mod_all, mod_sem, flip).start()
    for t in range(n - 1, 1, -1):
        for near in (True, False):
            merge_sums.pass_on(t, 0, near)
    for flip in range(1, n_dp):
        from_plane(own_mod, d_mod_all, mod_sem, flip).wait_recv()
    flat = d_mod_all[...].reshape(n_dp * images, own_cols).astype(low)
    terms[...] = mm_nt(flat, mod_w[...]).reshape(n_dp, images, k_rows)
    for turn in range(1, n):
        to_line(terms, terms_all, term_sem, turn, True).start()
    terms_all[i] = terms[...]
    for turn in range(1, n):
        from_line(terms, terms_all, term_sem, turn, True).wait_recv()
    noise_parts[...] = jnp.sum(terms_all[...], axis=0)
    for flip in range(1, n_dp):
        to_plane(noise_parts.at[d ^ flip], noise_sum, noise_sem, flip).start()
    noise_sum[d] = noise_parts[d]
    merge_out[...] = merge_sums.own_value(0)
    for flip in range(1, n_dp):
        from_plane(noise_parts.at[d ^ flip], noise_sum, noise_sem, flip).wait_recv()
    grad.landed_all()
    grad.finish()
    merge.finish()
    for turn in range(1, n):
        to_line(shares, shares_all, share_sem, turn).wait_send()
        to_line(terms, terms_all, term_sem, turn, True).wait_send()
    for flip in range(1, n_dp):
        to_plane(own_mod, d_mod_all, mod_sem, flip).wait_send()
        to_plane(noise_parts.at[d ^ flip], noise_sum, noise_sem, flip).wait_send()
    sums.all_sent()
    merge_sums.all_sent()


def last(n, n_dp, operands, shapes, number, tile=512):
    (rows, width), wide, k_rows, own_cols, (merge_rows, merge_cols), images = shapes
    total, chips, pieces = n * rows, n_dp // 2, 2 * width // tile
    low, f32 = jnp.bfloat16, jnp.float32
    sds = jax.ShapeDtypeStruct
    return call(
        functools.partial(last_kernel, n, n_dp, tile),
        number,
        "last",
        [VMEM] * 3 + [pl.BlockSpec(memory_space=pltpu.SMEM)] + [HBM] * 6,
        [
            sds((rows, width), low),
            sds((n_dp, images, own_cols), f32),
            sds((n_dp, images, k_rows), f32),
            sds((plane_slots(n_dp), k_rows, wide), low),
            sds((merge_rows, merge_cols), f32),
        ],
        [VMEM] * 3 + [HBM] + [VMEM],
        [
            pltpu.VMEM((total, width), low),
            pltpu.VMEM((rows, width), low),
            pltpu.VMEM((rows, width), f32),
            pltpu.VMEM((k_rows, own_cols), low),
            pltpu.VMEM((width, wide), low),
            pltpu.VMEM((total, width), low),
            pltpu.VMEM((total + rows, width), low),
            pltpu.VMEM((chips, k_rows, wide), low),
            pltpu.VMEM((chips, k_rows, wide), low),
            pltpu.VMEM((chips, k_rows, wide), low),
            pltpu.VMEM((k_rows, wide), low),
            pltpu.VMEM((chips, n * merge_rows, merge_cols), low),
            pltpu.VMEM((chips, n * merge_rows, merge_cols), low),
            pltpu.VMEM((n * merge_rows, merge_cols), low),
            pltpu.VMEM((plane_slots(n_dp), n * merge_rows, merge_cols), low),
            pltpu.VMEM((n * merge_rows, merge_cols), low),
            pltpu.VMEM(((n + 1) * merge_rows, merge_cols), low),
            pltpu.VMEM((8, width), f32),
            pltpu.VMEM((n, images, own_cols), f32),
            pltpu.VMEM((n, images, own_cols), f32),
            pltpu.VMEM((n_dp, images, k_rows), f32),
            pltpu.VMEM((n, n_dp, images, k_rows), f32),
            pltpu.VMEM((n_dp, images, k_rows), f32),
            DMA((n, pieces)),
            DMA((n + 1, pieces)),
            DMA((n, 1)),
            DMA((n + 1, 1)),
            scatter_sems(n_dp),
            scatter_sems(n_dp),
            DMA((2, n)),
            DMA((2, n_dp)),
            DMA((2, n)),
            DMA((2, n_dp)),
            DMA((4,)),
            DMA((chips,)),
            DMA((width // tile,)),
        ],
        flops=4 * total * width * wide,
    )(*operands)


def on_device(
    block_input,
    cotangent,
    noise_embed,
    image_sizes,
    attend_weight,
    merge_weight,
    up_weight,
    down_weight,
    modulate_weight,
):
    n = lax.axis_size("tensor")
    n_dp = lax.axis_size("dp")
    rows, width = block_input.shape
    tokens = n * rows
    images = image_sizes.shape[1]
    k_rows = modulate_weight.shape[0]

    (
        cot_full,
        hidden_first,
        packed,
        lse,
        att_rows,
        attn_out,
        middle,
        hidden_second,
        table,
        attend_full,
        merge_full,
        up_full,
        down_full,
        noise_all,
    ) = front(
        n,
        n_dp,
        block_input,
        cotangent,
        noise_embed,
        modulate_weight,
        image_sizes,
        attend_weight,
        merge_weight,
        up_weight,
        down_weight,
        0,
    )
    d_hidden_second, mlp_part, up_local, down_local = ffn(
        n, hidden_second, table, cot_full, up_full, down_full, 1
    )
    units = up_full.shape[1]
    wide = packed.shape[1]
    (
        block_output,
        d_middle,
        d_qkv,
        row_sums,
        merge_local,
        up_landed,
        down_landed,
    ) = back(
        n,
        n_dp,
        (
            d_hidden_second,
            middle,
            table,
            lse,
            image_sizes,
            cotangent,
            attn_out,
            att_rows,
            packed,
            mlp_part,
            merge_full,
            up_local,
            down_local,
        ),
        (block_input.shape, wide, units, k_rows, down_weight.shape[1], lse.shape[0]),
        2,
    )
    input_grad, d_mod_all, noise_sums, attend_landed, merge_part = last(
        n,
        n_dp,
        (
            d_qkv,
            row_sums,
            table,
            image_sizes,
            hidden_first,
            block_input,
            d_middle,
            modulate_weight,
            merge_local,
            attend_full,
        ),
        (
            block_input.shape,
            wide,
            k_rows,
            modulate_weight.shape[1],
            merge_weight.shape,
            images,
        ),
        3,
    )

    def chip_sum(landed):
        return sum(landed[slot].astype(jnp.float32) for slot in range(landed.shape[0]))

    up_part, down_part, attend_part = map(chip_sum, (up_landed, down_landed, attend_landed))
    modulate_part = dot(
        noise_all.reshape(n_dp * images, k_rows).astype(jnp.bfloat16),
        d_mod_all.reshape(n_dp * images, -1).astype(jnp.bfloat16),
        ROWS_ROWS,
    )
    noise_sum = noise_sums.transpose(1, 0, 2).reshape(images, width)
    silu_back = jax.vjp(jax.nn.silu, noise_embed.astype(jnp.float32))[1]
    noise_grad = silu_back(noise_sum)[0]
    return (
        block_output,
        input_grad,
        noise_grad,
        attend_part,
        merge_part,
        up_part,
        down_part,
        modulate_part,
    )


def solution(mesh):
    whole_rows = P(("dp", "tensor"), None)
    by_dp = P("dp", None)
    tall = P("dp", "tensor")
    wide = P("tensor", "dp")
    return jax.shard_map(
        on_device,
        mesh=mesh,
        in_specs=(whole_rows, whole_rows, by_dp, by_dp, tall, wide, tall, wide, tall),
        out_specs=(whole_rows, whole_rows, by_dp, tall, wide, tall, wide, tall),
        check_vma=False,
    )
```

```python
import functools
import math

import jax
import jax.numpy as jnp
from jax import lax
from jax.experimental import pallas as pl
from jax.experimental.pallas import tpu as pltpu
from jax.sharding import PartitionSpec as P

HEAD_DIM = 128
MASKED = -1e30


def dot(a, b, dims=(((1,), (0,)), ((), ()))):
    return lax.dot_general(a, b, dims, preferred_element_type=jnp.float32)


ROWS_ROWS = (((0,), (0,)), ((), ()))


MESH = pl.DeviceIdType.MESH
HBM = pl.BlockSpec(memory_space=pl.ANY)
VMEM = pl.BlockSpec(memory_space=pltpu.VMEM)
DMA = pltpu.SemaphoreType.DMA


def rows_of(j, rows):
    return pl.ds(pl.multiple_of(j * rows, rows), rows)


def beside(step):
    return (lax.axis_index("dp"), lax.axis_index("tensor") + step)


def greet_line(n, i):
    barrier = pltpu.get_barrier_semaphore()

    @pl.when(i > 0)
    def _():
        pl.semaphore_signal(barrier, inc=1, device_id=beside(-1), device_id_type=MESH)

    @pl.when(i < n - 1)
    def _():
        pl.semaphore_signal(barrier, inc=1, device_id=beside(1), device_id_type=MESH)

    pl.semaphore_wait(barrier, jnp.where(i > 0, 1, 0) + jnp.where(i < n - 1, 1, 0))


class LineGather:
    def __init__(self, n, i, rows, own, full, to_left, to_right, arrived):
        self.n, self.i, self.rows, self.own, self.full = n, i, rows, own, full
        self.to_left, self.to_right, self.arrived = to_left, to_right, arrived

    def copy(self, j, step, source=None):
        place = self.full.at[rows_of(j, self.rows)]
        return pltpu.make_async_remote_copy(
            src_ref=place if source is None else source,
            dst_ref=place,
            send_sem=(self.to_right if step > 0 else self.to_left).at[j],
            recv_sem=self.arrived.at[j],
            device_id=beside(step),
            device_id_type=MESH,
        )

    def start(self):
        @pl.when(self.i > 0)
        def _():
            self.copy(self.i, -1, self.own).start()

        @pl.when(self.i < self.n - 1)
        def _():
            self.copy(self.i, 1, self.own).start()

    def step(self, s):
        for side in (-1, 1):
            j = self.i + side * s
            there = (j >= 0) & (j < self.n)
            more = (self.i > 0) if side > 0 else (self.i < self.n - 1)

            @pl.when(there)
            def _():
                self.copy(j, side).wait_recv()

            @pl.when(there & more)
            def _():
                self.copy(j, -side).start()

    def finish(self):
        @pl.when(self.i > 0)
        def _():
            self.copy(self.i, -1, self.own).wait_send()

        @pl.when(self.i < self.n - 1)
        def _():
            self.copy(self.i, 1, self.own).wait_send()

        for j in range(self.n):

            @pl.when((j < self.i) & (self.i < self.n - 1))
            def _():
                self.copy(j, 1).wait_send()

            @pl.when((j > self.i) & (self.i > 0))
            def _():
                self.copy(j, -1).wait_send()


class LineScatter:
    def __init__(self, n, i, rows, width, part, got, sent, arrived):
        self.n, self.i, self.rows, self.width = n, i, rows, width
        self.part, self.got, self.sent, self.arrived = part, got, sent, arrived
        self.pieces = part.shape[1] // width

    def columns(self, c):
        if isinstance(c, int):
            return pl.ds(c * self.width, self.width)
        return pl.ds(pl.multiple_of(c * self.width, self.width), self.width)

    def copy(self, j, slot, c, step):
        return pltpu.make_async_remote_copy(
            src_ref=self.part.at[rows_of(j, self.rows), self.columns(c)],
            dst_ref=self.got.at[rows_of(slot, self.rows), self.columns(c)],
            send_sem=self.sent.at[j, c],
            recv_sem=self.arrived.at[slot, c],
            device_id=beside(step),
            device_id_type=MESH,
        )

    def slot_there(self, j, step):
        if step > 0:
            return j
        return jnp.where(j == self.i - 1, self.n, j)

    def at_end(self, j, c):
        @pl.when((self.i == 0) & (j > 0))
        def _():
            self.copy(j, j, c, 1).start()

        @pl.when((self.i == self.n - 1) & (j < self.i))
        def _():
            self.copy(j, self.slot_there(j, -1), c, -1).start()

    def pass_on(self, t, c, near):
        n, i = self.n, self.i
        rightward = (2 * i < n - 1) if near else (2 * i >= n - 1)
        j = jnp.where(rightward, t, n - 1 - t)
        step = jnp.where(rightward, 1, -1)
        right = rightward & (i > 0) & (j > i)
        left = jnp.logical_not(rightward) & (i < n - 1) & (j < i)

        @pl.when(right | left)
        def _():
            self.add(j, j, c)
            slot = jnp.where(left & (j == i - 1), n, j)
            self.copy(j, slot, c, step).start()

    def add(self, j, slot, c):
        self.copy(j, slot, c, 1).wait_recv()
        here = (rows_of(j, self.rows), self.columns(c))
        there = (rows_of(slot, self.rows), self.columns(c))
        total = self.part[here].astype(jnp.float32) + self.got[there].astype(jnp.float32)
        self.part[here] = total.astype(self.part.dtype)

    def own(self, c, out):
        i, n = self.i, self.n
        columns = self.columns(c)
        out[:, columns] = self.part[rows_of(i, self.rows), columns].astype(out.dtype)

        @pl.when(i > 0)
        def _():
            self.copy(i, i, c, 1).wait_recv()
            out[:, columns] += self.got[rows_of(i, self.rows), columns].astype(out.dtype)

        @pl.when(i < n - 1)
        def _():
            self.copy(i, n, c, -1).wait_recv()
            out[:, columns] += self.got[rows_of(n, self.rows), columns].astype(out.dtype)

    def own_value(self, c):
        i, n = self.i, self.n

        @pl.when(i > 0)
        def _():
            self.copy(i, i, c, 1).wait_recv()

        @pl.when(i < n - 1)
        def _():
            self.copy(i, n, c, -1).wait_recv()

        return self.own_total(c)

    def own_total(self, c):
        i, n, columns = self.i, self.n, self.columns(c)
        total = self.part[rows_of(i, self.rows), columns].astype(jnp.float32)
        left = self.got[rows_of(i, self.rows), columns].astype(jnp.float32)
        right = self.got[rows_of(n, self.rows), columns].astype(jnp.float32)
        return total + jnp.where(i > 0, left, 0.0) + jnp.where(i < n - 1, right, 0.0)

    def all_sent(self):
        def one(j, carry):
            @pl.when(j != self.i)
            def _():
                for c in range(self.pieces):
                    self.copy(j, 0, c, 1).wait_send()

            return carry

        lax.fori_loop(0, self.n, one, 0)


def mm(a, b):
    return lax.dot_general(a, b, (((1,), (0,)), ((), ())), preferred_element_type=jnp.float32)


def mm_nt(a, b):
    return lax.dot_general(a, b, (((1,), (1,)), ((), ())), preferred_element_type=jnp.float32)


def mm_tn(a, b):
    return lax.dot_general(a, b, (((0,), (0,)), ((), ())), preferred_element_type=jnp.float32)


def call(kernel, collective_id, name, in_specs, outs, out_specs, scratch, flops=0, limit=60):
    return pl.pallas_call(
        kernel,
        out_shape=outs,
        in_specs=in_specs,
        out_specs=out_specs,
        scratch_shapes=scratch,
        compiler_params=pltpu.CompilerParams(
            collective_id=collective_id,
            has_side_effects=True,
            vmem_limit_bytes=limit * 1024 * 1024,
        ),
        cost_estimate=pl.CostEstimate(flops=flops, bytes_accessed=1 << 20, transcendentals=0),
        name=name,
    )


def ffn_kernel(
    n,
    tile,
    grad_tile,
    own_hidden,
    table,
    d_mlp_hbm,
    up_hbm,
    down_hbm,
    d_hidden,
    mlp_part,
    up_grad,
    down_grad,
    up,
    down,
    d_mlp,
    hidden,
    activated,
    d_pre,
    part,
    got,
    stage,
    mlp,
    to_left,
    to_right,
    arrived,
    sent,
    came,
    local,
    stage_sem,
):
    i = lax.axis_index("tensor")
    rows, width = own_hidden.shape
    units = up.shape[1]
    loads = [
        pltpu.make_async_copy(source, target, local.at[k])
        for k, (source, target) in enumerate(((up_hbm, up), (d_mlp_hbm, d_mlp), (down_hbm, down)))
    ]
    for load in loads:
        load.start()
    greet_line(n, i)
    line = LineGather(n, i, rows, own_hidden, hidden, to_left, to_right, arrived)
    first_core = lax.rem(lax.axis_index("dp"), 2) == 0
    pl.when(first_core)(line.start)
    piece = tile // 2
    sums = LineScatter(n, i, rows, piece, part, got, sent, came)
    hidden[rows_of(i, rows), :] = own_hidden[...]
    for load in loads:
        load.wait()

    def one_block(j):
        here = rows_of(j, rows)

        def gated(c, carry):
            at = pl.ds(pl.multiple_of(c * tile, tile), tile)
            d_mlp[here, at] = (d_mlp[here, at].astype(jnp.float32) * table[j, 5:6, at]).astype(
                jnp.bfloat16
            )
            return carry

        lax.fori_loop(0, width // tile, gated, 0)

        def first(c, carry):
            at = pl.ds(pl.multiple_of(c * tile, tile), tile)
            pre = mm(hidden[here, :], up[:, at])
            d_act = mm_nt(d_mlp[here, :], down[at, :])
            cdf = 0.5 * (1.0 + lax.erf(pre * (0.5**0.5)))
            density = jnp.exp(-0.5 * pre * pre) * ((0.5 / math.pi) ** 0.5)
            activated[here, at] = (pre * cdf).astype(jnp.bfloat16)
            d_pre[here, at] = (d_act * (cdf + pre * density)).astype(jnp.bfloat16)
            return carry

        lax.fori_loop(0, units // tile, first, 0)

        def second(c, carry):
            at = pl.ds(pl.multiple_of(c * tile, tile), tile)
            part[here, at] = mm_nt(d_pre[here, :], up[at, :]).astype(jnp.bfloat16)
            for k in range(tile // piece):
                sums.at_end(j, c * (tile // piece) + k)
            return carry

        lax.fori_loop(0, width // tile, second, 0)

        def third(c, carry):
            at = pl.ds(pl.multiple_of(c * tile, tile), tile)
            mlp[here, at] = mm(activated[here, :], down[:, at]).astype(jnp.bfloat16)
            return carry

        lax.fori_loop(0, width // tile, third, 0)

    def visit(q, carry):
        s = (q + 1) // 2
        side = 1 - 2 * (q % 2)
        j = i + s * side

        @pl.when(q % 2 == 1)
        def _():
            line.step(s)

        @pl.when((j >= 0) & (j < n))
        def _():
            one_block(j)

        @pl.when((q == 0) & jnp.logical_not(first_core))
        def _():
            line.start()

        return carry

    lax.fori_loop(0, 2 * n - 1, visit, 0)
    keep_mlp = pltpu.make_async_copy(mlp, mlp_part, local.at[3])
    keep_mlp.start()

    count = (width // grad_tile) * (units // grad_tile)
    turns = 2 * max(n - 2, 1) * sums.pieces
    per_turn = -(-2 * count // turns)

    def square(ref, row, column):
        return ref.at[
            pl.ds(pl.multiple_of(row * grad_tile, grad_tile), grad_tile),
            pl.ds(pl.multiple_of(column * grad_tile, grad_tile), grad_tile),
        ]

    def put(slot, target):
        return pltpu.make_async_copy(stage.at[slot], target, stage_sem.at[slot])

    def one_grad(k, left, right, target):
        wide = right.shape[1] // grad_tile
        row, column = k // wide, k % wide
        slot = k % 2

        @pl.when(k >= 2)
        def _():
            put(slot, square(target, 0, 0)).wait()

        a = left[:, pl.ds(pl.multiple_of(row * grad_tile, grad_tile), grad_tile)]
        b = right[:, pl.ds(pl.multiple_of(column * grad_tile, grad_tile), grad_tile)]
        stage[slot] = mm_tn(a, b).astype(jnp.bfloat16)
        put(slot, square(target, row, column)).start()

    def tail(k, carry):
        t, c = 2 + k // (2 * sums.pieces), k % sums.pieces
        for near in (True, False):

            @pl.when((k // sums.pieces) % 2 == (0 if near else 1))
            def _():
                sums.pass_on(t, c, near)

        for extra in range(per_turn):
            item = k * per_turn + extra

            @pl.when(item < count)
            def _():
                one_grad(item, hidden, d_pre, up_grad)

            @pl.when(item == count)
            def _():
                for slot in range(2):
                    put(slot, square(up_grad, 0, 0)).wait()

            @pl.when((item >= count) & (item < 2 * count))
            def _():
                one_grad(item - count, activated, d_mlp, down_grad)

        return carry

    lax.fori_loop(0, turns, tail, 0)
    for slot in range(2):
        put(slot, square(down_grad, 0, 0)).wait()
    for c in range(sums.pieces):
        sums.own(c, d_hidden)
    line.finish()
    sums.all_sent()
    keep_mlp.wait()


def ffn(n, own_hidden, table, cotangents, up, down, collective_id, tile=512, grad_tile=512):
    rows, width = own_hidden.shape
    units = up.shape[1]
    pieces = 2 * width // tile
    low = jnp.bfloat16
    return call(
        functools.partial(ffn_kernel, n, tile, grad_tile),
        collective_id,
        "ffn",
        [VMEM, VMEM, HBM, HBM, HBM],
        [
            jax.ShapeDtypeStruct((rows, width), jnp.float32),
            jax.ShapeDtypeStruct((n * rows, width), low),
            jax.ShapeDtypeStruct((width, units), low),
            jax.ShapeDtypeStruct((units, width), low),
        ],
        [VMEM, HBM, HBM, HBM],
        [
            pltpu.VMEM((width, units), low),
            pltpu.VMEM((units, width), low),
            pltpu.VMEM((n * rows, width), low),
            pltpu.VMEM((n * rows, width), low),
            pltpu.VMEM((n * rows, units), low),
            pltpu.VMEM((n * rows, units), low),
            pltpu.VMEM((n * rows, width), low),
            pltpu.VMEM(((n + 1) * rows, width), low),
            pltpu.VMEM((2, grad_tile, grad_tile), low),
            pltpu.VMEM((n * rows, width), low),
            DMA((n,)),
            DMA((n,)),
            DMA((n,)),
            DMA((n, pieces)),
            DMA((n + 1, pieces)),
            DMA((4,)),
            DMA((2,)),
        ],
        flops=12 * n * rows * width * units,
    )(own_hidden, table, cotangents, up, down)


def image_at(sizes, place):
    end, count = 0, 0
    for k in range(sizes.shape[1]):
        end = end + sizes[0, k]
        count = count + jnp.where(place >= end, 1, 0)
    return count


def image_at(sizes, place):
    end, count = 0, 0
    for k in range(sizes.shape[1]):
        end = end + sizes[0, k]
        count = count + jnp.where(place >= end, 1, 0)
    return count


class PlaneGather:
    def __init__(self, n_dp, d, own, view, height, sent, came):
        self.n_dp, self.d, self.own, self.view, self.height = n_dp, d, own, view, height
        self.sent, self.came = sent, came
        self.square = n_dp == 8
        self.peers = [2 * k for k in range(1, n_dp // 2)]

    def copy(self, k, source, target, peer):
        return pltpu.make_async_remote_copy(
            src_ref=source,
            dst_ref=target,
            send_sem=self.sent.at[k],
            recv_sem=self.came.at[k],
            device_id=(self.d ^ peer, lax.axis_index("tensor")),
            device_id_type=MESH,
        )

    def slab(self, flip, half=None):
        if half is None:
            return self.view(self.d ^ flip, 0, self.height)
        return self.view(self.d ^ flip, half * (self.height // 2), self.height // 2)

    def owns(self):
        peers = [2, 4] if self.square else self.peers
        return [
            self.copy(k, self.own, self.slab(0), peer) for k, peer in enumerate([1] + peers)
        ]

    def relay_of(self, k):
        flip, half, peer = ((2, 0, 4), (4, 1, 2))[k - 1]
        return self.copy(2 + k, self.slab(flip, half), self.slab(flip, half), peer)

    def across(self):
        return [
            self.copy(3, self.slab(6, 0), self.slab(6, 0), 4),
            self.copy(4, self.slab(6, 1), self.slab(6, 1), 2),
        ]

    def hand(self, flip):
        base = 5 if self.square else len(self.peers) + 1
        k = base + flip // 2 - 1
        return self.copy(k, self.slab(flip), self.slab(flip), 1)

    def handed(self, flip):
        base = 5 if self.square else len(self.peers) + 1
        k = base + flip // 2 - 1
        return self.copy(k, self.slab(flip ^ 1), self.slab(flip ^ 1), 1)

    def start(self):
        for copy in self.owns():
            copy.start()

    def relay(self):
        if not self.square:
            return
        for k, flip in ((1, 2), (2, 4)):
            self.copy(k, self.own, self.slab(flip), flip).wait_recv()
            self.relay_of(k).start()
            self.hand(flip).start()

    def close(self):
        if self.square:
            for copy in self.across():
                copy.wait_recv()
            self.hand(6).start()
        else:
            for k, flip in enumerate(self.peers):
                self.copy(k + 1, self.own, self.slab(flip), flip).wait_recv()
                self.hand(flip).start()
        self.copy(0, self.own, self.slab(1), 1).wait_recv()
        for flip in self.peers:
            self.handed(flip).wait_recv()

    def finish(self):
        for copy in self.owns():
            copy.wait_send()
        if self.square:
            for k in (1, 2):
                self.relay_of(k).wait_send()
        for flip in self.peers:
            self.hand(flip).wait_send()


def plane_sems(n_dp):
    return 8 if n_dp == 8 else n_dp - 1


def greet_all(n, n_dp, d, i):
    barrier = pltpu.get_barrier_semaphore()
    for flip in range(1, n_dp):
        pl.semaphore_signal(barrier, inc=1, device_id=(d ^ flip, i), device_id_type=MESH)
    for turn in range(1, n):
        pl.semaphore_signal(
            barrier, inc=1, device_id=(d, lax.rem(i + turn, n)), device_id_type=MESH
        )
    pl.semaphore_wait(barrier, n_dp + n - 2)


def front_kernel(
    n,
    n_dp,
    heads,
    tile,
    x_own,
    cot_own,
    noise_own,
    mod_w,
    sizes,
    attend_w,
    merge_w,
    up_w,
    down_w,
    cot_full,
    hidden_out,
    qkv_out,
    lse,
    rows_out,
    attn_out_hbm,
    middle_out,
    second_out,
    table,
    attend_full,
    merge_full,
    up_full,
    down_full,
    noise_all,
    x_full,
    attend,
    merge,
    noise,
    hidden,
    qkv,
    attended,
    att_rows,
    attn_out,
    middle,
    hidden_second,
    terms,
    terms_all,
    columns,
    noise_sem,
    terms_sem,
    column_sem,
    x_sem,
    cot_sem,
    merge_sem,
    weight_sent,
    weight_came,
    out_sem,
    att_sem,
    local,
):
    d, i = lax.axis_index("dp"), lax.axis_index("tensor")
    rows, width = x_own.shape
    k_rows, own_cols = mod_w.shape
    head_cols = heads * HEAD_DIM
    low, f32 = jnp.bfloat16, jnp.float32
    merge_rows, merge_cols = merge_w.shape
    down_cols = down_w.shape[1]
    merge_slab = merge.at[:, pl.ds(pl.multiple_of(d * merge_cols, merge_cols), merge_cols)]

    def row_view(full, height):
        return lambda at, start, count: full.at[
            pl.ds(pl.multiple_of(at * height + start, 16), count), :
        ]

    def column_view(full, wide):
        return lambda at, start, count: full.at[
            pl.ds(start, count), pl.ds(pl.multiple_of(at * wide, wide), wide)
        ]

    weights = [
        PlaneGather(n_dp, d, own, view, height, weight_sent.at[k], weight_came.at[k])
        for k, (own, view, height) in enumerate(
            (
                (attend_w, row_view(attend, k_rows), k_rows),
                (merge_slab, column_view(merge, merge_cols), n * merge_rows),
                (up_w, row_view(up_full, k_rows), k_rows),
                (down_w, column_view(down_full, down_cols), down_w.shape[0]),
            )
        )
    ]
    attend_g, merge_g, up_g, down_g = weights
    copies = [
        pltpu.make_async_copy(source, target, local.at[k])
        for k, (source, target) in enumerate(
            (
                (attend_w, attend_g.slab(0)),
                (merge_w, merge_slab.at[rows_of(i, merge_rows)]),
                (cot_own, cot_full.at[rows_of(i, rows)]),
                (up_w, up_g.slab(0)),
                (down_w, down_g.slab(0)),
            )
        )
    ]
    for copy in copies:
        copy.start()
    greet_all(n, n_dp, d, i)

    def to_plane(source, target, sems, flip):
        return pltpu.make_async_remote_copy(
            src_ref=source.at[d ^ flip],
            dst_ref=target.at[d],
            send_sem=sems.at[0, flip],
            recv_sem=sems.at[1, flip],
            device_id=(d ^ flip, i),
            device_id_type=MESH,
        )

    def from_plane(target, sems, flip):
        return pltpu.make_async_remote_copy(
            src_ref=target.at[d ^ flip],
            dst_ref=target.at[d ^ flip],
            send_sem=sems.at[0, flip],
            recv_sem=sems.at[1, flip],
            device_id=(d ^ flip, i),
            device_id_type=MESH,
        )

    for k in range(n_dp):
        v = noise_own[:, k * k_rows : (k + 1) * k_rows].astype(f32)
        noise[k] = (v * (1.0 / (1.0 + jnp.exp(-v)))).astype(low).astype(f32)
    for flip in range(1, n_dp):
        to_plane(noise, noise_all, noise_sem, flip).start()
    merge_line = LineGather(
        n, i, merge_rows, merge_w, merge_slab, merge_sem.at[0], merge_sem.at[1], merge_sem.at[2]
    )
    x_line = LineGather(n, i, rows, x_own, x_full, x_sem.at[0], x_sem.at[1], x_sem.at[2])
    cot_line = LineGather(
        n, i, rows, cot_own, cot_full, cot_sem.at[0], cot_sem.at[1], cot_sem.at[2]
    )
    x_line.start()
    noise_all[d] = noise[d]
    x_full[rows_of(i, rows), :] = x_own[...]
    for flip in range(1, n_dp):
        from_plane(noise_all, noise_sem, flip).wait_recv()
    pictures = noise.shape[1]
    images = noise_all[...].reshape(n_dp * pictures, k_rows).astype(low)
    for c in range(own_cols // tile):
        terms[:, :, c * tile : (c + 1) * tile] = mm(
            images, mod_w[:, c * tile : (c + 1) * tile]
        ).reshape(n_dp, pictures, tile)
    for flip in range(1, n_dp):
        to_plane(terms, terms_all, terms_sem, flip).start()
    attend_g.start()
    terms_all[d] = terms[d]
    for flip in range(1, n_dp):
        from_plane(terms_all, terms_sem, flip).wait_recv()
    columns[i] = jnp.sum(terms_all[...], axis=0)

    def to_line(turn):
        t = lax.rem(i + turn, n)
        return pltpu.make_async_remote_copy(
            src_ref=columns.at[i],
            dst_ref=columns.at[i],
            send_sem=column_sem.at[0, t],
            recv_sem=column_sem.at[1, i],
            device_id=(d, t),
            device_id_type=MESH,
        )

    def from_line(turn):
        t = lax.rem(i + turn, n)
        return pltpu.make_async_remote_copy(
            src_ref=columns.at[t],
            dst_ref=columns.at[t],
            send_sem=column_sem.at[0, t],
            recv_sem=column_sem.at[1, t],
            device_id=(d, t),
            device_id_type=MESH,
        )

    for turn in range(1, n):
        to_line(turn).start()
    merge_line.start()
    x_line.step(1)
    for turn in range(1, n):
        from_line(turn).wait_recv()
    unit = math.gcd(width, own_cols)

    def fill(j, carry):
        image = image_at(sizes, j * rows)
        for number in range(6):
            for start in range(0, width, unit):
                at = number * width + start
                here = slice(at % own_cols, at % own_cols + unit)
                table[j, number : number + 1, start : start + unit] = sum(
                    columns[at // own_cols, k : k + 1, here] * jnp.where(image == k, 1.0, 0.0)
                    for k in range(pictures)
                )
        return carry

    lax.fori_loop(0, n, fill, 0)
    attend_g.relay()
    merge_line.step(1)
    for copy in copies[:2]:
        copy.wait()
    attend_g.close()
    up_g.start()
    keep_attend = pltpu.make_async_copy(attend, attend_full, out_sem.at[0])
    keep_merge = pltpu.make_async_copy(merge, merge_full, out_sem.at[1])
    keep_attend.start()
    keep_hidden = pltpu.make_async_copy(hidden, hidden_out, out_sem.at[2])
    keep_qkv = pltpu.make_async_copy(qkv, qkv_out, out_sem.at[3])

    def tiles(count):
        return [slice(c * tile, (c + 1) * tile) for c in range(count // tile)]

    def one_block(j):
        here = rows_of(j, rows)
        squares = jnp.zeros((rows, 1), f32)
        for at in tiles(width):
            v = x_full[here, at].astype(f32)
            squares += jnp.sum(v * v, axis=1, keepdims=True)
        root = lax.rsqrt(squares * (1.0 / width) + 1e-06)
        for at in tiles(width):
            v = x_full[here, at].astype(f32) * root
            hidden[here, at] = (v * (1.0 + table[j, 1:2, at]) + table[j, 0:1, at]).astype(low)
        wide = qkv.shape[1]
        step = math.gcd(wide, 512)
        for c in range(wide // step):
            at = slice(c * step, (c + 1) * step)
            qkv[here, at] = mm(hidden[here, :], attend[:, at]).astype(low)

    def visit(q, carry):
        s = (q + 1) // 2
        side = 1 - 2 * (q % 2)
        j = i + s * side

        @pl.when((q % 2 == 1) & (s + 1 < n))
        def _():
            x_line.step(s + 1)
            merge_line.step(s + 1)

        @pl.when(q == 2 * n - 5)
        def _():
            up_g.relay()
            merge_g.start()
            cot_line.start()

        @pl.when((j >= 0) & (j < n))
        def _():
            one_block(j)

        return carry

    lax.fori_loop(0, 2 * n - 1, visit, 0)

    keep_hidden.start()
    keep_qkv.start()

    area = min(256, n * rows)
    areas = n * rows // area
    owners = area // rows
    area_images = [image_at(sizes, b * area) for b in range(areas)]

    def to_owner(j):
        return pltpu.make_async_remote_copy(
            src_ref=attended.at[rows_of(j, rows), :],
            dst_ref=att_rows.at[:, pl.ds(pl.multiple_of(i * head_cols, head_cols), head_cols)],
            send_sem=att_sem.at[0, j],
            recv_sem=att_sem.at[1, i],
            device_id=(d, j),
            device_id_type=MESH,
        )

    def from_source(t):
        return pltpu.make_async_remote_copy(
            src_ref=attended.at[rows_of(t, rows), :],
            dst_ref=att_rows.at[:, pl.ds(pl.multiple_of(t * head_cols, head_cols), head_cols)],
            send_sem=att_sem.at[0, t],
            recv_sem=att_sem.at[1, t],
            device_id=(d, t),
            device_id_type=MESH,
        )

    def attend_area(turn, carry):
        here_at = lax.rem(i // owners + 1 + turn, areas)
        here = rows_of(here_at, area)
        image = image_at(sizes, here_at * area)
        for h in range(heads):
            first = h * 3 * HEAD_DIM
            q = qkv[here, first : first + HEAD_DIM]
            parts = []
            for b in range(areas):
                key = qkv[b * area : (b + 1) * area, first + HEAD_DIM : first + 2 * HEAD_DIM]
                parts.append(
                    mm_nt(key, q) * HEAD_DIM ** (-0.5)
                    + jnp.where(image == area_images[b], 0.0, MASKED)
                )
            highest = parts[0].max(axis=0, keepdims=True)
            for part in parts[1:]:
                highest = jnp.maximum(highest, part.max(axis=0, keepdims=True))
            parts = [jnp.exp(part - highest) for part in parts]
            totals = sum(jnp.sum(part, axis=0, keepdims=True) for part in parts)
            inverse = 1.0 / totals
            out = jnp.zeros((HEAD_DIM, area), f32)
            for b in range(areas):
                value = qkv[b * area : (b + 1) * area, first + 2 * HEAD_DIM : first + 3 * HEAD_DIM]
                out += mm_tn(value, (parts[b] * inverse).astype(low))
            attended[here, h * HEAD_DIM : (h + 1) * HEAD_DIM] = out.T.astype(low)
            lse[pl.ds(here_at * heads + h, 1), :] = highest + jnp.log(totals)
        for k in range(owners):
            j = here_at * owners + k

            @pl.when(j != i)
            def _():
                to_owner(j).start()

        @pl.when(turn == (areas - 1) // 2)
        def _():
            up_g.close()
            cot_line.step(1)

        @pl.when(turn == areas - 1)
        def _():
            merge_g.relay()
            down_g.start()

        return carry

    lax.fori_loop(0, areas, attend_area, 0)
    att_rows[:, pl.ds(pl.multiple_of(i * head_cols, head_cols), head_cols)] = attended[
        rows_of(i, rows), :
    ]
    if n > 2:
        cot_line.step(2)
    merge_g.close()
    keep_merge.start()
    for turn in range(1, n):
        from_source(lax.rem(i + turn, n)).wait_recv()
    squares = jnp.zeros((rows, 1), f32)
    for at in tiles(width):
        out = mm(att_rows[...], merge[:, at])
        attn_out[:, at] = out
        v = x_own[:, at].astype(f32) + table[i, 2:3, at] * out
        middle[:, at] = v
        squares += jnp.sum(v * v, axis=1, keepdims=True)
    root = lax.rsqrt(squares * (1.0 / width) + 1e-06)
    for at in tiles(width):
        v = middle[:, at] * root
        hidden_second[:, at] = (v * (1.0 + table[i, 4:5, at]) + table[i, 3:4, at]).astype(low)
    keeps = [
        pltpu.make_async_copy(source, target, out_sem.at[4 + k])
        for k, (source, target) in enumerate(
            (
                (att_rows, rows_out),
                (attn_out, attn_out_hbm),
                (middle, middle_out),
                (hidden_second, second_out),
            )
        )
    ]
    for keep in keeps:
        keep.start()
    down_g.relay()
    for s in range(3, n):
        cot_line.step(s)
    down_g.close()
    for copy in copies[2:]:
        copy.wait()
    keep_attend.wait()
    keep_merge.wait()
    keep_hidden.wait()
    keep_qkv.wait()
    for keep in keeps:
        keep.wait()
    for flip in range(1, n_dp):
        to_plane(noise, noise_all, noise_sem, flip).wait_send()
        to_plane(terms, terms_all, terms_sem, flip).wait_send()
    for line in (merge_line, x_line, cot_line):
        line.finish()
    for turn in range(1, n):
        to_line(turn).wait_send()
    for turn in range(1, n):
        to_owner(lax.rem(i + turn, n)).wait_send()
    for weight in weights:
        weight.finish()


def front(n, n_dp, x, cot, noise, mod_w, sizes, attend_w, merge_w, up_w, down_w, number):
    rows, width = x.shape
    k_rows, own_cols = mod_w.shape
    wide = attend_w.shape[1]
    heads = wide // (3 * HEAD_DIM)
    total = n * rows
    areas = total // min(256, total)
    pictures = noise.shape[0]
    low, f32 = jnp.bfloat16, jnp.float32
    sds = jax.ShapeDtypeStruct
    count = plane_sems(n_dp)
    return call(
        functools.partial(front_kernel, n, n_dp, heads, 512),
        number,
        "front",
        [VMEM, HBM, VMEM, VMEM, pl.BlockSpec(memory_space=pltpu.SMEM), VMEM, VMEM, HBM, HBM],
        [
            sds((total, width), low),
            sds((total, width), low),
            sds((total, wide), low),
            sds((areas * heads, total // areas), f32),
            sds((rows, width), low),
            sds((rows, width), f32),
            sds((rows, width), f32),
            sds((rows, width), low),
            sds((n, 8, width), f32),
            sds((n_dp * k_rows, wide), low),
            sds((n * merge_w.shape[0], n_dp * merge_w.shape[1]), low),
            sds((n_dp * k_rows, up_w.shape[1]), low),
            sds((down_w.shape[0], n_dp * down_w.shape[1]), low),
            sds((n_dp, pictures, k_rows), f32),
        ],
        [HBM] * 3 + [VMEM] + [HBM] * 4 + [VMEM] + [HBM] * 4 + [VMEM],
        [
            pltpu.VMEM((total, width), low),
            pltpu.VMEM((n_dp * k_rows, wide), low),
            pltpu.VMEM((n * merge_w.shape[0], n_dp * merge_w.shape[1]), low),
            pltpu.VMEM((n_dp, pictures, k_rows), f32),
            pltpu.VMEM((total, width), low),
            pltpu.VMEM((total, wide), low),
            pltpu.VMEM((total, heads * HEAD_DIM), low),
            pltpu.VMEM((rows, width), low),
            pltpu.VMEM((rows, width), f32),
            pltpu.VMEM((rows, width), f32),
            pltpu.VMEM((rows, width), low),
            pltpu.VMEM((n_dp, pictures, own_cols), f32),
            pltpu.VMEM((n_dp, pictures, own_cols), f32),
            pltpu.VMEM((n, pictures, own_cols), f32),
            DMA((2, n_dp)),
            DMA((2, n_dp)),
            DMA((3, n)),
            DMA((3, n)),
            DMA((3, n)),
            DMA((3, n)),
            DMA((4, count)),
            DMA((4, count)),
            DMA((8,)),
            DMA((2, n)),
            DMA((5,)),
        ],
        flops=2 * total * width * wide,
    )(x, cot, noise, mod_w, sizes, attend_w, merge_w, up_w, down_w)


class PlaneScatter:
    def __init__(self, n_dp, d, theirs, own, swapped, via, landed, sems):
        self.chips, self.d, self.square = n_dp // 2, d, n_dp == 8
        self.chip, self.side = d // 2, lax.rem(d, 2)
        self.theirs, self.own, self.swapped, self.via = theirs, own, swapped, via
        self.landed, self.sems = landed, sems

    def remote(self, source, target, sent, came, device):
        return pltpu.make_async_remote_copy(
            src_ref=source,
            dst_ref=target,
            send_sem=sent,
            recv_sem=came,
            device_id=(device, lax.axis_index("tensor")),
            device_id_type=MESH,
        )

    def swap(self, m):
        return self.remote(
            self.theirs(m), self.swapped.at[m], self.sems.at[0, m], self.sems.at[1, m], self.d ^ 1
        )

    def half(self, ref, which):
        height = self.own.shape[1] // 2
        return ref.at[pl.ds(which * height, height), :]

    def step(self, k):
        slab, which, peer = ((1, 0, 1), (3, 0, 1), (2, 1, 2), (3, 1, 2), (2, 0, 2), (1, 1, 1))[k]
        target = self.via if slab == 3 else self.landed.at[1 if k < 4 else 2]
        return self.remote(
            self.half(self.own.at[self.chip ^ slab], which),
            self.half(target, which),
            self.sems.at[2, k],
            self.sems.at[3, k],
            2 * (self.chip ^ peer) + self.side,
        )

    def send(self, m, slot, sem):
        return self.remote(
            self.own.at[m],
            self.landed.at[slot],
            self.sems.at[2, m],
            self.sems.at[3, sem],
            2 * m + self.side,
        )

    def keep(self):
        slot = 0 if self.square else self.chip
        return pltpu.make_async_copy(
            self.own.at[self.chip], self.landed.at[slot], self.sems.at[2, 6 if self.square else self.chip]
        )

    def swap_all(self):
        def one(m, carry):
            self.swap(m).start()
            return carry

        lax.fori_loop(0, self.chips, one, 0)

    def add(self, target, source):
        height, wide = target.shape
        chunk = math.gcd(height, 64 if wide > 512 else 256)

        def one(c, carry):
            at = pl.ds(pl.multiple_of(c * chunk, chunk), chunk)
            total = target[at, :].astype(jnp.float32) + source[at, :].astype(jnp.float32)
            target[at, :] = total.astype(target.dtype)
            return carry

        lax.fori_loop(0, height // chunk, one, 0)

    def add_and_send(self):
        def one(k, carry):
            m = self.chip ^ (self.chips - 1 - k)
            self.swap(m).wait_recv()
            self.add(self.own.at[m], self.swapped.at[m])
            if not self.square:

                @pl.when(m != self.chip)
                def _():
                    self.send(m, self.chip, self.chip).start()

            return carry

        lax.fori_loop(0, self.chips, one, 0)
        if self.square:
            for k in (1, 3, 0, 2):
                self.step(k).start()
        self.keep().start()

    def relay(self):
        if self.square:
            for k, slab, which in ((1, 2, 0), (3, 1, 1)):
                self.step(k).wait_recv()
                self.step(k).wait_send()
                self.add(self.half(self.own.at[self.chip ^ slab], which), self.half(self.via, which))
                self.step(4 if k == 1 else 5).start()

    def landed_all(self):
        if self.square:
            for k in (0, 2, 4, 5):
                self.step(k).wait_recv()
        else:
            for k in range(1, self.chips):
                self.send(self.chip ^ k, self.chip ^ k, self.chip ^ k).wait_recv()
        self.keep().wait()

    def finish(self):
        for m in range(self.chips):
            self.swap(m).wait_send()
        if self.square:
            for k in (0, 2, 4, 5):
                self.step(k).wait_send()
        else:
            for k in range(1, self.chips):
                self.send(self.chip ^ k, self.chip, self.chip).wait_send()


def plane_slots(n_dp):
    return 3 if n_dp == 8 else n_dp // 2


def scatter_sems(n_dp):
    return DMA((4, max(7, n_dp // 2)))


def flows(n, pieces, sums, turn):
    far, rest = turn // ((n - 2) * pieces), lax.rem(turn, (n - 2) * pieces)
    t, c = n - 1 - rest // pieces, lax.rem(rest, pieces)
    for near in (True, False):

        @pl.when(far == (0 if near else 1))
        def _():
            sums.pass_on(t, c, near)


def back_kernel(
    n,
    n_dp,
    heads,
    tile,
    d_hidden,
    middle,
    table,
    lse,
    sizes,
    cot_hbm,
    out_hbm,
    rows_hbm,
    qkv_hbm,
    mlp_hbm,
    merge_hbm,
    up_hbm,
    down_hbm,
    block_out,
    d_middle_out,
    d_qkv_out,
    sums_out,
    merge_grad,
    up_landed,
    down_landed,
    cot,
    attn_out,
    d_middle,
    d_qkv,
    att_rows,
    qkv,
    part,
    got,
    merge,
    d_att,
    d_send,
    d_attn,
    d_keys,
    d_values,
    up_own,
    up_swapped,
    up_via,
    down_own,
    down_swapped,
    down_via,
    stage,
    mlp_sent,
    mlp_came,
    up_sems,
    down_sems,
    att_sem,
    merge_sem,
    load_sem,
    stage_sem,
    own_sem,
):
    d, i = lax.axis_index("dp"), lax.axis_index("tensor")
    rows, width = middle.shape
    low, f32 = jnp.bfloat16, jnp.float32
    head_cols = heads * HEAD_DIM
    chips = n_dp // 2
    k_rows, down_cols = up_own.shape[1], down_own.shape[2]
    side = lax.rem(d, 2)

    def up_slab(at):
        return up_hbm.at[pl.ds(pl.multiple_of(at * k_rows, k_rows), k_rows), :]

    def down_slab(at):
        return down_hbm.at[:, pl.ds(pl.multiple_of(at * down_cols, down_cols), down_cols)]

    load_mlp = pltpu.make_async_copy(mlp_hbm, part, load_sem.at[0])
    load_mlp.start()
    load_cot = pltpu.make_async_copy(cot_hbm, cot, load_sem.at[3])
    load_out = pltpu.make_async_copy(out_hbm, attn_out, load_sem.at[4])
    load_cot.start()
    load_out.start()
    load_rows = pltpu.make_async_copy(rows_hbm, att_rows, load_sem.at[1])
    load_qkv = pltpu.make_async_copy(qkv_hbm, qkv, load_sem.at[2])

    some = merge.shape[1]
    shares = head_cols // some

    def load_merge(k, slot):
        return pltpu.make_async_copy(
            merge_hbm.at[pl.ds(pl.multiple_of(k * some, some), some), :],
            merge.at[slot],
            merge_sem.at[slot],
        )

    load_merge(0, 0).start()
    for m in range(chips):
        pltpu.make_async_copy(up_slab(2 * m + side), up_own.at[m], own_sem.at[0, m]).start()
        pltpu.make_async_copy(down_slab(2 * m + side), down_own.at[m], own_sem.at[1, m]).start()
    load_rows.start()
    load_qkv.start()
    greet_all(n, n_dp, d, i)
    up = PlaneScatter(
        n_dp, d, lambda m: up_slab(2 * m + 1 - side), up_own, up_swapped, up_via, up_landed, up_sems
    )
    down = PlaneScatter(
        n_dp,
        d,
        lambda m: down_slab(2 * m + 1 - side),
        down_own,
        down_swapped,
        down_via,
        down_landed,
        down_sems,
    )
    up.swap_all()
    down.swap_all()
    load_mlp.wait()
    piece = tile // 2
    sums = LineScatter(n, i, rows, piece, part, got, mlp_sent, mlp_came)
    pieces = sums.pieces

    def ends(k, carry):
        t, c = n - 1 - k // pieces, lax.rem(k, pieces)
        pl.when(i == 0)(functools.partial(sums.at_end, t, c))
        pl.when(i == n - 1)(functools.partial(sums.at_end, n - 1 - t, c))
        return carry

    lax.fori_loop(0, min(n - 1, 1) * pieces, ends, 0)

    tiles = [slice(c * tile, (c + 1) * tile) for c in range(width // tile)]
    squares = jnp.zeros((rows, 1), f32)
    for at in tiles:
        squares += jnp.sum(middle[:, at] * middle[:, at], axis=1, keepdims=True)
    root = lax.rsqrt(squares * (1.0 / width) + 1e-06)
    mean = jnp.zeros((rows, 1), f32)
    for at in tiles:
        v = middle[:, at] * root
        dh = d_hidden[:, at]
        mean += jnp.sum(dh * (1.0 + table[i, 4:5, at]) * v, axis=1, keepdims=True)
        sums_out[3:4, at] = jnp.sum(dh, axis=0, keepdims=True)
        sums_out[4:5, at] = jnp.sum(dh * v, axis=0, keepdims=True)
    mean = mean * (1.0 / width)
    load_cot.wait()
    load_out.wait()
    for at in tiles:
        v = middle[:, at] * root
        u = d_hidden[:, at] * (1.0 + table[i, 4:5, at])
        dm = cot[:, at].astype(f32) + root * (u - v * mean)
        d_middle[:, at] = dm
        d_attn[:, at] = (table[i, 2:3, at] * dm).astype(low)
        sums_out[2:3, at] = jnp.sum(dm * attn_out[:, at], axis=0, keepdims=True)

    keep_middle = pltpu.make_async_copy(d_middle, d_middle_out, load_sem.at[5])
    keep_middle.start()

    def to_heads(t):
        return pltpu.make_async_remote_copy(
            src_ref=d_send.at[t],
            dst_ref=d_att.at[rows_of(i, rows), :],
            send_sem=att_sem.at[0, t],
            recv_sem=att_sem.at[1, i],
            device_id=(d, t),
            device_id_type=MESH,
        )

    def from_rows(t):
        return pltpu.make_async_remote_copy(
            src_ref=d_send.at[t],
            dst_ref=d_att.at[rows_of(t, rows), :],
            send_sem=att_sem.at[0, t],
            recv_sem=att_sem.at[1, t],
            device_id=(d, t),
            device_id_type=MESH,
        )

    def head_part(t, carry):
        for share in range(shares):
            k = t * shares + share
            slot = lax.rem(k, 2)

            @pl.when(k + 1 < n * shares)
            def _():
                load_merge(k + 1, 1 - slot).start()

            load_merge(k, slot).wait()
            d_send[t, :, share * some : (share + 1) * some] = mm_nt(
                d_attn[...], merge[slot]
            ).astype(low)

        @pl.when(t != i)
        def _():
            to_heads(t).start()

        return carry

    lax.fori_loop(0, n, head_part, 0)
    lax.fori_loop(min(n - 1, 1) * pieces, (n - 1) * pieces, ends, 0)
    d_att[rows_of(i, rows), :] = d_send[i]
    for m in range(chips):
        pltpu.make_async_copy(up_slab(2 * m + side), up_own.at[m], own_sem.at[0, m]).wait()
        pltpu.make_async_copy(down_slab(2 * m + side), down_own.at[m], own_sem.at[1, m]).wait()
    up.add_and_send()

    load_rows.wait()
    load_qkv.wait()
    wide = width // tile
    short = stage.shape[1]

    def square(row, column):
        return merge_grad.at[
            pl.ds(pl.multiple_of(row * short, short), short),
            pl.ds(pl.multiple_of(column * tile, tile), tile),
        ]

    def merge_one(k, carry):
        row, column = k // wide, lax.rem(k, wide)
        slot = lax.rem(k, 2)

        @pl.when(k >= 2)
        def _():
            pltpu.make_async_copy(stage.at[slot], square(0, 0), stage_sem.at[slot]).wait()

        a = att_rows[:, pl.ds(pl.multiple_of(row * short, short), short)]
        b = d_attn[:, pl.ds(pl.multiple_of(column * tile, tile), tile)]
        stage[slot] = mm_tn(a, b).astype(low)
        pltpu.make_async_copy(stage.at[slot], square(row, column), stage_sem.at[slot]).start()
        return carry

    lax.fori_loop(0, width // short * wide, merge_one, 0)
    for slot in range(2):
        pltpu.make_async_copy(stage.at[slot], square(0, 0), stage_sem.at[slot]).wait()
    down.add_and_send()
    for turn in range(1, n):
        from_rows(lax.rem(i + turn, n)).wait_recv()

    area = lse.shape[1]
    areas = n * rows // area
    area_images = [image_at(sizes, b * area) for b in range(areas)]
    d_keys[...] = jnp.zeros_like(d_keys)
    d_values[...] = jnp.zeros_like(d_values)
    turns = 2 * max(n - 2, 0) * pieces
    scale = HEAD_DIM ** (-0.5)

    def back_area(here_at, carry):
        here = rows_of(here_at, area)
        image = image_at(sizes, here_at * area)
        for h in range(heads):
            first = h * 3 * HEAD_DIM
            head = slice(h * HEAD_DIM, (h + 1) * HEAD_DIM)
            q = qkv[here, first : first + HEAD_DIM]
            g = d_att[here, head]
            log_row = lse[pl.ds(here_at * heads + h, 1), :]
            probs, d_probs = [], []
            inner = jnp.zeros((1, area), f32)
            for b in range(areas):
                key = qkv[b * area : (b + 1) * area, first + HEAD_DIM : first + 2 * HEAD_DIM]
                value = qkv[b * area : (b + 1) * area, first + 2 * HEAD_DIM : first + 3 * HEAD_DIM]
                scores = mm_nt(key, q) * scale + jnp.where(image == area_images[b], 0.0, MASKED)
                probs.append(jnp.exp(scores - log_row))
                d_probs.append(mm_nt(value, g))
                inner += jnp.sum(probs[b] * d_probs[b], axis=0, keepdims=True)
            d_query = jnp.zeros((HEAD_DIM, area), f32)
            for b in range(areas):
                at = slice(b * area, (b + 1) * area)
                key = qkv[at, first + HEAD_DIM : first + 2 * HEAD_DIM]
                d_scores = (probs[b] * (d_probs[b] - inner)).astype(low)
                d_values[at, head] += mm(probs[b].astype(low), g)
                d_keys[at, head] += mm(d_scores, q)
                d_query += mm_tn(key, d_scores)
            d_qkv[here, first : first + HEAD_DIM] = (d_query * scale).T.astype(low)

        @pl.when(here_at == areas - 1)
        def _():
            up.relay()

        return carry

    def pass_by(turn, carry):
        flows(n, pieces, sums, turn)
        return carry

    early = min(turns, pieces)
    lax.fori_loop(0, early, pass_by, 0)
    lax.fori_loop(0, areas, back_area, 0)
    for h in range(heads):
        first = h * 3 * HEAD_DIM
        head = slice(h * HEAD_DIM, (h + 1) * HEAD_DIM)
        d_qkv[:, first + HEAD_DIM : first + 2 * HEAD_DIM] = (d_keys[:, head] * scale).astype(low)
        d_qkv[:, first + 2 * HEAD_DIM : first + 3 * HEAD_DIM] = d_values[:, head].astype(low)
    keep_qkv = pltpu.make_async_copy(d_qkv, d_qkv_out, load_sem.at[6])
    keep_qkv.start()
    lax.fori_loop(early, turns, pass_by, 0)
    for c in range(pieces):
        at = slice(c * piece, (c + 1) * piece)
        total = sums.own_value(c)
        block_out[:, at] = (middle[:, at] + table[i, 5:6, at] * total).astype(low)
        sums_out[5:6, at] = jnp.sum(cot[:, at].astype(f32) * total, axis=0, keepdims=True)
    sums_out[0:2, :] = jnp.zeros((2, width), f32)
    sums_out[6:8, :] = jnp.zeros((2, width), f32)
    down.relay()
    keep_middle.wait()
    keep_qkv.wait()
    for scatter in (up, down):
        scatter.landed_all()
        scatter.finish()
    for turn in range(1, n):
        to_heads(lax.rem(i + turn, n)).wait_send()
    sums.all_sent()


def back(n, n_dp, operands, shapes, number, tile=512):
    (rows, width), wide, units, k_rows, down_cols, areas = shapes
    heads = wide // (3 * HEAD_DIM)
    total, chips, pieces = n * rows, n_dp // 2, 2 * width // tile
    low, f32 = jnp.bfloat16, jnp.float32
    sds = jax.ShapeDtypeStruct
    return call(
        functools.partial(back_kernel, n, n_dp, heads, tile),
        number,
        "back",
        [VMEM] * 4 + [pl.BlockSpec(memory_space=pltpu.SMEM)] + [HBM] * 8,
        [
            sds((rows, width), low),
            sds((rows, width), f32),
            sds((total, wide), low),
            sds((8, width), f32),
            sds((width, width), low),
            sds((plane_slots(n_dp), k_rows, units), low),
            sds((plane_slots(n_dp), units, down_cols), low),
        ],
        [VMEM, HBM, HBM, VMEM] + [HBM] * 3,
        [
            pltpu.VMEM((rows, width), low),
            pltpu.VMEM((rows, width), f32),
            pltpu.VMEM((rows, width), f32),
            pltpu.VMEM((total, wide), low),
            pltpu.VMEM((rows, width), low),
            pltpu.VMEM((total, wide), low),
            pltpu.VMEM((total, width), low),
            pltpu.VMEM((total + rows, width), low),
            pltpu.VMEM((2, math.gcd(256, heads * HEAD_DIM), width), low),
            pltpu.VMEM((total, heads * HEAD_DIM), low),
            pltpu.VMEM((n, rows, heads * HEAD_DIM), low),
            pltpu.VMEM((rows, width), low),
            pltpu.VMEM((total, heads * HEAD_DIM), f32),
            pltpu.VMEM((total, heads * HEAD_DIM), f32),
            pltpu.VMEM((chips, k_rows, units), low),
            pltpu.VMEM((chips, k_rows, units), low),
            pltpu.VMEM((k_rows, units), low),
            pltpu.VMEM((chips, units, down_cols), low),
            pltpu.VMEM((chips, units, down_cols), low),
            pltpu.VMEM((units, down_cols), low),
            pltpu.VMEM((2, tile // 2, tile), low),
            DMA((n, pieces)),
            DMA((n + 1, pieces)),
            scatter_sems(n_dp),
            scatter_sems(n_dp),
            DMA((2, n)),
            DMA((2,)),
            DMA((7,)),
            DMA((2,)),
            DMA((2, chips)),
        ],
        flops=20 * total * total * wide // 3,
    )(*operands)


def last_kernel(
    n,
    n_dp,
    tile,
    d_qkv,
    sums_in,
    table,
    sizes,
    hidden_hbm,
    x_hbm,
    middle_hbm,
    mod_hbm,
    merge_hbm,
    attend_hbm,
    input_grad,
    d_mod_all,
    noise_sum,
    attend_landed,
    merge_out,
    hidden,
    x_own,
    d_middle,
    mod_w,
    attend,
    part,
    got,
    grad_own,
    grad_theirs,
    grad_swapped,
    grad_via,
    merge_own,
    merge_swapped,
    merge_via,
    merge_landed,
    merge_part,
    merge_got,
    sums_all,
    shares,
    shares_all,
    terms,
    terms_all,
    noise_parts,
    sent,
    came,
    merge_sent,
    merge_came,
    grad_sems,
    merge_sems,
    share_sem,
    mod_sem,
    term_sem,
    noise_sem,
    load_sem,
    own_sem,
    attend_sem,
):
    d, i = lax.axis_index("dp"), lax.axis_index("tensor")
    rows, width = input_grad.shape
    low, f32 = jnp.bfloat16, jnp.float32
    chips = n_dp // 2
    side = lax.rem(d, 2)
    k_rows, own_cols = mod_w.shape
    merge_cols = merge_own.shape[2]
    merge_rows = merge_out.shape[0]
    images = d_mod_all.shape[1]

    def merge_slab(at):
        return merge_hbm.at[:, pl.ds(pl.multiple_of(at * merge_cols, merge_cols), merge_cols)]

    load_hidden, load_x, load_middle, load_mod = (
        pltpu.make_async_copy(source, target, load_sem.at[k])
        for k, (source, target) in enumerate(
            (
                (hidden_hbm, hidden),
                (x_hbm, x_own),
                (middle_hbm, d_middle),
                (mod_hbm, mod_w),
            )
        )
    )

    def load_attend(c):
        at = pl.ds(pl.multiple_of(c * tile, tile), tile)
        return pltpu.make_async_copy(attend_hbm.at[at, :], attend.at[at, :], attend_sem.at[c])

    for c in range(width // tile):
        load_attend(c).start()
    for m in range(chips):
        pltpu.make_async_copy(merge_slab(2 * m + side), merge_own.at[m], own_sem.at[m]).start()
    greet_all(n, n_dp, d, i)
    merge = PlaneScatter(
        n_dp,
        d,
        lambda m: merge_slab(2 * m + 1 - side),
        merge_own,
        merge_swapped,
        merge_via,
        merge_landed,
        merge_sems,
    )
    grad = PlaneScatter(
        n_dp, d, lambda m: grad_theirs.at[m], grad_own, grad_swapped, grad_via, attend_landed, grad_sems
    )
    merge.swap_all()
    for late in (load_hidden, load_x, load_middle, load_mod):
        late.start()
    piece = tile // 2
    sums = LineScatter(n, i, rows, piece, part, got, sent, came)
    pieces = sums.pieces

    def partial_block(q, carry):
        j = jnp.where(2 * i < n - 1, n - 1 - q, q)
        here = rows_of(j, rows)

        def one(c, inner):
            at = pl.ds(pl.multiple_of(c * tile, tile), tile)

            @pl.when(q == 0)
            def _():
                load_attend(c).wait()

            part[here, at] = mm_nt(d_qkv[here, :], attend[at, :]).astype(low)
            for k in range(tile // piece):
                sums.at_end(j, c * (tile // piece) + k)
            return inner

        lax.fori_loop(0, width // tile, one, 0)
        return carry

    partial_block(0, 0)
    for m in range(chips):
        pltpu.make_async_copy(merge_slab(2 * m + side), merge_own.at[m], own_sem.at[m]).wait()
    merge.add_and_send()
    lax.fori_loop(1, n, partial_block, 0)

    def slab_grad(at):
        columns = pl.ds(pl.multiple_of(at * k_rows, k_rows), k_rows)
        return mm_tn(hidden[:, columns], d_qkv[...]).astype(low)

    def for_them(m, carry):
        grad_theirs[m] = slab_grad(2 * m + 1 - side)
        grad.swap(m).start()
        return carry

    def for_us(m, carry):
        grad_own[m] = slab_grad(2 * m + side)
        return carry

    load_hidden.wait()
    lax.fori_loop(0, chips, for_them, 0)
    lax.fori_loop(0, chips, for_us, 0)
    grad.add_and_send()
    merge.relay()
    turns = 2 * max(n - 2, 0) * pieces

    def pass_by(turn, carry):
        flows(n, pieces, sums, turn)
        return carry

    lax.fori_loop(0, turns, pass_by, 0)

    grad.relay()

    for late in (load_x, load_middle, load_mod):
        late.wait()
    tiles = [slice(c * piece, (c + 1) * piece) for c in range(pieces)]
    squares = jnp.zeros((rows, 1), f32)
    for at in tiles:
        v = x_own[:, at].astype(f32)
        squares += jnp.sum(v * v, axis=1, keepdims=True)
    root = lax.rsqrt(squares * (1.0 / width) + 1e-06)
    mean = jnp.zeros((rows, 1), f32)
    sums_all[...] = sums_in[...]
    for c, at in enumerate(tiles):
        v = x_own[:, at].astype(f32) * root
        dh = sums.own_value(c)
        mean += jnp.sum(dh * (1.0 + table[i, 1:2, at]) * v, axis=1, keepdims=True)
        sums_all[0:1, at] = jnp.sum(dh, axis=0, keepdims=True)
        sums_all[1:2, at] = jnp.sum(dh * v, axis=0, keepdims=True)

    unit = math.gcd(width, own_cols)
    image = image_at(sizes, i * rows)
    for number in range(6):
        for start in range(0, width, unit):
            at = number * width + start
            for k in range(images):
                shares[at // own_cols, k : k + 1, at % own_cols : at % own_cols + unit] = (
                    sums_all[number : number + 1, start : start + unit]
                    * jnp.where(image == k, 1.0, 0.0)
                )

    def to_line(source, target, sems, turn, whole=False):
        t = lax.rem(i + turn, n)
        return pltpu.make_async_remote_copy(
            src_ref=source if whole else source.at[t],
            dst_ref=target.at[i],
            send_sem=sems.at[0, t],
            recv_sem=sems.at[1, i],
            device_id=(d, t),
            device_id_type=MESH,
        )

    def from_line(source, target, sems, turn, whole=False):
        t = lax.rem(i + turn, n)
        return pltpu.make_async_remote_copy(
            src_ref=source if whole else source.at[t],
            dst_ref=target.at[t],
            send_sem=sems.at[0, t],
            recv_sem=sems.at[1, t],
            device_id=(d, t),
            device_id_type=MESH,
        )

    def to_plane(source, target, sems, flip):
        return pltpu.make_async_remote_copy(
            src_ref=source,
            dst_ref=target.at[d],
            send_sem=sems.at[0, flip],
            recv_sem=sems.at[1, flip],
            device_id=(d ^ flip, i),
            device_id_type=MESH,
        )

    def from_plane(source, target, sems, flip):
        return pltpu.make_async_remote_copy(
            src_ref=source,
            dst_ref=target.at[d ^ flip],
            send_sem=sems.at[0, flip],
            recv_sem=sems.at[1, flip],
            device_id=(d ^ flip, i),
            device_id_type=MESH,
        )

    for turn in range(1, n):
        to_line(shares, shares_all, share_sem, turn).start()

    merge.landed_all()
    merge_sums = LineScatter(
        n, i, merge_rows, merge_cols, merge_part, merge_got, merge_sent, merge_came
    )

    def merge_block(q, carry):
        j = jnp.where(2 * i < n - 1, n - 1 - q, q)
        here = rows_of(j, merge_rows)
        total = merge_landed[0, here, :].astype(f32)
        for m in range(1, merge_landed.shape[0]):
            total += merge_landed[m, here, :].astype(f32)
        merge_part[here, :] = total.astype(low)
        merge_sums.at_end(j, 0)
        return carry

    lax.fori_loop(0, n, merge_block, 0)

    mean = mean * (1.0 / width)
    for c, at in enumerate(tiles):
        v = x_own[:, at].astype(f32) * root
        u = sums.own_total(c) * (1.0 + table[i, 1:2, at])
        input_grad[:, at] = (d_middle[:, at] + root * (u - v * mean)).astype(low)
    shares_all[i] = shares[i]
    for turn in range(1, n):
        from_line(shares, shares_all, share_sem, turn).wait_recv()
    d_mod_all[d] = jnp.sum(shares_all[...], axis=0).astype(low).astype(f32)
    own_mod = d_mod_all.at[d]
    for flip in range(1, n_dp):
        to_plane(own_mod, d_mod_all, mod_sem, flip).start()
    for t in range(n - 1, 1, -1):
        for near in (True, False):
            merge_sums.pass_on(t, 0, near)
    for flip in range(1, n_dp):
        from_plane(own_mod, d_mod_all, mod_sem, flip).wait_recv()
    flat = d_mod_all[...].reshape(n_dp * images, own_cols).astype(low)
    terms[...] = mm_nt(flat, mod_w[...]).reshape(n_dp, images, k_rows)
    for turn in range(1, n):
        to_line(terms, terms_all, term_sem, turn, True).start()
    terms_all[i] = terms[...]
    for turn in range(1, n):
        from_line(terms, terms_all, term_sem, turn, True).wait_recv()
    noise_parts[...] = jnp.sum(terms_all[...], axis=0)
    for flip in range(1, n_dp):
        to_plane(noise_parts.at[d ^ flip], noise_sum, noise_sem, flip).start()
    noise_sum[d] = noise_parts[d]
    merge_out[...] = merge_sums.own_value(0)
    for flip in range(1, n_dp):
        from_plane(noise_parts.at[d ^ flip], noise_sum, noise_sem, flip).wait_recv()
    grad.landed_all()
    grad.finish()
    merge.finish()
    for turn in range(1, n):
        to_line(shares, shares_all, share_sem, turn).wait_send()
        to_line(terms, terms_all, term_sem, turn, True).wait_send()
    for flip in range(1, n_dp):
        to_plane(own_mod, d_mod_all, mod_sem, flip).wait_send()
        to_plane(noise_parts.at[d ^ flip], noise_sum, noise_sem, flip).wait_send()
    sums.all_sent()
    merge_sums.all_sent()


def last(n, n_dp, operands, shapes, number, tile=512):
    (rows, width), wide, k_rows, own_cols, (merge_rows, merge_cols), images = shapes
    total, chips, pieces = n * rows, n_dp // 2, 2 * width // tile
    low, f32 = jnp.bfloat16, jnp.float32
    sds = jax.ShapeDtypeStruct
    return call(
        functools.partial(last_kernel, n, n_dp, tile),
        number,
        "last",
        [VMEM] * 3 + [pl.BlockSpec(memory_space=pltpu.SMEM)] + [HBM] * 6,
        [
            sds((rows, width), low),
            sds((n_dp, images, own_cols), f32),
            sds((n_dp, images, k_rows), f32),
            sds((plane_slots(n_dp), k_rows, wide), low),
            sds((merge_rows, merge_cols), f32),
        ],
        [VMEM] * 3 + [HBM] + [VMEM],
        [
            pltpu.VMEM((total, width), low),
            pltpu.VMEM((rows, width), low),
            pltpu.VMEM((rows, width), f32),
            pltpu.VMEM((k_rows, own_cols), low),
            pltpu.VMEM((width, wide), low),
            pltpu.VMEM((total, width), low),
            pltpu.VMEM((total + rows, width), low),
            pltpu.VMEM((chips, k_rows, wide), low),
            pltpu.VMEM((chips, k_rows, wide), low),
            pltpu.VMEM((chips, k_rows, wide), low),
            pltpu.VMEM((k_rows, wide), low),
            pltpu.VMEM((chips, n * merge_rows, merge_cols), low),
            pltpu.VMEM((chips, n * merge_rows, merge_cols), low),
            pltpu.VMEM((n * merge_rows, merge_cols), low),
            pltpu.VMEM((plane_slots(n_dp), n * merge_rows, merge_cols), low),
            pltpu.VMEM((n * merge_rows, merge_cols), low),
            pltpu.VMEM(((n + 1) * merge_rows, merge_cols), low),
            pltpu.VMEM((8, width), f32),
            pltpu.VMEM((n, images, own_cols), f32),
            pltpu.VMEM((n, images, own_cols), f32),
            pltpu.VMEM((n_dp, images, k_rows), f32),
            pltpu.VMEM((n, n_dp, images, k_rows), f32),
            pltpu.VMEM((n_dp, images, k_rows), f32),
            DMA((n, pieces)),
            DMA((n + 1, pieces)),
            DMA((n, 1)),
            DMA((n + 1, 1)),
            scatter_sems(n_dp),
            scatter_sems(n_dp),
            DMA((2, n)),
            DMA((2, n_dp)),
            DMA((2, n)),
            DMA((2, n_dp)),
            DMA((4,)),
            DMA((chips,)),
            DMA((width // tile,)),
        ],
        flops=4 * total * width * wide,
    )(*operands)


def final_kernel(
    noise_own,
    noise_all,
    d_mod,
    noise_sums,
    up_in,
    down_in,
    attend_in,
    block_in,
    input_in,
    merge_in,
    block_out,
    input_out,
    noise_grad,
    attend_out,
    merge_out,
    up_out,
    down_out,
    modulate_out,
    up_slots,
    down_slots,
    attend_slots,
    up_sum,
    down_sum,
    attend_sum,
    modulate,
    block,
    inputs,
    merge,
    sems,
):
    low, f32 = jnp.bfloat16, jnp.float32
    loads = [
        pltpu.make_async_copy(source, target, sems.at[0, k])
        for k, (source, target) in enumerate(
            (
                (up_in, up_slots),
                (down_in, down_slots),
                (attend_in, attend_slots),
                (block_in, block),
                (input_in, inputs),
                (merge_in, merge),
            )
        )
    ]
    stores = [
        pltpu.make_async_copy(source, target, sems.at[1, k])
        for k, (source, target) in enumerate(
            (
                (up_sum, up_out),
                (down_sum, down_out),
                (attend_sum, attend_out),
                (block, block_out),
                (inputs, input_out),
                (merge, merge_out),
                (modulate, modulate_out),
            )
        )
    ]
    for load in loads:
        load.start()
    n_dp, images, k_rows = noise_all.shape
    left = noise_all[...].reshape(n_dp * images, k_rows).astype(low)
    right = d_mod[...].reshape(n_dp * images, -1).astype(low)
    modulate[...] = mm_tn(left, right)
    stores[6].start()
    for k in range(n_dp):
        at = slice(k * k_rows, (k + 1) * k_rows)
        v = noise_own[:, at].astype(f32)
        gate = 1.0 / (1.0 + jnp.exp(-v))
        noise_grad[:, at] = noise_sums[k] * (gate * (1.0 + v * (1.0 - gate)))

    def add(slots, total):
        count, height, wide = slots.shape
        chunk = math.gcd(height, 32 if wide > 512 else 256)

        def one(c, carry):
            at = pl.ds(pl.multiple_of(c * chunk, chunk), chunk)
            total[at, :] = sum(slots[s, at, :].astype(f32) for s in range(count))
            return carry

        lax.fori_loop(0, height // chunk, one, 0)

    for k, (slots, total) in enumerate(
        ((up_slots, up_sum), (down_slots, down_sum), (attend_slots, attend_sum))
    ):
        loads[k].wait()
        add(slots, total)
        stores[k].start()
    for k in range(3, 6):
        loads[k].wait()
        stores[k].start()
    for store in stores:
        store.wait()


def final(noise_own, noise_all, d_mod, noise_sums, up, down, attend, block, inputs, merge):
    sds, f32 = jax.ShapeDtypeStruct, jnp.float32
    own_cols, k_rows = d_mod.shape[2], noise_all.shape[2]
    sums = [sds(a.shape[1:], f32) for a in (up, down, attend)]
    modulate = sds((k_rows, own_cols), f32)
    return pl.pallas_call(
        final_kernel,
        out_shape=[
            sds(block.shape, block.dtype),
            sds(inputs.shape, inputs.dtype),
            sds(noise_own.shape, f32),
            sums[2],
            sds(merge.shape, f32),
            sums[0],
            sums[1],
            modulate,
        ],
        in_specs=[VMEM] * 4 + [HBM] * 6,
        out_specs=[HBM, HBM, VMEM] + [HBM] * 5,
        scratch_shapes=[
            pltpu.VMEM(a.shape, a.dtype)
            for a in (up, down, attend, *sums, modulate, block, inputs, merge)
        ]
        + [DMA((2, 7))],
        compiler_params=pltpu.CompilerParams(vmem_limit_bytes=60 * 1024 * 1024),
        name="final",
    )(noise_own, noise_all, d_mod, noise_sums, up, down, attend, block, inputs, merge)


def on_device(
    block_input,
    cotangent,
    noise_embed,
    image_sizes,
    attend_weight,
    merge_weight,
    up_weight,
    down_weight,
    modulate_weight,
):
    n = lax.axis_size("tensor")
    n_dp = lax.axis_size("dp")
    rows, width = block_input.shape
    tokens = n * rows
    images = image_sizes.shape[1]
    k_rows = modulate_weight.shape[0]

    (
        cot_full,
        hidden_first,
        packed,
        lse,
        att_rows,
        attn_out,
        middle,
        hidden_second,
        table,
        attend_full,
        merge_full,
        up_full,
        down_full,
        noise_all,
    ) = front(
        n,
        n_dp,
        block_input,
        cotangent,
        noise_embed,
        modulate_weight,
        image_sizes,
        attend_weight,
        merge_weight,
        up_weight,
        down_weight,
        0,
    )
    d_hidden_second, mlp_part, up_local, down_local = ffn(
        n, hidden_second, table, cot_full, up_full, down_full, 1
    )
    units = up_full.shape[1]
    wide = packed.shape[1]
    (
        block_output,
        d_middle,
        d_qkv,
        row_sums,
        merge_local,
        up_landed,
        down_landed,
    ) = back(
        n,
        n_dp,
        (
            d_hidden_second,
            middle,
            table,
            lse,
            image_sizes,
            cotangent,
            attn_out,
            att_rows,
            packed,
            mlp_part,
            merge_full,
            up_local,
            down_local,
        ),
        (block_input.shape, wide, units, k_rows, down_weight.shape[1], lse.shape[0]),
        2,
    )
    input_grad, d_mod_all, noise_sums, attend_landed, merge_part = last(
        n,
        n_dp,
        (
            d_qkv,
            row_sums,
            table,
            image_sizes,
            hidden_first,
            block_input,
            d_middle,
            modulate_weight,
            merge_local,
            attend_full,
        ),
        (
            block_input.shape,
            wide,
            k_rows,
            modulate_weight.shape[1],
            merge_weight.shape,
            images,
        ),
        3,
    )

    return tuple(
        final(
            noise_embed,
            noise_all,
            d_mod_all,
            noise_sums,
            up_landed,
            down_landed,
            attend_landed,
            block_output,
            input_grad,
            merge_part,
        )
    )


def solution(mesh):
    whole_rows = P(("dp", "tensor"), None)
    by_dp = P("dp", None)
    tall = P("dp", "tensor")
    wide = P("tensor", "dp")
    return jax.shard_map(
        on_device,
        mesh=mesh,
        in_specs=(whole_rows, whole_rows, by_dp, by_dp, tall, wide, tall, wide, tall),
        out_specs=(whole_rows, whole_rows, by_dp, tall, wide, tall, wide, tall),
        check_vma=False,
    )
```

```python
import functools
import math

import jax
import jax.numpy as jnp
from jax import lax
from jax.experimental import pallas as pl
from jax.experimental.pallas import tpu as pltpu
from jax.sharding import PartitionSpec as P

HEAD_DIM = 128
MASKED = -1e30


def dot(a, b, dims=(((1,), (0,)), ((), ()))):
    return lax.dot_general(a, b, dims, preferred_element_type=jnp.float32)


ROWS_ROWS = (((0,), (0,)), ((), ()))


MESH = pl.DeviceIdType.MESH
HBM = pl.BlockSpec(memory_space=pl.ANY)
VMEM = pl.BlockSpec(memory_space=pltpu.VMEM)
DMA = pltpu.SemaphoreType.DMA


def rows_of(j, rows):
    return pl.ds(pl.multiple_of(j * rows, rows), rows)


def beside(step):
    return (lax.axis_index("dp"), lax.axis_index("tensor") + step)


def greet_line(n, i):
    barrier = pltpu.get_barrier_semaphore()

    @pl.when(i > 0)
    def _():
        pl.semaphore_signal(barrier, inc=1, device_id=beside(-1), device_id_type=MESH)

    @pl.when(i < n - 1)
    def _():
        pl.semaphore_signal(barrier, inc=1, device_id=beside(1), device_id_type=MESH)

    pl.semaphore_wait(barrier, jnp.where(i > 0, 1, 0) + jnp.where(i < n - 1, 1, 0))


class LineGather:
    def __init__(self, n, i, rows, own, full, to_left, to_right, arrived):
        self.n, self.i, self.rows, self.own, self.full = n, i, rows, own, full
        self.to_left, self.to_right, self.arrived = to_left, to_right, arrived

    def copy(self, j, step, source=None):
        place = self.full.at[rows_of(j, self.rows)]
        return pltpu.make_async_remote_copy(
            src_ref=place if source is None else source,
            dst_ref=place,
            send_sem=(self.to_right if step > 0 else self.to_left).at[j],
            recv_sem=self.arrived.at[j],
            device_id=beside(step),
            device_id_type=MESH,
        )

    def start(self):
        @pl.when(self.i > 0)
        def _():
            self.copy(self.i, -1, self.own).start()

        @pl.when(self.i < self.n - 1)
        def _():
            self.copy(self.i, 1, self.own).start()

    def step(self, s):
        for side in (-1, 1):
            j = self.i + side * s
            there = (j >= 0) & (j < self.n)
            more = (self.i > 0) if side > 0 else (self.i < self.n - 1)

            @pl.when(there)
            def _():
                self.copy(j, side).wait_recv()

            @pl.when(there & more)
            def _():
                self.copy(j, -side).start()

    def finish(self):
        @pl.when(self.i > 0)
        def _():
            self.copy(self.i, -1, self.own).wait_send()

        @pl.when(self.i < self.n - 1)
        def _():
            self.copy(self.i, 1, self.own).wait_send()

        for j in range(self.n):

            @pl.when((j < self.i) & (self.i < self.n - 1))
            def _():
                self.copy(j, 1).wait_send()

            @pl.when((j > self.i) & (self.i > 0))
            def _():
                self.copy(j, -1).wait_send()


class LineScatter:
    def __init__(self, n, i, rows, width, part, got, sent, arrived):
        self.n, self.i, self.rows, self.width = n, i, rows, width
        self.part, self.got, self.sent, self.arrived = part, got, sent, arrived
        self.pieces = part.shape[1] // width

    def columns(self, c):
        if isinstance(c, int):
            return pl.ds(c * self.width, self.width)
        return pl.ds(pl.multiple_of(c * self.width, self.width), self.width)

    def copy(self, j, slot, c, step):
        return pltpu.make_async_remote_copy(
            src_ref=self.part.at[rows_of(j, self.rows), self.columns(c)],
            dst_ref=self.got.at[rows_of(slot, self.rows), self.columns(c)],
            send_sem=self.sent.at[j, c],
            recv_sem=self.arrived.at[slot, c],
            device_id=beside(step),
            device_id_type=MESH,
        )

    def slot_there(self, j, step):
        if step > 0:
            return j
        return jnp.where(j == self.i - 1, self.n, j)

    def at_end(self, j, c):
        @pl.when((self.i == 0) & (j > 0))
        def _():
            self.copy(j, j, c, 1).start()

        @pl.when((self.i == self.n - 1) & (j < self.i))
        def _():
            self.copy(j, self.slot_there(j, -1), c, -1).start()

    def pass_on(self, t, c, near):
        n, i = self.n, self.i
        rightward = (2 * i < n - 1) if near else (2 * i >= n - 1)
        j = jnp.where(rightward, t, n - 1 - t)
        step = jnp.where(rightward, 1, -1)
        right = rightward & (i > 0) & (j > i)
        left = jnp.logical_not(rightward) & (i < n - 1) & (j < i)

        @pl.when(right | left)
        def _():
            self.add(j, j, c)
            slot = jnp.where(left & (j == i - 1), n, j)
            self.copy(j, slot, c, step).start()

    def add(self, j, slot, c):
        self.copy(j, slot, c, 1).wait_recv()
        here = (rows_of(j, self.rows), self.columns(c))
        there = (rows_of(slot, self.rows), self.columns(c))
        total = self.part[here].astype(jnp.float32) + self.got[there].astype(jnp.float32)
        self.part[here] = total.astype(self.part.dtype)

    def own(self, c, out):
        i, n = self.i, self.n
        columns = self.columns(c)
        out[:, columns] = self.part[rows_of(i, self.rows), columns].astype(out.dtype)

        @pl.when(i > 0)
        def _():
            self.copy(i, i, c, 1).wait_recv()
            out[:, columns] += self.got[rows_of(i, self.rows), columns].astype(out.dtype)

        @pl.when(i < n - 1)
        def _():
            self.copy(i, n, c, -1).wait_recv()
            out[:, columns] += self.got[rows_of(n, self.rows), columns].astype(out.dtype)

    def own_value(self, c):
        i, n = self.i, self.n

        @pl.when(i > 0)
        def _():
            self.copy(i, i, c, 1).wait_recv()

        @pl.when(i < n - 1)
        def _():
            self.copy(i, n, c, -1).wait_recv()

        return self.own_total(c)

    def own_total(self, c):
        i, n, columns = self.i, self.n, self.columns(c)
        total = self.part[rows_of(i, self.rows), columns].astype(jnp.float32)
        left = self.got[rows_of(i, self.rows), columns].astype(jnp.float32)
        right = self.got[rows_of(n, self.rows), columns].astype(jnp.float32)
        return total + jnp.where(i > 0, left, 0.0) + jnp.where(i < n - 1, right, 0.0)

    def all_sent(self):
        def one(j, carry):
            @pl.when(j != self.i)
            def _():
                for c in range(self.pieces):
                    self.copy(j, 0, c, 1).wait_send()

            return carry

        lax.fori_loop(0, self.n, one, 0)


def mm(a, b):
    return lax.dot_general(a, b, (((1,), (0,)), ((), ())), preferred_element_type=jnp.float32)


def mm_nt(a, b):
    return lax.dot_general(a, b, (((1,), (1,)), ((), ())), preferred_element_type=jnp.float32)


def mm_tn(a, b):
    return lax.dot_general(a, b, (((0,), (0,)), ((), ())), preferred_element_type=jnp.float32)


def call(kernel, collective_id, name, in_specs, outs, out_specs, scratch, flops=0, limit=60):
    return pl.pallas_call(
        kernel,
        out_shape=outs,
        in_specs=in_specs,
        out_specs=out_specs,
        scratch_shapes=scratch,
        compiler_params=pltpu.CompilerParams(
            collective_id=collective_id,
            has_side_effects=True,
            vmem_limit_bytes=limit * 1024 * 1024,
        ),
        cost_estimate=pl.CostEstimate(flops=flops, bytes_accessed=1 << 20, transcendentals=0),
        name=name,
    )


def ffn_kernel(
    n,
    tile,
    grad_tile,
    own_hidden,
    table,
    d_mlp_hbm,
    up_hbm,
    down_hbm,
    d_hidden,
    mlp_part,
    up_grad,
    down_grad,
    up,
    down,
    d_mlp,
    hidden,
    activated,
    d_pre,
    part,
    got,
    stage,
    mlp,
    to_left,
    to_right,
    arrived,
    sent,
    came,
    local,
    stage_sem,
):
    i = lax.axis_index("tensor")
    rows, width = own_hidden.shape
    units = up.shape[1]
    loads = [
        pltpu.make_async_copy(source, target, local.at[k])
        for k, (source, target) in enumerate(((up_hbm, up), (d_mlp_hbm, d_mlp), (down_hbm, down)))
    ]
    for load in loads:
        load.start()
    greet_line(n, i)
    line = LineGather(n, i, rows, own_hidden, hidden, to_left, to_right, arrived)
    first_core = lax.rem(lax.axis_index("dp"), 2) == 0
    pl.when(first_core)(line.start)
    piece = tile // 2
    sums = LineScatter(n, i, rows, piece, part, got, sent, came)
    hidden[rows_of(i, rows), :] = own_hidden[...]
    for load in loads:
        load.wait()

    def one_block(j):
        here = rows_of(j, rows)

        def gated(c, carry):
            at = pl.ds(pl.multiple_of(c * tile, tile), tile)
            d_mlp[here, at] = (d_mlp[here, at].astype(jnp.float32) * table[j, 5:6, at]).astype(
                jnp.bfloat16
            )
            return carry

        lax.fori_loop(0, width // tile, gated, 0)

        def first(c, carry):
            at = pl.ds(pl.multiple_of(c * tile, tile), tile)
            pre = mm(hidden[here, :], up[:, at])
            d_act = mm_nt(d_mlp[here, :], down[at, :])
            cdf = 0.5 * (1.0 + lax.erf(pre * (0.5**0.5)))
            density = jnp.exp(-0.5 * pre * pre) * ((0.5 / math.pi) ** 0.5)
            activated[here, at] = (pre * cdf).astype(jnp.bfloat16)
            d_pre[here, at] = (d_act * (cdf + pre * density)).astype(jnp.bfloat16)
            return carry

        lax.fori_loop(0, units // tile, first, 0)

        def second(c, carry):
            at = pl.ds(pl.multiple_of(c * tile, tile), tile)
            part[here, at] = mm_nt(d_pre[here, :], up[at, :]).astype(jnp.bfloat16)
            for k in range(tile // piece):
                sums.at_end(j, c * (tile // piece) + k)
            return carry

        lax.fori_loop(0, width // tile, second, 0)

        def third(c, carry):
            at = pl.ds(pl.multiple_of(c * tile, tile), tile)
            mlp[here, at] = mm(activated[here, :], down[:, at]).astype(jnp.bfloat16)
            return carry

        lax.fori_loop(0, width // tile, third, 0)

    def visit(q, carry):
        s = (q + 1) // 2
        side = 1 - 2 * (q % 2)
        j = i + s * side

        @pl.when(q % 2 == 1)
        def _():
            line.step(s)

        @pl.when((j >= 0) & (j < n))
        def _():
            one_block(j)

        @pl.when((q == 0) & jnp.logical_not(first_core))
        def _():
            line.start()

        return carry

    lax.fori_loop(0, 2 * n - 1, visit, 0)
    keep_mlp = pltpu.make_async_copy(mlp, mlp_part, local.at[3])
    keep_mlp.start()

    count = (width // grad_tile) * (units // grad_tile)
    turns = 2 * max(n - 2, 1) * sums.pieces
    per_turn = -(-2 * count // turns)

    def square(ref, row, column):
        return ref.at[
            pl.ds(pl.multiple_of(row * grad_tile, grad_tile), grad_tile),
            pl.ds(pl.multiple_of(column * grad_tile, grad_tile), grad_tile),
        ]

    def put(slot, target):
        return pltpu.make_async_copy(stage.at[slot], target, stage_sem.at[slot])

    def one_grad(k, left, right, target):
        wide = right.shape[1] // grad_tile
        row, column = k // wide, k % wide
        slot = k % 2

        @pl.when(k >= 2)
        def _():
            put(slot, square(target, 0, 0)).wait()

        a = left[:, pl.ds(pl.multiple_of(row * grad_tile, grad_tile), grad_tile)]
        b = right[:, pl.ds(pl.multiple_of(column * grad_tile, grad_tile), grad_tile)]
        stage[slot] = mm_tn(a, b).astype(jnp.bfloat16)
        put(slot, square(target, row, column)).start()

    def tail(k, carry):
        t, c = 2 + k // (2 * sums.pieces), k % sums.pieces
        for near in (True, False):

            @pl.when((k // sums.pieces) % 2 == (0 if near else 1))
            def _():
                sums.pass_on(t, c, near)

        for extra in range(per_turn):
            item = k * per_turn + extra

            @pl.when(item < count)
            def _():
                one_grad(item, hidden, d_pre, up_grad)

            @pl.when(item == count)
            def _():
                for slot in range(2):
                    put(slot, square(up_grad, 0, 0)).wait()

            @pl.when((item >= count) & (item < 2 * count))
            def _():
                one_grad(item - count, activated, d_mlp, down_grad)

        return carry

    lax.fori_loop(0, turns, tail, 0)
    for slot in range(2):
        put(slot, square(down_grad, 0, 0)).wait()
    for c in range(sums.pieces):
        sums.own(c, d_hidden)
    line.finish()
    sums.all_sent()
    keep_mlp.wait()


def ffn(n, own_hidden, table, cotangents, up, down, collective_id, tile=512, grad_tile=512):
    rows, width = own_hidden.shape
    units = up.shape[1]
    pieces = 2 * width // tile
    low = jnp.bfloat16
    return call(
        functools.partial(ffn_kernel, n, tile, grad_tile),
        collective_id,
        "ffn",
        [VMEM, VMEM, HBM, HBM, HBM],
        [
            jax.ShapeDtypeStruct((rows, width), jnp.float32),
            jax.ShapeDtypeStruct((n * rows, width), low),
            jax.ShapeDtypeStruct((width, units), low),
            jax.ShapeDtypeStruct((units, width), low),
        ],
        [VMEM, HBM, HBM, HBM],
        [
            pltpu.VMEM((width, units), low),
            pltpu.VMEM((units, width), low),
            pltpu.VMEM((n * rows, width), low),
            pltpu.VMEM((n * rows, width), low),
            pltpu.VMEM((n * rows, units), low),
            pltpu.VMEM((n * rows, units), low),
            pltpu.VMEM((n * rows, width), low),
            pltpu.VMEM(((n + 1) * rows, width), low),
            pltpu.VMEM((2, grad_tile, grad_tile), low),
            pltpu.VMEM((n * rows, width), low),
            DMA((n,)),
            DMA((n,)),
            DMA((n,)),
            DMA((n, pieces)),
            DMA((n + 1, pieces)),
            DMA((4,)),
            DMA((2,)),
        ],
        flops=12 * n * rows * width * units,
    )(own_hidden, table, cotangents, up, down)


def image_at(sizes, place):
    end, count = 0, 0
    for k in range(sizes.shape[1]):
        end = end + sizes[0, k]
        count = count + jnp.where(place >= end, 1, 0)
    return count


def image_at(sizes, place):
    end, count = 0, 0
    for k in range(sizes.shape[1]):
        end = end + sizes[0, k]
        count = count + jnp.where(place >= end, 1, 0)
    return count


class PlaneGather:
    def __init__(self, n_dp, d, own, view, height, sent, came):
        self.n_dp, self.d, self.own, self.view, self.height = n_dp, d, own, view, height
        self.sent, self.came = sent, came
        self.square = n_dp == 8
        self.peers = [2 * k for k in range(1, n_dp // 2)]

    def copy(self, k, source, target, peer):
        return pltpu.make_async_remote_copy(
            src_ref=source,
            dst_ref=target,
            send_sem=self.sent.at[k],
            recv_sem=self.came.at[k],
            device_id=(self.d ^ peer, lax.axis_index("tensor")),
            device_id_type=MESH,
        )

    def slab(self, flip, half=None):
        if half is None:
            return self.view(self.d ^ flip, 0, self.height)
        return self.view(self.d ^ flip, half * (self.height // 2), self.height // 2)

    def owns(self):
        peers = [2, 4] if self.square else self.peers
        return [
            self.copy(k, self.own, self.slab(0), peer) for k, peer in enumerate([1] + peers)
        ]

    def relay_of(self, k):
        flip, half, peer = ((2, 0, 4), (4, 1, 2))[k - 1]
        return self.copy(2 + k, self.slab(flip, half), self.slab(flip, half), peer)

    def across(self):
        return [
            self.copy(3, self.slab(6, 0), self.slab(6, 0), 4),
            self.copy(4, self.slab(6, 1), self.slab(6, 1), 2),
        ]

    def hand(self, flip):
        base = 5 if self.square else len(self.peers) + 1
        k = base + flip // 2 - 1
        return self.copy(k, self.slab(flip), self.slab(flip), 1)

    def handed(self, flip):
        base = 5 if self.square else len(self.peers) + 1
        k = base + flip // 2 - 1
        return self.copy(k, self.slab(flip ^ 1), self.slab(flip ^ 1), 1)

    def start(self):
        for copy in self.owns():
            copy.start()

    def relay(self):
        if not self.square:
            return
        for k, flip in ((1, 2), (2, 4)):
            self.copy(k, self.own, self.slab(flip), flip).wait_recv()
            self.relay_of(k).start()
            self.hand(flip).start()

    def close(self):
        if self.square:
            for copy in self.across():
                copy.wait_recv()
            self.hand(6).start()
        else:
            for k, flip in enumerate(self.peers):
                self.copy(k + 1, self.own, self.slab(flip), flip).wait_recv()
                self.hand(flip).start()
        self.copy(0, self.own, self.slab(1), 1).wait_recv()
        for flip in self.peers:
            self.handed(flip).wait_recv()

    def finish(self):
        for copy in self.owns():
            copy.wait_send()
        if self.square:
            for k in (1, 2):
                self.relay_of(k).wait_send()
        for flip in self.peers:
            self.hand(flip).wait_send()


def plane_sems(n_dp):
    return 8 if n_dp == 8 else n_dp - 1


def greet_all(n, n_dp, d, i):
    barrier = pltpu.get_barrier_semaphore()
    for flip in range(1, n_dp):
        pl.semaphore_signal(barrier, inc=1, device_id=(d ^ flip, i), device_id_type=MESH)
    for turn in range(1, n):
        pl.semaphore_signal(
            barrier, inc=1, device_id=(d, lax.rem(i + turn, n)), device_id_type=MESH
        )
    pl.semaphore_wait(barrier, n_dp + n - 2)


def front_kernel(
    n,
    n_dp,
    heads,
    tile,
    x_own,
    cot_own,
    noise_own,
    mod_w,
    sizes,
    attend_w,
    merge_w,
    up_w,
    down_w,
    cot_full,
    hidden_out,
    qkv_out,
    lse,
    attended_out,
    attn_out_hbm,
    middle_out,
    second_out,
    table,
    attend_full,
    merge_full,
    up_full,
    down_full,
    noise_all,
    x_full,
    attend,
    merge,
    noise,
    hidden,
    qkv,
    attended,
    att_rows,
    attn_out,
    middle,
    hidden_second,
    terms,
    terms_all,
    columns,
    noise_sem,
    terms_sem,
    column_sem,
    x_sem,
    cot_sem,
    merge_sem,
    weight_sent,
    weight_came,
    out_sem,
    att_sem,
    local,
):
    d, i = lax.axis_index("dp"), lax.axis_index("tensor")
    rows, width = x_own.shape
    k_rows, own_cols = mod_w.shape
    head_cols = heads * HEAD_DIM
    low, f32 = jnp.bfloat16, jnp.float32
    merge_rows, merge_cols = merge_w.shape
    down_cols = down_w.shape[1]
    merge_slab = merge.at[:, pl.ds(pl.multiple_of(d * merge_cols, merge_cols), merge_cols)]

    def row_view(full, height):
        return lambda at, start, count: full.at[
            pl.ds(pl.multiple_of(at * height + start, 16), count), :
        ]

    def column_view(full, wide):
        return lambda at, start, count: full.at[
            pl.ds(start, count), pl.ds(pl.multiple_of(at * wide, wide), wide)
        ]

    weights = [
        PlaneGather(n_dp, d, own, view, height, weight_sent.at[k], weight_came.at[k])
        for k, (own, view, height) in enumerate(
            (
                (attend_w, row_view(attend, k_rows), k_rows),
                (merge_slab, column_view(merge, merge_cols), n * merge_rows),
                (up_w, row_view(up_full, k_rows), k_rows),
                (down_w, column_view(down_full, down_cols), down_w.shape[0]),
            )
        )
    ]
    attend_g, merge_g, up_g, down_g = weights
    copies = [
        pltpu.make_async_copy(source, target, local.at[k])
        for k, (source, target) in enumerate(
            (
                (attend_w, attend_g.slab(0)),
                (merge_w, merge_slab.at[rows_of(i, merge_rows)]),
                (cot_own, cot_full.at[rows_of(i, rows)]),
                (up_w, up_g.slab(0)),
                (down_w, down_g.slab(0)),
            )
        )
    ]
    for copy in copies:
        copy.start()
    greet_all(n, n_dp, d, i)

    def to_plane(source, target, sems, flip):
        return pltpu.make_async_remote_copy(
            src_ref=source.at[d ^ flip],
            dst_ref=target.at[d],
            send_sem=sems.at[0, flip],
            recv_sem=sems.at[1, flip],
            device_id=(d ^ flip, i),
            device_id_type=MESH,
        )

    def from_plane(target, sems, flip):
        return pltpu.make_async_remote_copy(
            src_ref=target.at[d ^ flip],
            dst_ref=target.at[d ^ flip],
            send_sem=sems.at[0, flip],
            recv_sem=sems.at[1, flip],
            device_id=(d ^ flip, i),
            device_id_type=MESH,
        )

    for k in range(n_dp):
        v = noise_own[:, k * k_rows : (k + 1) * k_rows].astype(f32)
        noise[k] = (v * (1.0 / (1.0 + jnp.exp(-v)))).astype(low).astype(f32)
    for flip in range(1, n_dp):
        to_plane(noise, noise_all, noise_sem, flip).start()
    merge_line = LineGather(
        n, i, merge_rows, merge_w, merge_slab, merge_sem.at[0], merge_sem.at[1], merge_sem.at[2]
    )
    x_line = LineGather(n, i, rows, x_own, x_full, x_sem.at[0], x_sem.at[1], x_sem.at[2])
    cot_line = LineGather(
        n, i, rows, cot_own, cot_full, cot_sem.at[0], cot_sem.at[1], cot_sem.at[2]
    )
    x_line.start()
    noise_all[d] = noise[d]
    x_full[rows_of(i, rows), :] = x_own[...]
    for flip in range(1, n_dp):
        from_plane(noise_all, noise_sem, flip).wait_recv()
    pictures = noise.shape[1]
    images = noise_all[...].reshape(n_dp * pictures, k_rows).astype(low)
    for c in range(own_cols // tile):
        terms[:, :, c * tile : (c + 1) * tile] = mm(
            images, mod_w[:, c * tile : (c + 1) * tile]
        ).reshape(n_dp, pictures, tile)
    for flip in range(1, n_dp):
        to_plane(terms, terms_all, terms_sem, flip).start()
    attend_g.start()
    terms_all[d] = terms[d]
    for flip in range(1, n_dp):
        from_plane(terms_all, terms_sem, flip).wait_recv()
    columns[i] = jnp.sum(terms_all[...], axis=0)

    def to_line(turn):
        t = lax.rem(i + turn, n)
        return pltpu.make_async_remote_copy(
            src_ref=columns.at[i],
            dst_ref=columns.at[i],
            send_sem=column_sem.at[0, t],
            recv_sem=column_sem.at[1, i],
            device_id=(d, t),
            device_id_type=MESH,
        )

    def from_line(turn):
        t = lax.rem(i + turn, n)
        return pltpu.make_async_remote_copy(
            src_ref=columns.at[t],
            dst_ref=columns.at[t],
            send_sem=column_sem.at[0, t],
            recv_sem=column_sem.at[1, t],
            device_id=(d, t),
            device_id_type=MESH,
        )

    for turn in range(1, n):
        to_line(turn).start()
    merge_line.start()
    x_line.step(1)
    for turn in range(1, n):
        from_line(turn).wait_recv()
    unit = math.gcd(width, own_cols)

    def fill(j, carry):
        image = image_at(sizes, j * rows)
        for number in range(6):
            for start in range(0, width, unit):
                at = number * width + start
                here = slice(at % own_cols, at % own_cols + unit)
                table[j, number : number + 1, start : start + unit] = sum(
                    columns[at // own_cols, k : k + 1, here] * jnp.where(image == k, 1.0, 0.0)
                    for k in range(pictures)
                )
        return carry

    lax.fori_loop(0, n, fill, 0)
    attend_g.relay()
    merge_line.step(1)
    for copy in copies[:2]:
        copy.wait()
    attend_g.close()
    up_g.start()
    keep_attend = pltpu.make_async_copy(attend, attend_full, out_sem.at[0])
    keep_merge = pltpu.make_async_copy(
        merge.at[rows_of(i, merge_rows)], merge_full, out_sem.at[1]
    )
    keep_attend.start()
    keep_hidden = pltpu.make_async_copy(hidden, hidden_out, out_sem.at[2])
    keep_qkv = pltpu.make_async_copy(qkv, qkv_out, out_sem.at[3])

    def tiles(count):
        return [slice(c * tile, (c + 1) * tile) for c in range(count // tile)]

    def one_block(j):
        here = rows_of(j, rows)
        squares = jnp.zeros((rows, 1), f32)
        for at in tiles(width):
            v = x_full[here, at].astype(f32)
            squares += jnp.sum(v * v, axis=1, keepdims=True)
        root = lax.rsqrt(squares * (1.0 / width) + 1e-06)
        for at in tiles(width):
            v = x_full[here, at].astype(f32) * root
            hidden[here, at] = (v * (1.0 + table[j, 1:2, at]) + table[j, 0:1, at]).astype(low)
        wide = qkv.shape[1]
        step = math.gcd(wide, 512)
        for c in range(wide // step):
            at = slice(c * step, (c + 1) * step)
            qkv[here, at] = mm(hidden[here, :], attend[:, at]).astype(low)

    def visit(q, carry):
        s = (q + 1) // 2
        side = 1 - 2 * (q % 2)
        j = i + s * side

        @pl.when((q % 2 == 1) & (s + 1 < n))
        def _():
            x_line.step(s + 1)
            merge_line.step(s + 1)

        @pl.when(q == 2 * n - 5)
        def _():
            up_g.relay()
            merge_g.start()
            cot_line.start()

        @pl.when((j >= 0) & (j < n))
        def _():
            one_block(j)

        return carry

    lax.fori_loop(0, 2 * n - 1, visit, 0)

    keep_hidden.start()
    keep_qkv.start()

    area = min(256, n * rows)
    areas = n * rows // area
    owners = area // rows
    area_images = [image_at(sizes, b * area) for b in range(areas)]

    def to_owner(j):
        return pltpu.make_async_remote_copy(
            src_ref=attended.at[rows_of(j, rows), :],
            dst_ref=att_rows.at[:, pl.ds(pl.multiple_of(i * head_cols, head_cols), head_cols)],
            send_sem=att_sem.at[0, j],
            recv_sem=att_sem.at[1, i],
            device_id=(d, j),
            device_id_type=MESH,
        )

    def from_source(t):
        return pltpu.make_async_remote_copy(
            src_ref=attended.at[rows_of(t, rows), :],
            dst_ref=att_rows.at[:, pl.ds(pl.multiple_of(t * head_cols, head_cols), head_cols)],
            send_sem=att_sem.at[0, t],
            recv_sem=att_sem.at[1, t],
            device_id=(d, t),
            device_id_type=MESH,
        )

    def attend_area(turn, carry):
        here_at = lax.rem(i // owners + 1 + turn, areas)
        here = rows_of(here_at, area)
        image = image_at(sizes, here_at * area)
        for h in range(heads):
            first = h * 3 * HEAD_DIM
            q = qkv[here, first : first + HEAD_DIM]
            parts = []
            for b in range(areas):
                key = qkv[b * area : (b + 1) * area, first + HEAD_DIM : first + 2 * HEAD_DIM]
                parts.append(
                    mm_nt(key, q) * HEAD_DIM ** (-0.5)
                    + jnp.where(image == area_images[b], 0.0, MASKED)
                )
            highest = parts[0].max(axis=0, keepdims=True)
            for part in parts[1:]:
                highest = jnp.maximum(highest, part.max(axis=0, keepdims=True))
            parts = [jnp.exp(part - highest) for part in parts]
            totals = sum(jnp.sum(part, axis=0, keepdims=True) for part in parts)
            inverse = 1.0 / totals
            out = jnp.zeros((HEAD_DIM, area), f32)
            for b in range(areas):
                value = qkv[b * area : (b + 1) * area, first + 2 * HEAD_DIM : first + 3 * HEAD_DIM]
                out += mm_tn(value, (parts[b] * inverse).astype(low))
            attended[here, h * HEAD_DIM : (h + 1) * HEAD_DIM] = out.T.astype(low)
            lse[pl.ds(here_at * heads + h, 1), :] = highest + jnp.log(totals)
        for k in range(owners):
            j = here_at * owners + k

            @pl.when(j != i)
            def _():
                to_owner(j).start()

        @pl.when(turn == (areas - 1) // 2)
        def _():
            up_g.close()
            cot_line.step(1)

        @pl.when(turn == areas - 1)
        def _():
            merge_g.relay()
            down_g.start()

        return carry

    lax.fori_loop(0, areas, attend_area, 0)
    att_rows[:, pl.ds(pl.multiple_of(i * head_cols, head_cols), head_cols)] = attended[
        rows_of(i, rows), :
    ]
    if n > 2:
        cot_line.step(2)
    merge_g.close()
    keep_merge.start()
    for turn in range(1, n):
        from_source(lax.rem(i + turn, n)).wait_recv()
    squares = jnp.zeros((rows, 1), f32)
    for at in tiles(width):
        out = mm(att_rows[...], merge[:, at])
        attn_out[:, at] = out
        v = x_own[:, at].astype(f32) + table[i, 2:3, at] * out
        middle[:, at] = v
        squares += jnp.sum(v * v, axis=1, keepdims=True)
    root = lax.rsqrt(squares * (1.0 / width) + 1e-06)
    for at in tiles(width):
        v = middle[:, at] * root
        hidden_second[:, at] = (v * (1.0 + table[i, 4:5, at]) + table[i, 3:4, at]).astype(low)
    keeps = [
        pltpu.make_async_copy(source, target, out_sem.at[4 + k])
        for k, (source, target) in enumerate(
            (
                (attended, attended_out),
                (attn_out, attn_out_hbm),
                (middle, middle_out),
                (hidden_second, second_out),
            )
        )
    ]
    for keep in keeps:
        keep.start()
    down_g.relay()
    for s in range(3, n):
        cot_line.step(s)
    down_g.close()
    for copy in copies[2:]:
        copy.wait()
    keep_attend.wait()
    keep_merge.wait()
    keep_hidden.wait()
    keep_qkv.wait()
    for keep in keeps:
        keep.wait()
    for flip in range(1, n_dp):
        to_plane(noise, noise_all, noise_sem, flip).wait_send()
        to_plane(terms, terms_all, terms_sem, flip).wait_send()
    for line in (merge_line, x_line, cot_line):
        line.finish()
    for turn in range(1, n):
        to_line(turn).wait_send()
    for turn in range(1, n):
        to_owner(lax.rem(i + turn, n)).wait_send()
    for weight in weights:
        weight.finish()


def front(n, n_dp, x, cot, noise, mod_w, sizes, attend_w, merge_w, up_w, down_w, number):
    rows, width = x.shape
    k_rows, own_cols = mod_w.shape
    wide = attend_w.shape[1]
    heads = wide // (3 * HEAD_DIM)
    total = n * rows
    areas = total // min(256, total)
    pictures = noise.shape[0]
    low, f32 = jnp.bfloat16, jnp.float32
    sds = jax.ShapeDtypeStruct
    count = plane_sems(n_dp)
    return call(
        functools.partial(front_kernel, n, n_dp, heads, 512),
        number,
        "front",
        [VMEM, HBM, VMEM, VMEM, pl.BlockSpec(memory_space=pltpu.SMEM), VMEM, VMEM, HBM, HBM],
        [
            sds((total, width), low),
            sds((total, width), low),
            sds((total, wide), low),
            sds((areas * heads, total // areas), f32),
            sds((total, heads * HEAD_DIM), low),
            sds((rows, width), f32),
            sds((rows, width), f32),
            sds((rows, width), low),
            sds((n, 8, width), f32),
            sds((n_dp * k_rows, wide), low),
            sds((merge_w.shape[0], width), low),
            sds((n_dp * k_rows, up_w.shape[1]), low),
            sds((down_w.shape[0], n_dp * down_w.shape[1]), low),
            sds((n_dp, pictures, k_rows), f32),
        ],
        [HBM] * 3 + [VMEM] + [HBM] * 4 + [VMEM] + [HBM] * 4 + [VMEM],
        [
            pltpu.VMEM((total, width), low),
            pltpu.VMEM((n_dp * k_rows, wide), low),
            pltpu.VMEM((n * merge_w.shape[0], n_dp * merge_w.shape[1]), low),
            pltpu.VMEM((n_dp, pictures, k_rows), f32),
            pltpu.VMEM((total, width), low),
            pltpu.VMEM((total, wide), low),
            pltpu.VMEM((total, heads * HEAD_DIM), low),
            pltpu.VMEM((rows, width), low),
            pltpu.VMEM((rows, width), f32),
            pltpu.VMEM((rows, width), f32),
            pltpu.VMEM((rows, width), low),
            pltpu.VMEM((n_dp, pictures, own_cols), f32),
            pltpu.VMEM((n_dp, pictures, own_cols), f32),
            pltpu.VMEM((n, pictures, own_cols), f32),
            DMA((2, n_dp)),
            DMA((2, n_dp)),
            DMA((3, n)),
            DMA((3, n)),
            DMA((3, n)),
            DMA((3, n)),
            DMA((4, count)),
            DMA((4, count)),
            DMA((8,)),
            DMA((2, n)),
            DMA((5,)),
        ],
        flops=2 * total * width * wide,
    )(x, cot, noise, mod_w, sizes, attend_w, merge_w, up_w, down_w)


class PlaneScatter:
    def __init__(self, n_dp, d, theirs, own, swapped, via, landed, sems):
        self.chips, self.d, self.square = n_dp // 2, d, n_dp == 8
        self.chip, self.side = d // 2, lax.rem(d, 2)
        self.theirs, self.own, self.swapped, self.via = theirs, own, swapped, via
        self.landed, self.sems = landed, sems

    def remote(self, source, target, sent, came, device):
        return pltpu.make_async_remote_copy(
            src_ref=source,
            dst_ref=target,
            send_sem=sent,
            recv_sem=came,
            device_id=(device, lax.axis_index("tensor")),
            device_id_type=MESH,
        )

    def swap(self, m):
        return self.remote(
            self.theirs(m), self.swapped.at[m], self.sems.at[0, m], self.sems.at[1, m], self.d ^ 1
        )

    def half(self, ref, which):
        height = self.own.shape[1] // 2
        return ref.at[pl.ds(which * height, height), :]

    def step(self, k):
        slab, which, peer = ((1, 0, 1), (3, 0, 1), (2, 1, 2), (3, 1, 2), (2, 0, 2), (1, 1, 1))[k]
        target = self.via if slab == 3 else self.landed.at[1 if k < 4 else 2]
        return self.remote(
            self.half(self.own.at[self.chip ^ slab], which),
            self.half(target, which),
            self.sems.at[2, k],
            self.sems.at[3, k],
            2 * (self.chip ^ peer) + self.side,
        )

    def send(self, m, slot, sem):
        return self.remote(
            self.own.at[m],
            self.landed.at[slot],
            self.sems.at[2, m],
            self.sems.at[3, sem],
            2 * m + self.side,
        )

    def keep(self):
        slot = 0 if self.square else self.chip
        return pltpu.make_async_copy(
            self.own.at[self.chip], self.landed.at[slot], self.sems.at[2, 6 if self.square else self.chip]
        )

    def swap_all(self):
        def one(m, carry):
            self.swap(m).start()
            return carry

        lax.fori_loop(0, self.chips, one, 0)

    def add(self, target, source):
        height, wide = target.shape
        chunk = math.gcd(height, 64 if wide > 512 else 256)

        def one(c, carry):
            at = pl.ds(pl.multiple_of(c * chunk, chunk), chunk)
            total = target[at, :].astype(jnp.float32) + source[at, :].astype(jnp.float32)
            target[at, :] = total.astype(target.dtype)
            return carry

        lax.fori_loop(0, height // chunk, one, 0)

    def add_and_send(self):
        def one(k, carry):
            m = self.chip ^ (self.chips - 1 - k)
            self.swap(m).wait_recv()
            self.add(self.own.at[m], self.swapped.at[m])
            if not self.square:

                @pl.when(m != self.chip)
                def _():
                    self.send(m, self.chip, self.chip).start()

            return carry

        lax.fori_loop(0, self.chips, one, 0)
        if self.square:
            for k in (1, 3, 0, 2):
                self.step(k).start()
        self.keep().start()

    def relay(self):
        if self.square:
            for k, slab, which in ((1, 2, 0), (3, 1, 1)):
                self.step(k).wait_recv()
                self.step(k).wait_send()
                self.add(self.half(self.own.at[self.chip ^ slab], which), self.half(self.via, which))
                self.step(4 if k == 1 else 5).start()

    def landed_all(self):
        if self.square:
            for k in (0, 2, 4, 5):
                self.step(k).wait_recv()
        else:
            for k in range(1, self.chips):
                self.send(self.chip ^ k, self.chip ^ k, self.chip ^ k).wait_recv()
        self.keep().wait()

    def finish(self):
        for m in range(self.chips):
            self.swap(m).wait_send()
        if self.square:
            for k in (0, 2, 4, 5):
                self.step(k).wait_send()
        else:
            for k in range(1, self.chips):
                self.send(self.chip ^ k, self.chip, self.chip).wait_send()


def plane_slots(n_dp):
    return 3 if n_dp == 8 else n_dp // 2


def scatter_sems(n_dp):
    return DMA((4, max(7, n_dp // 2)))


def flows(n, pieces, sums, turn):
    far, rest = turn // ((n - 2) * pieces), lax.rem(turn, (n - 2) * pieces)
    t, c = n - 1 - rest // pieces, lax.rem(rest, pieces)
    for near in (True, False):

        @pl.when(far == (0 if near else 1))
        def _():
            sums.pass_on(t, c, near)


def back_kernel(
    n,
    n_dp,
    heads,
    tile,
    d_hidden,
    middle,
    table,
    lse,
    sizes,
    cot_hbm,
    out_hbm,
    rows_hbm,
    qkv_hbm,
    mlp_hbm,
    merge_hbm,
    up_hbm,
    down_hbm,
    block_out,
    d_middle_out,
    d_qkv_out,
    sums_out,
    merge_grad,
    up_landed,
    down_landed,
    cot,
    attn_out,
    d_middle,
    d_qkv,
    attended,
    qkv,
    part,
    got,
    merge,
    d_att,
    d_attn,
    d_keys,
    d_values,
    up_own,
    up_swapped,
    up_via,
    down_own,
    down_swapped,
    down_via,
    stage,
    mlp_sent,
    mlp_came,
    up_sems,
    down_sems,
    line_sem,
    merge_sem,
    load_sem,
    stage_sem,
    own_sem,
):
    d, i = lax.axis_index("dp"), lax.axis_index("tensor")
    rows, width = middle.shape
    low, f32 = jnp.bfloat16, jnp.float32
    head_cols = heads * HEAD_DIM
    chips = n_dp // 2
    k_rows, down_cols = up_own.shape[1], down_own.shape[2]
    side = lax.rem(d, 2)

    def up_slab(at):
        return up_hbm.at[pl.ds(pl.multiple_of(at * k_rows, k_rows), k_rows), :]

    def down_slab(at):
        return down_hbm.at[:, pl.ds(pl.multiple_of(at * down_cols, down_cols), down_cols)]

    load_mlp = pltpu.make_async_copy(mlp_hbm, part, load_sem.at[0])
    load_mlp.start()
    load_cot = pltpu.make_async_copy(cot_hbm, cot, load_sem.at[3])
    load_out = pltpu.make_async_copy(out_hbm, attn_out, load_sem.at[4])
    load_cot.start()
    load_out.start()
    load_rows = pltpu.make_async_copy(rows_hbm, attended, load_sem.at[1])
    load_qkv = pltpu.make_async_copy(qkv_hbm, qkv, load_sem.at[2])

    load_merge = pltpu.make_async_copy(merge_hbm, merge, merge_sem)
    load_merge.start()
    for m in range(chips):
        pltpu.make_async_copy(up_slab(2 * m + side), up_own.at[m], own_sem.at[0, m]).start()
        pltpu.make_async_copy(down_slab(2 * m + side), down_own.at[m], own_sem.at[1, m]).start()
    load_rows.start()
    load_qkv.start()
    greet_all(n, n_dp, d, i)
    up = PlaneScatter(
        n_dp, d, lambda m: up_slab(2 * m + 1 - side), up_own, up_swapped, up_via, up_landed, up_sems
    )
    down = PlaneScatter(
        n_dp,
        d,
        lambda m: down_slab(2 * m + 1 - side),
        down_own,
        down_swapped,
        down_via,
        down_landed,
        down_sems,
    )
    up.swap_all()
    down.swap_all()
    load_mlp.wait()
    piece = tile // 2
    sums = LineScatter(n, i, rows, piece, part, got, mlp_sent, mlp_came)
    pieces = sums.pieces

    def ends(k, carry):
        t, c = n - 1 - k // pieces, lax.rem(k, pieces)
        pl.when(i == 0)(functools.partial(sums.at_end, t, c))
        pl.when(i == n - 1)(functools.partial(sums.at_end, n - 1 - t, c))
        return carry

    tiles = [slice(c * tile, (c + 1) * tile) for c in range(width // tile)]
    own_rows = rows_of(i, rows)
    squares = jnp.zeros((rows, 1), f32)
    for at in tiles:
        squares += jnp.sum(middle[:, at] * middle[:, at], axis=1, keepdims=True)
    root = lax.rsqrt(squares * (1.0 / width) + 1e-06)
    mean = jnp.zeros((rows, 1), f32)
    for at in tiles:
        v = middle[:, at] * root
        dh = d_hidden[:, at]
        mean += jnp.sum(dh * (1.0 + table[i, 4:5, at]) * v, axis=1, keepdims=True)
        sums_out[3:4, at] = jnp.sum(dh, axis=0, keepdims=True)
        sums_out[4:5, at] = jnp.sum(dh * v, axis=0, keepdims=True)
    mean = mean * (1.0 / width)
    load_cot.wait()
    load_out.wait()
    for at in tiles:
        v = middle[:, at] * root
        u = d_hidden[:, at] * (1.0 + table[i, 4:5, at])
        dm = cot[:, at].astype(f32) + root * (u - v * mean)
        d_middle[:, at] = dm
        d_attn[own_rows, at] = (table[i, 2:3, at] * dm).astype(low)
        sums_out[2:3, at] = jnp.sum(dm * attn_out[:, at], axis=0, keepdims=True)

    keep_middle = pltpu.make_async_copy(d_middle, d_middle_out, load_sem.at[5])
    keep_middle.start()

    line = LineGather(
        n, i, rows, d_attn.at[own_rows], d_attn, line_sem.at[0], line_sem.at[1], line_sem.at[2]
    )
    line.start()
    lax.fori_loop(0, (n - 1) * pieces, ends, 0)
    for m in range(chips):
        pltpu.make_async_copy(up_slab(2 * m + side), up_own.at[m], own_sem.at[0, m]).wait()
        pltpu.make_async_copy(down_slab(2 * m + side), down_own.at[m], own_sem.at[1, m]).wait()
    load_rows.wait()
    load_qkv.wait()
    load_merge.wait()

    area = lse.shape[1]
    areas = n * rows // area
    area_images = [image_at(sizes, b * area) for b in range(areas)]
    d_keys[...] = jnp.zeros_like(d_keys)
    d_values[...] = jnp.zeros_like(d_values)
    turns = 2 * max(n - 2, 0) * pieces
    scale = HEAD_DIM ** (-0.5)

    def back_area(here_at, carry):
        here = rows_of(here_at, area)
        image = image_at(sizes, here_at * area)
        for h in range(heads):
            first = h * 3 * HEAD_DIM
            head = slice(h * HEAD_DIM, (h + 1) * HEAD_DIM)
            q = qkv[here, first : first + HEAD_DIM]
            g = d_att[here, head]
            log_row = lse[pl.ds(here_at * heads + h, 1), :]
            probs, d_probs = [], []
            inner = jnp.zeros((1, area), f32)
            for b in range(areas):
                key = qkv[b * area : (b + 1) * area, first + HEAD_DIM : first + 2 * HEAD_DIM]
                value = qkv[b * area : (b + 1) * area, first + 2 * HEAD_DIM : first + 3 * HEAD_DIM]
                scores = mm_nt(key, q) * scale + jnp.where(image == area_images[b], 0.0, MASKED)
                probs.append(jnp.exp(scores - log_row))
                d_probs.append(mm_nt(value, g))
                inner += jnp.sum(probs[b] * d_probs[b], axis=0, keepdims=True)
            d_query = jnp.zeros((HEAD_DIM, area), f32)
            for b in range(areas):
                at = slice(b * area, (b + 1) * area)
                key = qkv[at, first + HEAD_DIM : first + 2 * HEAD_DIM]
                d_scores = (probs[b] * (d_probs[b] - inner)).astype(low)
                d_values[at, head] += mm(probs[b].astype(low), g)
                d_keys[at, head] += mm(d_scores, q)
                d_query += mm_tn(key, d_scores)
            d_qkv[here, first : first + HEAD_DIM] = (d_query * scale).T.astype(low)

        return carry

    def pass_by(turn, carry):
        flows(n, pieces, sums, turn)
        return carry

    early = min(turns, pieces)

    def visit(q, carry):
        s = (q + 1) // 2
        j = i + s * (1 - 2 * (q % 2))

        @pl.when(q % 2 == 1)
        def _():
            line.step(s)

        @pl.when((j >= 0) & (j < n))
        def _():
            here = rows_of(j, rows)
            d_att[here, :] = mm_nt(d_attn[here, :], merge[...]).astype(low)
            if area == rows:
                back_area(j, 0)

        @pl.when(q == 0)
        def _():
            up.add_and_send()
            down.add_and_send()

        @pl.when(q == 2 * (n - 2))
        def _():
            up.relay()
            lax.fori_loop(0, early, pass_by, 0)

        return carry

    lax.fori_loop(0, 2 * n - 1, visit, 0)
    if area != rows:
        lax.fori_loop(0, areas, back_area, 0)
    for h in range(heads):
        first = h * 3 * HEAD_DIM
        head = slice(h * HEAD_DIM, (h + 1) * HEAD_DIM)
        d_qkv[:, first + HEAD_DIM : first + 2 * HEAD_DIM] = (d_keys[:, head] * scale).astype(low)
        d_qkv[:, first + 2 * HEAD_DIM : first + 3 * HEAD_DIM] = d_values[:, head].astype(low)
    keep_qkv = pltpu.make_async_copy(d_qkv, d_qkv_out, load_sem.at[6])
    keep_qkv.start()
    wide = width // tile
    short = stage.shape[1]

    def square(row, column):
        return merge_grad.at[
            pl.ds(pl.multiple_of(row * short, short), short),
            pl.ds(pl.multiple_of(column * tile, tile), tile),
        ]

    def merge_one(k, carry):
        row, column = k // wide, lax.rem(k, wide)
        slot = lax.rem(k, 2)

        @pl.when(k >= 2)
        def _():
            pltpu.make_async_copy(stage.at[slot], square(0, 0), stage_sem.at[slot]).wait()

        a = attended[:, pl.ds(pl.multiple_of(row * short, short), short)]
        b = d_attn[:, pl.ds(pl.multiple_of(column * tile, tile), tile)]
        stage[slot] = mm_tn(a, b).astype(low)
        pltpu.make_async_copy(stage.at[slot], square(row, column), stage_sem.at[slot]).start()
        return carry

    lax.fori_loop(0, attended.shape[1] // short * wide, merge_one, 0)
    for slot in range(2):
        pltpu.make_async_copy(stage.at[slot], square(0, 0), stage_sem.at[slot]).wait()
    lax.fori_loop(early, turns, pass_by, 0)
    for c in range(pieces):
        at = slice(c * piece, (c + 1) * piece)
        total = sums.own_value(c)
        block_out[:, at] = (middle[:, at] + table[i, 5:6, at] * total).astype(low)
        sums_out[5:6, at] = jnp.sum(cot[:, at].astype(f32) * total, axis=0, keepdims=True)
    sums_out[0:2, :] = jnp.zeros((2, width), f32)
    sums_out[6:8, :] = jnp.zeros((2, width), f32)
    down.relay()
    keep_middle.wait()
    keep_qkv.wait()
    for scatter in (up, down):
        scatter.landed_all()
        scatter.finish()
    line.finish()
    sums.all_sent()


def back(n, n_dp, operands, shapes, number, tile=512):
    (rows, width), wide, units, k_rows, down_cols, areas = shapes
    heads = wide // (3 * HEAD_DIM)
    total, chips, pieces = n * rows, n_dp // 2, 2 * width // tile
    low, f32 = jnp.bfloat16, jnp.float32
    sds = jax.ShapeDtypeStruct
    return call(
        functools.partial(back_kernel, n, n_dp, heads, tile),
        number,
        "back",
        [VMEM] * 4 + [pl.BlockSpec(memory_space=pltpu.SMEM)] + [HBM] * 8,
        [
            sds((rows, width), low),
            sds((rows, width), f32),
            sds((total, wide), low),
            sds((8, width), f32),
            sds((heads * HEAD_DIM, width), low),
            sds((plane_slots(n_dp), k_rows, units), low),
            sds((plane_slots(n_dp), units, down_cols), low),
        ],
        [VMEM, HBM, HBM, VMEM] + [HBM] * 3,
        [
            pltpu.VMEM((rows, width), low),
            pltpu.VMEM((rows, width), f32),
            pltpu.VMEM((rows, width), f32),
            pltpu.VMEM((total, wide), low),
            pltpu.VMEM((total, heads * HEAD_DIM), low),
            pltpu.VMEM((total, wide), low),
            pltpu.VMEM((total, width), low),
            pltpu.VMEM((total + rows, width), low),
            pltpu.VMEM((heads * HEAD_DIM, width), low),
            pltpu.VMEM((total, heads * HEAD_DIM), low),
            pltpu.VMEM((total, width), low),
            pltpu.VMEM((total, heads * HEAD_DIM), f32),
            pltpu.VMEM((total, heads * HEAD_DIM), f32),
            pltpu.VMEM((chips, k_rows, units), low),
            pltpu.VMEM((chips, k_rows, units), low),
            pltpu.VMEM((k_rows, units), low),
            pltpu.VMEM((chips, units, down_cols), low),
            pltpu.VMEM((chips, units, down_cols), low),
            pltpu.VMEM((units, down_cols), low),
            pltpu.VMEM((2, tile // 2, tile), low),
            DMA((n, pieces)),
            DMA((n + 1, pieces)),
            scatter_sems(n_dp),
            scatter_sems(n_dp),
            DMA((3, n)),
            DMA,
            DMA((7,)),
            DMA((2,)),
            DMA((2, chips)),
        ],
        flops=20 * total * total * wide // 3,
    )(*operands)


def last_kernel(
    n,
    n_dp,
    tile,
    d_qkv,
    sums_in,
    table,
    sizes,
    hidden_hbm,
    x_hbm,
    middle_hbm,
    mod_hbm,
    merge_hbm,
    attend_hbm,
    input_grad,
    d_mod_all,
    noise_sum,
    attend_landed,
    merge_landed,
    hidden,
    x_own,
    d_middle,
    mod_w,
    attend,
    part,
    got,
    grad_own,
    grad_theirs,
    grad_swapped,
    grad_via,
    merge_own,
    merge_swapped,
    merge_via,
    sums_all,
    shares,
    shares_all,
    terms,
    terms_all,
    noise_parts,
    sent,
    came,
    grad_sems,
    merge_sems,
    share_sem,
    mod_sem,
    term_sem,
    noise_sem,
    load_sem,
    own_sem,
    attend_sem,
):
    d, i = lax.axis_index("dp"), lax.axis_index("tensor")
    rows, width = input_grad.shape
    low, f32 = jnp.bfloat16, jnp.float32
    chips = n_dp // 2
    side = lax.rem(d, 2)
    k_rows, own_cols = mod_w.shape
    merge_cols = merge_own.shape[2]
    images = d_mod_all.shape[1]

    def merge_slab(at):
        return merge_hbm.at[:, pl.ds(pl.multiple_of(at * merge_cols, merge_cols), merge_cols)]

    load_hidden, load_x, load_middle, load_mod = (
        pltpu.make_async_copy(source, target, load_sem.at[k])
        for k, (source, target) in enumerate(
            (
                (hidden_hbm, hidden),
                (x_hbm, x_own),
                (middle_hbm, d_middle),
                (mod_hbm, mod_w),
            )
        )
    )

    def load_attend(c):
        at = pl.ds(pl.multiple_of(c * tile, tile), tile)
        return pltpu.make_async_copy(attend_hbm.at[at, :], attend.at[at, :], attend_sem.at[c])

    for c in range(width // tile):
        load_attend(c).start()
    for m in range(chips):
        pltpu.make_async_copy(merge_slab(2 * m + side), merge_own.at[m], own_sem.at[m]).start()
    greet_all(n, n_dp, d, i)
    merge = PlaneScatter(
        n_dp,
        d,
        lambda m: merge_slab(2 * m + 1 - side),
        merge_own,
        merge_swapped,
        merge_via,
        merge_landed,
        merge_sems,
    )
    grad = PlaneScatter(
        n_dp, d, lambda m: grad_theirs.at[m], grad_own, grad_swapped, grad_via, attend_landed, grad_sems
    )
    merge.swap_all()
    for late in (load_hidden, load_x, load_middle, load_mod):
        late.start()
    piece = tile // 2
    sums = LineScatter(n, i, rows, piece, part, got, sent, came)
    pieces = sums.pieces

    def partial_block(q, carry):
        j = jnp.where(2 * i < n - 1, n - 1 - q, q)
        here = rows_of(j, rows)

        def one(c, inner):
            at = pl.ds(pl.multiple_of(c * tile, tile), tile)

            @pl.when(q == 0)
            def _():
                load_attend(c).wait()

            part[here, at] = mm_nt(d_qkv[here, :], attend[at, :]).astype(low)
            for k in range(tile // piece):
                sums.at_end(j, c * (tile // piece) + k)
            return inner

        lax.fori_loop(0, width // tile, one, 0)
        return carry

    partial_block(0, 0)
    for m in range(chips):
        pltpu.make_async_copy(merge_slab(2 * m + side), merge_own.at[m], own_sem.at[m]).wait()
    merge.add_and_send()
    lax.fori_loop(1, n, partial_block, 0)

    def slab_grad(at):
        columns = pl.ds(pl.multiple_of(at * k_rows, k_rows), k_rows)
        return mm_tn(hidden[:, columns], d_qkv[...]).astype(low)

    def for_them(m, carry):
        grad_theirs[m] = slab_grad(2 * m + 1 - side)
        grad.swap(m).start()
        return carry

    def for_us(m, carry):
        grad_own[m] = slab_grad(2 * m + side)
        return carry

    load_hidden.wait()
    lax.fori_loop(0, chips, for_them, 0)
    lax.fori_loop(0, chips, for_us, 0)
    grad.add_and_send()
    merge.relay()
    turns = 2 * max(n - 2, 0) * pieces

    def pass_by(turn, carry):
        flows(n, pieces, sums, turn)
        return carry

    lax.fori_loop(0, turns, pass_by, 0)

    grad.relay()

    for late in (load_x, load_middle, load_mod):
        late.wait()
    tiles = [slice(c * piece, (c + 1) * piece) for c in range(pieces)]
    squares = jnp.zeros((rows, 1), f32)
    for at in tiles:
        v = x_own[:, at].astype(f32)
        squares += jnp.sum(v * v, axis=1, keepdims=True)
    root = lax.rsqrt(squares * (1.0 / width) + 1e-06)
    mean = jnp.zeros((rows, 1), f32)
    sums_all[...] = sums_in[...]
    for c, at in enumerate(tiles):
        v = x_own[:, at].astype(f32) * root
        dh = sums.own_value(c)
        mean += jnp.sum(dh * (1.0 + table[i, 1:2, at]) * v, axis=1, keepdims=True)
        sums_all[0:1, at] = jnp.sum(dh, axis=0, keepdims=True)
        sums_all[1:2, at] = jnp.sum(dh * v, axis=0, keepdims=True)

    unit = math.gcd(width, own_cols)
    image = image_at(sizes, i * rows)
    for number in range(6):
        for start in range(0, width, unit):
            at = number * width + start
            for k in range(images):
                shares[at // own_cols, k : k + 1, at % own_cols : at % own_cols + unit] = (
                    sums_all[number : number + 1, start : start + unit]
                    * jnp.where(image == k, 1.0, 0.0)
                )

    def to_line(source, target, sems, turn, whole=False):
        t = lax.rem(i + turn, n)
        return pltpu.make_async_remote_copy(
            src_ref=source if whole else source.at[t],
            dst_ref=target.at[i],
            send_sem=sems.at[0, t],
            recv_sem=sems.at[1, i],
            device_id=(d, t),
            device_id_type=MESH,
        )

    def from_line(source, target, sems, turn, whole=False):
        t = lax.rem(i + turn, n)
        return pltpu.make_async_remote_copy(
            src_ref=source if whole else source.at[t],
            dst_ref=target.at[t],
            send_sem=sems.at[0, t],
            recv_sem=sems.at[1, t],
            device_id=(d, t),
            device_id_type=MESH,
        )

    def to_plane(source, target, sems, flip):
        return pltpu.make_async_remote_copy(
            src_ref=source,
            dst_ref=target.at[d],
            send_sem=sems.at[0, flip],
            recv_sem=sems.at[1, flip],
            device_id=(d ^ flip, i),
            device_id_type=MESH,
        )

    def from_plane(source, target, sems, flip):
        return pltpu.make_async_remote_copy(
            src_ref=source,
            dst_ref=target.at[d ^ flip],
            send_sem=sems.at[0, flip],
            recv_sem=sems.at[1, flip],
            device_id=(d ^ flip, i),
            device_id_type=MESH,
        )

    for turn in range(1, n):
        to_line(shares, shares_all, share_sem, turn).start()

    mean = mean * (1.0 / width)
    for c, at in enumerate(tiles):
        v = x_own[:, at].astype(f32) * root
        u = sums.own_total(c) * (1.0 + table[i, 1:2, at])
        input_grad[:, at] = (d_middle[:, at] + root * (u - v * mean)).astype(low)
    shares_all[i] = shares[i]
    for turn in range(1, n):
        from_line(shares, shares_all, share_sem, turn).wait_recv()
    d_mod_all[d] = jnp.sum(shares_all[...], axis=0).astype(low).astype(f32)
    own_mod = d_mod_all.at[d]
    for flip in range(1, n_dp):
        to_plane(own_mod, d_mod_all, mod_sem, flip).start()
    for flip in range(1, n_dp):
        from_plane(own_mod, d_mod_all, mod_sem, flip).wait_recv()
    flat = d_mod_all[...].reshape(n_dp * images, own_cols).astype(low)
    terms[...] = mm_nt(flat, mod_w[...]).reshape(n_dp, images, k_rows)
    for turn in range(1, n):
        to_line(terms, terms_all, term_sem, turn, True).start()
    terms_all[i] = terms[...]
    for turn in range(1, n):
        from_line(terms, terms_all, term_sem, turn, True).wait_recv()
    noise_parts[...] = jnp.sum(terms_all[...], axis=0)
    for flip in range(1, n_dp):
        to_plane(noise_parts.at[d ^ flip], noise_sum, noise_sem, flip).start()
    noise_sum[d] = noise_parts[d]
    for flip in range(1, n_dp):
        from_plane(noise_parts.at[d ^ flip], noise_sum, noise_sem, flip).wait_recv()
    merge.landed_all()
    grad.landed_all()
    grad.finish()
    merge.finish()
    for turn in range(1, n):
        to_line(shares, shares_all, share_sem, turn).wait_send()
        to_line(terms, terms_all, term_sem, turn, True).wait_send()
    for flip in range(1, n_dp):
        to_plane(own_mod, d_mod_all, mod_sem, flip).wait_send()
        to_plane(noise_parts.at[d ^ flip], noise_sum, noise_sem, flip).wait_send()
    sums.all_sent()


def last(n, n_dp, operands, shapes, number, tile=512):
    (rows, width), wide, k_rows, own_cols, (merge_rows, merge_cols), images = shapes
    total, chips, pieces = n * rows, n_dp // 2, 2 * width // tile
    low, f32 = jnp.bfloat16, jnp.float32
    sds = jax.ShapeDtypeStruct
    return call(
        functools.partial(last_kernel, n, n_dp, tile),
        number,
        "last",
        [VMEM] * 3 + [pl.BlockSpec(memory_space=pltpu.SMEM)] + [HBM] * 6,
        [
            sds((rows, width), low),
            sds((n_dp, images, own_cols), f32),
            sds((n_dp, images, k_rows), f32),
            sds((plane_slots(n_dp), k_rows, wide), low),
            sds((plane_slots(n_dp), merge_rows, merge_cols), low),
        ],
        [VMEM] * 3 + [HBM] * 2,
        [
            pltpu.VMEM((total, width), low),
            pltpu.VMEM((rows, width), low),
            pltpu.VMEM((rows, width), f32),
            pltpu.VMEM((k_rows, own_cols), low),
            pltpu.VMEM((width, wide), low),
            pltpu.VMEM((total, width), low),
            pltpu.VMEM((total + rows, width), low),
            pltpu.VMEM((chips, k_rows, wide), low),
            pltpu.VMEM((chips, k_rows, wide), low),
            pltpu.VMEM((chips, k_rows, wide), low),
            pltpu.VMEM((k_rows, wide), low),
            pltpu.VMEM((chips, merge_rows, merge_cols), low),
            pltpu.VMEM((chips, merge_rows, merge_cols), low),
            pltpu.VMEM((merge_rows, merge_cols), low),
            pltpu.VMEM((8, width), f32),
            pltpu.VMEM((n, images, own_cols), f32),
            pltpu.VMEM((n, images, own_cols), f32),
            pltpu.VMEM((n_dp, images, k_rows), f32),
            pltpu.VMEM((n, n_dp, images, k_rows), f32),
            pltpu.VMEM((n_dp, images, k_rows), f32),
            DMA((n, pieces)),
            DMA((n + 1, pieces)),
            scatter_sems(n_dp),
            scatter_sems(n_dp),
            DMA((2, n)),
            DMA((2, n_dp)),
            DMA((2, n)),
            DMA((2, n_dp)),
            DMA((4,)),
            DMA((chips,)),
            DMA((width // tile,)),
        ],
        flops=4 * total * width * wide,
    )(*operands)


def final_kernel(
    noise_own,
    noise_all,
    d_mod,
    noise_sums,
    up_in,
    down_in,
    attend_in,
    block_in,
    input_in,
    merge_in,
    block_out,
    input_out,
    noise_grad,
    attend_out,
    merge_out,
    up_out,
    down_out,
    modulate_out,
    up_slots,
    down_slots,
    attend_slots,
    merge_slots,
    up_sum,
    down_sum,
    attend_sum,
    merge_sum,
    modulate,
    block,
    inputs,
    sems,
):
    low, f32 = jnp.bfloat16, jnp.float32
    loads = [
        pltpu.make_async_copy(source, target, sems.at[0, k])
        for k, (source, target) in enumerate(
            (
                (up_in, up_slots),
                (down_in, down_slots),
                (attend_in, attend_slots),
                (merge_in, merge_slots),
                (block_in, block),
                (input_in, inputs),
            )
        )
    ]
    stores = [
        pltpu.make_async_copy(source, target, sems.at[1, k])
        for k, (source, target) in enumerate(
            (
                (up_sum, up_out),
                (down_sum, down_out),
                (attend_sum, attend_out),
                (merge_sum, merge_out),
                (block, block_out),
                (inputs, input_out),
                (modulate, modulate_out),
            )
        )
    ]
    for load in loads:
        load.start()
    n_dp, images, k_rows = noise_all.shape
    left = noise_all[...].reshape(n_dp * images, k_rows).astype(low)
    right = d_mod[...].reshape(n_dp * images, -1).astype(low)
    modulate[...] = mm_tn(left, right)
    stores[6].start()
    for k in range(n_dp):
        at = slice(k * k_rows, (k + 1) * k_rows)
        v = noise_own[:, at].astype(f32)
        gate = 1.0 / (1.0 + jnp.exp(-v))
        noise_grad[:, at] = noise_sums[k] * (gate * (1.0 + v * (1.0 - gate)))

    def add(slots, total):
        count, height, wide = slots.shape
        chunk = math.gcd(height, 32 if wide > 512 else 256)

        def one(c, carry):
            at = pl.ds(pl.multiple_of(c * chunk, chunk), chunk)
            total[at, :] = sum(slots[s, at, :].astype(f32) for s in range(count))
            return carry

        lax.fori_loop(0, height // chunk, one, 0)

    for k, (slots, total) in enumerate(
        (
            (up_slots, up_sum),
            (down_slots, down_sum),
            (attend_slots, attend_sum),
            (merge_slots, merge_sum),
        )
    ):
        loads[k].wait()
        add(slots, total)
        stores[k].start()
    for k in range(4, 6):
        loads[k].wait()
        stores[k].start()
    for store in stores:
        store.wait()


def final(noise_own, noise_all, d_mod, noise_sums, up, down, attend, block, inputs, merge):
    sds, f32 = jax.ShapeDtypeStruct, jnp.float32
    own_cols, k_rows = d_mod.shape[2], noise_all.shape[2]
    sums = [sds(a.shape[1:], f32) for a in (up, down, attend, merge)]
    modulate = sds((k_rows, own_cols), f32)
    return pl.pallas_call(
        final_kernel,
        out_shape=[
            sds(block.shape, block.dtype),
            sds(inputs.shape, inputs.dtype),
            sds(noise_own.shape, f32),
            sums[2],
            sums[3],
            sums[0],
            sums[1],
            modulate,
        ],
        in_specs=[VMEM] * 4 + [HBM] * 6,
        out_specs=[HBM, HBM, VMEM] + [HBM] * 5,
        scratch_shapes=[
            pltpu.VMEM(a.shape, a.dtype)
            for a in (up, down, attend, merge, *sums, modulate, block, inputs)
        ]
        + [DMA((2, 7))],
        compiler_params=pltpu.CompilerParams(vmem_limit_bytes=60 * 1024 * 1024),
        name="final",
    )(noise_own, noise_all, d_mod, noise_sums, up, down, attend, block, inputs, merge)


def on_device(
    block_input,
    cotangent,
    noise_embed,
    image_sizes,
    attend_weight,
    merge_weight,
    up_weight,
    down_weight,
    modulate_weight,
):
    n = lax.axis_size("tensor")
    n_dp = lax.axis_size("dp")
    rows, width = block_input.shape
    tokens = n * rows
    images = image_sizes.shape[1]
    k_rows = modulate_weight.shape[0]

    (
        cot_full,
        hidden_first,
        packed,
        lse,
        attended,
        attn_out,
        middle,
        hidden_second,
        table,
        attend_full,
        merge_full,
        up_full,
        down_full,
        noise_all,
    ) = front(
        n,
        n_dp,
        block_input,
        cotangent,
        noise_embed,
        modulate_weight,
        image_sizes,
        attend_weight,
        merge_weight,
        up_weight,
        down_weight,
        0,
    )
    d_hidden_second, mlp_part, up_local, down_local = ffn(
        n, hidden_second, table, cot_full, up_full, down_full, 1
    )
    units = up_full.shape[1]
    wide = packed.shape[1]
    (
        block_output,
        d_middle,
        d_qkv,
        row_sums,
        merge_local,
        up_landed,
        down_landed,
    ) = back(
        n,
        n_dp,
        (
            d_hidden_second,
            middle,
            table,
            lse,
            image_sizes,
            cotangent,
            attn_out,
            attended,
            packed,
            mlp_part,
            merge_full,
            up_local,
            down_local,
        ),
        (block_input.shape, wide, units, k_rows, down_weight.shape[1], lse.shape[0]),
        2,
    )
    input_grad, d_mod_all, noise_sums, attend_landed, merge_landed = last(
        n,
        n_dp,
        (
            d_qkv,
            row_sums,
            table,
            image_sizes,
            hidden_first,
            block_input,
            d_middle,
            modulate_weight,
            merge_local,
            attend_full,
        ),
        (
            block_input.shape,
            wide,
            k_rows,
            modulate_weight.shape[1],
            merge_weight.shape,
            images,
        ),
        3,
    )

    return tuple(
        final(
            noise_embed,
            noise_all,
            d_mod_all,
            noise_sums,
            up_landed,
            down_landed,
            attend_landed,
            block_output,
            input_grad,
            merge_landed,
        )
    )


def solution(mesh):
    whole_rows = P(("dp", "tensor"), None)
    by_dp = P("dp", None)
    tall = P("dp", "tensor")
    wide = P("tensor", "dp")
    return jax.shard_map(
        on_device,
        mesh=mesh,
        in_specs=(whole_rows, whole_rows, by_dp, by_dp, tall, wide, tall, wide, tall),
        out_specs=(whole_rows, whole_rows, by_dp, tall, wide, tall, wide, tall),
        check_vma=False,
    )
```

```python
import functools
import math

import jax
import jax.numpy as jnp
from jax import lax
from jax.experimental import pallas as pl
from jax.experimental.pallas import tpu as pltpu
from jax.sharding import PartitionSpec as P

HEAD_DIM = 128
MASKED = -1e30


def dot(a, b, dims=(((1,), (0,)), ((), ()))):
    return lax.dot_general(a, b, dims, preferred_element_type=jnp.float32)


ROWS_ROWS = (((0,), (0,)), ((), ()))


MESH = pl.DeviceIdType.MESH
HBM = pl.BlockSpec(memory_space=pl.ANY)
VMEM = pl.BlockSpec(memory_space=pltpu.VMEM)
DMA = pltpu.SemaphoreType.DMA


def rows_of(j, rows):
    return pl.ds(pl.multiple_of(j * rows, rows), rows)


def beside(step):
    return (lax.axis_index("dp"), lax.axis_index("tensor") + step)


def greet_line(n, i):
    barrier = pltpu.get_barrier_semaphore()

    @pl.when(i > 0)
    def _():
        pl.semaphore_signal(barrier, inc=1, device_id=beside(-1), device_id_type=MESH)

    @pl.when(i < n - 1)
    def _():
        pl.semaphore_signal(barrier, inc=1, device_id=beside(1), device_id_type=MESH)

    pl.semaphore_wait(barrier, jnp.where(i > 0, 1, 0) + jnp.where(i < n - 1, 1, 0))


class LineGather:
    def __init__(self, n, i, rows, own, full, to_left, to_right, arrived):
        self.n, self.i, self.rows, self.own, self.full = n, i, rows, own, full
        self.to_left, self.to_right, self.arrived = to_left, to_right, arrived

    def copy(self, j, step, source=None):
        place = self.full.at[rows_of(j, self.rows)]
        return pltpu.make_async_remote_copy(
            src_ref=place if source is None else source,
            dst_ref=place,
            send_sem=(self.to_right if step > 0 else self.to_left).at[j],
            recv_sem=self.arrived.at[j],
            device_id=beside(step),
            device_id_type=MESH,
        )

    def start(self):
        @pl.when(self.i > 0)
        def _():
            self.copy(self.i, -1, self.own).start()

        @pl.when(self.i < self.n - 1)
        def _():
            self.copy(self.i, 1, self.own).start()

    def step(self, s):
        for side in (-1, 1):
            j = self.i + side * s
            there = (j >= 0) & (j < self.n)
            more = (self.i > 0) if side > 0 else (self.i < self.n - 1)

            @pl.when(there)
            def _():
                self.copy(j, side).wait_recv()

            @pl.when(there & more)
            def _():
                self.copy(j, -side).start()

    def finish(self):
        @pl.when(self.i > 0)
        def _():
            self.copy(self.i, -1, self.own).wait_send()

        @pl.when(self.i < self.n - 1)
        def _():
            self.copy(self.i, 1, self.own).wait_send()

        for j in range(self.n):

            @pl.when((j < self.i) & (self.i < self.n - 1))
            def _():
                self.copy(j, 1).wait_send()

            @pl.when((j > self.i) & (self.i > 0))
            def _():
                self.copy(j, -1).wait_send()


class LineScatter:
    def __init__(self, n, i, rows, width, part, got, sent, arrived):
        self.n, self.i, self.rows, self.width = n, i, rows, width
        self.part, self.got, self.sent, self.arrived = part, got, sent, arrived
        self.pieces = part.shape[1] // width

    def columns(self, c):
        if isinstance(c, int):
            return pl.ds(c * self.width, self.width)
        return pl.ds(pl.multiple_of(c * self.width, self.width), self.width)

    def copy(self, j, slot, c, step):
        return pltpu.make_async_remote_copy(
            src_ref=self.part.at[rows_of(j, self.rows), self.columns(c)],
            dst_ref=self.got.at[rows_of(slot, self.rows), self.columns(c)],
            send_sem=self.sent.at[j, c],
            recv_sem=self.arrived.at[slot, c],
            device_id=beside(step),
            device_id_type=MESH,
        )

    def slot_there(self, j, step):
        if step > 0:
            return j
        return jnp.where(j == self.i - 1, self.n, j)

    def at_end(self, j, c):
        @pl.when((self.i == 0) & (j > 0))
        def _():
            self.copy(j, j, c, 1).start()

        @pl.when((self.i == self.n - 1) & (j < self.i))
        def _():
            self.copy(j, self.slot_there(j, -1), c, -1).start()

    def pass_on(self, t, c, near):
        n, i = self.n, self.i
        rightward = (2 * i < n - 1) if near else (2 * i >= n - 1)
        j = jnp.where(rightward, t, n - 1 - t)
        step = jnp.where(rightward, 1, -1)
        right = rightward & (i > 0) & (j > i)
        left = jnp.logical_not(rightward) & (i < n - 1) & (j < i)

        @pl.when(right | left)
        def _():
            self.add(j, j, c)
            slot = jnp.where(left & (j == i - 1), n, j)
            self.copy(j, slot, c, step).start()

    def add(self, j, slot, c):
        self.copy(j, slot, c, 1).wait_recv()
        here = (rows_of(j, self.rows), self.columns(c))
        there = (rows_of(slot, self.rows), self.columns(c))
        total = self.part[here].astype(jnp.float32) + self.got[there].astype(jnp.float32)
        self.part[here] = total.astype(self.part.dtype)

    def own(self, c, out):
        i, n = self.i, self.n
        columns = self.columns(c)
        out[:, columns] = self.part[rows_of(i, self.rows), columns].astype(out.dtype)

        @pl.when(i > 0)
        def _():
            self.copy(i, i, c, 1).wait_recv()
            out[:, columns] += self.got[rows_of(i, self.rows), columns].astype(out.dtype)

        @pl.when(i < n - 1)
        def _():
            self.copy(i, n, c, -1).wait_recv()
            out[:, columns] += self.got[rows_of(n, self.rows), columns].astype(out.dtype)

    def own_value(self, c):
        i, n = self.i, self.n

        @pl.when(i > 0)
        def _():
            self.copy(i, i, c, 1).wait_recv()

        @pl.when(i < n - 1)
        def _():
            self.copy(i, n, c, -1).wait_recv()

        return self.own_total(c)

    def own_total(self, c):
        i, n, columns = self.i, self.n, self.columns(c)
        total = self.part[rows_of(i, self.rows), columns].astype(jnp.float32)
        left = self.got[rows_of(i, self.rows), columns].astype(jnp.float32)
        right = self.got[rows_of(n, self.rows), columns].astype(jnp.float32)
        return total + jnp.where(i > 0, left, 0.0) + jnp.where(i < n - 1, right, 0.0)

    def all_sent(self):
        def one(j, carry):
            @pl.when(j != self.i)
            def _():
                for c in range(self.pieces):
                    self.copy(j, 0, c, 1).wait_send()

            return carry

        lax.fori_loop(0, self.n, one, 0)


def mm(a, b):
    return lax.dot_general(a, b, (((1,), (0,)), ((), ())), preferred_element_type=jnp.float32)


def mm_nt(a, b):
    return lax.dot_general(a, b, (((1,), (1,)), ((), ())), preferred_element_type=jnp.float32)


def mm_tn(a, b):
    return lax.dot_general(a, b, (((0,), (0,)), ((), ())), preferred_element_type=jnp.float32)


def call(kernel, collective_id, name, in_specs, outs, out_specs, scratch, flops=0, limit=60):
    return pl.pallas_call(
        kernel,
        out_shape=outs,
        in_specs=in_specs,
        out_specs=out_specs,
        scratch_shapes=scratch,
        compiler_params=pltpu.CompilerParams(
            collective_id=collective_id,
            has_side_effects=True,
            vmem_limit_bytes=limit * 1024 * 1024,
        ),
        cost_estimate=pl.CostEstimate(flops=flops, bytes_accessed=1 << 20, transcendentals=0),
        name=name,
    )


def ffn_kernel(
    n,
    tile,
    grad_tile,
    own_hidden,
    table,
    d_mlp_hbm,
    up_hbm,
    down_hbm,
    d_hidden,
    mlp_part,
    up_grad,
    down_grad,
    up,
    down,
    d_mlp,
    hidden,
    activated,
    d_pre,
    part,
    got,
    stage,
    mlp,
    to_left,
    to_right,
    arrived,
    sent,
    came,
    local,
    stage_sem,
):
    i = lax.axis_index("tensor")
    rows, width = own_hidden.shape
    units = up.shape[1]
    loads = [
        pltpu.make_async_copy(source, target, local.at[k])
        for k, (source, target) in enumerate(((up_hbm, up), (d_mlp_hbm, d_mlp), (down_hbm, down)))
    ]
    for load in loads:
        load.start()
    greet_line(n, i)
    line = LineGather(n, i, rows, own_hidden, hidden, to_left, to_right, arrived)
    first_core = lax.rem(lax.axis_index("dp"), 2) == 0
    pl.when(first_core)(line.start)
    piece = tile // 2
    sums = LineScatter(n, i, rows, piece, part, got, sent, came)
    hidden[rows_of(i, rows), :] = own_hidden[...]
    for load in loads:
        load.wait()

    def one_block(j):
        here = rows_of(j, rows)

        def gated(c, carry):
            at = pl.ds(pl.multiple_of(c * tile, tile), tile)
            d_mlp[here, at] = (d_mlp[here, at].astype(jnp.float32) * table[j, 5:6, at]).astype(
                jnp.bfloat16
            )
            return carry

        lax.fori_loop(0, width // tile, gated, 0)

        def first(c, carry):
            at = pl.ds(pl.multiple_of(c * tile, tile), tile)
            pre = mm(hidden[here, :], up[:, at])
            d_act = mm_nt(d_mlp[here, :], down[at, :])
            cdf = 0.5 * (1.0 + lax.erf(pre * (0.5**0.5)))
            density = jnp.exp(-0.5 * pre * pre) * ((0.5 / math.pi) ** 0.5)
            activated[here, at] = (pre * cdf).astype(jnp.bfloat16)
            d_pre[here, at] = (d_act * (cdf + pre * density)).astype(jnp.bfloat16)
            return carry

        lax.fori_loop(0, units // tile, first, 0)

        def second(c, carry):
            at = pl.ds(pl.multiple_of(c * tile, tile), tile)
            part[here, at] = mm_nt(d_pre[here, :], up[at, :]).astype(jnp.bfloat16)
            for k in range(tile // piece):
                sums.at_end(j, c * (tile // piece) + k)
            return carry

        lax.fori_loop(0, width // tile, second, 0)

        def third(c, carry):
            at = pl.ds(pl.multiple_of(c * tile, tile), tile)
            mlp[here, at] = mm(activated[here, :], down[:, at]).astype(jnp.bfloat16)
            return carry

        lax.fori_loop(0, width // tile, third, 0)

    def visit(q, carry):
        s = (q + 1) // 2
        side = 1 - 2 * (q % 2)
        j = i + s * side

        @pl.when(q % 2 == 1)
        def _():
            line.step(s)

        @pl.when((j >= 0) & (j < n))
        def _():
            one_block(j)

        @pl.when((q == 0) & jnp.logical_not(first_core))
        def _():
            line.start()

        return carry

    lax.fori_loop(0, 2 * n - 1, visit, 0)
    keep_mlp = pltpu.make_async_copy(mlp, mlp_part, local.at[3])
    keep_mlp.start()

    count = (width // grad_tile) * (units // grad_tile)
    turns = 2 * max(n - 2, 1) * sums.pieces
    per_turn = -(-2 * count // turns)

    def square(ref, row, column):
        return ref.at[
            pl.ds(pl.multiple_of(row * grad_tile, grad_tile), grad_tile),
            pl.ds(pl.multiple_of(column * grad_tile, grad_tile), grad_tile),
        ]

    def put(slot, target):
        return pltpu.make_async_copy(stage.at[slot], target, stage_sem.at[slot])

    def one_grad(k, left, right, target):
        wide = right.shape[1] // grad_tile
        row, column = k // wide, k % wide
        slot = k % 2

        @pl.when(k >= 2)
        def _():
            put(slot, square(target, 0, 0)).wait()

        a = left[:, pl.ds(pl.multiple_of(row * grad_tile, grad_tile), grad_tile)]
        b = right[:, pl.ds(pl.multiple_of(column * grad_tile, grad_tile), grad_tile)]
        stage[slot] = mm_tn(a, b).astype(jnp.bfloat16)
        put(slot, square(target, row, column)).start()

    def tail(k, carry):
        t, c = 2 + k // (2 * sums.pieces), k % sums.pieces
        for near in (True, False):

            @pl.when((k // sums.pieces) % 2 == (0 if near else 1))
            def _():
                sums.pass_on(t, c, near)

        for extra in range(per_turn):
            item = k * per_turn + extra

            @pl.when(item < count)
            def _():
                one_grad(item, hidden, d_pre, up_grad)

            @pl.when(item == count)
            def _():
                for slot in range(2):
                    put(slot, square(up_grad, 0, 0)).wait()

            @pl.when((item >= count) & (item < 2 * count))
            def _():
                one_grad(item - count, activated, d_mlp, down_grad)

        return carry

    lax.fori_loop(0, turns, tail, 0)
    for slot in range(2):
        put(slot, square(down_grad, 0, 0)).wait()
    for c in range(sums.pieces):
        sums.own(c, d_hidden)
    line.finish()
    sums.all_sent()
    keep_mlp.wait()


def ffn(n, own_hidden, table, cotangents, up, down, collective_id, tile=512, grad_tile=512):
    rows, width = own_hidden.shape
    units = up.shape[1]
    pieces = 2 * width // tile
    low = jnp.bfloat16
    return call(
        functools.partial(ffn_kernel, n, tile, grad_tile),
        collective_id,
        "ffn",
        [VMEM, VMEM, HBM, HBM, HBM],
        [
            jax.ShapeDtypeStruct((rows, width), jnp.float32),
            jax.ShapeDtypeStruct((n * rows, width), low),
            jax.ShapeDtypeStruct((width, units), low),
            jax.ShapeDtypeStruct((units, width), low),
        ],
        [VMEM, HBM, HBM, HBM],
        [
            pltpu.VMEM((width, units), low),
            pltpu.VMEM((units, width), low),
            pltpu.VMEM((n * rows, width), low),
            pltpu.VMEM((n * rows, width), low),
            pltpu.VMEM((n * rows, units), low),
            pltpu.VMEM((n * rows, units), low),
            pltpu.VMEM((n * rows, width), low),
            pltpu.VMEM(((n + 1) * rows, width), low),
            pltpu.VMEM((2, grad_tile, grad_tile), low),
            pltpu.VMEM((n * rows, width), low),
            DMA((n,)),
            DMA((n,)),
            DMA((n,)),
            DMA((n, pieces)),
            DMA((n + 1, pieces)),
            DMA((4,)),
            DMA((2,)),
        ],
        flops=12 * n * rows * width * units,
    )(own_hidden, table, cotangents, up, down)


def image_at(sizes, place):
    end, count = 0, 0
    for k in range(sizes.shape[1]):
        end = end + sizes[0, k]
        count = count + jnp.where(place >= end, 1, 0)
    return count


def image_at(sizes, place):
    end, count = 0, 0
    for k in range(sizes.shape[1]):
        end = end + sizes[0, k]
        count = count + jnp.where(place >= end, 1, 0)
    return count


class PlaneGather:
    def __init__(self, n_dp, d, own, view, height, sent, came):
        self.n_dp, self.d, self.own, self.view, self.height = n_dp, d, own, view, height
        self.sent, self.came = sent, came
        self.square = n_dp == 8
        self.peers = [2 * k for k in range(1, n_dp // 2)]

    def copy(self, k, source, target, peer):
        return pltpu.make_async_remote_copy(
            src_ref=source,
            dst_ref=target,
            send_sem=self.sent.at[k],
            recv_sem=self.came.at[k],
            device_id=(self.d ^ peer, lax.axis_index("tensor")),
            device_id_type=MESH,
        )

    def slab(self, flip, half=None):
        if half is None:
            return self.view(self.d ^ flip, 0, self.height)
        return self.view(self.d ^ flip, half * (self.height // 2), self.height // 2)

    def owns(self):
        peers = [2, 4] if self.square else self.peers
        return [
            self.copy(k, self.own, self.slab(0), peer) for k, peer in enumerate([1] + peers)
        ]

    def relay_of(self, k):
        flip, half, peer = ((2, 0, 4), (4, 1, 2))[k - 1]
        return self.copy(2 + k, self.slab(flip, half), self.slab(flip, half), peer)

    def across(self):
        return [
            self.copy(3, self.slab(6, 0), self.slab(6, 0), 4),
            self.copy(4, self.slab(6, 1), self.slab(6, 1), 2),
        ]

    def hand(self, flip):
        base = 5 if self.square else len(self.peers) + 1
        k = base + flip // 2 - 1
        return self.copy(k, self.slab(flip), self.slab(flip), 1)

    def handed(self, flip):
        base = 5 if self.square else len(self.peers) + 1
        k = base + flip // 2 - 1
        return self.copy(k, self.slab(flip ^ 1), self.slab(flip ^ 1), 1)

    def start(self):
        for copy in self.owns():
            copy.start()

    def relay(self):
        if not self.square:
            return
        for k, flip in ((1, 2), (2, 4)):
            self.copy(k, self.own, self.slab(flip), flip).wait_recv()
            self.relay_of(k).start()
            self.hand(flip).start()

    def close(self):
        if self.square:
            for copy in self.across():
                copy.wait_recv()
            self.hand(6).start()
        else:
            for k, flip in enumerate(self.peers):
                self.copy(k + 1, self.own, self.slab(flip), flip).wait_recv()
                self.hand(flip).start()
        self.copy(0, self.own, self.slab(1), 1).wait_recv()
        for flip in self.peers:
            self.handed(flip).wait_recv()

    def finish(self):
        for copy in self.owns():
            copy.wait_send()
        if self.square:
            for k in (1, 2):
                self.relay_of(k).wait_send()
        for flip in self.peers:
            self.hand(flip).wait_send()


def plane_sems(n_dp):
    return 8 if n_dp == 8 else n_dp - 1


def greet_all(n, n_dp, d, i):
    barrier = pltpu.get_barrier_semaphore()
    for flip in range(1, n_dp):
        pl.semaphore_signal(barrier, inc=1, device_id=(d ^ flip, i), device_id_type=MESH)
    for turn in range(1, n):
        pl.semaphore_signal(
            barrier, inc=1, device_id=(d, lax.rem(i + turn, n)), device_id_type=MESH
        )
    pl.semaphore_wait(barrier, n_dp + n - 2)


def front_kernel(
    n,
    n_dp,
    heads,
    tile,
    x_own,
    cot_own,
    noise_own,
    mod_w,
    sizes,
    attend_w,
    merge_w,
    up_w,
    down_w,
    cot_full,
    hidden_out,
    qkv_out,
    lse,
    attended_out,
    attn_out_hbm,
    middle_out,
    second_out,
    table,
    attend_full,
    merge_full,
    up_full,
    down_full,
    noise_all,
    x_full,
    attend,
    merge,
    noise,
    hidden,
    qkv,
    attended,
    att_rows,
    attn_out,
    middle,
    hidden_second,
    terms,
    terms_all,
    columns,
    noise_sem,
    terms_sem,
    column_sem,
    x_sem,
    cot_sem,
    merge_sem,
    weight_sent,
    weight_came,
    out_sem,
    att_sem,
    local,
):
    d, i = lax.axis_index("dp"), lax.axis_index("tensor")
    rows, width = x_own.shape
    k_rows, own_cols = mod_w.shape
    head_cols = heads * HEAD_DIM
    low, f32 = jnp.bfloat16, jnp.float32
    merge_rows, merge_cols = merge_w.shape
    down_cols = down_w.shape[1]
    merge_slab = merge.at[:, pl.ds(pl.multiple_of(d * merge_cols, merge_cols), merge_cols)]

    def row_view(full, height):
        return lambda at, start, count: full.at[
            pl.ds(pl.multiple_of(at * height + start, 16), count), :
        ]

    def column_view(full, wide):
        return lambda at, start, count: full.at[
            pl.ds(start, count), pl.ds(pl.multiple_of(at * wide, wide), wide)
        ]

    weights = [
        PlaneGather(n_dp, d, own, view, height, weight_sent.at[k], weight_came.at[k])
        for k, (own, view, height) in enumerate(
            (
                (attend_w, row_view(attend, k_rows), k_rows),
                (merge_slab, column_view(merge, merge_cols), n * merge_rows),
                (up_w, row_view(up_full, k_rows), k_rows),
                (down_w, column_view(down_full, down_cols), down_w.shape[0]),
            )
        )
    ]
    attend_g, merge_g, up_g, down_g = weights
    copies = [
        pltpu.make_async_copy(source, target, local.at[k])
        for k, (source, target) in enumerate(
            (
                (attend_w, attend_g.slab(0)),
                (merge_w, merge_slab.at[rows_of(i, merge_rows)]),
                (cot_own, cot_full.at[rows_of(i, rows)]),
                (up_w, up_g.slab(0)),
                (down_w, down_g.slab(0)),
            )
        )
    ]
    for copy in copies:
        copy.start()
    greet_all(n, n_dp, d, i)

    def to_plane(source, target, sems, flip):
        return pltpu.make_async_remote_copy(
            src_ref=source.at[d ^ flip],
            dst_ref=target.at[d],
            send_sem=sems.at[0, flip],
            recv_sem=sems.at[1, flip],
            device_id=(d ^ flip, i),
            device_id_type=MESH,
        )

    def from_plane(target, sems, flip):
        return pltpu.make_async_remote_copy(
            src_ref=target.at[d ^ flip],
            dst_ref=target.at[d ^ flip],
            send_sem=sems.at[0, flip],
            recv_sem=sems.at[1, flip],
            device_id=(d ^ flip, i),
            device_id_type=MESH,
        )

    for k in range(n_dp):
        v = noise_own[:, k * k_rows : (k + 1) * k_rows].astype(f32)
        noise[k] = (v * (1.0 / (1.0 + jnp.exp(-v)))).astype(low).astype(f32)
    for flip in range(1, n_dp):
        to_plane(noise, noise_all, noise_sem, flip).start()
    merge_line = LineGather(
        n, i, merge_rows, merge_w, merge_slab, merge_sem.at[0], merge_sem.at[1], merge_sem.at[2]
    )
    x_line = LineGather(n, i, rows, x_own, x_full, x_sem.at[0], x_sem.at[1], x_sem.at[2])
    cot_line = LineGather(
        n, i, rows, cot_own, cot_full, cot_sem.at[0], cot_sem.at[1], cot_sem.at[2]
    )
    x_line.start()
    noise_all[d] = noise[d]
    x_full[rows_of(i, rows), :] = x_own[...]
    for flip in range(1, n_dp):
        from_plane(noise_all, noise_sem, flip).wait_recv()
    pictures = noise.shape[1]
    images = noise_all[...].reshape(n_dp * pictures, k_rows).astype(low)
    for c in range(own_cols // tile):
        terms[:, :, c * tile : (c + 1) * tile] = mm(
            images, mod_w[:, c * tile : (c + 1) * tile]
        ).reshape(n_dp, pictures, tile)
    for flip in range(1, n_dp):
        to_plane(terms, terms_all, terms_sem, flip).start()
    attend_g.start()
    terms_all[d] = terms[d]
    for flip in range(1, n_dp):
        from_plane(terms_all, terms_sem, flip).wait_recv()
    columns[i] = jnp.sum(terms_all[...], axis=0)

    def to_line(turn):
        t = lax.rem(i + turn, n)
        return pltpu.make_async_remote_copy(
            src_ref=columns.at[i],
            dst_ref=columns.at[i],
            send_sem=column_sem.at[0, t],
            recv_sem=column_sem.at[1, i],
            device_id=(d, t),
            device_id_type=MESH,
        )

    def from_line(turn):
        t = lax.rem(i + turn, n)
        return pltpu.make_async_remote_copy(
            src_ref=columns.at[t],
            dst_ref=columns.at[t],
            send_sem=column_sem.at[0, t],
            recv_sem=column_sem.at[1, t],
            device_id=(d, t),
            device_id_type=MESH,
        )

    for turn in range(1, n):
        to_line(turn).start()
    merge_line.start()
    x_line.step(1)
    for turn in range(1, n):
        from_line(turn).wait_recv()
    unit = math.gcd(width, own_cols)

    def fill(j, carry):
        image = image_at(sizes, j * rows)
        for number in range(6):
            for start in range(0, width, unit):
                at = number * width + start
                here = slice(at % own_cols, at % own_cols + unit)
                table[j, number : number + 1, start : start + unit] = sum(
                    columns[at // own_cols, k : k + 1, here] * jnp.where(image == k, 1.0, 0.0)
                    for k in range(pictures)
                )
        return carry

    lax.fori_loop(0, n, fill, 0)
    attend_g.relay()
    merge_line.step(1)
    for copy in copies[:2]:
        copy.wait()
    attend_g.close()
    up_g.start()
    keep_attend = pltpu.make_async_copy(attend, attend_full, out_sem.at[0])
    keep_merge = pltpu.make_async_copy(
        merge.at[rows_of(i, merge_rows)], merge_full, out_sem.at[1]
    )
    keep_attend.start()
    keep_hidden = pltpu.make_async_copy(hidden, hidden_out, out_sem.at[2])
    keep_qkv = pltpu.make_async_copy(qkv, qkv_out, out_sem.at[3])

    def tiles(count):
        return [slice(c * tile, (c + 1) * tile) for c in range(count // tile)]

    def one_block(j):
        here = rows_of(j, rows)
        squares = jnp.zeros((rows, 1), f32)
        for at in tiles(width):
            v = x_full[here, at].astype(f32)
            squares += jnp.sum(v * v, axis=1, keepdims=True)
        root = lax.rsqrt(squares * (1.0 / width) + 1e-06)
        for at in tiles(width):
            v = x_full[here, at].astype(f32) * root
            hidden[here, at] = (v * (1.0 + table[j, 1:2, at]) + table[j, 0:1, at]).astype(low)
        wide = qkv.shape[1]
        step = math.gcd(wide, 512)
        for c in range(wide // step):
            at = slice(c * step, (c + 1) * step)
            qkv[here, at] = mm(hidden[here, :], attend[:, at]).astype(low)

    def visit(q, carry):
        s = (q + 1) // 2
        side = 1 - 2 * (q % 2)
        j = i + s * side

        @pl.when((q % 2 == 1) & (s + 1 < n))
        def _():
            x_line.step(s + 1)
            merge_line.step(s + 1)

        @pl.when(q == 2 * n - 5)
        def _():
            up_g.relay()
            merge_g.start()
            cot_line.start()

        @pl.when((j >= 0) & (j < n))
        def _():
            one_block(j)

        return carry

    lax.fori_loop(0, 2 * n - 1, visit, 0)

    keep_hidden.start()
    keep_qkv.start()

    area = min(256, n * rows)
    areas = n * rows // area
    owners = area // rows
    area_images = [image_at(sizes, b * area) for b in range(areas)]

    def to_owner(j):
        return pltpu.make_async_remote_copy(
            src_ref=attended.at[rows_of(j, rows), :],
            dst_ref=att_rows.at[:, pl.ds(pl.multiple_of(i * head_cols, head_cols), head_cols)],
            send_sem=att_sem.at[0, j],
            recv_sem=att_sem.at[1, i],
            device_id=(d, j),
            device_id_type=MESH,
        )

    def from_source(t):
        return pltpu.make_async_remote_copy(
            src_ref=attended.at[rows_of(t, rows), :],
            dst_ref=att_rows.at[:, pl.ds(pl.multiple_of(t * head_cols, head_cols), head_cols)],
            send_sem=att_sem.at[0, t],
            recv_sem=att_sem.at[1, t],
            device_id=(d, t),
            device_id_type=MESH,
        )

    def attend_area(turn, carry):
        here_at = lax.rem(i // owners + 1 + turn, areas)
        here = rows_of(here_at, area)
        image = image_at(sizes, here_at * area)
        for h in range(heads):
            first = h * 3 * HEAD_DIM
            q = qkv[here, first : first + HEAD_DIM]
            parts = []
            for b in range(areas):
                key = qkv[b * area : (b + 1) * area, first + HEAD_DIM : first + 2 * HEAD_DIM]
                parts.append(
                    mm_nt(key, q) * HEAD_DIM ** (-0.5)
                    + jnp.where(image == area_images[b], 0.0, MASKED)
                )
            highest = parts[0].max(axis=0, keepdims=True)
            for part in parts[1:]:
                highest = jnp.maximum(highest, part.max(axis=0, keepdims=True))
            parts = [jnp.exp(part - highest) for part in parts]
            totals = sum(jnp.sum(part, axis=0, keepdims=True) for part in parts)
            inverse = 1.0 / totals
            out = jnp.zeros((HEAD_DIM, area), f32)
            for b in range(areas):
                value = qkv[b * area : (b + 1) * area, first + 2 * HEAD_DIM : first + 3 * HEAD_DIM]
                out += mm_tn(value, (parts[b] * inverse).astype(low))
            attended[here, h * HEAD_DIM : (h + 1) * HEAD_DIM] = out.T.astype(low)
            lse[pl.ds(here_at * heads + h, 1), :] = highest + jnp.log(totals)
        for k in range(owners):
            j = here_at * owners + k

            @pl.when(j != i)
            def _():
                to_owner(j).start()

        @pl.when(turn == (areas - 1) // 2)
        def _():
            up_g.close()
            cot_line.step(1)

        @pl.when(turn == areas - 1)
        def _():
            merge_g.relay()
            down_g.start()

        return carry

    lax.fori_loop(0, areas, attend_area, 0)
    att_rows[:, pl.ds(pl.multiple_of(i * head_cols, head_cols), head_cols)] = attended[
        rows_of(i, rows), :
    ]
    if n > 2:
        cot_line.step(2)
    merge_g.close()
    keep_merge.start()
    for turn in range(1, n):
        from_source(lax.rem(i + turn, n)).wait_recv()
    squares = jnp.zeros((rows, 1), f32)
    for at in tiles(width):
        out = mm(att_rows[...], merge[:, at])
        attn_out[:, at] = out
        v = x_own[:, at].astype(f32) + table[i, 2:3, at] * out
        middle[:, at] = v
        squares += jnp.sum(v * v, axis=1, keepdims=True)
    root = lax.rsqrt(squares * (1.0 / width) + 1e-06)
    for at in tiles(width):
        v = middle[:, at] * root
        hidden_second[:, at] = (v * (1.0 + table[i, 4:5, at]) + table[i, 3:4, at]).astype(low)
    keeps = [
        pltpu.make_async_copy(source, target, out_sem.at[4 + k])
        for k, (source, target) in enumerate(
            (
                (attended, attended_out),
                (attn_out, attn_out_hbm),
                (middle, middle_out),
                (hidden_second, second_out),
            )
        )
    ]
    for keep in keeps:
        keep.start()
    down_g.relay()
    for s in range(3, n):
        cot_line.step(s)
    down_g.close()
    for copy in copies[2:]:
        copy.wait()
    keep_attend.wait()
    keep_merge.wait()
    keep_hidden.wait()
    keep_qkv.wait()
    for keep in keeps:
        keep.wait()
    for flip in range(1, n_dp):
        to_plane(noise, noise_all, noise_sem, flip).wait_send()
        to_plane(terms, terms_all, terms_sem, flip).wait_send()
    for line in (merge_line, x_line, cot_line):
        line.finish()
    for turn in range(1, n):
        to_line(turn).wait_send()
    for turn in range(1, n):
        to_owner(lax.rem(i + turn, n)).wait_send()
    for weight in weights:
        weight.finish()


def front(n, n_dp, x, cot, noise, mod_w, sizes, attend_w, merge_w, up_w, down_w, number):
    rows, width = x.shape
    k_rows, own_cols = mod_w.shape
    wide = attend_w.shape[1]
    heads = wide // (3 * HEAD_DIM)
    total = n * rows
    areas = total // min(256, total)
    pictures = noise.shape[0]
    low, f32 = jnp.bfloat16, jnp.float32
    sds = jax.ShapeDtypeStruct
    count = plane_sems(n_dp)
    return call(
        functools.partial(front_kernel, n, n_dp, heads, 512),
        number,
        "front",
        [VMEM, HBM, VMEM, VMEM, pl.BlockSpec(memory_space=pltpu.SMEM), VMEM, VMEM, HBM, HBM],
        [
            sds((total, width), low),
            sds((total, width), low),
            sds((total, wide), low),
            sds((areas * heads, total // areas), f32),
            sds((total, heads * HEAD_DIM), low),
            sds((rows, width), f32),
            sds((rows, width), f32),
            sds((rows, width), low),
            sds((n, 8, width), f32),
            sds((n_dp * k_rows, wide), low),
            sds((merge_w.shape[0], width), low),
            sds((n_dp * k_rows, up_w.shape[1]), low),
            sds((down_w.shape[0], n_dp * down_w.shape[1]), low),
            sds((n_dp, pictures, k_rows), f32),
        ],
        [HBM] * 3 + [VMEM] + [HBM] * 4 + [VMEM] + [HBM] * 4 + [VMEM],
        [
            pltpu.VMEM((total, width), low),
            pltpu.VMEM((n_dp * k_rows, wide), low),
            pltpu.VMEM((n * merge_w.shape[0], n_dp * merge_w.shape[1]), low),
            pltpu.VMEM((n_dp, pictures, k_rows), f32),
            pltpu.VMEM((total, width), low),
            pltpu.VMEM((total, wide), low),
            pltpu.VMEM((total, heads * HEAD_DIM), low),
            pltpu.VMEM((rows, width), low),
            pltpu.VMEM((rows, width), f32),
            pltpu.VMEM((rows, width), f32),
            pltpu.VMEM((rows, width), low),
            pltpu.VMEM((n_dp, pictures, own_cols), f32),
            pltpu.VMEM((n_dp, pictures, own_cols), f32),
            pltpu.VMEM((n, pictures, own_cols), f32),
            DMA((2, n_dp)),
            DMA((2, n_dp)),
            DMA((3, n)),
            DMA((3, n)),
            DMA((3, n)),
            DMA((3, n)),
            DMA((4, count)),
            DMA((4, count)),
            DMA((8,)),
            DMA((2, n)),
            DMA((5,)),
        ],
        flops=2 * total * width * wide,
    )(x, cot, noise, mod_w, sizes, attend_w, merge_w, up_w, down_w)


class PlaneScatter:
    def __init__(self, n_dp, d, theirs, own, swapped, via, landed, sems):
        self.chips, self.d, self.square = n_dp // 2, d, n_dp == 8
        self.chip, self.side = d // 2, lax.rem(d, 2)
        self.theirs, self.own, self.swapped, self.via = theirs, own, swapped, via
        self.landed, self.sems = landed, sems

    def remote(self, source, target, sent, came, device):
        return pltpu.make_async_remote_copy(
            src_ref=source,
            dst_ref=target,
            send_sem=sent,
            recv_sem=came,
            device_id=(device, lax.axis_index("tensor")),
            device_id_type=MESH,
        )

    def swap(self, m):
        return self.remote(
            self.theirs(m), self.swapped.at[m], self.sems.at[0, m], self.sems.at[1, m], self.d ^ 1
        )

    def half(self, ref, which):
        height = self.own.shape[1] // 2
        return ref.at[pl.ds(which * height, height), :]

    def step(self, k):
        slab, which, peer = ((1, 0, 1), (3, 0, 1), (2, 1, 2), (3, 1, 2), (2, 0, 2), (1, 1, 1))[k]
        target = self.via if slab == 3 else self.landed.at[1 if k < 4 else 2]
        return self.remote(
            self.half(self.own.at[self.chip ^ slab], which),
            self.half(target, which),
            self.sems.at[2, k],
            self.sems.at[3, k],
            2 * (self.chip ^ peer) + self.side,
        )

    def send(self, m, slot, sem):
        return self.remote(
            self.own.at[m],
            self.landed.at[slot],
            self.sems.at[2, m],
            self.sems.at[3, sem],
            2 * m + self.side,
        )

    def keep(self):
        slot = 0 if self.square else self.chip
        return pltpu.make_async_copy(
            self.own.at[self.chip], self.landed.at[slot], self.sems.at[2, 6 if self.square else self.chip]
        )

    def swap_all(self):
        def one(m, carry):
            self.swap(m).start()
            return carry

        lax.fori_loop(0, self.chips, one, 0)

    def add(self, target, source):
        height, wide = target.shape
        chunk = math.gcd(height, 64 if wide > 512 else 256)

        def one(c, carry):
            at = pl.ds(pl.multiple_of(c * chunk, chunk), chunk)
            total = target[at, :].astype(jnp.float32) + source[at, :].astype(jnp.float32)
            target[at, :] = total.astype(target.dtype)
            return carry

        lax.fori_loop(0, height // chunk, one, 0)

    def add_and_send(self):
        def one(k, carry):
            m = self.chip ^ (self.chips - 1 - k)
            self.swap(m).wait_recv()
            self.add(self.own.at[m], self.swapped.at[m])
            if not self.square:

                @pl.when(m != self.chip)
                def _():
                    self.send(m, self.chip, self.chip).start()

            return carry

        lax.fori_loop(0, self.chips, one, 0)
        if self.square:
            for k in (1, 3, 0, 2):
                self.step(k).start()
        self.keep().start()

    def relay(self):
        if self.square:
            for k, slab, which in ((1, 2, 0), (3, 1, 1)):
                self.step(k).wait_recv()
                self.step(k).wait_send()
                self.add(self.half(self.own.at[self.chip ^ slab], which), self.half(self.via, which))
                self.step(4 if k == 1 else 5).start()

    def landed_all(self):
        if self.square:
            for k in (0, 2, 4, 5):
                self.step(k).wait_recv()
        else:
            for k in range(1, self.chips):
                self.send(self.chip ^ k, self.chip ^ k, self.chip ^ k).wait_recv()
        self.keep().wait()

    def finish(self):
        for m in range(self.chips):
            self.swap(m).wait_send()
        if self.square:
            for k in (0, 2, 4, 5):
                self.step(k).wait_send()
        else:
            for k in range(1, self.chips):
                self.send(self.chip ^ k, self.chip, self.chip).wait_send()


def plane_slots(n_dp):
    return 3 if n_dp == 8 else n_dp // 2


def scatter_sems(n_dp):
    return DMA((4, max(7, n_dp // 2)))


def flows(n, pieces, sums, turn):
    far, rest = turn // ((n - 2) * pieces), lax.rem(turn, (n - 2) * pieces)
    t, c = n - 1 - rest // pieces, lax.rem(rest, pieces)
    for near in (True, False):

        @pl.when(far == (0 if near else 1))
        def _():
            sums.pass_on(t, c, near)


def back_kernel(
    n,
    n_dp,
    heads,
    tile,
    d_hidden,
    middle,
    table,
    lse,
    sizes,
    cot_hbm,
    out_hbm,
    rows_hbm,
    qkv_hbm,
    mlp_hbm,
    merge_hbm,
    up_hbm,
    down_hbm,
    block_out,
    d_middle_out,
    d_qkv_out,
    sums_out,
    merge_grad,
    up_landed,
    down_landed,
    cot,
    attn_out,
    d_middle,
    d_qkv,
    attended,
    qkv,
    part,
    got,
    merge,
    d_att,
    d_attn,
    d_keys,
    d_values,
    up_own,
    up_swapped,
    up_via,
    down_own,
    down_swapped,
    down_via,
    stage,
    mlp_sent,
    mlp_came,
    up_sems,
    down_sems,
    line_sem,
    merge_sem,
    load_sem,
    stage_sem,
    own_sem,
):
    d, i = lax.axis_index("dp"), lax.axis_index("tensor")
    rows, width = middle.shape
    low, f32 = jnp.bfloat16, jnp.float32
    head_cols = heads * HEAD_DIM
    chips = n_dp // 2
    k_rows, down_cols = up_own.shape[1], down_own.shape[2]
    side = lax.rem(d, 2)

    def up_slab(at):
        return up_hbm.at[pl.ds(pl.multiple_of(at * k_rows, k_rows), k_rows), :]

    def down_slab(at):
        return down_hbm.at[:, pl.ds(pl.multiple_of(at * down_cols, down_cols), down_cols)]

    load_mlp = pltpu.make_async_copy(mlp_hbm, part, load_sem.at[0])
    load_mlp.start()
    load_cot = pltpu.make_async_copy(cot_hbm, cot, load_sem.at[3])
    load_out = pltpu.make_async_copy(out_hbm, attn_out, load_sem.at[4])
    load_cot.start()
    load_out.start()
    load_rows = pltpu.make_async_copy(rows_hbm, attended, load_sem.at[1])
    load_qkv = pltpu.make_async_copy(qkv_hbm, qkv, load_sem.at[2])

    load_merge = pltpu.make_async_copy(merge_hbm, merge, merge_sem)
    load_merge.start()
    for m in range(chips):
        pltpu.make_async_copy(up_slab(2 * m + side), up_own.at[m], own_sem.at[0, m]).start()
        pltpu.make_async_copy(down_slab(2 * m + side), down_own.at[m], own_sem.at[1, m]).start()
    load_rows.start()
    load_qkv.start()
    greet_all(n, n_dp, d, i)
    up = PlaneScatter(
        n_dp, d, lambda m: up_slab(2 * m + 1 - side), up_own, up_swapped, up_via, up_landed, up_sems
    )
    down = PlaneScatter(
        n_dp,
        d,
        lambda m: down_slab(2 * m + 1 - side),
        down_own,
        down_swapped,
        down_via,
        down_landed,
        down_sems,
    )
    up.swap_all()
    down.swap_all()
    load_mlp.wait()
    piece = tile // 2
    sums = LineScatter(n, i, rows, piece, part, got, mlp_sent, mlp_came)
    pieces = sums.pieces

    def ends(k, carry):
        t, c = n - 1 - k // pieces, lax.rem(k, pieces)
        pl.when(i == 0)(functools.partial(sums.at_end, t, c))
        pl.when(i == n - 1)(functools.partial(sums.at_end, n - 1 - t, c))
        return carry

    tiles = [slice(c * tile, (c + 1) * tile) for c in range(width // tile)]
    own_rows = rows_of(i, rows)
    squares = jnp.zeros((rows, 1), f32)
    for at in tiles:
        squares += jnp.sum(middle[:, at] * middle[:, at], axis=1, keepdims=True)
    root = lax.rsqrt(squares * (1.0 / width) + 1e-06)
    mean = jnp.zeros((rows, 1), f32)
    for at in tiles:
        v = middle[:, at] * root
        dh = d_hidden[:, at]
        mean += jnp.sum(dh * (1.0 + table[i, 4:5, at]) * v, axis=1, keepdims=True)
        sums_out[3:4, at] = jnp.sum(dh, axis=0, keepdims=True)
        sums_out[4:5, at] = jnp.sum(dh * v, axis=0, keepdims=True)
    mean = mean * (1.0 / width)
    load_cot.wait()
    load_out.wait()
    for at in tiles:
        v = middle[:, at] * root
        u = d_hidden[:, at] * (1.0 + table[i, 4:5, at])
        dm = cot[:, at].astype(f32) + root * (u - v * mean)
        d_middle[:, at] = dm
        d_attn[own_rows, at] = (table[i, 2:3, at] * dm).astype(low)
        sums_out[2:3, at] = jnp.sum(dm * attn_out[:, at], axis=0, keepdims=True)

    keep_middle = pltpu.make_async_copy(d_middle, d_middle_out, load_sem.at[5])
    keep_middle.start()

    line = LineGather(
        n, i, rows, d_attn.at[own_rows], d_attn, line_sem.at[0], line_sem.at[1], line_sem.at[2]
    )
    first_core = side == 0

    def send_rows():
        line.start()
        lax.fori_loop(0, (n - 1) * pieces, ends, 0)

    pl.when(first_core)(send_rows)
    for m in range(chips):
        pltpu.make_async_copy(up_slab(2 * m + side), up_own.at[m], own_sem.at[0, m]).wait()
        pltpu.make_async_copy(down_slab(2 * m + side), down_own.at[m], own_sem.at[1, m]).wait()
    load_rows.wait()
    load_qkv.wait()
    load_merge.wait()

    area = lse.shape[1]
    areas = n * rows // area
    area_images = [image_at(sizes, b * area) for b in range(areas)]
    d_keys[...] = jnp.zeros_like(d_keys)
    d_values[...] = jnp.zeros_like(d_values)
    turns = 2 * max(n - 2, 0) * pieces
    scale = HEAD_DIM ** (-0.5)

    def back_area(here_at, carry):
        here = rows_of(here_at, area)
        image = image_at(sizes, here_at * area)
        for h in range(heads):
            first = h * 3 * HEAD_DIM
            head = slice(h * HEAD_DIM, (h + 1) * HEAD_DIM)
            q = qkv[here, first : first + HEAD_DIM]
            g = d_att[here, head]
            log_row = lse[pl.ds(here_at * heads + h, 1), :]
            probs, d_probs = [], []
            inner = jnp.zeros((1, area), f32)
            for b in range(areas):
                key = qkv[b * area : (b + 1) * area, first + HEAD_DIM : first + 2 * HEAD_DIM]
                value = qkv[b * area : (b + 1) * area, first + 2 * HEAD_DIM : first + 3 * HEAD_DIM]
                scores = mm_nt(key, q) * scale + jnp.where(image == area_images[b], 0.0, MASKED)
                probs.append(jnp.exp(scores - log_row))
                d_probs.append(mm_nt(value, g))
                inner += jnp.sum(probs[b] * d_probs[b], axis=0, keepdims=True)
            d_query = jnp.zeros((HEAD_DIM, area), f32)
            for b in range(areas):
                at = slice(b * area, (b + 1) * area)
                key = qkv[at, first + HEAD_DIM : first + 2 * HEAD_DIM]
                d_scores = (probs[b] * (d_probs[b] - inner)).astype(low)
                d_values[at, head] += mm(probs[b].astype(low), g)
                d_keys[at, head] += mm(d_scores, q)
                d_query += mm_tn(key, d_scores)
            d_qkv[here, first : first + HEAD_DIM] = (d_query * scale).T.astype(low)

        return carry

    def pass_by(turn, carry):
        flows(n, pieces, sums, turn)
        return carry

    early = min(turns, pieces)

    def visit(q, carry):
        s = (q + 1) // 2
        j = i + s * (1 - 2 * (q % 2))

        @pl.when(q % 2 == 1)
        def _():
            line.step(s)

        @pl.when((j >= 0) & (j < n))
        def _():
            here = rows_of(j, rows)
            d_att[here, :] = mm_nt(d_attn[here, :], merge[...]).astype(low)
            if area == rows:
                back_area(j, 0)

        @pl.when((q == 0) & jnp.logical_not(first_core))
        def _():
            send_rows()

        @pl.when(q == 0)
        def _():
            up.add_and_send()
            down.add_and_send()

        @pl.when(q == 2 * (n - 2))
        def _():
            up.relay()
            lax.fori_loop(0, early, pass_by, 0)

        return carry

    lax.fori_loop(0, 2 * n - 1, visit, 0)
    if area != rows:
        lax.fori_loop(0, areas, back_area, 0)
    for h in range(heads):
        first = h * 3 * HEAD_DIM
        head = slice(h * HEAD_DIM, (h + 1) * HEAD_DIM)
        d_qkv[:, first + HEAD_DIM : first + 2 * HEAD_DIM] = (d_keys[:, head] * scale).astype(low)
        d_qkv[:, first + 2 * HEAD_DIM : first + 3 * HEAD_DIM] = d_values[:, head].astype(low)
    keep_qkv = pltpu.make_async_copy(d_qkv, d_qkv_out, load_sem.at[6])
    keep_qkv.start()
    wide = width // tile
    short = stage.shape[1]

    def square(row, column):
        return merge_grad.at[
            pl.ds(pl.multiple_of(row * short, short), short),
            pl.ds(pl.multiple_of(column * tile, tile), tile),
        ]

    def merge_one(k, carry):
        row, column = k // wide, lax.rem(k, wide)
        slot = lax.rem(k, 2)

        @pl.when(k >= 2)
        def _():
            pltpu.make_async_copy(stage.at[slot], square(0, 0), stage_sem.at[slot]).wait()

        a = attended[:, pl.ds(pl.multiple_of(row * short, short), short)]
        b = d_attn[:, pl.ds(pl.multiple_of(column * tile, tile), tile)]
        stage[slot] = mm_tn(a, b).astype(low)
        pltpu.make_async_copy(stage.at[slot], square(row, column), stage_sem.at[slot]).start()
        return carry

    lax.fori_loop(0, attended.shape[1] // short * wide, merge_one, 0)
    for slot in range(2):
        pltpu.make_async_copy(stage.at[slot], square(0, 0), stage_sem.at[slot]).wait()
    lax.fori_loop(early, turns, pass_by, 0)
    for c in range(pieces):
        at = slice(c * piece, (c + 1) * piece)
        total = sums.own_value(c)
        block_out[:, at] = (middle[:, at] + table[i, 5:6, at] * total).astype(low)
        sums_out[5:6, at] = jnp.sum(cot[:, at].astype(f32) * total, axis=0, keepdims=True)
    sums_out[0:2, :] = jnp.zeros((2, width), f32)
    sums_out[6:8, :] = jnp.zeros((2, width), f32)
    down.relay()
    keep_middle.wait()
    keep_qkv.wait()
    for scatter in (up, down):
        scatter.landed_all()
        scatter.finish()
    line.finish()
    sums.all_sent()


def back(n, n_dp, operands, shapes, number, tile=512):
    (rows, width), wide, units, k_rows, down_cols, areas = shapes
    heads = wide // (3 * HEAD_DIM)
    total, chips, pieces = n * rows, n_dp // 2, 2 * width // tile
    low, f32 = jnp.bfloat16, jnp.float32
    sds = jax.ShapeDtypeStruct
    return call(
        functools.partial(back_kernel, n, n_dp, heads, tile),
        number,
        "back",
        [VMEM] * 4 + [pl.BlockSpec(memory_space=pltpu.SMEM)] + [HBM] * 8,
        [
            sds((rows, width), low),
            sds((rows, width), f32),
            sds((total, wide), low),
            sds((8, width), f32),
            sds((heads * HEAD_DIM, width), low),
            sds((plane_slots(n_dp), k_rows, units), low),
            sds((plane_slots(n_dp), units, down_cols), low),
        ],
        [VMEM, HBM, HBM, VMEM] + [HBM] * 3,
        [
            pltpu.VMEM((rows, width), low),
            pltpu.VMEM((rows, width), f32),
            pltpu.VMEM((rows, width), f32),
            pltpu.VMEM((total, wide), low),
            pltpu.VMEM((total, heads * HEAD_DIM), low),
            pltpu.VMEM((total, wide), low),
            pltpu.VMEM((total, width), low),
            pltpu.VMEM((total + rows, width), low),
            pltpu.VMEM((heads * HEAD_DIM, width), low),
            pltpu.VMEM((total, heads * HEAD_DIM), low),
            pltpu.VMEM((total, width), low),
            pltpu.VMEM((total, heads * HEAD_DIM), f32),
            pltpu.VMEM((total, heads * HEAD_DIM), f32),
            pltpu.VMEM((chips, k_rows, units), low),
            pltpu.VMEM((chips, k_rows, units), low),
            pltpu.VMEM((k_rows, units), low),
            pltpu.VMEM((chips, units, down_cols), low),
            pltpu.VMEM((chips, units, down_cols), low),
            pltpu.VMEM((units, down_cols), low),
            pltpu.VMEM((2, tile // 2, tile), low),
            DMA((n, pieces)),
            DMA((n + 1, pieces)),
            scatter_sems(n_dp),
            scatter_sems(n_dp),
            DMA((3, n)),
            DMA,
            DMA((7,)),
            DMA((2,)),
            DMA((2, chips)),
        ],
        flops=20 * total * total * wide // 3,
    )(*operands)


def last_kernel(
    n,
    n_dp,
    tile,
    d_qkv,
    sums_in,
    table,
    sizes,
    hidden_hbm,
    x_hbm,
    middle_hbm,
    mod_hbm,
    merge_hbm,
    attend_hbm,
    input_grad,
    d_mod_all,
    noise_sum,
    attend_landed,
    merge_landed,
    hidden,
    x_own,
    d_middle,
    mod_w,
    attend,
    part,
    got,
    grad_own,
    grad_theirs,
    grad_swapped,
    grad_via,
    merge_own,
    merge_swapped,
    merge_via,
    sums_all,
    shares,
    shares_all,
    terms,
    terms_all,
    noise_parts,
    sent,
    came,
    grad_sems,
    merge_sems,
    share_sem,
    mod_sem,
    term_sem,
    noise_sem,
    load_sem,
    own_sem,
    attend_sem,
):
    d, i = lax.axis_index("dp"), lax.axis_index("tensor")
    rows, width = input_grad.shape
    low, f32 = jnp.bfloat16, jnp.float32
    chips = n_dp // 2
    side = lax.rem(d, 2)
    k_rows, own_cols = mod_w.shape
    merge_cols = merge_own.shape[2]
    images = d_mod_all.shape[1]

    def merge_slab(at):
        return merge_hbm.at[:, pl.ds(pl.multiple_of(at * merge_cols, merge_cols), merge_cols)]

    load_hidden, load_x, load_middle, load_mod = (
        pltpu.make_async_copy(source, target, load_sem.at[k])
        for k, (source, target) in enumerate(
            (
                (hidden_hbm, hidden),
                (x_hbm, x_own),
                (middle_hbm, d_middle),
                (mod_hbm, mod_w),
            )
        )
    )

    def load_attend(c):
        at = pl.ds(pl.multiple_of(c * tile, tile), tile)
        return pltpu.make_async_copy(attend_hbm.at[at, :], attend.at[at, :], attend_sem.at[c])

    for c in range(width // tile):
        load_attend(c).start()
    for m in range(chips):
        pltpu.make_async_copy(merge_slab(2 * m + side), merge_own.at[m], own_sem.at[m]).start()
    greet_all(n, n_dp, d, i)
    merge = PlaneScatter(
        n_dp,
        d,
        lambda m: merge_slab(2 * m + 1 - side),
        merge_own,
        merge_swapped,
        merge_via,
        merge_landed,
        merge_sems,
    )
    grad = PlaneScatter(
        n_dp, d, lambda m: grad_theirs.at[m], grad_own, grad_swapped, grad_via, attend_landed, grad_sems
    )
    merge.swap_all()
    for late in (load_hidden, load_x, load_middle, load_mod):
        late.start()
    piece = tile // 2
    sums = LineScatter(n, i, rows, piece, part, got, sent, came)
    pieces = sums.pieces

    def partial_block(q, carry):
        j = jnp.where(2 * i < n - 1, n - 1 - q, q)
        here = rows_of(j, rows)

        def one(c, inner):
            at = pl.ds(pl.multiple_of(c * tile, tile), tile)

            @pl.when(q == 0)
            def _():
                load_attend(c).wait()

            part[here, at] = mm_nt(d_qkv[here, :], attend[at, :]).astype(low)
            for k in range(tile // piece):
                sums.at_end(j, c * (tile // piece) + k)
            return inner

        lax.fori_loop(0, width // tile, one, 0)
        return carry

    partial_block(0, 0)
    for m in range(chips):
        pltpu.make_async_copy(merge_slab(2 * m + side), merge_own.at[m], own_sem.at[m]).wait()
    merge.add_and_send()
    lax.fori_loop(1, n, partial_block, 0)

    def slab_grad(at):
        columns = pl.ds(pl.multiple_of(at * k_rows, k_rows), k_rows)
        return mm_tn(hidden[:, columns], d_qkv[...]).astype(low)

    def for_them(m, carry):
        grad_theirs[m] = slab_grad(2 * m + 1 - side)
        grad.swap(m).start()
        return carry

    def for_us(m, carry):
        grad_own[m] = slab_grad(2 * m + side)
        return carry

    load_hidden.wait()
    lax.fori_loop(0, chips, for_them, 0)
    lax.fori_loop(0, chips, for_us, 0)
    grad.add_and_send()
    merge.relay()
    turns = 2 * max(n - 2, 0) * pieces

    def pass_by(turn, carry):
        flows(n, pieces, sums, turn)
        return carry

    lax.fori_loop(0, turns, pass_by, 0)

    grad.relay()

    for late in (load_x, load_middle, load_mod):
        late.wait()
    tiles = [slice(c * piece, (c + 1) * piece) for c in range(pieces)]
    squares = jnp.zeros((rows, 1), f32)
    for at in tiles:
        v = x_own[:, at].astype(f32)
        squares += jnp.sum(v * v, axis=1, keepdims=True)
    root = lax.rsqrt(squares * (1.0 / width) + 1e-06)
    mean = jnp.zeros((rows, 1), f32)
    sums_all[...] = sums_in[...]
    for c, at in enumerate(tiles):
        v = x_own[:, at].astype(f32) * root
        dh = sums.own_value(c)
        mean += jnp.sum(dh * (1.0 + table[i, 1:2, at]) * v, axis=1, keepdims=True)
        sums_all[0:1, at] = jnp.sum(dh, axis=0, keepdims=True)
        sums_all[1:2, at] = jnp.sum(dh * v, axis=0, keepdims=True)

    unit = math.gcd(width, own_cols)
    image = image_at(sizes, i * rows)
    for number in range(6):
        for start in range(0, width, unit):
            at = number * width + start
            for k in range(images):
                shares[at // own_cols, k : k + 1, at % own_cols : at % own_cols + unit] = (
                    sums_all[number : number + 1, start : start + unit]
                    * jnp.where(image == k, 1.0, 0.0)
                )

    def to_line(source, target, sems, turn, whole=False):
        t = lax.rem(i + turn, n)
        return pltpu.make_async_remote_copy(
            src_ref=source if whole else source.at[t],
            dst_ref=target.at[i],
            send_sem=sems.at[0, t],
            recv_sem=sems.at[1, i],
            device_id=(d, t),
            device_id_type=MESH,
        )

    def from_line(source, target, sems, turn, whole=False):
        t = lax.rem(i + turn, n)
        return pltpu.make_async_remote_copy(
            src_ref=source if whole else source.at[t],
            dst_ref=target.at[t],
            send_sem=sems.at[0, t],
            recv_sem=sems.at[1, t],
            device_id=(d, t),
            device_id_type=MESH,
        )

    def to_plane(source, target, sems, flip):
        return pltpu.make_async_remote_copy(
            src_ref=source,
            dst_ref=target.at[d],
            send_sem=sems.at[0, flip],
            recv_sem=sems.at[1, flip],
            device_id=(d ^ flip, i),
            device_id_type=MESH,
        )

    def from_plane(source, target, sems, flip):
        return pltpu.make_async_remote_copy(
            src_ref=source,
            dst_ref=target.at[d ^ flip],
            send_sem=sems.at[0, flip],
            recv_sem=sems.at[1, flip],
            device_id=(d ^ flip, i),
            device_id_type=MESH,
        )

    for turn in range(1, n):
        to_line(shares, shares_all, share_sem, turn).start()

    mean = mean * (1.0 / width)
    for c, at in enumerate(tiles):
        v = x_own[:, at].astype(f32) * root
        u = sums.own_total(c) * (1.0 + table[i, 1:2, at])
        input_grad[:, at] = (d_middle[:, at] + root * (u - v * mean)).astype(low)
    shares_all[i] = shares[i]
    for turn in range(1, n):
        from_line(shares, shares_all, share_sem, turn).wait_recv()
    d_mod_all[d] = jnp.sum(shares_all[...], axis=0).astype(low).astype(f32)
    own_mod = d_mod_all.at[d]
    for flip in range(1, n_dp):
        to_plane(own_mod, d_mod_all, mod_sem, flip).start()
    for flip in range(1, n_dp):
        from_plane(own_mod, d_mod_all, mod_sem, flip).wait_recv()
    flat = d_mod_all[...].reshape(n_dp * images, own_cols).astype(low)
    terms[...] = mm_nt(flat, mod_w[...]).reshape(n_dp, images, k_rows)
    for turn in range(1, n):
        to_line(terms, terms_all, term_sem, turn, True).start()
    terms_all[i] = terms[...]
    for turn in range(1, n):
        from_line(terms, terms_all, term_sem, turn, True).wait_recv()
    noise_parts[...] = jnp.sum(terms_all[...], axis=0)
    for flip in range(1, n_dp):
        to_plane(noise_parts.at[d ^ flip], noise_sum, noise_sem, flip).start()
    noise_sum[d] = noise_parts[d]
    for flip in range(1, n_dp):
        from_plane(noise_parts.at[d ^ flip], noise_sum, noise_sem, flip).wait_recv()
    merge.landed_all()
    grad.landed_all()
    grad.finish()
    merge.finish()
    for turn in range(1, n):
        to_line(shares, shares_all, share_sem, turn).wait_send()
        to_line(terms, terms_all, term_sem, turn, True).wait_send()
    for flip in range(1, n_dp):
        to_plane(own_mod, d_mod_all, mod_sem, flip).wait_send()
        to_plane(noise_parts.at[d ^ flip], noise_sum, noise_sem, flip).wait_send()
    sums.all_sent()


def last(n, n_dp, operands, shapes, number, tile=512):
    (rows, width), wide, k_rows, own_cols, (merge_rows, merge_cols), images = shapes
    total, chips, pieces = n * rows, n_dp // 2, 2 * width // tile
    low, f32 = jnp.bfloat16, jnp.float32
    sds = jax.ShapeDtypeStruct
    return call(
        functools.partial(last_kernel, n, n_dp, tile),
        number,
        "last",
        [VMEM] * 3 + [pl.BlockSpec(memory_space=pltpu.SMEM)] + [HBM] * 6,
        [
            sds((rows, width), low),
            sds((n_dp, images, own_cols), f32),
            sds((n_dp, images, k_rows), f32),
            sds((plane_slots(n_dp), k_rows, wide), low),
            sds((plane_slots(n_dp), merge_rows, merge_cols), low),
        ],
        [VMEM] * 3 + [HBM] * 2,
        [
            pltpu.VMEM((total, width), low),
            pltpu.VMEM((rows, width), low),
            pltpu.VMEM((rows, width), f32),
            pltpu.VMEM((k_rows, own_cols), low),
            pltpu.VMEM((width, wide), low),
            pltpu.VMEM((total, width), low),
            pltpu.VMEM((total + rows, width), low),
            pltpu.VMEM((chips, k_rows, wide), low),
            pltpu.VMEM((chips, k_rows, wide), low),
            pltpu.VMEM((chips, k_rows, wide), low),
            pltpu.VMEM((k_rows, wide), low),
            pltpu.VMEM((chips, merge_rows, merge_cols), low),
            pltpu.VMEM((chips, merge_rows, merge_cols), low),
            pltpu.VMEM((merge_rows, merge_cols), low),
            pltpu.VMEM((8, width), f32),
            pltpu.VMEM((n, images, own_cols), f32),
            pltpu.VMEM((n, images, own_cols), f32),
            pltpu.VMEM((n_dp, images, k_rows), f32),
            pltpu.VMEM((n, n_dp, images, k_rows), f32),
            pltpu.VMEM((n_dp, images, k_rows), f32),
            DMA((n, pieces)),
            DMA((n + 1, pieces)),
            scatter_sems(n_dp),
            scatter_sems(n_dp),
            DMA((2, n)),
            DMA((2, n_dp)),
            DMA((2, n)),
            DMA((2, n_dp)),
            DMA((4,)),
            DMA((chips,)),
            DMA((width // tile,)),
        ],
        flops=4 * total * width * wide,
    )(*operands)


def final_kernel(
    noise_own,
    noise_all,
    d_mod,
    noise_sums,
    up_in,
    down_in,
    attend_in,
    block_in,
    input_in,
    merge_in,
    block_out,
    input_out,
    noise_grad,
    attend_out,
    merge_out,
    up_out,
    down_out,
    modulate_out,
    up_slots,
    down_slots,
    attend_slots,
    merge_slots,
    up_sum,
    down_sum,
    attend_sum,
    merge_sum,
    modulate,
    block,
    inputs,
    sems,
):
    low, f32 = jnp.bfloat16, jnp.float32
    loads = [
        pltpu.make_async_copy(source, target, sems.at[0, k])
        for k, (source, target) in enumerate(
            (
                (up_in, up_slots),
                (down_in, down_slots),
                (attend_in, attend_slots),
                (merge_in, merge_slots),
                (block_in, block),
                (input_in, inputs),
            )
        )
    ]
    stores = [
        pltpu.make_async_copy(source, target, sems.at[1, k])
        for k, (source, target) in enumerate(
            (
                (up_sum, up_out),
                (down_sum, down_out),
                (attend_sum, attend_out),
                (merge_sum, merge_out),
                (block, block_out),
                (inputs, input_out),
                (modulate, modulate_out),
            )
        )
    ]
    for load in loads:
        load.start()
    n_dp, images, k_rows = noise_all.shape
    left = noise_all[...].reshape(n_dp * images, k_rows).astype(low)
    right = d_mod[...].reshape(n_dp * images, -1).astype(low)
    modulate[...] = mm_tn(left, right)
    stores[6].start()
    for k in range(n_dp):
        at = slice(k * k_rows, (k + 1) * k_rows)
        v = noise_own[:, at].astype(f32)
        gate = 1.0 / (1.0 + jnp.exp(-v))
        noise_grad[:, at] = noise_sums[k] * (gate * (1.0 + v * (1.0 - gate)))

    def add(slots, total):
        count, height, wide = slots.shape
        chunk = math.gcd(height, 32 if wide > 512 else 256)

        def one(c, carry):
            at = pl.ds(pl.multiple_of(c * chunk, chunk), chunk)
            total[at, :] = sum(slots[s, at, :].astype(f32) for s in range(count))
            return carry

        lax.fori_loop(0, height // chunk, one, 0)

    for k, (slots, total) in enumerate(
        (
            (up_slots, up_sum),
            (down_slots, down_sum),
            (attend_slots, attend_sum),
            (merge_slots, merge_sum),
        )
    ):
        loads[k].wait()
        add(slots, total)
        stores[k].start()
    for k in range(4, 6):
        loads[k].wait()
        stores[k].start()
    for store in stores:
        store.wait()


def final(noise_own, noise_all, d_mod, noise_sums, up, down, attend, block, inputs, merge):
    sds, f32 = jax.ShapeDtypeStruct, jnp.float32
    own_cols, k_rows = d_mod.shape[2], noise_all.shape[2]
    sums = [sds(a.shape[1:], f32) for a in (up, down, attend, merge)]
    modulate = sds((k_rows, own_cols), f32)
    return pl.pallas_call(
        final_kernel,
        out_shape=[
            sds(block.shape, block.dtype),
            sds(inputs.shape, inputs.dtype),
            sds(noise_own.shape, f32),
            sums[2],
            sums[3],
            sums[0],
            sums[1],
            modulate,
        ],
        in_specs=[VMEM] * 4 + [HBM] * 6,
        out_specs=[HBM, HBM, VMEM] + [HBM] * 5,
        scratch_shapes=[
            pltpu.VMEM(a.shape, a.dtype)
            for a in (up, down, attend, merge, *sums, modulate, block, inputs)
        ]
        + [DMA((2, 7))],
        compiler_params=pltpu.CompilerParams(vmem_limit_bytes=60 * 1024 * 1024),
        name="final",
    )(noise_own, noise_all, d_mod, noise_sums, up, down, attend, block, inputs, merge)


def on_device(
    block_input,
    cotangent,
    noise_embed,
    image_sizes,
    attend_weight,
    merge_weight,
    up_weight,
    down_weight,
    modulate_weight,
):
    n = lax.axis_size("tensor")
    n_dp = lax.axis_size("dp")
    rows, width = block_input.shape
    tokens = n * rows
    images = image_sizes.shape[1]
    k_rows = modulate_weight.shape[0]

    (
        cot_full,
        hidden_first,
        packed,
        lse,
        attended,
        attn_out,
        middle,
        hidden_second,
        table,
        attend_full,
        merge_full,
        up_full,
        down_full,
        noise_all,
    ) = front(
        n,
        n_dp,
        block_input,
        cotangent,
        noise_embed,
        modulate_weight,
        image_sizes,
        attend_weight,
        merge_weight,
        up_weight,
        down_weight,
        0,
    )
    d_hidden_second, mlp_part, up_local, down_local = ffn(
        n, hidden_second, table, cot_full, up_full, down_full, 1
    )
    units = up_full.shape[1]
    wide = packed.shape[1]
    (
        block_output,
        d_middle,
        d_qkv,
        row_sums,
        merge_local,
        up_landed,
        down_landed,
    ) = back(
        n,
        n_dp,
        (
            d_hidden_second,
            middle,
            table,
            lse,
            image_sizes,
            cotangent,
            attn_out,
            attended,
            packed,
            mlp_part,
            merge_full,
            up_local,
            down_local,
        ),
        (block_input.shape, wide, units, k_rows, down_weight.shape[1], lse.shape[0]),
        2,
    )
    input_grad, d_mod_all, noise_sums, attend_landed, merge_landed = last(
        n,
        n_dp,
        (
            d_qkv,
            row_sums,
            table,
            image_sizes,
            hidden_first,
            block_input,
            d_middle,
            modulate_weight,
            merge_local,
            attend_full,
        ),
        (
            block_input.shape,
            wide,
            k_rows,
            modulate_weight.shape[1],
            merge_weight.shape,
            images,
        ),
        3,
    )

    return tuple(
        final(
            noise_embed,
            noise_all,
            d_mod_all,
            noise_sums,
            up_landed,
            down_landed,
            attend_landed,
            block_output,
            input_grad,
            merge_landed,
        )
    )


def solution(mesh):
    whole_rows = P(("dp", "tensor"), None)
    by_dp = P("dp", None)
    tall = P("dp", "tensor")
    wide = P("tensor", "dp")
    return jax.shard_map(
        on_device,
        mesh=mesh,
        in_specs=(whole_rows, whole_rows, by_dp, by_dp, tall, wide, tall, wide, tall),
        out_specs=(whole_rows, whole_rows, by_dp, tall, wide, tall, wide, tall),
        check_vma=False,
    )
```

```python
import functools
import math

import jax
import jax.numpy as jnp
from jax import lax
from jax.experimental import pallas as pl
from jax.experimental.pallas import tpu as pltpu
from jax.sharding import PartitionSpec as P

HEAD_DIM = 128
MASKED = -1e30


def dot(a, b, dims=(((1,), (0,)), ((), ()))):
    return lax.dot_general(a, b, dims, preferred_element_type=jnp.float32)


ROWS_ROWS = (((0,), (0,)), ((), ()))


MESH = pl.DeviceIdType.MESH
HBM = pl.BlockSpec(memory_space=pl.ANY)
VMEM = pl.BlockSpec(memory_space=pltpu.VMEM)
DMA = pltpu.SemaphoreType.DMA


def rows_of(j, rows):
    return pl.ds(pl.multiple_of(j * rows, rows), rows)


def beside(step):
    return (lax.axis_index("dp"), lax.axis_index("tensor") + step)


def greet_line(n, i):
    barrier = pltpu.get_barrier_semaphore()

    @pl.when(i > 0)
    def _():
        pl.semaphore_signal(barrier, inc=1, device_id=beside(-1), device_id_type=MESH)

    @pl.when(i < n - 1)
    def _():
        pl.semaphore_signal(barrier, inc=1, device_id=beside(1), device_id_type=MESH)

    pl.semaphore_wait(barrier, jnp.where(i > 0, 1, 0) + jnp.where(i < n - 1, 1, 0))


class LineGather:
    def __init__(self, n, i, rows, own, full, to_left, to_right, arrived):
        self.n, self.i, self.rows, self.own, self.full = n, i, rows, own, full
        self.to_left, self.to_right, self.arrived = to_left, to_right, arrived

    def copy(self, j, step, source=None):
        place = self.full.at[rows_of(j, self.rows)]
        return pltpu.make_async_remote_copy(
            src_ref=place if source is None else source,
            dst_ref=place,
            send_sem=(self.to_right if step > 0 else self.to_left).at[j],
            recv_sem=self.arrived.at[j],
            device_id=beside(step),
            device_id_type=MESH,
        )

    def start(self):
        @pl.when(self.i > 0)
        def _():
            self.copy(self.i, -1, self.own).start()

        @pl.when(self.i < self.n - 1)
        def _():
            self.copy(self.i, 1, self.own).start()

    def step(self, s):
        for side in (-1, 1):
            j = self.i + side * s
            there = (j >= 0) & (j < self.n)
            more = (self.i > 0) if side > 0 else (self.i < self.n - 1)

            @pl.when(there)
            def _():
                self.copy(j, side).wait_recv()

            @pl.when(there & more)
            def _():
                self.copy(j, -side).start()

    def finish(self):
        @pl.when(self.i > 0)
        def _():
            self.copy(self.i, -1, self.own).wait_send()

        @pl.when(self.i < self.n - 1)
        def _():
            self.copy(self.i, 1, self.own).wait_send()

        for j in range(self.n):

            @pl.when((j < self.i) & (self.i < self.n - 1))
            def _():
                self.copy(j, 1).wait_send()

            @pl.when((j > self.i) & (self.i > 0))
            def _():
                self.copy(j, -1).wait_send()


class LineScatter:
    def __init__(self, n, i, rows, width, part, got, sent, arrived):
        self.n, self.i, self.rows, self.width = n, i, rows, width
        self.part, self.got, self.sent, self.arrived = part, got, sent, arrived
        self.pieces = part.shape[1] // width

    def columns(self, c):
        if isinstance(c, int):
            return pl.ds(c * self.width, self.width)
        return pl.ds(pl.multiple_of(c * self.width, self.width), self.width)

    def copy(self, j, slot, c, step):
        return pltpu.make_async_remote_copy(
            src_ref=self.part.at[rows_of(j, self.rows), self.columns(c)],
            dst_ref=self.got.at[rows_of(slot, self.rows), self.columns(c)],
            send_sem=self.sent.at[j, c],
            recv_sem=self.arrived.at[slot, c],
            device_id=beside(step),
            device_id_type=MESH,
        )

    def slot_there(self, j, step):
        if step > 0:
            return j
        return jnp.where(j == self.i - 1, self.n, j)

    def at_end(self, j, c):
        @pl.when((self.i == 0) & (j > 0))
        def _():
            self.copy(j, j, c, 1).start()

        @pl.when((self.i == self.n - 1) & (j < self.i))
        def _():
            self.copy(j, self.slot_there(j, -1), c, -1).start()

    def pass_on(self, t, c, near):
        n, i = self.n, self.i
        rightward = (2 * i < n - 1) if near else (2 * i >= n - 1)
        j = jnp.where(rightward, t, n - 1 - t)
        step = jnp.where(rightward, 1, -1)
        right = rightward & (i > 0) & (j > i)
        left = jnp.logical_not(rightward) & (i < n - 1) & (j < i)

        @pl.when(right | left)
        def _():
            self.add(j, j, c)
            slot = jnp.where(left & (j == i - 1), n, j)
            self.copy(j, slot, c, step).start()

    def add(self, j, slot, c):
        self.copy(j, slot, c, 1).wait_recv()
        here = (rows_of(j, self.rows), self.columns(c))
        there = (rows_of(slot, self.rows), self.columns(c))
        total = self.part[here].astype(jnp.float32) + self.got[there].astype(jnp.float32)
        self.part[here] = total.astype(self.part.dtype)

    def own(self, c, out):
        i, n = self.i, self.n
        columns = self.columns(c)
        out[:, columns] = self.part[rows_of(i, self.rows), columns].astype(out.dtype)

        @pl.when(i > 0)
        def _():
            self.copy(i, i, c, 1).wait_recv()
            out[:, columns] += self.got[rows_of(i, self.rows), columns].astype(out.dtype)

        @pl.when(i < n - 1)
        def _():
            self.copy(i, n, c, -1).wait_recv()
            out[:, columns] += self.got[rows_of(n, self.rows), columns].astype(out.dtype)

    def own_value(self, c):
        i, n = self.i, self.n

        @pl.when(i > 0)
        def _():
            self.copy(i, i, c, 1).wait_recv()

        @pl.when(i < n - 1)
        def _():
            self.copy(i, n, c, -1).wait_recv()

        return self.own_total(c)

    def own_total(self, c):
        i, n, columns = self.i, self.n, self.columns(c)
        total = self.part[rows_of(i, self.rows), columns].astype(jnp.float32)
        left = self.got[rows_of(i, self.rows), columns].astype(jnp.float32)
        right = self.got[rows_of(n, self.rows), columns].astype(jnp.float32)
        return total + jnp.where(i > 0, left, 0.0) + jnp.where(i < n - 1, right, 0.0)

    def all_sent(self):
        def one(j, carry):
            @pl.when(j != self.i)
            def _():
                for c in range(self.pieces):
                    self.copy(j, 0, c, 1).wait_send()

            return carry

        lax.fori_loop(0, self.n, one, 0)


def mm(a, b):
    return lax.dot_general(a, b, (((1,), (0,)), ((), ())), preferred_element_type=jnp.float32)


def mm_nt(a, b):
    return lax.dot_general(a, b, (((1,), (1,)), ((), ())), preferred_element_type=jnp.float32)


def mm_tn(a, b):
    return lax.dot_general(a, b, (((0,), (0,)), ((), ())), preferred_element_type=jnp.float32)


def call(kernel, collective_id, name, in_specs, outs, out_specs, scratch, flops=0, limit=60):
    return pl.pallas_call(
        kernel,
        out_shape=outs,
        in_specs=in_specs,
        out_specs=out_specs,
        scratch_shapes=scratch,
        compiler_params=pltpu.CompilerParams(
            collective_id=collective_id,
            has_side_effects=True,
            vmem_limit_bytes=limit * 1024 * 1024,
        ),
        cost_estimate=pl.CostEstimate(flops=flops, bytes_accessed=1 << 20, transcendentals=0),
        name=name,
    )


def ffn_kernel(
    n,
    tile,
    grad_tile,
    own_hidden,
    table,
    d_mlp_hbm,
    up_hbm,
    down_hbm,
    d_hidden,
    mlp_part,
    up_grad,
    down_grad,
    up,
    down,
    d_mlp,
    hidden,
    activated,
    d_pre,
    part,
    got,
    stage,
    mlp,
    to_left,
    to_right,
    arrived,
    sent,
    came,
    local,
    stage_sem,
):
    i = lax.axis_index("tensor")
    rows, width = own_hidden.shape
    units = up.shape[1]
    loads = [
        pltpu.make_async_copy(source, target, local.at[k])
        for k, (source, target) in enumerate(((up_hbm, up), (d_mlp_hbm, d_mlp), (down_hbm, down)))
    ]
    for load in loads:
        load.start()
    greet_line(n, i)
    line = LineGather(n, i, rows, own_hidden, hidden, to_left, to_right, arrived)
    first_core = lax.rem(lax.axis_index("dp"), 2) == 0
    pl.when(first_core)(line.start)
    piece = tile // 2
    sums = LineScatter(n, i, rows, piece, part, got, sent, came)
    hidden[rows_of(i, rows), :] = own_hidden[...]
    for load in loads:
        load.wait()

    def one_block(j):
        here = rows_of(j, rows)

        def gated(c, carry):
            at = pl.ds(pl.multiple_of(c * tile, tile), tile)
            d_mlp[here, at] = (d_mlp[here, at].astype(jnp.float32) * table[j, 5:6, at]).astype(
                jnp.bfloat16
            )
            return carry

        lax.fori_loop(0, width // tile, gated, 0)

        wide = math.gcd(units, 2 * tile)

        def first(c, carry):
            at = pl.ds(pl.multiple_of(c * wide, wide), wide)
            pre = mm(hidden[here, :], up[:, at])
            d_act = mm_nt(d_mlp[here, :], down[at, :])
            cdf = 0.5 * (1.0 + lax.erf(pre * (0.5**0.5)))
            density = jnp.exp(-0.5 * pre * pre) * ((0.5 / math.pi) ** 0.5)
            activated[here, at] = (pre * cdf).astype(jnp.bfloat16)
            d_pre[here, at] = (d_act * (cdf + pre * density)).astype(jnp.bfloat16)
            return carry

        lax.fori_loop(0, units // wide, first, 0)

        def second(c, carry):
            at = pl.ds(pl.multiple_of(c * tile, tile), tile)
            part[here, at] = mm_nt(d_pre[here, :], up[at, :]).astype(jnp.bfloat16)
            for k in range(tile // piece):
                sums.at_end(j, c * (tile // piece) + k)
            return carry

        lax.fori_loop(0, width // tile, second, 0)

        broad = math.gcd(width, 2 * tile)

        def third(c, carry):
            at = pl.ds(pl.multiple_of(c * broad, broad), broad)
            mlp[here, at] = mm(activated[here, :], down[:, at]).astype(jnp.bfloat16)
            return carry

        lax.fori_loop(0, width // broad, third, 0)

    def visit(q, carry):
        s = (q + 1) // 2
        side = 1 - 2 * (q % 2)
        j = i + s * side

        @pl.when(q % 2 == 1)
        def _():
            line.step(s)

        @pl.when((j >= 0) & (j < n))
        def _():
            one_block(j)

        @pl.when((q == 0) & jnp.logical_not(first_core))
        def _():
            line.start()

        return carry

    lax.fori_loop(0, 2 * n - 1, visit, 0)
    keep_mlp = pltpu.make_async_copy(mlp, mlp_part, local.at[3])
    keep_mlp.start()

    count = (width // grad_tile) * (units // grad_tile)
    turns = 2 * max(n - 2, 1) * sums.pieces
    per_turn = -(-2 * count // turns)

    def square(ref, row, column):
        return ref.at[
            pl.ds(pl.multiple_of(row * grad_tile, grad_tile), grad_tile),
            pl.ds(pl.multiple_of(column * grad_tile, grad_tile), grad_tile),
        ]

    def put(slot, target):
        return pltpu.make_async_copy(stage.at[slot], target, stage_sem.at[slot])

    def one_grad(k, left, right, target):
        wide = right.shape[1] // grad_tile
        row, column = k // wide, k % wide
        slot = k % 2

        @pl.when(k >= 2)
        def _():
            put(slot, square(target, 0, 0)).wait()

        a = left[:, pl.ds(pl.multiple_of(row * grad_tile, grad_tile), grad_tile)]
        b = right[:, pl.ds(pl.multiple_of(column * grad_tile, grad_tile), grad_tile)]
        stage[slot] = mm_tn(a, b).astype(jnp.bfloat16)
        put(slot, square(target, row, column)).start()

    def tail(k, carry):
        t, c = 2 + k // (2 * sums.pieces), k % sums.pieces
        for near in (True, False):

            @pl.when((k // sums.pieces) % 2 == (0 if near else 1))
            def _():
                sums.pass_on(t, c, near)

        for extra in range(per_turn):
            item = k * per_turn + extra

            @pl.when(item < count)
            def _():
                one_grad(item, hidden, d_pre, up_grad)

            @pl.when(item == count)
            def _():
                for slot in range(2):
                    put(slot, square(up_grad, 0, 0)).wait()

            @pl.when((item >= count) & (item < 2 * count))
            def _():
                one_grad(item - count, activated, d_mlp, down_grad)

        return carry

    lax.fori_loop(0, turns, tail, 0)
    for slot in range(2):
        put(slot, square(down_grad, 0, 0)).wait()
    for c in range(sums.pieces):
        sums.own(c, d_hidden)
    line.finish()
    sums.all_sent()
    keep_mlp.wait()


def ffn(n, own_hidden, table, cotangents, up, down, collective_id, tile=512, grad_tile=512):
    rows, width = own_hidden.shape
    units = up.shape[1]
    pieces = 2 * width // tile
    low = jnp.bfloat16
    return call(
        functools.partial(ffn_kernel, n, tile, grad_tile),
        collective_id,
        "ffn",
        [VMEM, VMEM, HBM, HBM, HBM],
        [
            jax.ShapeDtypeStruct((rows, width), jnp.float32),
            jax.ShapeDtypeStruct((n * rows, width), low),
            jax.ShapeDtypeStruct((width, units), low),
            jax.ShapeDtypeStruct((units, width), low),
        ],
        [VMEM, HBM, HBM, HBM],
        [
            pltpu.VMEM((width, units), low),
            pltpu.VMEM((units, width), low),
            pltpu.VMEM((n * rows, width), low),
            pltpu.VMEM((n * rows, width), low),
            pltpu.VMEM((n * rows, units), low),
            pltpu.VMEM((n * rows, units), low),
            pltpu.VMEM((n * rows, width), low),
            pltpu.VMEM(((n + 1) * rows, width), low),
            pltpu.VMEM((2, grad_tile, grad_tile), low),
            pltpu.VMEM((n * rows, width), low),
            DMA((n,)),
            DMA((n,)),
            DMA((n,)),
            DMA((n, pieces)),
            DMA((n + 1, pieces)),
            DMA((4,)),
            DMA((2,)),
        ],
        flops=12 * n * rows * width * units,
    )(own_hidden, table, cotangents, up, down)


def image_at(sizes, place):
    end, count = 0, 0
    for k in range(sizes.shape[1]):
        end = end + sizes[0, k]
        count = count + jnp.where(place >= end, 1, 0)
    return count


def image_at(sizes, place):
    end, count = 0, 0
    for k in range(sizes.shape[1]):
        end = end + sizes[0, k]
        count = count + jnp.where(place >= end, 1, 0)
    return count


class PlaneGather:
    def __init__(self, n_dp, d, own, view, height, sent, came):
        self.n_dp, self.d, self.own, self.view, self.height = n_dp, d, own, view, height
        self.sent, self.came = sent, came
        self.square = n_dp == 8
        self.peers = [2 * k for k in range(1, n_dp // 2)]

    def copy(self, k, source, target, peer):
        return pltpu.make_async_remote_copy(
            src_ref=source,
            dst_ref=target,
            send_sem=self.sent.at[k],
            recv_sem=self.came.at[k],
            device_id=(self.d ^ peer, lax.axis_index("tensor")),
            device_id_type=MESH,
        )

    def slab(self, flip, half=None):
        if half is None:
            return self.view(self.d ^ flip, 0, self.height)
        return self.view(self.d ^ flip, half * (self.height // 2), self.height // 2)

    def owns(self):
        peers = [2, 4] if self.square else self.peers
        return [
            self.copy(k, self.own, self.slab(0), peer) for k, peer in enumerate([1] + peers)
        ]

    def relay_of(self, k):
        flip, half, peer = ((2, 0, 4), (4, 1, 2))[k - 1]
        return self.copy(2 + k, self.slab(flip, half), self.slab(flip, half), peer)

    def across(self):
        return [
            self.copy(3, self.slab(6, 0), self.slab(6, 0), 4),
            self.copy(4, self.slab(6, 1), self.slab(6, 1), 2),
        ]

    def hand(self, flip):
        base = 5 if self.square else len(self.peers) + 1
        k = base + flip // 2 - 1
        return self.copy(k, self.slab(flip), self.slab(flip), 1)

    def handed(self, flip):
        base = 5 if self.square else len(self.peers) + 1
        k = base + flip // 2 - 1
        return self.copy(k, self.slab(flip ^ 1), self.slab(flip ^ 1), 1)

    def start(self):
        for copy in self.owns():
            copy.start()

    def relay(self):
        if not self.square:
            return
        for k, flip in ((1, 2), (2, 4)):
            self.copy(k, self.own, self.slab(flip), flip).wait_recv()
            self.relay_of(k).start()
            self.hand(flip).start()

    def close(self):
        if self.square:
            for copy in self.across():
                copy.wait_recv()
            self.hand(6).start()
        else:
            for k, flip in enumerate(self.peers):
                self.copy(k + 1, self.own, self.slab(flip), flip).wait_recv()
                self.hand(flip).start()
        self.copy(0, self.own, self.slab(1), 1).wait_recv()
        for flip in self.peers:
            self.handed(flip).wait_recv()

    def finish(self):
        for copy in self.owns():
            copy.wait_send()
        if self.square:
            for k in (1, 2):
                self.relay_of(k).wait_send()
        for flip in self.peers:
            self.hand(flip).wait_send()


def plane_sems(n_dp):
    return 8 if n_dp == 8 else n_dp - 1


def greet_all(n, n_dp, d, i):
    barrier = pltpu.get_barrier_semaphore()
    for flip in range(1, n_dp):
        pl.semaphore_signal(barrier, inc=1, device_id=(d ^ flip, i), device_id_type=MESH)
    for turn in range(1, n):
        pl.semaphore_signal(
            barrier, inc=1, device_id=(d, lax.rem(i + turn, n)), device_id_type=MESH
        )
    pl.semaphore_wait(barrier, n_dp + n - 2)


def front_kernel(
    n,
    n_dp,
    heads,
    tile,
    x_own,
    cot_own,
    noise_own,
    mod_w,
    sizes,
    attend_w,
    merge_w,
    up_w,
    down_w,
    cot_full,
    hidden_out,
    qkv_out,
    lse,
    attended_out,
    attn_out_hbm,
    middle_out,
    second_out,
    table,
    attend_full,
    merge_full,
    up_full,
    down_full,
    noise_all,
    x_full,
    attend,
    merge,
    noise,
    hidden,
    qkv,
    attended,
    att_rows,
    attn_out,
    middle,
    hidden_second,
    terms,
    terms_all,
    columns,
    noise_sem,
    terms_sem,
    column_sem,
    x_sem,
    cot_sem,
    merge_sem,
    weight_sent,
    weight_came,
    out_sem,
    att_sem,
    local,
):
    d, i = lax.axis_index("dp"), lax.axis_index("tensor")
    rows, width = x_own.shape
    k_rows, own_cols = mod_w.shape
    head_cols = heads * HEAD_DIM
    low, f32 = jnp.bfloat16, jnp.float32
    merge_rows, merge_cols = merge_w.shape
    down_cols = down_w.shape[1]
    merge_slab = merge.at[:, pl.ds(pl.multiple_of(d * merge_cols, merge_cols), merge_cols)]

    def row_view(full, height):
        return lambda at, start, count: full.at[
            pl.ds(pl.multiple_of(at * height + start, 16), count), :
        ]

    def column_view(full, wide):
        return lambda at, start, count: full.at[
            pl.ds(start, count), pl.ds(pl.multiple_of(at * wide, wide), wide)
        ]

    weights = [
        PlaneGather(n_dp, d, own, view, height, weight_sent.at[k], weight_came.at[k])
        for k, (own, view, height) in enumerate(
            (
                (attend_w, row_view(attend, k_rows), k_rows),
                (merge_slab, column_view(merge, merge_cols), n * merge_rows),
                (up_w, row_view(up_full, k_rows), k_rows),
                (down_w, column_view(down_full, down_cols), down_w.shape[0]),
            )
        )
    ]
    attend_g, merge_g, up_g, down_g = weights
    copies = [
        pltpu.make_async_copy(source, target, local.at[k])
        for k, (source, target) in enumerate(
            (
                (attend_w, attend_g.slab(0)),
                (merge_w, merge_slab.at[rows_of(i, merge_rows)]),
                (cot_own, cot_full.at[rows_of(i, rows)]),
                (up_w, up_g.slab(0)),
                (down_w, down_g.slab(0)),
            )
        )
    ]
    for copy in copies:
        copy.start()
    greet_all(n, n_dp, d, i)

    def to_plane(source, target, sems, flip):
        return pltpu.make_async_remote_copy(
            src_ref=source.at[d ^ flip],
            dst_ref=target.at[d],
            send_sem=sems.at[0, flip],
            recv_sem=sems.at[1, flip],
            device_id=(d ^ flip, i),
            device_id_type=MESH,
        )

    def from_plane(target, sems, flip):
        return pltpu.make_async_remote_copy(
            src_ref=target.at[d ^ flip],
            dst_ref=target.at[d ^ flip],
            send_sem=sems.at[0, flip],
            recv_sem=sems.at[1, flip],
            device_id=(d ^ flip, i),
            device_id_type=MESH,
        )

    for k in range(n_dp):
        v = noise_own[:, k * k_rows : (k + 1) * k_rows].astype(f32)
        noise[k] = (v * (1.0 / (1.0 + jnp.exp(-v)))).astype(low).astype(f32)
    for flip in range(1, n_dp):
        to_plane(noise, noise_all, noise_sem, flip).start()
    merge_line = LineGather(
        n, i, merge_rows, merge_w, merge_slab, merge_sem.at[0], merge_sem.at[1], merge_sem.at[2]
    )
    x_line = LineGather(n, i, rows, x_own, x_full, x_sem.at[0], x_sem.at[1], x_sem.at[2])
    cot_line = LineGather(
        n, i, rows, cot_own, cot_full, cot_sem.at[0], cot_sem.at[1], cot_sem.at[2]
    )
    x_line.start()
    noise_all[d] = noise[d]
    x_full[rows_of(i, rows), :] = x_own[...]
    for flip in range(1, n_dp):
        from_plane(noise_all, noise_sem, flip).wait_recv()
    pictures = noise.shape[1]
    images = noise_all[...].reshape(n_dp * pictures, k_rows).astype(low)
    for c in range(own_cols // tile):
        terms[:, :, c * tile : (c + 1) * tile] = mm(
            images, mod_w[:, c * tile : (c + 1) * tile]
        ).reshape(n_dp, pictures, tile)
    for flip in range(1, n_dp):
        to_plane(terms, terms_all, terms_sem, flip).start()
    attend_g.start()
    terms_all[d] = terms[d]
    for flip in range(1, n_dp):
        from_plane(terms_all, terms_sem, flip).wait_recv()
    columns[i] = jnp.sum(terms_all[...], axis=0)

    def to_line(turn):
        t = lax.rem(i + turn, n)
        return pltpu.make_async_remote_copy(
            src_ref=columns.at[i],
            dst_ref=columns.at[i],
            send_sem=column_sem.at[0, t],
            recv_sem=column_sem.at[1, i],
            device_id=(d, t),
            device_id_type=MESH,
        )

    def from_line(turn):
        t = lax.rem(i + turn, n)
        return pltpu.make_async_remote_copy(
            src_ref=columns.at[t],
            dst_ref=columns.at[t],
            send_sem=column_sem.at[0, t],
            recv_sem=column_sem.at[1, t],
            device_id=(d, t),
            device_id_type=MESH,
        )

    for turn in range(1, n):
        to_line(turn).start()
    merge_line.start()
    x_line.step(1)
    for turn in range(1, n):
        from_line(turn).wait_recv()
    unit = math.gcd(width, own_cols)

    def fill(j, carry):
        image = image_at(sizes, j * rows)
        for number in range(6):
            for start in range(0, width, unit):
                at = number * width + start
                here = slice(at % own_cols, at % own_cols + unit)
                table[j, number : number + 1, start : start + unit] = sum(
                    columns[at // own_cols, k : k + 1, here] * jnp.where(image == k, 1.0, 0.0)
                    for k in range(pictures)
                )
        return carry

    lax.fori_loop(0, n, fill, 0)
    attend_g.relay()
    merge_line.step(1)
    for copy in copies[:2]:
        copy.wait()
    attend_g.close()
    up_g.start()
    keep_attend = pltpu.make_async_copy(attend, attend_full, out_sem.at[0])
    keep_merge = pltpu.make_async_copy(
        merge.at[rows_of(i, merge_rows)], merge_full, out_sem.at[1]
    )
    keep_attend.start()
    keep_hidden = pltpu.make_async_copy(hidden, hidden_out, out_sem.at[2])
    keep_qkv = pltpu.make_async_copy(qkv, qkv_out, out_sem.at[3])

    def tiles(count):
        return [slice(c * tile, (c + 1) * tile) for c in range(count // tile)]

    def one_block(j):
        here = rows_of(j, rows)
        squares = jnp.zeros((rows, 1), f32)
        for at in tiles(width):
            v = x_full[here, at].astype(f32)
            squares += jnp.sum(v * v, axis=1, keepdims=True)
        root = lax.rsqrt(squares * (1.0 / width) + 1e-06)
        for at in tiles(width):
            v = x_full[here, at].astype(f32) * root
            hidden[here, at] = (v * (1.0 + table[j, 1:2, at]) + table[j, 0:1, at]).astype(low)
        wide = qkv.shape[1]
        step = math.gcd(wide, 512)
        for c in range(wide // step):
            at = slice(c * step, (c + 1) * step)
            qkv[here, at] = mm(hidden[here, :], attend[:, at]).astype(low)

    def visit(q, carry):
        s = (q + 1) // 2
        side = 1 - 2 * (q % 2)
        j = i + s * side

        @pl.when((q % 2 == 1) & (s + 1 < n))
        def _():
            x_line.step(s + 1)
            merge_line.step(s + 1)

        @pl.when(q == 2 * n - 5)
        def _():
            up_g.relay()
            merge_g.start()
            cot_line.start()

        @pl.when((j >= 0) & (j < n))
        def _():
            one_block(j)

        return carry

    lax.fori_loop(0, 2 * n - 1, visit, 0)

    keep_hidden.start()
    keep_qkv.start()

    area = min(256, n * rows)
    areas = n * rows // area
    owners = area // rows
    area_images = [image_at(sizes, b * area) for b in range(areas)]

    def to_owner(j):
        return pltpu.make_async_remote_copy(
            src_ref=attended.at[rows_of(j, rows), :],
            dst_ref=att_rows.at[:, pl.ds(pl.multiple_of(i * head_cols, head_cols), head_cols)],
            send_sem=att_sem.at[0, j],
            recv_sem=att_sem.at[1, i],
            device_id=(d, j),
            device_id_type=MESH,
        )

    def from_source(t):
        return pltpu.make_async_remote_copy(
            src_ref=attended.at[rows_of(t, rows), :],
            dst_ref=att_rows.at[:, pl.ds(pl.multiple_of(t * head_cols, head_cols), head_cols)],
            send_sem=att_sem.at[0, t],
            recv_sem=att_sem.at[1, t],
            device_id=(d, t),
            device_id_type=MESH,
        )

    def attend_area(turn, carry):
        here_at = lax.rem(i // owners + 1 + turn, areas)
        here = rows_of(here_at, area)
        image = image_at(sizes, here_at * area)
        for h in range(heads):
            first = h * 3 * HEAD_DIM
            q = qkv[here, first : first + HEAD_DIM]
            parts = []
            for b in range(areas):
                key = qkv[b * area : (b + 1) * area, first + HEAD_DIM : first + 2 * HEAD_DIM]
                parts.append(
                    mm_nt(key, q) * HEAD_DIM ** (-0.5)
                    + jnp.where(image == area_images[b], 0.0, MASKED)
                )
            highest = parts[0].max(axis=0, keepdims=True)
            for part in parts[1:]:
                highest = jnp.maximum(highest, part.max(axis=0, keepdims=True))
            parts = [jnp.exp(part - highest) for part in parts]
            totals = sum(jnp.sum(part, axis=0, keepdims=True) for part in parts)
            inverse = 1.0 / totals
            out = jnp.zeros((HEAD_DIM, area), f32)
            for b in range(areas):
                value = qkv[b * area : (b + 1) * area, first + 2 * HEAD_DIM : first + 3 * HEAD_DIM]
                out += mm_tn(value, (parts[b] * inverse).astype(low))
            attended[here, h * HEAD_DIM : (h + 1) * HEAD_DIM] = out.T.astype(low)
            lse[pl.ds(here_at * heads + h, 1), :] = highest + jnp.log(totals)
        for k in range(owners):
            j = here_at * owners + k

            @pl.when(j != i)
            def _():
                to_owner(j).start()

        @pl.when(turn == (areas - 1) // 2)
        def _():
            up_g.close()
            cot_line.step(1)

        @pl.when(turn == areas - 1)
        def _():
            merge_g.relay()
            down_g.start()

        return carry

    lax.fori_loop(0, areas, attend_area, 0)
    att_rows[:, pl.ds(pl.multiple_of(i * head_cols, head_cols), head_cols)] = attended[
        rows_of(i, rows), :
    ]
    if n > 2:
        cot_line.step(2)
    merge_g.close()
    keep_merge.start()
    for turn in range(1, n):
        from_source(lax.rem(i + turn, n)).wait_recv()
    squares = jnp.zeros((rows, 1), f32)
    for at in tiles(width):
        out = mm(att_rows[...], merge[:, at])
        attn_out[:, at] = out
        v = x_own[:, at].astype(f32) + table[i, 2:3, at] * out
        middle[:, at] = v
        squares += jnp.sum(v * v, axis=1, keepdims=True)
    root = lax.rsqrt(squares * (1.0 / width) + 1e-06)
    for at in tiles(width):
        v = middle[:, at] * root
        hidden_second[:, at] = (v * (1.0 + table[i, 4:5, at]) + table[i, 3:4, at]).astype(low)
    keeps = [
        pltpu.make_async_copy(source, target, out_sem.at[4 + k])
        for k, (source, target) in enumerate(
            (
                (attended, attended_out),
                (attn_out, attn_out_hbm),
                (middle, middle_out),
                (hidden_second, second_out),
            )
        )
    ]
    for keep in keeps:
        keep.start()
    down_g.relay()
    for s in range(3, n):
        cot_line.step(s)
    down_g.close()
    for copy in copies[2:]:
        copy.wait()
    keep_attend.wait()
    keep_merge.wait()
    keep_hidden.wait()
    keep_qkv.wait()
    for keep in keeps:
        keep.wait()
    for flip in range(1, n_dp):
        to_plane(noise, noise_all, noise_sem, flip).wait_send()
        to_plane(terms, terms_all, terms_sem, flip).wait_send()
    for line in (merge_line, x_line, cot_line):
        line.finish()
    for turn in range(1, n):
        to_line(turn).wait_send()
    for turn in range(1, n):
        to_owner(lax.rem(i + turn, n)).wait_send()
    for weight in weights:
        weight.finish()


def front(n, n_dp, x, cot, noise, mod_w, sizes, attend_w, merge_w, up_w, down_w, number):
    rows, width = x.shape
    k_rows, own_cols = mod_w.shape
    wide = attend_w.shape[1]
    heads = wide // (3 * HEAD_DIM)
    total = n * rows
    areas = total // min(256, total)
    pictures = noise.shape[0]
    low, f32 = jnp.bfloat16, jnp.float32
    sds = jax.ShapeDtypeStruct
    count = plane_sems(n_dp)
    return call(
        functools.partial(front_kernel, n, n_dp, heads, 512),
        number,
        "front",
        [VMEM, HBM, VMEM, VMEM, pl.BlockSpec(memory_space=pltpu.SMEM), VMEM, VMEM, HBM, HBM],
        [
            sds((total, width), low),
            sds((total, width), low),
            sds((total, wide), low),
            sds((areas * heads, total // areas), f32),
            sds((total, heads * HEAD_DIM), low),
            sds((rows, width), f32),
            sds((rows, width), f32),
            sds((rows, width), low),
            sds((n, 8, width), f32),
            sds((n_dp * k_rows, wide), low),
            sds((merge_w.shape[0], width), low),
            sds((n_dp * k_rows, up_w.shape[1]), low),
            sds((down_w.shape[0], n_dp * down_w.shape[1]), low),
            sds((n_dp, pictures, k_rows), f32),
        ],
        [HBM] * 3 + [VMEM] + [HBM] * 4 + [VMEM] + [HBM] * 4 + [VMEM],
        [
            pltpu.VMEM((total, width), low),
            pltpu.VMEM((n_dp * k_rows, wide), low),
            pltpu.VMEM((n * merge_w.shape[0], n_dp * merge_w.shape[1]), low),
            pltpu.VMEM((n_dp, pictures, k_rows), f32),
            pltpu.VMEM((total, width), low),
            pltpu.VMEM((total, wide), low),
            pltpu.VMEM((total, heads * HEAD_DIM), low),
            pltpu.VMEM((rows, width), low),
            pltpu.VMEM((rows, width), f32),
            pltpu.VMEM((rows, width), f32),
            pltpu.VMEM((rows, width), low),
            pltpu.VMEM((n_dp, pictures, own_cols), f32),
            pltpu.VMEM((n_dp, pictures, own_cols), f32),
            pltpu.VMEM((n, pictures, own_cols), f32),
            DMA((2, n_dp)),
            DMA((2, n_dp)),
            DMA((3, n)),
            DMA((3, n)),
            DMA((3, n)),
            DMA((3, n)),
            DMA((4, count)),
            DMA((4, count)),
            DMA((8,)),
            DMA((2, n)),
            DMA((5,)),
        ],
        flops=2 * total * width * wide,
    )(x, cot, noise, mod_w, sizes, attend_w, merge_w, up_w, down_w)


class PlaneScatter:
    def __init__(self, n_dp, d, theirs, own, swapped, via, landed, sems):
        self.chips, self.d, self.square = n_dp // 2, d, n_dp == 8
        self.chip, self.side = d // 2, lax.rem(d, 2)
        self.theirs, self.own, self.swapped, self.via = theirs, own, swapped, via
        self.landed, self.sems = landed, sems

    def remote(self, source, target, sent, came, device):
        return pltpu.make_async_remote_copy(
            src_ref=source,
            dst_ref=target,
            send_sem=sent,
            recv_sem=came,
            device_id=(device, lax.axis_index("tensor")),
            device_id_type=MESH,
        )

    def swap(self, m):
        return self.remote(
            self.theirs(m), self.swapped.at[m], self.sems.at[0, m], self.sems.at[1, m], self.d ^ 1
        )

    def half(self, ref, which):
        height = self.own.shape[1] // 2
        return ref.at[pl.ds(which * height, height), :]

    def step(self, k):
        slab, which, peer = ((1, 0, 1), (3, 0, 1), (2, 1, 2), (3, 1, 2), (2, 0, 2), (1, 1, 1))[k]
        target = self.via if slab == 3 else self.landed.at[1 if k < 4 else 2]
        return self.remote(
            self.half(self.own.at[self.chip ^ slab], which),
            self.half(target, which),
            self.sems.at[2, k],
            self.sems.at[3, k],
            2 * (self.chip ^ peer) + self.side,
        )

    def send(self, m, slot, sem):
        return self.remote(
            self.own.at[m],
            self.landed.at[slot],
            self.sems.at[2, m],
            self.sems.at[3, sem],
            2 * m + self.side,
        )

    def keep(self):
        slot = 0 if self.square else self.chip
        return pltpu.make_async_copy(
            self.own.at[self.chip], self.landed.at[slot], self.sems.at[2, 6 if self.square else self.chip]
        )

    def swap_all(self):
        def one(m, carry):
            self.swap(m).start()
            return carry

        lax.fori_loop(0, self.chips, one, 0)

    def add(self, target, source):
        height, wide = target.shape
        chunk = math.gcd(height, 64 if wide > 512 else 256)

        def one(c, carry):
            at = pl.ds(pl.multiple_of(c * chunk, chunk), chunk)
            total = target[at, :].astype(jnp.float32) + source[at, :].astype(jnp.float32)
            target[at, :] = total.astype(target.dtype)
            return carry

        lax.fori_loop(0, height // chunk, one, 0)

    def add_and_send(self):
        def one(k, carry):
            m = self.chip ^ (self.chips - 1 - k)
            self.swap(m).wait_recv()
            self.add(self.own.at[m], self.swapped.at[m])
            if not self.square:

                @pl.when(m != self.chip)
                def _():
                    self.send(m, self.chip, self.chip).start()

            return carry

        lax.fori_loop(0, self.chips, one, 0)
        if self.square:
            for k in (1, 3, 0, 2):
                self.step(k).start()
        self.keep().start()

    def relay(self):
        if self.square:
            for k, slab, which in ((1, 2, 0), (3, 1, 1)):
                self.step(k).wait_recv()
                self.step(k).wait_send()
                self.add(self.half(self.own.at[self.chip ^ slab], which), self.half(self.via, which))
                self.step(4 if k == 1 else 5).start()

    def landed_all(self):
        if self.square:
            for k in (0, 2, 4, 5):
                self.step(k).wait_recv()
        else:
            for k in range(1, self.chips):
                self.send(self.chip ^ k, self.chip ^ k, self.chip ^ k).wait_recv()
        self.keep().wait()

    def finish(self):
        for m in range(self.chips):
            self.swap(m).wait_send()
        if self.square:
            for k in (0, 2, 4, 5):
                self.step(k).wait_send()
        else:
            for k in range(1, self.chips):
                self.send(self.chip ^ k, self.chip, self.chip).wait_send()


def plane_slots(n_dp):
    return 3 if n_dp == 8 else n_dp // 2


def scatter_sems(n_dp):
    return DMA((4, max(7, n_dp // 2)))


def flows(n, pieces, sums, turn):
    far, rest = turn // ((n - 2) * pieces), lax.rem(turn, (n - 2) * pieces)
    t, c = n - 1 - rest // pieces, lax.rem(rest, pieces)
    for near in (True, False):

        @pl.when(far == (0 if near else 1))
        def _():
            sums.pass_on(t, c, near)


def back_kernel(
    n,
    n_dp,
    heads,
    tile,
    d_hidden,
    middle,
    table,
    lse,
    sizes,
    cot_hbm,
    out_hbm,
    rows_hbm,
    qkv_hbm,
    mlp_hbm,
    merge_hbm,
    up_hbm,
    down_hbm,
    block_out,
    d_middle_out,
    d_qkv_out,
    sums_out,
    merge_grad,
    up_landed,
    down_landed,
    cot,
    attn_out,
    d_middle,
    d_qkv,
    attended,
    qkv,
    part,
    got,
    merge,
    d_att,
    d_attn,
    d_keys,
    d_values,
    up_own,
    up_swapped,
    up_via,
    down_own,
    down_swapped,
    down_via,
    stage,
    mlp_sent,
    mlp_came,
    up_sems,
    down_sems,
    line_sem,
    merge_sem,
    load_sem,
    stage_sem,
    own_sem,
):
    d, i = lax.axis_index("dp"), lax.axis_index("tensor")
    rows, width = middle.shape
    low, f32 = jnp.bfloat16, jnp.float32
    head_cols = heads * HEAD_DIM
    chips = n_dp // 2
    k_rows, down_cols = up_own.shape[1], down_own.shape[2]
    side = lax.rem(d, 2)

    def up_slab(at):
        return up_hbm.at[pl.ds(pl.multiple_of(at * k_rows, k_rows), k_rows), :]

    def down_slab(at):
        return down_hbm.at[:, pl.ds(pl.multiple_of(at * down_cols, down_cols), down_cols)]

    load_mlp = pltpu.make_async_copy(mlp_hbm, part, load_sem.at[0])
    load_mlp.start()
    load_cot = pltpu.make_async_copy(cot_hbm, cot, load_sem.at[3])
    load_out = pltpu.make_async_copy(out_hbm, attn_out, load_sem.at[4])
    load_cot.start()
    load_out.start()
    load_rows = pltpu.make_async_copy(rows_hbm, attended, load_sem.at[1])
    load_qkv = pltpu.make_async_copy(qkv_hbm, qkv, load_sem.at[2])

    load_merge = pltpu.make_async_copy(merge_hbm, merge, merge_sem)
    load_merge.start()
    for m in range(chips):
        pltpu.make_async_copy(up_slab(2 * m + side), up_own.at[m], own_sem.at[0, m]).start()
        pltpu.make_async_copy(down_slab(2 * m + side), down_own.at[m], own_sem.at[1, m]).start()
    load_rows.start()
    load_qkv.start()
    greet_all(n, n_dp, d, i)
    up = PlaneScatter(
        n_dp, d, lambda m: up_slab(2 * m + 1 - side), up_own, up_swapped, up_via, up_landed, up_sems
    )
    down = PlaneScatter(
        n_dp,
        d,
        lambda m: down_slab(2 * m + 1 - side),
        down_own,
        down_swapped,
        down_via,
        down_landed,
        down_sems,
    )
    up.swap_all()
    down.swap_all()
    load_mlp.wait()
    piece = tile // 2
    sums = LineScatter(n, i, rows, piece, part, got, mlp_sent, mlp_came)
    pieces = sums.pieces

    def ends(k, carry):
        t, c = n - 1 - k // pieces, lax.rem(k, pieces)
        pl.when(i == 0)(functools.partial(sums.at_end, t, c))
        pl.when(i == n - 1)(functools.partial(sums.at_end, n - 1 - t, c))
        return carry

    tiles = [slice(c * tile, (c + 1) * tile) for c in range(width // tile)]
    own_rows = rows_of(i, rows)
    squares = jnp.zeros((rows, 1), f32)
    for at in tiles:
        squares += jnp.sum(middle[:, at] * middle[:, at], axis=1, keepdims=True)
    root = lax.rsqrt(squares * (1.0 / width) + 1e-06)
    mean = jnp.zeros((rows, 1), f32)
    for at in tiles:
        v = middle[:, at] * root
        dh = d_hidden[:, at]
        mean += jnp.sum(dh * (1.0 + table[i, 4:5, at]) * v, axis=1, keepdims=True)
        sums_out[3:4, at] = jnp.sum(dh, axis=0, keepdims=True)
        sums_out[4:5, at] = jnp.sum(dh * v, axis=0, keepdims=True)
    mean = mean * (1.0 / width)
    load_cot.wait()
    load_out.wait()
    for at in tiles:
        v = middle[:, at] * root
        u = d_hidden[:, at] * (1.0 + table[i, 4:5, at])
        dm = cot[:, at].astype(f32) + root * (u - v * mean)
        d_middle[:, at] = dm
        d_attn[own_rows, at] = (table[i, 2:3, at] * dm).astype(low)
        sums_out[2:3, at] = jnp.sum(dm * attn_out[:, at], axis=0, keepdims=True)

    keep_middle = pltpu.make_async_copy(d_middle, d_middle_out, load_sem.at[5])
    keep_middle.start()

    line = LineGather(
        n, i, rows, d_attn.at[own_rows], d_attn, line_sem.at[0], line_sem.at[1], line_sem.at[2]
    )
    first_core = side == 0

    def send_rows():
        line.start()
        lax.fori_loop(0, (n - 1) * pieces, ends, 0)

    pl.when(first_core)(send_rows)
    for m in range(chips):
        pltpu.make_async_copy(up_slab(2 * m + side), up_own.at[m], own_sem.at[0, m]).wait()
        pltpu.make_async_copy(down_slab(2 * m + side), down_own.at[m], own_sem.at[1, m]).wait()
    load_rows.wait()
    load_qkv.wait()
    load_merge.wait()

    area = lse.shape[1]
    areas = n * rows // area
    area_images = [image_at(sizes, b * area) for b in range(areas)]
    d_keys[...] = jnp.zeros_like(d_keys)
    d_values[...] = jnp.zeros_like(d_values)
    turns = 2 * max(n - 2, 0) * pieces
    scale = HEAD_DIM ** (-0.5)

    def back_area(here_at, carry):
        here = rows_of(here_at, area)
        image = image_at(sizes, here_at * area)
        for h in range(heads):
            first = h * 3 * HEAD_DIM
            head = slice(h * HEAD_DIM, (h + 1) * HEAD_DIM)
            q = qkv[here, first : first + HEAD_DIM]
            g = d_att[here, head]
            log_row = lse[pl.ds(here_at * heads + h, 1), :]
            probs, d_probs = [], []
            inner = jnp.zeros((1, area), f32)
            for b in range(areas):
                key = qkv[b * area : (b + 1) * area, first + HEAD_DIM : first + 2 * HEAD_DIM]
                value = qkv[b * area : (b + 1) * area, first + 2 * HEAD_DIM : first + 3 * HEAD_DIM]
                scores = mm_nt(key, q) * scale + jnp.where(image == area_images[b], 0.0, MASKED)
                probs.append(jnp.exp(scores - log_row))
                d_probs.append(mm_nt(value, g))
                inner += jnp.sum(probs[b] * d_probs[b], axis=0, keepdims=True)
            d_query = jnp.zeros((HEAD_DIM, area), f32)
            for b in range(areas):
                at = slice(b * area, (b + 1) * area)
                key = qkv[at, first + HEAD_DIM : first + 2 * HEAD_DIM]
                d_scores = (probs[b] * (d_probs[b] - inner)).astype(low)
                d_values[at, head] += mm(probs[b].astype(low), g)
                d_keys[at, head] += mm(d_scores, q)
                d_query += mm_tn(key, d_scores)
            d_qkv[here, first : first + HEAD_DIM] = (d_query * scale).T.astype(low)

        return carry

    def pass_by(turn, carry):
        flows(n, pieces, sums, turn)
        return carry

    early = min(turns, pieces)

    def visit(q, carry):
        s = (q + 1) // 2
        j = i + s * (1 - 2 * (q % 2))

        @pl.when(q % 2 == 1)
        def _():
            line.step(s)

        @pl.when((j >= 0) & (j < n))
        def _():
            here = rows_of(j, rows)
            d_att[here, :] = mm_nt(d_attn[here, :], merge[...]).astype(low)
            if area == rows:
                back_area(j, 0)

        @pl.when((q == 0) & jnp.logical_not(first_core))
        def _():
            send_rows()

        @pl.when(q == 0)
        def _():
            up.add_and_send()
            down.add_and_send()

        @pl.when(q == 2 * (n - 2))
        def _():
            up.relay()
            lax.fori_loop(0, early, pass_by, 0)

        return carry

    lax.fori_loop(0, 2 * n - 1, visit, 0)
    if area != rows:
        lax.fori_loop(0, areas, back_area, 0)
    for h in range(heads):
        first = h * 3 * HEAD_DIM
        head = slice(h * HEAD_DIM, (h + 1) * HEAD_DIM)
        d_qkv[:, first + HEAD_DIM : first + 2 * HEAD_DIM] = (d_keys[:, head] * scale).astype(low)
        d_qkv[:, first + 2 * HEAD_DIM : first + 3 * HEAD_DIM] = d_values[:, head].astype(low)
    keep_qkv = pltpu.make_async_copy(d_qkv, d_qkv_out, load_sem.at[6])
    keep_qkv.start()
    wide = width // tile
    short = stage.shape[1]

    def square(row, column):
        return merge_grad.at[
            pl.ds(pl.multiple_of(row * short, short), short),
            pl.ds(pl.multiple_of(column * tile, tile), tile),
        ]

    def merge_one(k, carry):
        row, column = k // wide, lax.rem(k, wide)
        slot = lax.rem(k, 2)

        @pl.when(k >= 2)
        def _():
            pltpu.make_async_copy(stage.at[slot], square(0, 0), stage_sem.at[slot]).wait()

        a = attended[:, pl.ds(pl.multiple_of(row * short, short), short)]
        b = d_attn[:, pl.ds(pl.multiple_of(column * tile, tile), tile)]
        stage[slot] = mm_tn(a, b).astype(low)
        pltpu.make_async_copy(stage.at[slot], square(row, column), stage_sem.at[slot]).start()
        return carry

    lax.fori_loop(0, attended.shape[1] // short * wide, merge_one, 0)
    for slot in range(2):
        pltpu.make_async_copy(stage.at[slot], square(0, 0), stage_sem.at[slot]).wait()
    lax.fori_loop(early, turns, pass_by, 0)
    for c in range(pieces):
        at = slice(c * piece, (c + 1) * piece)
        total = sums.own_value(c)
        block_out[:, at] = (middle[:, at] + table[i, 5:6, at] * total).astype(low)
        sums_out[5:6, at] = jnp.sum(cot[:, at].astype(f32) * total, axis=0, keepdims=True)
    sums_out[0:2, :] = jnp.zeros((2, width), f32)
    sums_out[6:8, :] = jnp.zeros((2, width), f32)
    down.relay()
    keep_middle.wait()
    keep_qkv.wait()
    for scatter in (up, down):
        scatter.landed_all()
        scatter.finish()
    line.finish()
    sums.all_sent()


def back(n, n_dp, operands, shapes, number, tile=512):
    (rows, width), wide, units, k_rows, down_cols, areas = shapes
    heads = wide // (3 * HEAD_DIM)
    total, chips, pieces = n * rows, n_dp // 2, 2 * width // tile
    low, f32 = jnp.bfloat16, jnp.float32
    sds = jax.ShapeDtypeStruct
    return call(
        functools.partial(back_kernel, n, n_dp, heads, tile),
        number,
        "back",
        [VMEM] * 4 + [pl.BlockSpec(memory_space=pltpu.SMEM)] + [HBM] * 8,
        [
            sds((rows, width), low),
            sds((rows, width), f32),
            sds((total, wide), low),
            sds((8, width), f32),
            sds((heads * HEAD_DIM, width), low),
            sds((plane_slots(n_dp), k_rows, units), low),
            sds((plane_slots(n_dp), units, down_cols), low),
        ],
        [VMEM, HBM, HBM, VMEM] + [HBM] * 3,
        [
            pltpu.VMEM((rows, width), low),
            pltpu.VMEM((rows, width), f32),
            pltpu.VMEM((rows, width), f32),
            pltpu.VMEM((total, wide), low),
            pltpu.VMEM((total, heads * HEAD_DIM), low),
            pltpu.VMEM((total, wide), low),
            pltpu.VMEM((total, width), low),
            pltpu.VMEM((total + rows, width), low),
            pltpu.VMEM((heads * HEAD_DIM, width), low),
            pltpu.VMEM((total, heads * HEAD_DIM), low),
            pltpu.VMEM((total, width), low),
            pltpu.VMEM((total, heads * HEAD_DIM), f32),
            pltpu.VMEM((total, heads * HEAD_DIM), f32),
            pltpu.VMEM((chips, k_rows, units), low),
            pltpu.VMEM((chips, k_rows, units), low),
            pltpu.VMEM((k_rows, units), low),
            pltpu.VMEM((chips, units, down_cols), low),
            pltpu.VMEM((chips, units, down_cols), low),
            pltpu.VMEM((units, down_cols), low),
            pltpu.VMEM((2, tile // 2, tile), low),
            DMA((n, pieces)),
            DMA((n + 1, pieces)),
            scatter_sems(n_dp),
            scatter_sems(n_dp),
            DMA((3, n)),
            DMA,
            DMA((7,)),
            DMA((2,)),
            DMA((2, chips)),
        ],
        flops=20 * total * total * wide // 3,
    )(*operands)


def last_kernel(
    n,
    n_dp,
    tile,
    d_qkv,
    sums_in,
    table,
    sizes,
    hidden_hbm,
    x_hbm,
    middle_hbm,
    mod_hbm,
    merge_hbm,
    attend_hbm,
    input_grad,
    d_mod_all,
    noise_sum,
    attend_landed,
    merge_landed,
    hidden,
    x_own,
    d_middle,
    mod_w,
    attend,
    part,
    got,
    grad_own,
    grad_theirs,
    grad_swapped,
    grad_via,
    merge_own,
    merge_swapped,
    merge_via,
    sums_all,
    shares,
    shares_all,
    terms,
    terms_all,
    noise_parts,
    sent,
    came,
    grad_sems,
    merge_sems,
    share_sem,
    mod_sem,
    term_sem,
    noise_sem,
    load_sem,
    own_sem,
    attend_sem,
):
    d, i = lax.axis_index("dp"), lax.axis_index("tensor")
    rows, width = input_grad.shape
    low, f32 = jnp.bfloat16, jnp.float32
    chips = n_dp // 2
    side = lax.rem(d, 2)
    k_rows, own_cols = mod_w.shape
    merge_cols = merge_own.shape[2]
    images = d_mod_all.shape[1]

    def merge_slab(at):
        return merge_hbm.at[:, pl.ds(pl.multiple_of(at * merge_cols, merge_cols), merge_cols)]

    load_hidden, load_x, load_middle, load_mod = (
        pltpu.make_async_copy(source, target, load_sem.at[k])
        for k, (source, target) in enumerate(
            (
                (hidden_hbm, hidden),
                (x_hbm, x_own),
                (middle_hbm, d_middle),
                (mod_hbm, mod_w),
            )
        )
    )

    def load_attend(c):
        at = pl.ds(pl.multiple_of(c * tile, tile), tile)
        return pltpu.make_async_copy(attend_hbm.at[at, :], attend.at[at, :], attend_sem.at[c])

    for c in range(width // tile):
        load_attend(c).start()
    for m in range(chips):
        pltpu.make_async_copy(merge_slab(2 * m + side), merge_own.at[m], own_sem.at[m]).start()
    greet_all(n, n_dp, d, i)
    merge = PlaneScatter(
        n_dp,
        d,
        lambda m: merge_slab(2 * m + 1 - side),
        merge_own,
        merge_swapped,
        merge_via,
        merge_landed,
        merge_sems,
    )
    grad = PlaneScatter(
        n_dp, d, lambda m: grad_theirs.at[m], grad_own, grad_swapped, grad_via, attend_landed, grad_sems
    )
    merge.swap_all()
    for late in (load_hidden, load_x, load_middle, load_mod):
        late.start()
    piece = tile // 2
    sums = LineScatter(n, i, rows, piece, part, got, sent, came)
    pieces = sums.pieces

    def partial_block(q, carry):
        j = jnp.where(2 * i < n - 1, n - 1 - q, q)
        here = rows_of(j, rows)

        def one(c, inner):
            at = pl.ds(pl.multiple_of(c * tile, tile), tile)

            @pl.when(q == 0)
            def _():
                load_attend(c).wait()

            part[here, at] = mm_nt(d_qkv[here, :], attend[at, :]).astype(low)
            for k in range(tile // piece):
                sums.at_end(j, c * (tile // piece) + k)
            return inner

        lax.fori_loop(0, width // tile, one, 0)
        return carry

    partial_block(0, 0)
    for m in range(chips):
        pltpu.make_async_copy(merge_slab(2 * m + side), merge_own.at[m], own_sem.at[m]).wait()
    merge.add_and_send()
    lax.fori_loop(1, n, partial_block, 0)

    def slab_grad(at):
        columns = pl.ds(pl.multiple_of(at * k_rows, k_rows), k_rows)
        return mm_tn(hidden[:, columns], d_qkv[...]).astype(low)

    def for_them(m, carry):
        grad_theirs[m] = slab_grad(2 * m + 1 - side)
        grad.swap(m).start()
        return carry

    def for_us(m, carry):
        grad_own[m] = slab_grad(2 * m + side)
        return carry

    load_hidden.wait()
    lax.fori_loop(0, chips, for_them, 0)
    lax.fori_loop(0, chips, for_us, 0)
    grad.add_and_send()
    merge.relay()
    turns = 2 * max(n - 2, 0) * pieces

    def pass_by(turn, carry):
        flows(n, pieces, sums, turn)
        return carry

    lax.fori_loop(0, turns, pass_by, 0)

    grad.relay()

    for late in (load_x, load_middle, load_mod):
        late.wait()
    tiles = [slice(c * piece, (c + 1) * piece) for c in range(pieces)]
    squares = jnp.zeros((rows, 1), f32)
    for at in tiles:
        v = x_own[:, at].astype(f32)
        squares += jnp.sum(v * v, axis=1, keepdims=True)
    root = lax.rsqrt(squares * (1.0 / width) + 1e-06)
    mean = jnp.zeros((rows, 1), f32)
    sums_all[...] = sums_in[...]
    for c, at in enumerate(tiles):
        v = x_own[:, at].astype(f32) * root
        dh = sums.own_value(c)
        mean += jnp.sum(dh * (1.0 + table[i, 1:2, at]) * v, axis=1, keepdims=True)
        sums_all[0:1, at] = jnp.sum(dh, axis=0, keepdims=True)
        sums_all[1:2, at] = jnp.sum(dh * v, axis=0, keepdims=True)

    unit = math.gcd(width, own_cols)
    image = image_at(sizes, i * rows)
    for number in range(6):
        for start in range(0, width, unit):
            at = number * width + start
            for k in range(images):
                shares[at // own_cols, k : k + 1, at % own_cols : at % own_cols + unit] = (
                    sums_all[number : number + 1, start : start + unit]
                    * jnp.where(image == k, 1.0, 0.0)
                )

    def to_line(source, target, sems, turn, whole=False):
        t = lax.rem(i + turn, n)
        return pltpu.make_async_remote_copy(
            src_ref=source if whole else source.at[t],
            dst_ref=target.at[i],
            send_sem=sems.at[0, t],
            recv_sem=sems.at[1, i],
            device_id=(d, t),
            device_id_type=MESH,
        )

    def from_line(source, target, sems, turn, whole=False):
        t = lax.rem(i + turn, n)
        return pltpu.make_async_remote_copy(
            src_ref=source if whole else source.at[t],
            dst_ref=target.at[t],
            send_sem=sems.at[0, t],
            recv_sem=sems.at[1, t],
            device_id=(d, t),
            device_id_type=MESH,
        )

    def to_plane(source, target, sems, flip):
        return pltpu.make_async_remote_copy(
            src_ref=source,
            dst_ref=target.at[d],
            send_sem=sems.at[0, flip],
            recv_sem=sems.at[1, flip],
            device_id=(d ^ flip, i),
            device_id_type=MESH,
        )

    def from_plane(source, target, sems, flip):
        return pltpu.make_async_remote_copy(
            src_ref=source,
            dst_ref=target.at[d ^ flip],
            send_sem=sems.at[0, flip],
            recv_sem=sems.at[1, flip],
            device_id=(d ^ flip, i),
            device_id_type=MESH,
        )

    for turn in range(1, n):
        to_line(shares, shares_all, share_sem, turn).start()

    mean = mean * (1.0 / width)
    for c, at in enumerate(tiles):
        v = x_own[:, at].astype(f32) * root
        u = sums.own_total(c) * (1.0 + table[i, 1:2, at])
        input_grad[:, at] = (d_middle[:, at] + root * (u - v * mean)).astype(low)
    shares_all[i] = shares[i]
    for turn in range(1, n):
        from_line(shares, shares_all, share_sem, turn).wait_recv()
    d_mod_all[d] = jnp.sum(shares_all[...], axis=0).astype(low).astype(f32)
    own_mod = d_mod_all.at[d]
    for flip in range(1, n_dp):
        to_plane(own_mod, d_mod_all, mod_sem, flip).start()
    for flip in range(1, n_dp):
        from_plane(own_mod, d_mod_all, mod_sem, flip).wait_recv()
    flat = d_mod_all[...].reshape(n_dp * images, own_cols).astype(low)
    terms[...] = mm_nt(flat, mod_w[...]).reshape(n_dp, images, k_rows)
    for turn in range(1, n):
        to_line(terms, terms_all, term_sem, turn, True).start()
    terms_all[i] = terms[...]
    for turn in range(1, n):
        from_line(terms, terms_all, term_sem, turn, True).wait_recv()
    noise_parts[...] = jnp.sum(terms_all[...], axis=0)
    for flip in range(1, n_dp):
        to_plane(noise_parts.at[d ^ flip], noise_sum, noise_sem, flip).start()
    noise_sum[d] = noise_parts[d]
    for flip in range(1, n_dp):
        from_plane(noise_parts.at[d ^ flip], noise_sum, noise_sem, flip).wait_recv()
    merge.landed_all()
    grad.landed_all()
    grad.finish()
    merge.finish()
    for turn in range(1, n):
        to_line(shares, shares_all, share_sem, turn).wait_send()
        to_line(terms, terms_all, term_sem, turn, True).wait_send()
    for flip in range(1, n_dp):
        to_plane(own_mod, d_mod_all, mod_sem, flip).wait_send()
        to_plane(noise_parts.at[d ^ flip], noise_sum, noise_sem, flip).wait_send()
    sums.all_sent()


def last(n, n_dp, operands, shapes, number, tile=512):
    (rows, width), wide, k_rows, own_cols, (merge_rows, merge_cols), images = shapes
    total, chips, pieces = n * rows, n_dp // 2, 2 * width // tile
    low, f32 = jnp.bfloat16, jnp.float32
    sds = jax.ShapeDtypeStruct
    return call(
        functools.partial(last_kernel, n, n_dp, tile),
        number,
        "last",
        [VMEM] * 3 + [pl.BlockSpec(memory_space=pltpu.SMEM)] + [HBM] * 6,
        [
            sds((rows, width), low),
            sds((n_dp, images, own_cols), f32),
            sds((n_dp, images, k_rows), f32),
            sds((plane_slots(n_dp), k_rows, wide), low),
            sds((plane_slots(n_dp), merge_rows, merge_cols), low),
        ],
        [VMEM] * 3 + [HBM] * 2,
        [
            pltpu.VMEM((total, width), low),
            pltpu.VMEM((rows, width), low),
            pltpu.VMEM((rows, width), f32),
            pltpu.VMEM((k_rows, own_cols), low),
            pltpu.VMEM((width, wide), low),
            pltpu.VMEM((total, width), low),
            pltpu.VMEM((total + rows, width), low),
            pltpu.VMEM((chips, k_rows, wide), low),
            pltpu.VMEM((chips, k_rows, wide), low),
            pltpu.VMEM((chips, k_rows, wide), low),
            pltpu.VMEM((k_rows, wide), low),
            pltpu.VMEM((chips, merge_rows, merge_cols), low),
            pltpu.VMEM((chips, merge_rows, merge_cols), low),
            pltpu.VMEM((merge_rows, merge_cols), low),
            pltpu.VMEM((8, width), f32),
            pltpu.VMEM((n, images, own_cols), f32),
            pltpu.VMEM((n, images, own_cols), f32),
            pltpu.VMEM((n_dp, images, k_rows), f32),
            pltpu.VMEM((n, n_dp, images, k_rows), f32),
            pltpu.VMEM((n_dp, images, k_rows), f32),
            DMA((n, pieces)),
            DMA((n + 1, pieces)),
            scatter_sems(n_dp),
            scatter_sems(n_dp),
            DMA((2, n)),
            DMA((2, n_dp)),
            DMA((2, n)),
            DMA((2, n_dp)),
            DMA((4,)),
            DMA((chips,)),
            DMA((width // tile,)),
        ],
        flops=4 * total * width * wide,
    )(*operands)


def final_kernel(
    noise_own,
    noise_all,
    d_mod,
    noise_sums,
    up_in,
    down_in,
    attend_in,
    block_in,
    input_in,
    merge_in,
    block_out,
    input_out,
    noise_grad,
    attend_out,
    merge_out,
    up_out,
    down_out,
    modulate_out,
    up_slots,
    down_slots,
    attend_slots,
    merge_slots,
    up_sum,
    down_sum,
    attend_sum,
    merge_sum,
    modulate,
    block,
    inputs,
    sems,
):
    low, f32 = jnp.bfloat16, jnp.float32
    loads = [
        pltpu.make_async_copy(source, target, sems.at[0, k])
        for k, (source, target) in enumerate(
            (
                (up_in, up_slots),
                (down_in, down_slots),
                (attend_in, attend_slots),
                (merge_in, merge_slots),
                (block_in, block),
                (input_in, inputs),
            )
        )
    ]
    stores = [
        pltpu.make_async_copy(source, target, sems.at[1, k])
        for k, (source, target) in enumerate(
            (
                (up_sum, up_out),
                (down_sum, down_out),
                (attend_sum, attend_out),
                (merge_sum, merge_out),
                (block, block_out),
                (inputs, input_out),
                (modulate, modulate_out),
            )
        )
    ]
    for load in loads:
        load.start()
    n_dp, images, k_rows = noise_all.shape
    left = noise_all[...].reshape(n_dp * images, k_rows).astype(low)
    right = d_mod[...].reshape(n_dp * images, -1).astype(low)
    modulate[...] = mm_tn(left, right)
    stores[6].start()
    for k in range(n_dp):
        at = slice(k * k_rows, (k + 1) * k_rows)
        v = noise_own[:, at].astype(f32)
        gate = 1.0 / (1.0 + jnp.exp(-v))
        noise_grad[:, at] = noise_sums[k] * (gate * (1.0 + v * (1.0 - gate)))

    def add(slots, total):
        count, height, wide = slots.shape
        chunk = math.gcd(height, 32 if wide > 512 else 256)

        def one(c, carry):
            at = pl.ds(pl.multiple_of(c * chunk, chunk), chunk)
            total[at, :] = sum(slots[s, at, :].astype(f32) for s in range(count))
            return carry

        lax.fori_loop(0, height // chunk, one, 0)

    for k, (slots, total) in enumerate(
        (
            (up_slots, up_sum),
            (down_slots, down_sum),
            (attend_slots, attend_sum),
            (merge_slots, merge_sum),
        )
    ):
        loads[k].wait()
        add(slots, total)
        stores[k].start()
    for k in range(4, 6):
        loads[k].wait()
        stores[k].start()
    for store in stores:
        store.wait()


def final(noise_own, noise_all, d_mod, noise_sums, up, down, attend, block, inputs, merge):
    sds, f32 = jax.ShapeDtypeStruct, jnp.float32
    own_cols, k_rows = d_mod.shape[2], noise_all.shape[2]
    sums = [sds(a.shape[1:], f32) for a in (up, down, attend, merge)]
    modulate = sds((k_rows, own_cols), f32)
    return pl.pallas_call(
        final_kernel,
        out_shape=[
            sds(block.shape, block.dtype),
            sds(inputs.shape, inputs.dtype),
            sds(noise_own.shape, f32),
            sums[2],
            sums[3],
            sums[0],
            sums[1],
            modulate,
        ],
        in_specs=[VMEM] * 4 + [HBM] * 6,
        out_specs=[HBM, HBM, VMEM] + [HBM] * 5,
        scratch_shapes=[
            pltpu.VMEM(a.shape, a.dtype)
            for a in (up, down, attend, merge, *sums, modulate, block, inputs)
        ]
        + [DMA((2, 7))],
        compiler_params=pltpu.CompilerParams(vmem_limit_bytes=60 * 1024 * 1024),
        name="final",
    )(noise_own, noise_all, d_mod, noise_sums, up, down, attend, block, inputs, merge)


def on_device(
    block_input,
    cotangent,
    noise_embed,
    image_sizes,
    attend_weight,
    merge_weight,
    up_weight,
    down_weight,
    modulate_weight,
):
    n = lax.axis_size("tensor")
    n_dp = lax.axis_size("dp")
    rows, width = block_input.shape
    tokens = n * rows
    images = image_sizes.shape[1]
    k_rows = modulate_weight.shape[0]

    (
        cot_full,
        hidden_first,
        packed,
        lse,
        attended,
        attn_out,
        middle,
        hidden_second,
        table,
        attend_full,
        merge_full,
        up_full,
        down_full,
        noise_all,
    ) = front(
        n,
        n_dp,
        block_input,
        cotangent,
        noise_embed,
        modulate_weight,
        image_sizes,
        attend_weight,
        merge_weight,
        up_weight,
        down_weight,
        0,
    )
    d_hidden_second, mlp_part, up_local, down_local = ffn(
        n, hidden_second, table, cot_full, up_full, down_full, 1
    )
    units = up_full.shape[1]
    wide = packed.shape[1]
    (
        block_output,
        d_middle,
        d_qkv,
        row_sums,
        merge_local,
        up_landed,
        down_landed,
    ) = back(
        n,
        n_dp,
        (
            d_hidden_second,
            middle,
            table,
            lse,
            image_sizes,
            cotangent,
            attn_out,
            attended,
            packed,
            mlp_part,
            merge_full,
            up_local,
            down_local,
        ),
        (block_input.shape, wide, units, k_rows, down_weight.shape[1], lse.shape[0]),
        2,
    )
    input_grad, d_mod_all, noise_sums, attend_landed, merge_landed = last(
        n,
        n_dp,
        (
            d_qkv,
            row_sums,
            table,
            image_sizes,
            hidden_first,
            block_input,
            d_middle,
            modulate_weight,
            merge_local,
            attend_full,
        ),
        (
            block_input.shape,
            wide,
            k_rows,
            modulate_weight.shape[1],
            merge_weight.shape,
            images,
        ),
        3,
    )

    return tuple(
        final(
            noise_embed,
            noise_all,
            d_mod_all,
            noise_sums,
            up_landed,
            down_landed,
            attend_landed,
            block_output,
            input_grad,
            merge_landed,
        )
    )


def solution(mesh):
    whole_rows = P(("dp", "tensor"), None)
    by_dp = P("dp", None)
    tall = P("dp", "tensor")
    wide = P("tensor", "dp")
    return jax.shard_map(
        on_device,
        mesh=mesh,
        in_specs=(whole_rows, whole_rows, by_dp, by_dp, tall, wide, tall, wide, tall),
        out_specs=(whole_rows, whole_rows, by_dp, tall, wide, tall, wide, tall),
        check_vma=False,
    )
```
